32 devices in a mesh: seq: 8 (over z, y), mp: 4 (over x, core).
Axes of the slice: x: 2, y: 2, z: 4, core: 2. Of those that a mesh axis runs over, the one named last changes fastest.
Arguments:
- activations: bfloat16 [8192, 768], P('seq'), may hold values from -6 to 6
- cotangent: bfloat16 [8192, 768], P('seq'), may hold values from -6 to 6
- segments: int32 [8192], P('seq'), may hold values from 1 to 8, as said below
- dilated_heads: int32 [2], replicated, may hold values from 0 to 11, as said below
- owners: int32 [8], replicated, may hold values from 0 to 7, each once
- attn_weights: float32 [2, 4, 768, 768], P(None, None, 'seq', 'mp')
- attn_first: float32 [2, 4, 768, 768], P(None, None, 'seq', 'mp')
- attn_second: float32 [2, 4, 768, 768], P(None, None, 'seq', 'mp'), as said below
- attn_average: float32 [2, 4, 768, 768], P(None, None, 'seq', 'mp')
- attn_basis: float32 [2, 4, 8, 4, 192, 192], P(None, None, 'seq', 'mp'), as said below
- ffn_weights: float32 [2, 2, 768, 3072], P(None, None, 'seq', 'mp')
- ffn_first: float32 [2, 2, 768, 3072], P(None, None, 'seq', 'mp')
- ffn_second: float32 [2, 2, 768, 3072], P(None, None, 'seq', 'mp'), as said below
- ffn_average: float32 [2, 2, 768, 3072], P(None, None, 'seq', 'mp')
- ffn_basis: float32 [2, 2, 8, 4, 768, 768], P(None, None, 'seq', 'mp'), as said below
- split_biases: float32 [2, 4, 1152], P(None, 'mp'), may hold values from -1.8 to 1.8
- split_first: float32 [2, 4, 1152], P(None, 'mp')
- split_second: float32 [2, 4, 1152], P(None, 'mp'), as said below
- shared_vectors: float32 [2, 6, 768], replicated
- shared_first: float32 [2, 6, 768], replicated
- shared_second: float32 [2, 6, 768], replicated, as said below
Outputs:
- output: float32 [8192, 768], P('seq')
- input_grad: float32 [8192, 768], P('seq')
- attn_new: float32 [2, 4, 768, 768], P(None, None, 'seq', 'mp')
- attn_first_new: float32 [2, 4, 768, 768], P(None, None, 'seq', 'mp')
- attn_second_new: float32 [2, 3, 768, 768], P(None, None, 'seq', 'mp')
- projection_second: float32 [2, 768, 768], P(None, 'seq', 'mp')
- attn_average_new: float32 [2, 4, 768, 768], P(None, None, 'seq', 'mp')
- updated_ffn_weights: float32 [2, 2, 768, 3072], P(None, None, 'seq', 'mp')
- ffn_first_new: float32 [2, 2, 768, 3072], P(None, None, 'seq', 'mp')
- ffn_second_new: float32 [2, 2, 768, 3072], P(None, None, 'seq', 'mp')
- ffn_average_new: float32 [2, 2, 768, 3072], P(None, None, 'seq', 'mp')
- split_new: float32 [2, 4, 1152], P(None, 'mp')
- updated_split_first_moment: float32 [2, 4, 1152], P(None, 'mp')
- split_second_new: float32 [2, 4, 1152], P(None, 'mp')
- shared_new: float32 [2, 6, 768], replicated
- shared_first_new: float32 [2, 6, 768], replicated
- shared_second_new: float32 [2, 6, 768], replicated
- grad_norm: float32 [], replicated
The draws below stay inside these ranges and needn't reach their ends.
Inputs may be any that keep to these rules, and one draw needn't show every extreme that they name: `segments`: ids never fall and rise by one at each new document, starting at 1; there are 8 documents, and the i-th document boundary lies within 256 tokens of i * 1024. `dilated_heads`: 2 different head numbers, the last of them 12 - 1. `attn_basis`: every block [l, m, s, j] is an orthogonal matrix. `ffn_basis`: every block [l, m, s, j] is an orthogonal matrix. `attn_second`: positive. `ffn_second`: positive. `split_second`: positive. `shared_second`: positive.
All inputs are finite; a program needn't handle non-finite values.
Results may differ from the reference program's by a relative error of at most 0.03.
Values may be sent and summed in bfloat16 or wider, within the bound.
A program may use at most 192 MiB of HBM per device.

```python
import math
import jax
import jax.numpy as jnp
from jax import lax

D = 768
HEAD_TOTAL = 12
DH = 64
FF = 3072
WIN = 256
LAYERS = 2
STEP = 10
TOK_DEV = 1024
TOKENS = 8192
SLOTS = 8
SPLIT = 1152
N_SEQ = 8
N_MP = 4


def grad_size():
    return 1.0 / math.sqrt(LAYERS * (D * D * (3 * 0.36 + 0.5 / WIN) + D * FF * 0.51 + 8 * D + FF))


def attn_kind():
    return jnp.array([0.6, 0.6, 0.6, (0.5 / WIN) ** 0.5], jnp.float32)[None, :, None, None] * grad_size()


def ffn_kind():
    return jnp.array([0.3, 0.65], jnp.float32)[None, :, None, None] * grad_size()


def first_draw(key, shape, scale):
    return jax.random.normal(key, shape, jnp.float32) * scale


def second_draw(key, shape, scale):
    spread = jax.random.uniform(key, shape, jnp.float32, 0.0, math.log(4.0))
    return jnp.exp(spread) * scale * scale


def attn_spread():
    return jnp.array([D ** (-0.5), D ** (-0.5), D ** (-0.5), (WIN / D) ** 0.5], jnp.float32)[None, :, None, None]


def ffn_spread():
    return jnp.array([D ** (-0.5), FF ** (-0.5)], jnp.float32)[None, :, None, None]


def orthogonal(key, lead, width):
    sign_key, order_key = jax.random.split(key)
    signs = 2.0 * jax.random.randint(sign_key, lead + (width, 1), 0, 2).astype(jnp.float32) - 1.0
    scores = jax.random.randint(order_key, lead + (width,), 0, 1 << 20) * width + jnp.arange(width, dtype=jnp.int32)
    order = jnp.argsort(scores, axis=-1).astype(jnp.int32)
    column = order[..., None, :]
    index_of_row = jnp.arange(width, dtype=jnp.int32)[:, None]
    phase = (2 * index_of_row + 1) * column % (4 * width)
    table = jnp.cos(math.pi * phase.astype(jnp.float32) / (2.0 * width))
    amplitude = jnp.where(column == 0, math.sqrt(1.0 / width), math.sqrt(2.0 / width))
    return signs * amplitude * table


def draw_segments(key, part):
    key = jax.random.fold_in(key, 5)
    reach = TOK_DEV // 4
    offsets = jax.random.randint(key, (N_SEQ - 1,), -reach, reach + 1)
    ends = (jnp.arange(1, N_SEQ, dtype=jnp.int32) * TOK_DEV + offsets).astype(jnp.int32)
    places = jnp.arange(TOKENS, dtype=jnp.int32)
    return (1 + jnp.sum((ends[None, :] <= places[:, None]).astype(jnp.int32), axis=1)).astype(jnp.int32)


def draw_dilated_heads(key, part):
    key = jax.random.fold_in(key, 7)
    first_head = jax.random.randint(key, (1,), 0, HEAD_TOTAL - 1)
    return jnp.concatenate([first_head, jnp.array([HEAD_TOTAL - 1], jnp.int32)]).astype(jnp.int32)


def draw_attn_weights(key, part):
    key = jax.random.fold_in(key, 3)
    return jax.random.normal(key, (LAYERS, 4, D, D), jnp.float32) * attn_spread()


def draw_attn_average(key, part):
    key = jax.random.fold_in(key, 4)
    return jax.random.normal(key, (LAYERS, 4, D, D), jnp.float32) * attn_spread()


def draw_ffn_weights(key, part):
    key = jax.random.fold_in(key, 21)
    return jax.random.normal(key, (LAYERS, 2, D, FF), jnp.float32) * ffn_spread()


def draw_ffn_average(key, part):
    key = jax.random.fold_in(key, 22)
    return jax.random.normal(key, (LAYERS, 2, D, FF), jnp.float32) * ffn_spread()


def draw_attn_basis(key, part):
    key = jax.random.fold_in(key, 8)
    return orthogonal(key, (LAYERS, 4, SLOTS, N_MP), D // N_MP)


def draw_ffn_basis(key, part):
    key = jax.random.fold_in(key, 9)
    return orthogonal(key, (LAYERS, 2, SLOTS, N_MP), FF // N_MP)


def draw_attn_first(key, part):
    key = jax.random.fold_in(key, 11)
    return first_draw(key, (LAYERS, 4, D, D), attn_kind())


def draw_attn_second(key, part):
    key = jax.random.fold_in(key, 12)
    return second_draw(key, (LAYERS, 4, D, D), attn_kind())


def draw_ffn_first(key, part):
    key = jax.random.fold_in(key, 13)
    return first_draw(key, (LAYERS, 2, D, FF), ffn_kind())


def draw_ffn_second(key, part):
    key = jax.random.fold_in(key, 14)
    return second_draw(key, (LAYERS, 2, D, FF), ffn_kind())


def draw_split_first(key, part):
    key = jax.random.fold_in(key, 15)
    return first_draw(key, (LAYERS, N_MP, SPLIT), grad_size())


def draw_split_second(key, part):
    key = jax.random.fold_in(key, 16)
    return second_draw(key, (LAYERS, N_MP, SPLIT), grad_size())


def draw_shared_first(key, part):
    key = jax.random.fold_in(key, 17)
    return first_draw(key, (LAYERS, 6, D), grad_size())


def draw_shared_second(key, part):
    key = jax.random.fold_in(key, 18)
    return second_draw(key, (LAYERS, 6, D), grad_size())


def draw_shared_vectors(key, part):
    key = jax.random.fold_in(key, 10)
    noise_key, factor_key = jax.random.split(key)
    noise = jax.random.normal(noise_key, (LAYERS, 6, D), jnp.float32) * 0.3
    ramp = 0.5 + jnp.arange(D, dtype=jnp.float32) / (D - 1)
    gains = ramp[None, None, :] * jnp.exp(jax.random.uniform(factor_key, (LAYERS, 6, D), jnp.float32, -0.2, 0.2))
    is_gain = jnp.array([0, 1, 0, 0, 1, 0], jnp.int32) == 1
    return jnp.where(is_gain[None, :, None], gains, noise)


def level_of(key, shape, cuts, low, largest):
    loudness, own = 1.0, jax.random.fold_in(key, 6)
    for dim, blocks in cuts:
        heights = jnp.exp(jax.random.uniform(jax.random.fold_in(own, dim), (blocks,), jnp.float32, low / len(cuts), largest / len(cuts)))
        loudness = loudness * jnp.repeat(heights, shape[dim] // blocks).reshape([-1 if axis == dim else 1 for axis in range(len(shape))])
    return loudness


def normal_values(rng, shape, scale, limit, pieces=(), kind=jnp.bfloat16):
    entries = jax.random.normal(rng, shape, jnp.float32) * scale
    if len(pieces) > 0:
        entries = level_of(rng, shape, pieces, -0.22, 0.18) * entries
    return jnp.clip(entries, min=-limit, max=limit).astype(kind)


def setup_inputs(seed: int = 0) -> dict:
    arg_keys = jax.random.split(jax.random.key(seed), 22)
    activations = normal_values(arg_keys[0], (TOKENS, D), 1.0, 6.0, ((0, 8),))
    cotangent = normal_values(arg_keys[1], (TOKENS, D), 1.0, 6.0, ((0, 8),))
    segments = draw_segments(jax.random.fold_in(arg_keys[21], 71), 0)
    dilated_heads = draw_dilated_heads(jax.random.fold_in(arg_keys[21], 71), 0)
    owners = jax.random.permutation(arg_keys[4], SLOTS).astype(jnp.int32)
    attn_weights = draw_attn_weights(jax.random.fold_in(arg_keys[21], 71), 0)
    attn_first = draw_attn_first(jax.random.fold_in(arg_keys[21], 71), 0)
    attn_second = draw_attn_second(jax.random.fold_in(arg_keys[21], 71), 0)
    attn_average = draw_attn_average(jax.random.fold_in(arg_keys[21], 71), 0)
    attn_basis = draw_attn_basis(jax.random.fold_in(arg_keys[21], 71), 0)
    ffn_weights = draw_ffn_weights(jax.random.fold_in(arg_keys[21], 71), 0)
    ffn_first = draw_ffn_first(jax.random.fold_in(arg_keys[21], 71), 0)
    ffn_second = draw_ffn_second(jax.random.fold_in(arg_keys[21], 71), 0)
    ffn_average = draw_ffn_average(jax.random.fold_in(arg_keys[21], 71), 0)
    ffn_basis = draw_ffn_basis(jax.random.fold_in(arg_keys[21], 71), 0)
    split_biases = normal_values(arg_keys[15], (LAYERS, N_MP, SPLIT), 0.3, 1.8, ((1, 4),), jnp.float32)
    split_first = draw_split_first(jax.random.fold_in(arg_keys[21], 71), 0)
    split_second = draw_split_second(jax.random.fold_in(arg_keys[21], 71), 0)
    shared_vectors = draw_shared_vectors(jax.random.fold_in(arg_keys[21], 71), 0)
    shared_first = draw_shared_first(jax.random.fold_in(arg_keys[21], 71), 0)
    shared_second = draw_shared_second(jax.random.fold_in(arg_keys[21], 71), 0)
    return dict(activations=activations, cotangent=cotangent, segments=segments, dilated_heads=dilated_heads, owners=owners, attn_weights=attn_weights, attn_first=attn_first, attn_second=attn_second, attn_average=attn_average, attn_basis=attn_basis, ffn_weights=ffn_weights, ffn_first=ffn_first, ffn_second=ffn_second, ffn_average=ffn_average, ffn_basis=ffn_basis, split_biases=split_biases, split_first=split_first, split_second=split_second, shared_vectors=shared_vectors, shared_first=shared_first, shared_second=shared_second)


HIGHEST_PRECISION = lax.Precision.HIGHEST
NORM_EPSILON = 1e-05
MASK_FILL = -1e+30
CLIP_LEVEL = 1.0
BETA_FIRST = 0.5
BETA_SECOND = 0.5
ADAM_EPSILON = 1e-08
DECAY_RATE = 0.01
AVERAGE_RATE = 0.7
VECTOR_RATE = 0.3

@jax.custom_vjp
def low(v):
    return lax.optimization_barrier(v.astype(jnp.bfloat16)).astype(jnp.float32)

@jax.custom_vjp
def low_back(v):
    return v

def low_keep(v):
    return (low(v), None)

def low_pass(kept, grad):
    return (grad,)

def back_keep(v):
    return (v, None)

def back_low(kept, grad):
    return (low(grad),)
low.defvjp(low_keep, low_pass)
low_back.defvjp(back_keep, back_low)

def normalize_layer(values, gain, shift):
    center = values - lax.optimization_barrier(jnp.mean(values, axis=-1, keepdims=True))
    spread = lax.optimization_barrier(jnp.mean(center * center, axis=-1, keepdims=True))
    return center * lax.rsqrt(spread + NORM_EPSILON) * gain + shift

def head_masks(offsets, dilated):
    near = jnp.abs(offsets) <= WIN
    far = jnp.logical_and(jnp.abs(offsets) <= 2 * WIN, offsets % 2 == 0)
    return jnp.where(dilated[:, None, None], far[None, :, :], near[None, :, :])

def attention(query, keys, values, segments, dilated):
    rim_width = 2 * WIN
    block_rows = min(512, TOK_DEV)
    key_rows = block_rows + 2 * rim_width
    pad_rows = ((rim_width, rim_width), (0, 0), (0, 0))
    key_pad = jnp.pad(keys, pad_rows)
    value_pad = jnp.pad(values, pad_rows)
    seg_pad = jnp.pad(segments, (rim_width, rim_width))
    offsets = jnp.arange(block_rows, dtype=jnp.int32)[:, None] - jnp.arange(key_rows, dtype=jnp.int32)[None, :] + rim_width
    window = head_masks(offsets, dilated)

    def one_block(first_row):
        query_block = lax.dynamic_slice_in_dim(query, first_row, block_rows, 0)
        key_block = lax.dynamic_slice_in_dim(key_pad, first_row, key_rows, 0)
        value_block = lax.dynamic_slice_in_dim(value_pad, first_row, key_rows, 0)
        seg_query = lax.dynamic_slice_in_dim(segments, first_row, block_rows, 0)
        seg_keys = lax.dynamic_slice_in_dim(seg_pad, first_row, key_rows, 0)
        allowed = jnp.logical_and(window, (seg_query[:, None] == seg_keys[None, :])[None, :, :])
        raw = low_back(jnp.einsum('qhd,khd->hqk', query_block, key_block, precision=HIGHEST_PRECISION) * DH ** (-0.5))
        scores = jnp.where(allowed, raw, MASK_FILL)
        row_max = lax.optimization_barrier(jnp.max(scores, axis=2, keepdims=True))
        exponent = jnp.exp(scores - row_max)
        softmax = low(exponent / lax.optimization_barrier(jnp.sum(exponent, axis=2, keepdims=True)))
        return jnp.einsum('hqk,khd->qhd', softmax, value_block, precision=HIGHEST_PRECISION)
    starts = jnp.arange(TOKENS // block_rows, dtype=jnp.int32) * block_rows
    mixed_heads = lax.map(jax.checkpoint(one_block), starts)
    return mixed_heads.reshape(TOKENS, HEAD_TOTAL * DH)

def one_layer(inputs, attn_real, ffn_real, shared, split, dilated, segments):
    head_width = D // N_MP
    unit_width = FF // N_MP
    bias_query = split[:, :head_width].reshape(D)
    bias_value = split[:, head_width:2 * head_width].reshape(D)
    bias_hidden = split[:, 2 * head_width:].reshape(FF)
    attn_low = low(attn_real)
    ffn_low = low(ffn_real)
    inputs_low = low(inputs)
    query = low(low_back(jnp.dot(inputs_low, attn_low[0], precision=HIGHEST_PRECISION) + bias_query))
    keys = low(low_back(jnp.dot(inputs_low, attn_low[1], precision=HIGHEST_PRECISION)))
    values = low(low_back(jnp.dot(inputs_low, attn_low[2], precision=HIGHEST_PRECISION) + bias_value))
    mixed_heads = attention(query.reshape(TOKENS, HEAD_TOTAL, DH), keys.reshape(TOKENS, HEAD_TOTAL, DH), values.reshape(TOKENS, HEAD_TOTAL, DH), segments, dilated)
    mixed_heads = low(low_back(mixed_heads))
    partial_attn = jnp.einsum('tjc,djc->jtd', mixed_heads.reshape(TOKENS, N_MP, head_width), attn_low[3].reshape(D, N_MP, head_width), precision=HIGHEST_PRECISION)
    attn_sum = inputs + low_back(lax.optimization_barrier(jnp.sum(low(partial_attn), axis=0))) + shared[0]
    normed = normalize_layer(attn_sum, shared[1], shared[2])
    normed_low = low(normed)
    pre_gelu = low_back(jnp.dot(normed_low, ffn_low[0], precision=HIGHEST_PRECISION) + bias_hidden)
    hidden = low(jax.nn.gelu(pre_gelu, approximate=False))
    partial_ffn = jnp.einsum('tjc,djc->jtd', hidden.reshape(TOKENS, N_MP, unit_width), ffn_low[1].reshape(D, N_MP, unit_width), precision=HIGHEST_PRECISION)
    ffn_sum = normed + low_back(lax.optimization_barrier(jnp.sum(low(partial_ffn), axis=0))) + shared[3]
    return normalize_layer(ffn_sum, shared[4], shared[5])

def to_real(stored, owners):
    layer_count, matrix_count, row_count, col_count = stored.shape
    blocks = stored.reshape(layer_count, matrix_count, SLOTS, row_count // SLOTS, col_count)
    return jnp.take(blocks, owners, axis=2).reshape(stored.shape)

def to_slots(real, owners):
    inverse = jnp.argsort(owners).astype(jnp.int32)
    return to_real(real, inverse)

def rotate_update(weight, grad_now, first, second, running_average, basis, rates):
    layer_count, matrix_count, row_count, col_count = weight.shape
    width = col_count // N_MP
    shape = (layer_count, matrix_count, SLOTS, row_count // SLOTS, N_MP, width)
    turned = jnp.einsum('lmsrje,lmsjec->lmsrjc', grad_now.reshape(shape), basis, precision=HIGHEST_PRECISION).reshape(weight.shape)
    first_new = BETA_FIRST * first + (1.0 - BETA_FIRST) * turned
    second_new = BETA_SECOND * second + (1.0 - BETA_SECOND) * turned * turned
    direction = first_new / (1.0 - BETA_FIRST ** STEP) / (jnp.sqrt(second_new / (1.0 - BETA_SECOND ** STEP)) + ADAM_EPSILON)
    back = jnp.einsum('lmsrjc,lmsjec->lmsrje', direction.reshape(shape), basis, precision=HIGHEST_PRECISION).reshape(weight.shape)
    weight_new = weight - rates[None, :, None, None] * (back + DECAY_RATE * weight)
    average_new = AVERAGE_RATE * running_average + (1.0 - AVERAGE_RATE) * weight_new
    return (weight_new, first_new, second_new, average_new)

def vector_update(current, grad_now, first, second):
    first_new = BETA_FIRST * first + (1.0 - BETA_FIRST) * grad_now
    second_new = BETA_SECOND * second + (1.0 - BETA_SECOND) * grad_now * grad_now
    direction = first_new / (1.0 - BETA_FIRST ** STEP) / (jnp.sqrt(second_new / (1.0 - BETA_SECOND ** STEP)) + ADAM_EPSILON)
    return (current - VECTOR_RATE * direction, first_new, second_new)

def reference(activations, cotangent, segments, dilated_heads, owners, attn_weights, attn_first, attn_second, attn_average, attn_basis, ffn_weights, ffn_first, ffn_second, ffn_average, ffn_basis, split_biases, split_first, split_second, shared_vectors, shared_first, shared_second):
    head_flags = jnp.any(dilated_heads[:, None] == jnp.arange(HEAD_TOTAL, dtype=jnp.int32)[None, :], axis=0)

    def forward(inputs, attn_real, ffn_real, shared_all, split_all):
        current = inputs
        for layer_index in range(LAYERS):
            dilated = jnp.logical_and(head_flags, layer_index % 2 == 1)
            current = one_layer(current, attn_real[layer_index], ffn_real[layer_index], shared_all[layer_index], split_all[layer_index], dilated, segments)
        return current
    result, pullback = jax.vjp(forward, activations.astype(jnp.float32), to_real(attn_weights, owners), to_real(ffn_weights, owners), shared_vectors, split_biases)
    grad_input, grad_attn, feedforward_gradient, grad_shared, grad_split = pullback(cotangent.astype(jnp.float32))
    grad_attn = to_slots(grad_attn, owners)
    feedforward_gradient = to_slots(feedforward_gradient, owners)
    total = jnp.sum(grad_attn * grad_attn) + jnp.sum(feedforward_gradient * feedforward_gradient) + jnp.sum(grad_shared * grad_shared) + jnp.sum(grad_split * grad_split)
    grad_norm = jnp.sqrt(total)
    factor = CLIP_LEVEL / jnp.maximum(grad_norm, CLIP_LEVEL)
    attn_rates = jnp.array([0.5 * D ** (-0.5)] * 3 + [0.5 * (WIN / D) ** 0.5], jnp.float32)
    ffn_rates = jnp.array([0.5 * D ** (-0.5), 0.5 * FF ** (-0.5)], jnp.float32)
    attn_out = rotate_update(attn_weights, factor * grad_attn, attn_first, attn_second, attn_average, attn_basis, attn_rates)
    ffn_out = rotate_update(ffn_weights, factor * feedforward_gradient, ffn_first, ffn_second, ffn_average, ffn_basis, ffn_rates)
    split_out = vector_update(split_biases, factor * grad_split, split_first, split_second)
    shared_out = vector_update(shared_vectors, factor * grad_shared, shared_first, shared_second)
    return (result, grad_input, attn_out[0], attn_out[1], attn_out[2][:, :3], attn_out[2][:, 3], attn_out[3], ffn_out[0], ffn_out[1], ffn_out[2], ffn_out[3], split_out[0], split_out[1], split_out[2], shared_out[0], shared_out[1], shared_out[2], grad_norm)
```

```python
from types import SimpleNamespace

import jax
import jax.numpy as jnp
from jax import lax
from jax.experimental import pallas as pl
from jax.experimental.pallas import tpu as pltpu
from jax.sharding import PartitionSpec as P

D = 768
DH = 64
FF = 3072
WIN = 256
STEP = 10

HIGHEST_PRECISION = lax.Precision.HIGHEST
NORM_EPSILON = 1e-05
MASK_FILL = -1e30
CLIP_LEVEL = 1.0
BETA_FIRST = 0.5
BETA_SECOND = 0.5
ADAM_EPSILON = 1e-08
DECAY_RATE = 0.01
AVERAGE_RATE = 0.7
VECTOR_RATE = 0.3

BF = jnp.bfloat16
F32 = jnp.float32
MESH = pl.DeviceIdType.MESH
BLOCK = 256
CHUNK = 128
HALF = 64
VMEM_LIMIT = 56 * 1024 * 1024
SCORE_SCALE = DH ** (-0.5)


def dot(left, right):
    return jnp.dot(left, right, preferred_element_type=F32)


def dot_nt(left, right):
    return lax.dot_general(left, right, (((1,), (1,)), ((), ())), preferred_element_type=F32)


def dot_tn(left, right):
    return lax.dot_general(left, right, (((0,), (0,)), ((), ())), preferred_element_type=F32)


def run_kernel(body, name, inputs, outputs, scratch, collective=None, flops=0, grid=None, specs=None, in_smem=()):
    specs = specs or {}
    labels = list(inputs) + list(outputs) + list(scratch)

    def kernel(*refs):
        body(SimpleNamespace(**dict(zip(labels, refs))))

    def spec_of(key):
        if key in specs:
            return specs[key]
        return pl.BlockSpec(memory_space=pltpu.SMEM if key in in_smem else pltpu.VMEM)

    shapes = [jax.ShapeDtypeStruct(shape, dtype) for shape, dtype in outputs.values()]
    moved = sum(v.size * v.dtype.itemsize for v in inputs.values())
    moved += sum(v.size * v.dtype.itemsize for v in shapes)
    extra = {} if grid is None else {"grid": grid}
    params = {"vmem_limit_bytes": VMEM_LIMIT}
    if collective is not None:
        params["collective_id"] = collective
        params["has_side_effects"] = True
    results = pl.pallas_call(
        kernel,
        out_shape=shapes,
        in_specs=[spec_of(key) for key in inputs],
        out_specs=[spec_of(key) for key in outputs],
        scratch_shapes=list(scratch.values()),
        compiler_params=pltpu.CompilerParams(**params),
        cost_estimate=pl.CostEstimate(flops=int(flops), bytes_accessed=int(moved), transcendentals=0),
        name=name,
        **extra,
    )(*inputs.values())
    return SimpleNamespace(**dict(zip(outputs, results)))


def parity_matrix():
    row = lax.broadcasted_iota(jnp.int32, (2 * BLOCK, 2 * BLOCK), 0)
    col = lax.broadcasted_iota(jnp.int32, (2 * BLOCK, 2 * BLOCK), 1)
    source = 2 * (row % BLOCK) + row // BLOCK
    return jnp.where(col == source, 1.0, 0.0).astype(BF)


def head_lanes(count):
    lane = lax.broadcasted_iota(jnp.int32, (1, count * DH), 1)
    return [lane // DH == head for head in range(count)]


def arrange_rows(natural, sort):
    groups = natural.shape[0] // (2 * BLOCK)
    parts = [
        dot(sort, natural[g * 2 * BLOCK : (g + 1) * 2 * BLOCK]).astype(BF) for g in range(groups)
    ]
    return jnp.concatenate([p[:BLOCK] for p in parts] + [p[BLOCK:] for p in parts], axis=0)


def restore_rows(arranged, sort):
    groups = arranged.shape[0] // (2 * BLOCK)
    half = groups * BLOCK
    parts = []
    for g in range(groups):
        pair = jnp.concatenate(
            [
                arranged[g * BLOCK : (g + 1) * BLOCK],
                arranged[half + g * BLOCK : half + (g + 1) * BLOCK],
            ],
            axis=0,
        )
        parts.append(dot_tn(sort, pair))
    return jnp.concatenate(parts, axis=0)


def attend(qkv, left, right, seg_query, seg_keys, flags, flag_lanes, mixed):
    rows, width = qkv.shape[1:]
    rim = left.shape[1]
    heads = width // DH
    blocks = rows // BLOCK
    keys = 3 * BLOCK
    slots = 2 * blocks if mixed else blocks + 2

    def body(r):
        step = pl.program_id(0)

        @pl.when(step == 0)
        def _():
            for which, held in ((1, r.keys), (2, r.values)):
                padded = jnp.concatenate(
                    [r.left[which - 1], r.qkv[which], r.right[which - 1]], axis=0
                )
                if mixed:
                    middle = jnp.concatenate(
                        [
                            padded[BLOCK : (blocks + 1) * BLOCK],
                            padded[(blocks - 1) * BLOCK : (2 * blocks - 1) * BLOCK],
                        ],
                        axis=0,
                    )
                    sort = parity_matrix()
                    held[...] = jnp.where(r.lanes[...] > 0, arrange_rows(padded, sort), middle)
                else:
                    held[...] = padded
            query = (r.qkv[0].astype(F32) * SCORE_SCALE).astype(BF)
            if mixed:
                query = jnp.where(r.lanes[...] > 0, arrange_rows(query, parity_matrix()), query)
            r.query[...] = query

        row = lax.broadcasted_iota(jnp.int32, (BLOCK, keys), 0)
        col = lax.broadcasted_iota(jnp.int32, (BLOCK, keys), 1)
        window = jnp.abs(row - col + BLOCK) <= WIN
        first = step + 2 * (step >= blocks // 2) if mixed else step
        own = pl.ds(pl.multiple_of(step * BLOCK, BLOCK), BLOCK)
        near = pl.ds(pl.multiple_of(first * BLOCK, BLOCK), keys)
        key_block = r.keys[near, :]
        value_block = r.values[near, :]
        query_block = r.query[own, :]
        gathered = jnp.zeros((BLOCK, width), F32)
        for head, lanes in enumerate(head_lanes(heads)):
            if mixed:
                flag = r.flags[head] > 0
                mine = jnp.where(flag, r.seg_query[own, 1:2], r.seg_query[own, 0:1])
                theirs = jnp.where(flag, r.seg_keys[1:2, near], r.seg_keys[0:1, near])
            else:
                mine = r.seg_query[own, 0:1]
                theirs = r.seg_keys[0:1, near]
            allowed = jnp.logical_and(window, mine == theirs)
            raw = dot_nt(jnp.where(lanes, query_block, 0.0).astype(BF), key_block)
            scores = jnp.where(allowed, raw, MASK_FILL)
            top = jnp.max(scores, axis=1, keepdims=True)
            exponent = jnp.exp(scores - top)
            total = jnp.sum(exponent, axis=1, keepdims=True)
            soft = (exponent * (1.0 / total)).astype(BF)
            r.soft[head] = soft
            gathered = jnp.where(lanes, dot(soft, value_block), gathered)
        r.arranged[own, :] = gathered.astype(BF)

        @pl.when(step == blocks - 1)
        def _():
            arranged = r.arranged[...]
            if mixed:
                natural = restore_rows(arranged, parity_matrix()).astype(BF)
                r.out[...] = jnp.where(r.lanes[...] > 0, natural, arranged)
            else:
                r.out[...] = arranged

    return run_kernel(
        body,
        "attend",
        dict(
            qkv=qkv, left=left, right=right, seg_query=seg_query, seg_keys=seg_keys, flags=flags, lanes=flag_lanes
        ),
        dict(
            out=((rows, width), BF),
            arranged=((rows, width), BF),
            query=((rows, width), BF),
            keys=((slots * BLOCK, width), BF),
            values=((slots * BLOCK, width), BF),
            soft=((heads, rows, keys), BF),
        ),
        {},
        flops=4 * rows * keys * 256 * heads,
        grid=(blocks,),
        specs=dict(soft=pl.BlockSpec((heads, BLOCK, keys), lambda i: (0, i, 0))),
        in_smem=("flags",),
    )


def attend_back(saved, grad_out, flag_lanes, rim, mixed):
    rows, width = grad_out.shape
    heads = width // DH
    blocks = rows // BLOCK
    keys = 3 * BLOCK
    slots = 2 * blocks if mixed else blocks + 2

    def body(r):
        step = pl.program_id(0)

        @pl.when(step == 0)
        def _():
            grad = r.grad_out[...]
            if mixed:
                grad = jnp.where(r.lanes[...] > 0, arrange_rows(grad, parity_matrix()), grad)
            r.grad[...] = grad
            r.grad_keys[...] = jnp.zeros_like(r.grad_keys)
            r.grad_values[...] = jnp.zeros_like(r.grad_values)

        first = step + 2 * (step >= blocks // 2) if mixed else step
        own = pl.ds(pl.multiple_of(step * BLOCK, BLOCK), BLOCK)
        near = pl.ds(pl.multiple_of(first * BLOCK, BLOCK), keys)
        key_block = r.keys[near, :]
        value_block = r.values[near, :]
        query_block = r.query[own, :]
        grad_block = r.grad[own, :]
        product = grad_block.astype(F32) * r.arranged[own, :].astype(F32)
        grad_query = jnp.zeros((BLOCK, width), F32)
        grad_key = jnp.zeros((keys, width), F32)
        grad_value = jnp.zeros((keys, width), F32)
        for head, lanes in enumerate(head_lanes(heads)):
            soft = r.soft[head]
            grad_head = jnp.where(lanes, grad_block, 0.0).astype(BF)
            row_dot = jnp.sum(jnp.where(lanes, product, 0.0), axis=1, keepdims=True)
            grad_soft = dot_nt(grad_head, value_block)
            grad_scores = (soft.astype(F32) * (grad_soft - row_dot)).astype(BF)
            grad_value += dot_tn(soft, grad_head)
            grad_key += dot_tn(grad_scores, jnp.where(lanes, query_block, 0.0).astype(BF))
            grad_query = jnp.where(lanes, dot(grad_scores, key_block), grad_query)
        r.grad_query[own, :] = (grad_query * SCORE_SCALE).astype(BF)
        r.grad_keys[near, :] += grad_key
        r.grad_values[near, :] += grad_value

        @pl.when(step == blocks - 1)
        def _():
            if mixed:
                sort = parity_matrix()
                marked = r.lanes[...] > 0
                arranged = r.grad_query[...]
                natural = restore_rows(arranged, sort).astype(BF)
                r.out_query[...] = jnp.where(marked, natural, arranged)
            else:
                r.out_query[...] = r.grad_query[...]
            for which, held in ((0, r.grad_keys), (1, r.grad_values)):
                total = held[...]
                if mixed:
                    half = blocks * BLOCK
                    edge = jnp.zeros((BLOCK, width), F32)
                    lap = 2 * BLOCK
                    middle = jnp.concatenate(
                        [
                            edge,
                            total[:lap],
                            total[lap:half] + total[half : half + lap],
                            total[half + lap :],
                            edge,
                        ],
                        axis=0,
                    )
                    total = jnp.where(marked, restore_rows(total.astype(BF), sort), middle)
                r.out_left[which] = total[:rim].astype(BF)
                r.out_own[which] = total[rim : rim + rows].astype(BF)
                r.out_right[which] = total[rim + rows :].astype(BF)

    return run_kernel(
        body,
        "attend_back",
        dict(
            grad_out=grad_out,
            arranged=saved.arranged,
            query=saved.query,
            keys=saved.keys,
            values=saved.values,
            soft=saved.soft,
            lanes=flag_lanes,
        ),
        dict(
            out_query=((rows, width), BF),
            out_own=((2, rows, width), BF),
            out_left=((2, rim, width), BF),
            out_right=((2, rim, width), BF),
        ),
        dict(
            grad=pltpu.VMEM((rows, width), BF),
            grad_query=pltpu.VMEM((rows, width), BF),
            grad_keys=pltpu.VMEM((slots * BLOCK, width), F32),
            grad_values=pltpu.VMEM((slots * BLOCK, width), F32),
        ),
        flops=8 * rows * keys * 256 * heads,
        grid=(blocks,),
        specs=dict(soft=pl.BlockSpec((heads, BLOCK, keys), lambda i: (0, i, 0))),
    )


class Partners:
    def __init__(self):
        seq = lax.axis_index("seq")
        here = lax.axis_index("mp")
        self.core = lax.rem(here, 2)
        self.sibling = (seq, here + 1 - 2 * self.core)
        self.across = (seq, lax.rem(here + 2, 4))

    def meet(self):
        barrier = pltpu.get_barrier_semaphore()
        for other in (self.sibling, self.across):
            pl.semaphore_signal(barrier, inc=1, device_id=other, device_id_type=MESH)
        pl.semaphore_wait(barrier, 2)

    def chunk(self, t):
        return pl.ds(pl.multiple_of(t * CHUNK, CHUNK), CHUNK)

    def own(self, t):
        return pl.ds(pl.multiple_of(t * CHUNK + self.core * HALF, HALF), HALF)

    def other(self, t):
        return pl.ds(pl.multiple_of(t * CHUNK + (1 - self.core) * HALF, HALF), HALF)

    def half(self, t):
        return pl.ds(pl.multiple_of(t * HALF, HALF), HALF)


def copy_to(source, target, sent, arrived, device):
    return pltpu.make_async_remote_copy(
        src_ref=source, dst_ref=target, send_sem=sent, recv_sem=arrived, device_id=device, device_id_type=MESH
    )


def exchange_scratch(rows):
    count = rows // CHUNK
    return dict(
        part=pltpu.VMEM((rows, D), BF),
        near=pltpu.VMEM((rows // 2, D), BF),
        pair=pltpu.VMEM((rows // 2, D), BF),
        far=pltpu.VMEM((rows // 2, D), BF),
        core_sent=pltpu.SemaphoreType.DMA((count,)),
        core_came=pltpu.SemaphoreType.DMA((count,)),
        far_sent=pltpu.SemaphoreType.DMA((count,)),
        far_came=pltpu.SemaphoreType.DMA((count,)),
    )


def gather_scratch(rows, width=D, dtype=BF):
    count = rows // CHUNK
    return dict(
        full=pltpu.VMEM((rows, width), dtype),
        sent=pltpu.SemaphoreType.DMA((count,)),
        came=pltpu.SemaphoreType.DMA((count,)),
    )


class Exchange:
    def __init__(self, who, refs):
        self.who, self.r = who, refs

    def core_copy(self, t):
        who, r = self.who, self.r
        return copy_to(
            r.part.at[who.other(t), :], r.near.at[who.half(t), :], r.core_sent.at[t], r.core_came.at[t], who.sibling
        )

    def far_copy(self, t):
        who, r = self.who, self.r
        rows = who.half(t)
        return copy_to(r.pair.at[rows, :], r.far.at[rows, :], r.far_sent.at[t], r.far_came.at[t], who.across)

    def give(self, t, part):
        self.r.part[self.who.chunk(t), :] = part.astype(BF)
        self.core_copy(t).start()

    def add(self, t):
        who, r = self.who, self.r
        self.core_copy(t).wait_recv()
        pair = r.part[who.own(t), :].astype(F32) + r.near[who.half(t), :].astype(F32)
        r.pair[who.half(t), :] = pair.astype(BF)
        self.far_copy(t).start()

    def take(self, t):
        who, r = self.who, self.r
        self.far_copy(t).wait_recv()
        return r.pair[who.half(t), :].astype(F32) + r.far[who.half(t), :].astype(F32)

    def finish(self, t):
        self.core_copy(t).wait_send()
        self.far_copy(t).wait_send()


class Gather:
    def __init__(self, who, refs):
        self.who, self.r = who, refs

    def copy(self, rows, t):
        r = self.r
        return copy_to(r.full.at[rows, :], r.full.at[rows, :], r.sent.at[t], r.came.at[t], self.who.sibling)

    def give(self, t, value):
        rows = self.who.own(t)
        self.r.full[rows, :] = value.astype(self.r.full.dtype)
        self.copy(rows, t).start()

    def take(self, t):
        self.wait(t)
        return self.r.full[self.who.chunk(t), :]

    def wait(self, t):
        self.copy(self.who.other(t), t).wait_recv()

    def finish(self, t):
        self.copy(self.who.own(t), t).wait_send()


def pick(r, prefix):
    start = prefix + "_"
    return SimpleNamespace(
        **{key[len(start) :]: value for key, value in vars(r).items() if key.startswith(start)}
    )


def prefixed(prefix, entries):
    return {prefix + "_" + key: value for key, value in entries.items()}


def run_stages(count, stages):
    last = max(delay for delay, _ in stages)

    def step(i, carry):
        for delay, stage in stages:

            @pl.when(jnp.logical_and(i >= delay, i < count + delay))
            def _(delay=delay, stage=stage):
                stage(i - delay)

        return carry

    lax.fori_loop(0, count + last, step, 0)


def norm_forward(total, gain, shift):
    center = total - jnp.mean(total, axis=1, keepdims=True)
    spread = jnp.mean(center * center, axis=1, keepdims=True)
    inverse = lax.rsqrt(spread + NORM_EPSILON)
    unit = center * inverse
    return unit, inverse, unit * gain + shift


def norm_back(grad, unit, inverse, gain):
    grad_unit = grad * gain
    first = jnp.mean(grad_unit, axis=1, keepdims=True)
    second = jnp.mean(grad_unit * unit, axis=1, keepdims=True)
    return inverse * (grad_unit - first - unit * second)


def column_sum(value):
    return jnp.sum(value, axis=0, keepdims=True)


def split_two(value):
    high = value.astype(BF)
    return high, (value - high.astype(F32)).astype(BF)


def unturned(value, turn):
    high, rest = split_two(value)
    return dot_nt(high, turn) + dot_nt(rest, turn)


def wide(column):
    return jnp.broadcast_to(column, (column.shape[0], 128))


def forward_refs(rows, width, units):
    return dict(
        unit_one=((rows // 2, D), F32),
        inverse_one=((rows // 2, 128), F32),
        unit_two=((rows // 2, D), F32),
        inverse_two=((rows // 2, 128), F32),
        hidden=((rows, units), BF),
        slope=((rows, units), BF),
    )


def forward_stages(r, who, first, second, spread):
    def project(t):
        first.give(t, dot_nt(r.mixed[who.chunk(t), :], r.attn[3]))

    def middle(t):
        rows = who.own(t) if r.residual.shape[0] == r.mixed.shape[0] else who.half(t)
        total = r.residual[rows, :].astype(F32) + first.take(t) + r.shared[0:1, :]
        unit, inverse, normed = norm_forward(total, r.shared[1:2, :], r.shared[2:3, :])
        r.unit_one[who.half(t), :] = unit
        r.inverse_one[who.half(t), :] = wide(inverse)
        r.normed[who.half(t), :] = normed
        spread.give(t, normed)

    def feed(t):
        pre = dot(spread.take(t), r.ffn[0]) + r.hidden_bias[...]
        chance = 0.5 + 0.5 * lax.erf(pre * (0.5**0.5))
        hidden = (pre * chance).astype(BF)
        r.hidden[who.chunk(t), :] = hidden
        bell = jnp.exp(-0.5 * pre * pre) * 0.3989422804014327
        r.slope[who.chunk(t), :] = (chance + pre * bell).astype(BF)
        second.give(t, dot_nt(hidden, r.ffn[1]))

    def final(t):
        total = r.normed[who.half(t), :] + second.take(t) + r.shared[3:4, :]
        unit, inverse, result = norm_forward(total, r.shared[4:5, :], r.shared[5:6, :])
        r.unit_two[who.half(t), :] = unit
        r.inverse_two[who.half(t), :] = wide(inverse)
        return unit, inverse, result

    return project, middle, feed, final


def backward_stages(r, who, ends, third, mids):
    def enter(t, grad, unit, inverse):
        grad_total = norm_back(grad, unit, inverse, r.shared[4:5, :])
        r.vectors[3:4, :] += column_sum(grad_total)
        r.vectors[4:5, :] += column_sum(grad * unit)
        r.vectors[5:6, :] += column_sum(grad)
        r.kept[who.half(t), :] = grad_total
        ends.give(t, grad_total)

    def feed_back(t):
        rows = who.chunk(t)
        grad = ends.take(t)
        hidden = r.hidden[rows, :]
        grad_pre = (dot(grad, r.ffn[1]) * r.slope[rows, :].astype(F32)).astype(BF)
        r.units[0:1, :] += column_sum(grad_pre.astype(F32))
        third.give(t, dot_nt(grad_pre, r.ffn[0]))
        r.sum_up[...] += dot_tn(r.spread_full[rows, :], grad_pre)
        r.sum_down[...] += dot_tn(grad, hidden)

    def leave(t):
        grad = r.kept[who.half(t), :] + third.take(t)
        unit = r.unit_one[who.half(t), :]
        grad_total = norm_back(grad, unit, r.inverse_one[who.half(t), 0:1], r.shared[1:2, :])
        r.vectors[0:1, :] += column_sum(grad_total)
        r.vectors[1:2, :] += column_sum(grad * unit)
        r.vectors[2:3, :] += column_sum(grad)
        r.grad_one[who.half(t), :] = grad_total
        mids.give(t, grad_total)

    def project_back(t):
        rows = who.chunk(t)
        grad = mids.take(t)
        r.grad_mixed[rows, :] = dot(grad, r.attn[3]).astype(BF)
        r.sum_out[...] += dot_tn(grad, r.mixed[rows, :])

    return enter, feed_back, leave, project_back


def clear(*refs):
    for ref in refs:
        ref[...] = jnp.zeros_like(ref)


def finish_all(count, parts):
    def step(t, carry):
        for part in parts:
            part.finish(t)
        return carry

    lax.fori_loop(0, count, step, 0)


def middle_forward(mixed, attn, ffn, residual, shared, hidden_bias, next_attn, next_bias):
    rows, width = mixed.shape
    units = ffn.shape[2]
    count = rows // CHUNK

    def body(r):
        who = Partners()
        first, second = Exchange(who, pick(r, "first")), Exchange(who, pick(r, "second"))
        spread = Gather(who, SimpleNamespace(full=r.spread_full, sent=r.spread_sent, came=r.spread_came))
        last = Gather(who, SimpleNamespace(full=r.last_full, sent=r.last_sent, came=r.last_came))
        who.meet()
        project, middle, feed, final = forward_stages(r, who, first, second, spread)

        def close(t):
            _, _, result = final(t)
            r.result[who.half(t), :] = result
            last.give(t, result)

        def next_project(t):
            low = last.take(t)
            for which in range(3):
                value = dot(low, r.next_attn[which]) + r.next_bias[which : which + 1, :]
                r.qkv[which, who.chunk(t), :] = value.astype(BF)

        run_stages(
            count,
            [
                (5, second.add),
                (1, first.add),
                (7, close),
                (3, middle),
                (8, next_project),
                (4, feed),
                (0, project),
            ],
        )
        finish_all(count, (first, second, spread, last))

    outputs = forward_refs(rows, width, units)
    outputs.update(
        spread_full=((rows, D), BF), last_full=((rows, D), BF), result=((rows // 2, D), F32), qkv=((3, rows, width), BF)
    )
    scratch = dict(normed=pltpu.VMEM((rows // 2, D), F32))
    scratch.update(prefixed("first", exchange_scratch(rows)))
    scratch.update(prefixed("second", exchange_scratch(rows)))
    for key in ("spread", "last"):
        for part in ("sent", "came"):
            scratch[key + "_" + part] = pltpu.SemaphoreType.DMA((count,))
    return run_kernel(
        body,
        "middle_forward",
        dict(
            mixed=mixed,
            attn=attn,
            ffn=ffn,
            residual=residual,
            shared=shared,
            hidden_bias=hidden_bias,
            next_attn=next_attn,
            next_bias=next_bias,
        ),
        outputs,
        scratch,
        collective=1,
        flops=2 * rows * D * (4 * width + 2 * units),
    )


def turning(mixed, attn, ffn, residual, shared, hidden_bias, cotangent, turn):
    rows, width = mixed.shape
    units = ffn.shape[2]
    count = rows // CHUNK

    def body(r):
        who = Partners()
        first, second = Exchange(who, pick(r, "first")), Exchange(who, pick(r, "second"))
        third = Exchange(who, pick(r, "third"))
        spread = Gather(who, pick(r, "spread"))
        ends, mids = Gather(who, pick(r, "ends")), Gather(who, pick(r, "mids"))
        out = Gather(who, SimpleNamespace(full=r.output, sent=r.out_sent, came=r.out_came))
        who.meet()
        clear(r.vectors, r.units, r.sum_up, r.sum_down, r.sum_out)
        project, middle, feed, final = forward_stages(r, who, first, second, spread)
        enter, feed_back, leave, project_back = backward_stages(r, who, ends, third, mids)

        def close(t):
            unit, inverse, result = final(t)
            grad = dot(r.cotangent[who.own(t), :], r.turn[...])
            enter(t, grad, unit, inverse)
            out.give(t, unturned(result, r.turn[...]))

        run_stages(
            count,
            [
                (9, third.add),
                (5, second.add),
                (1, first.add),
                (11, leave),
                (7, close),
                (3, middle),
                (12, project_back),
                (8, feed_back),
                (4, feed),
                (0, project),
            ],
        )

        def arrive(t, carry):
            out.wait(t)
            return carry

        lax.fori_loop(0, count, arrive, 0)
        finish_all(count, (first, second, third, spread, ends, mids, out))
        r.weights[:, :units] = r.sum_up[...].astype(BF)
        r.weights[:, units : 2 * units] = r.sum_down[...].astype(BF)
        r.weights[:, 2 * units :] = r.sum_out[...].astype(BF)

    outputs = dict(
        output=((rows, D), F32),
        weights=((D, 2 * units + width), BF),
        grad_one=((rows // 2, D), F32),
        grad_mixed=((rows, width), BF),
        vectors=((8, D), F32),
        units=((8, units), F32),
    )
    scratch = dict(
        normed=pltpu.VMEM((rows // 2, D), F32),
        kept=pltpu.VMEM((rows // 2, D), F32),
        sum_up=pltpu.VMEM((D, units), F32),
        sum_down=pltpu.VMEM((D, units), F32),
        sum_out=pltpu.VMEM((D, width), F32),
        out_sent=pltpu.SemaphoreType.DMA((count,)),
        out_came=pltpu.SemaphoreType.DMA((count,)),
    )
    for key, (shape, dtype) in forward_refs(rows, width, units).items():
        scratch[key] = pltpu.VMEM(shape, dtype)
    for key in ("first", "second", "third"):
        scratch.update(prefixed(key, exchange_scratch(rows)))
    for key in ("spread", "ends", "mids"):
        scratch.update(prefixed(key, gather_scratch(rows)))
    return run_kernel(
        body,
        "turning",
        dict(
            mixed=mixed,
            attn=attn,
            ffn=ffn,
            residual=residual,
            shared=shared,
            hidden_bias=hidden_bias,
            cotangent=cotangent,
            turn=turn,
        ),
        outputs,
        scratch,
        collective=2,
        flops=2 * rows * D * (3 * width + 6 * units),
    )


def projection_back_stage(r, who, exchange):
    rows, width = r.grad_query.shape
    rim = r.from_left.shape[1]

    def gather_parts():
        own = r.grad_own[...].astype(F32)
        for which in range(2):
            r.grad_pair[which] = r.grad_own[which]
            head = own[which, :rim] + r.from_left[which].astype(F32)
            r.grad_pair[which, :rim, :] = head.astype(BF)
            held = r.grad_pair[which, rows - rim :, :].astype(F32)
            r.grad_pair[which, rows - rim :, :] = (held + r.from_right[which].astype(F32)).astype(BF)

    def stage(t):
        chunk = who.chunk(t)
        parts = [r.grad_query[chunk, :], r.grad_pair[0, chunk, :], r.grad_pair[1, chunk, :]]
        low = r.low[chunk, :]
        part = sum(dot_nt(value, r.next_attn[which]) for which, value in enumerate(parts))
        exchange.give(t, part)
        for which, value in enumerate(parts):
            r.sum_three[which] += dot_tn(low, value)
        r.biases[0:1, :] += column_sum(parts[0].astype(F32))
        r.biases[1:2, :] += column_sum(parts[2].astype(F32))

    return gather_parts, stage


def middle_backward(back, from_left, from_right, next_attn, grad_above, low, saved, mixed, attn, ffn, shared):
    rows, width = mixed.shape
    units = ffn.shape[2]
    count = rows // CHUNK

    def body(r):
        who = Partners()
        zeroth, third = Exchange(who, pick(r, "zeroth")), Exchange(who, pick(r, "third"))
        ends, mids = Gather(who, pick(r, "ends")), Gather(who, pick(r, "mids"))
        who.meet()
        clear(r.vectors, r.units, r.biases, r.sum_up, r.sum_down, r.sum_out, r.sum_three)
        gather_parts, inputs_back = projection_back_stage(r, who, zeroth)
        gather_parts()
        enter, feed_back, leave, project_back = backward_stages(r, who, ends, third, mids)

        def start(t):
            half = who.half(t)
            enter(t, r.grad_above[half, :] + zeroth.take(t), r.unit_two[half, :], r.inverse_two[half, 0:1])

        run_stages(
            count,
            [
                (5, third.add),
                (1, zeroth.add),
                (7, leave),
                (3, start),
                (8, project_back),
                (4, feed_back),
                (0, inputs_back),
            ],
        )
        finish_all(count, (zeroth, third, ends, mids))
        r.weights[:, :units] = r.sum_up[...].astype(BF)
        r.weights[:, units : 2 * units] = r.sum_down[...].astype(BF)
        tail = jnp.concatenate([r.sum_three[0], r.sum_three[1], r.sum_three[2], r.sum_out[...]], axis=1)
        r.weights[:, 2 * units :] = tail.astype(BF)

    outputs = dict(
        weights=((D, 2 * units + 4 * width), BF),
        grad_one=((rows // 2, D), F32),
        grad_mixed=((rows, width), BF),
        vectors=((8, D), F32),
        units=((8, units), F32),
        biases=((8, width), F32),
    )
    scratch = dict(
        kept=pltpu.VMEM((rows // 2, D), F32),
        grad_pair=pltpu.VMEM((2, rows, width), BF),
        sum_up=pltpu.VMEM((D, units), F32),
        sum_down=pltpu.VMEM((D, units), F32),
        sum_out=pltpu.VMEM((D, width), F32),
        sum_three=pltpu.VMEM((3, D, width), F32),
    )
    for key in ("zeroth", "third"):
        scratch.update(prefixed(key, exchange_scratch(rows)))
    for key in ("ends", "mids"):
        scratch.update(prefixed(key, gather_scratch(rows)))
    return run_kernel(
        body,
        "middle_backward",
        dict(
            grad_query=back.out_query,
            grad_own=back.out_own,
            from_left=from_left,
            from_right=from_right,
            next_attn=next_attn,
            grad_above=grad_above,
            low=low,
            unit_one=saved.unit_one,
            inverse_one=saved.inverse_one,
            unit_two=saved.unit_two,
            inverse_two=saved.inverse_two,
            hidden=saved.hidden,
            slope=saved.slope,
            spread_full=saved.spread_full,
            mixed=mixed,
            attn=attn,
            ffn=ffn,
            shared=shared,
        ),
        outputs,
        scratch,
        collective=3,
        flops=2 * rows * D * (8 * width + 4 * units),
    )


def ending(back, from_left, from_right, next_attn, grad_above, low, turn):
    rows, width = back.out_query.shape
    count = rows // CHUNK

    def body(r):
        who = Partners()
        zeroth = Exchange(who, pick(r, "zeroth"))
        out = Gather(who, SimpleNamespace(full=r.output, sent=r.out_sent, came=r.out_came))
        who.meet()
        clear(r.biases, r.sum_three)
        gather_parts, inputs_back = projection_back_stage(r, who, zeroth)
        gather_parts()

        def close(t):
            out.give(t, unturned(r.grad_above[who.half(t), :] + zeroth.take(t), r.turn[...]))

        run_stages(count, [(1, zeroth.add), (3, close), (0, inputs_back)])

        def arrive(t, carry):
            out.wait(t)
            return carry

        lax.fori_loop(0, count, arrive, 0)
        finish_all(count, (zeroth, out))
        tail = jnp.concatenate([r.sum_three[0], r.sum_three[1], r.sum_three[2]], axis=1)
        r.weights[...] = tail.astype(BF)

    outputs = dict(output=((rows, D), F32), weights=((D, 3 * width), BF), biases=((8, width), F32))
    scratch = dict(
        grad_pair=pltpu.VMEM((2, rows, width), BF),
        sum_three=pltpu.VMEM((3, D, width), F32),
        out_sent=pltpu.SemaphoreType.DMA((count,)),
        out_came=pltpu.SemaphoreType.DMA((count,)),
    )
    scratch.update(prefixed("zeroth", exchange_scratch(rows)))
    return run_kernel(
        body,
        "ending",
        dict(
            grad_query=back.out_query,
            grad_own=back.out_own,
            from_left=from_left,
            from_right=from_right,
            next_attn=next_attn,
            grad_above=grad_above,
            low=low,
            turn=turn,
        ),
        outputs,
        scratch,
        collective=4,
        flops=2 * rows * D * 6 * width,
    )


def beginning(activations, turn, attn, bias):
    rows = activations.shape[0]
    width = attn.shape[2]

    def body(r):
        for start in range(0, rows, BLOCK):
            chunk = pl.ds(start, BLOCK)
            low = dot(r.activations[chunk, :], r.turn[...]).astype(BF)
            r.low[chunk, :] = low
            for which in range(3):
                value = dot(low, r.attn[which]) + r.bias[which : which + 1, :]
                r.qkv[which, chunk, :] = value.astype(BF)

    return run_kernel(
        body,
        "beginning",
        dict(activations=activations, turn=turn, attn=attn, bias=bias),
        dict(low=((rows, D), BF), qkv=((3, rows, width), BF)),
        {},
        flops=2 * rows * D * (D + 3 * width),
    )


def to_next(block):
    count = lax.axis_size("seq")
    return lax.ppermute(block, "seq", [(i, i + 1) for i in range(count - 1)])


def to_previous(block):
    count = lax.axis_size("seq")
    return lax.ppermute(block, "seq", [(i + 1, i) for i in range(count - 1)])


def rotate_update(weight, grad_now, first, second, running_average, basis, rates):
    turn = basis[:, :, 0, 0]
    turned = jnp.einsum("lmre,lmec->lmrc", grad_now, turn)
    first_new = BETA_FIRST * first + (1.0 - BETA_FIRST) * turned
    second_new = BETA_SECOND * second + (1.0 - BETA_SECOND) * turned * turned
    direction = (
        first_new
        / (1.0 - BETA_FIRST**STEP)
        / (jnp.sqrt(second_new / (1.0 - BETA_SECOND**STEP)) + ADAM_EPSILON)
    )
    back = jnp.einsum("lmrc,lmec->lmre", direction, turn)
    weight_new = weight - rates[None, :, None, None] * (back + DECAY_RATE * weight)
    average_new = AVERAGE_RATE * running_average + (1.0 - AVERAGE_RATE) * weight_new
    return (weight_new, first_new, second_new, average_new)


def vector_update(current, grad_now, first, second):
    first_new = BETA_FIRST * first + (1.0 - BETA_FIRST) * grad_now
    second_new = BETA_SECOND * second + (1.0 - BETA_SECOND) * grad_now * grad_now
    direction = (
        first_new
        / (1.0 - BETA_FIRST**STEP)
        / (jnp.sqrt(second_new / (1.0 - BETA_SECOND**STEP)) + ADAM_EPSILON)
    )
    return (current - VECTOR_RATE * direction, first_new, second_new)


def scatter_sum(grads):
    return lax.psum_scatter(grads, "seq", scatter_dimension=0, tiled=True).astype(F32)


def local(
    activations,
    cotangent,
    segments,
    dilated_heads,
    owners,
    attn_weights,
    attn_first,
    attn_second,
    attn_average,
    attn_basis,
    ffn_weights,
    ffn_first,
    ffn_second,
    ffn_average,
    ffn_basis,
    split_biases,
    split_first,
    split_second,
    shared_vectors,
    shared_first,
    shared_second,
):
    slot_count = lax.axis_size("seq")
    rows = activations.shape[0]
    width = attn_weights.shape[3]
    units = ffn_weights.shape[3]
    heads = width // DH
    attn_low, ffn_low = attn_weights.astype(BF), ffn_weights.astype(BF)
    attn, ffn = [], []
    for layer in range(2):
        attn.append(lax.all_gather(attn_low[layer], "seq", axis=1, tiled=True))
        ffn.append(lax.all_gather(ffn_low[layer], "seq", axis=1, tiled=True))
    block = D // slot_count
    place = (owners[:, None] * block + jnp.arange(block, dtype=jnp.int32)[None, :]).reshape(D)
    turn = (place[:, None] == jnp.arange(D, dtype=jnp.int32)[None, :]).astype(BF)
    turn_wide = turn.astype(F32)
    shared = jnp.dot(shared_vectors.reshape(12, D), turn_wide, precision=HIGHEST_PRECISION).reshape(2, 6, D)

    seg_pad = jnp.concatenate([to_next(segments[rows - 2 * WIN :]), segments, to_previous(segments[: 2 * WIN])])
    seg_keys = [
        seg_pad[WIN : rows + 3 * WIN][None],
        jnp.stack(
            [
                jnp.concatenate([seg_pad[WIN : rows + WIN], seg_pad[rows - WIN : 2 * rows - WIN]]),
                seg_pad.reshape(4, WIN, 2).transpose(2, 0, 1).reshape(8 * WIN),
            ]
        ),
    ]
    seg_query = [
        segments[:, None],
        jnp.stack([segments, segments.reshape(2, WIN, 2).transpose(2, 0, 1).reshape(rows)], axis=1),
    ]
    heads_here = lax.axis_index("mp") * heads + jnp.arange(heads, dtype=jnp.int32)
    flags = jnp.any(heads_here[:, None] == dilated_heads[None, :], axis=1).astype(jnp.int32)
    flag_lanes = jnp.repeat(flags, DH)[None, :]

    def biases_of(layer):
        both = split_biases[layer, 0, : 2 * width].reshape(2, width)
        return jnp.stack([both[0], jnp.zeros_like(both[0]), both[1]])

    def hidden_bias(layer):
        return split_biases[layer, :, 2 * width :]

    def halo(qkv, rim):
        return to_next(qkv[1:, rows - rim :]), to_previous(qkv[1:, :rim])

    begin = beginning(activations, turn, attn[0], biases_of(0))
    left, right = halo(begin.qkv, WIN)
    near = attend(begin.qkv, left, right, seg_query[0], seg_keys[0], flags, flag_lanes, False)
    mid = middle_forward(
        near.out, attn[0], ffn[0], begin.low, shared[0], hidden_bias(0), attn[1], biases_of(1)
    )
    left, right = halo(mid.qkv, 2 * WIN)
    far = attend(mid.qkv, left, right, seg_query[1], seg_keys[1], flags, flag_lanes, True)
    top = turning(far.out, attn[1], ffn[1], mid.result, shared[1], hidden_bias(1), cotangent, turn)
    far_back = attend_back(far, top.grad_mixed, flag_lanes, 2 * WIN, True)
    from_left, from_right = to_next(far_back.out_right), to_previous(far_back.out_left)
    low = middle_backward(
        far_back, from_left, from_right, attn[1], top.grad_one, mid.last_full, mid, near.out, attn[0], ffn[0], shared[0]
    )
    near_back = attend_back(near, low.grad_mixed, flag_lanes, WIN, False)
    from_left, from_right = to_next(near_back.out_right), to_previous(near_back.out_left)
    end = ending(near_back, from_left, from_right, attn[0], low.grad_one, begin.low, turn)

    top_sum, low_sum, end_sum = scatter_sum(top.weights), scatter_sum(low.weights), scatter_sum(end.weights)

    def columns(value, start, size, count):
        return [value[:, start + i * size : start + (i + 1) * size] for i in range(count)]

    attn_grads = jnp.stack(
        [
            jnp.stack(columns(end_sum, 0, width, 3) + columns(low_sum, 2 * units + 3 * width, width, 1)),
            jnp.stack(columns(low_sum, 2 * units, width, 3) + columns(top_sum, 2 * units, width, 1)),
        ]
    )
    ffn_grads = jnp.stack(
        [jnp.stack(columns(low_sum, 0, units, 2)), jnp.stack(columns(top_sum, 0, units, 2))]
    )
    shared_grads = lax.psum(jnp.stack([low.vectors[:6], top.vectors[:6]]), ("seq", "mp")) * 0.5
    shared_grads = jnp.dot(
        shared_grads.reshape(12, D), turn_wide.T, precision=HIGHEST_PRECISION
    ).reshape(2, 6, D)
    split_grads = lax.psum(
        jnp.stack(
            [
                jnp.concatenate([end.biases[0], end.biases[1], low.units[0]]),
                jnp.concatenate([low.biases[0], low.biases[1], top.units[0]]),
            ]
        )[:, None, :],
        "seq",
    )
    first_seq = lax.axis_index("seq") == 0
    first_both = jnp.logical_and(first_seq, lax.axis_index("mp") == 0)
    local_sum = jnp.sum(attn_grads * attn_grads) + jnp.sum(ffn_grads * ffn_grads)
    local_sum = (
        local_sum
        + jnp.where(first_seq, jnp.sum(split_grads * split_grads), 0.0)
        + jnp.where(first_both, jnp.sum(shared_grads * shared_grads), 0.0)
    )
    grad_norm = jnp.sqrt(lax.psum(local_sum, ("seq", "mp")))
    factor = CLIP_LEVEL / jnp.maximum(grad_norm, CLIP_LEVEL)
    attn_rates = jnp.array([0.5 * D ** (-0.5)] * 3 + [0.5 * (WIN / D) ** 0.5], F32)
    ffn_rates = jnp.array([0.5 * D ** (-0.5), 0.5 * FF ** (-0.5)], F32)
    attn_out = rotate_update(
        attn_weights, factor * attn_grads, attn_first, attn_second, attn_average, attn_basis, attn_rates
    )
    ffn_out = rotate_update(
        ffn_weights, factor * ffn_grads, ffn_first, ffn_second, ffn_average, ffn_basis, ffn_rates
    )
    split_out = vector_update(split_biases, factor * split_grads, split_first, split_second)
    shared_out = vector_update(shared_vectors, factor * shared_grads, shared_first, shared_second)
    return (
        top.output,
        end.output,
        attn_out[0],
        attn_out[1],
        attn_out[2][:, :3],
        attn_out[2][:, 3],
        attn_out[3],
        ffn_out[0],
        ffn_out[1],
        ffn_out[2],
        ffn_out[3],
        split_out[0],
        split_out[1],
        split_out[2],
        shared_out[0],
        shared_out[1],
        shared_out[2],
        grad_norm,
    )


def solution(mesh):
    placed = (
        P("seq", None),
        P("seq", None),
        P("seq"),
        P(),
        P(),
        P(None, None, "seq", "mp"),
        P(None, None, "seq", "mp"),
        P(None, None, "seq", "mp"),
        P(None, None, "seq", "mp"),
        P(None, None, "seq", "mp", None, None),
        P(None, None, "seq", "mp"),
        P(None, None, "seq", "mp"),
        P(None, None, "seq", "mp"),
        P(None, None, "seq", "mp"),
        P(None, None, "seq", "mp", None, None),
        P(None, "mp", None),
        P(None, "mp", None),
        P(None, "mp", None),
        P(),
        P(),
        P(),
    )
    return jax.shard_map(
        local,
        mesh=mesh,
        in_specs=placed,
        out_specs=(
            P("seq", None),
            P("seq", None),
            P(None, None, "seq", "mp"),
            P(None, None, "seq", "mp"),
            P(None, None, "seq", "mp"),
            P(None, "seq", "mp"),
            P(None, None, "seq", "mp"),
            P(None, None, "seq", "mp"),
            P(None, None, "seq", "mp"),
            P(None, None, "seq", "mp"),
            P(None, None, "seq", "mp"),
            P(None, "mp", None),
            P(None, "mp", None),
            P(None, "mp", None),
            P(),
            P(),
            P(),
            P(),
        ),
        check_vma=False,
    )
```

```python
from types import SimpleNamespace

import jax
import jax.numpy as jnp
from jax import lax
from jax.experimental import pallas as pl
from jax.experimental.pallas import tpu as pltpu
from jax.sharding import PartitionSpec as P

D = 768
DH = 64
FF = 3072
WIN = 256
STEP = 10

HIGHEST_PRECISION = lax.Precision.HIGHEST
NORM_EPSILON = 1e-05
MASK_FILL = -1e30
CLIP_LEVEL = 1.0
BETA_FIRST = 0.5
BETA_SECOND = 0.5
ADAM_EPSILON = 1e-08
DECAY_RATE = 0.01
AVERAGE_RATE = 0.7
VECTOR_RATE = 0.3

BF = jnp.bfloat16
SEQ, MP = "seq", "mp"
F32 = jnp.float32
MESH = pl.DeviceIdType.MESH
BLOCK = 256
CHUNK = 128
HALF = 64
VMEM_LIMIT = 56 * 1024 * 1024
SCORE_SCALE = DH ** (-0.5)

GATHER_TIMES = ((2, 4, 5), (3, 5), (6, 7, 9), (7, 10, 13, 16))
BACK_TIMES = ((1, 4, 7, 10, 12), (6, 8, 10, 12), (10, 13, 15, 17))
END_TIMES = ((1, 4, 7, 10, 13), (5, 8, 10, 12), (11, 14, 15, 16))


def dot(left, right):
    return jnp.dot(left, right, preferred_element_type=F32)


def dot_nt(left, right):
    return lax.dot_general(left, right, (((1,), (1,)), ((), ())), preferred_element_type=F32)


def dot_tn(left, right):
    return lax.dot_general(left, right, (((0,), (0,)), ((), ())), preferred_element_type=F32)


class Flush:
    def __init__(self, held, out, sems):
        self.held, self.out, self.sems = held, out, sems

    def copy(self, rows, t):
        return pltpu.make_async_copy(self.held.at[rows, :], self.out.at[rows, :], self.sems.at[t])


def run_kernel(
    body,
    name,
    inputs,
    outputs,
    scratch,
    collective=None,
    flops=0,
    grid=None,
    specs=None,
    in_smem=(),
    in_hbm=(),
    late=None,
    flushed=None,
    pieces=0,
):
    specs, late, flushed = specs or {}, late or {}, flushed or {}

    def kernel(*refs):
        refs = list(refs)

        def take(keys):
            got = refs[: len(keys)]
            del refs[: len(keys)]
            return dict(zip(keys, got))

        given, distant, made, written, held = (take(keys) for keys in (inputs, late, outputs, flushed, scratch))
        fetched, fetched_sems, filled, filled_sems = (take(keys) for keys in (late, late, flushed, flushed))
        r = SimpleNamespace(**given, **made, **held, **fetched, **filled)
        r.late = SimpleNamespace(
            **{key: pltpu.make_async_copy(distant[key], fetched[key], fetched_sems[key]) for key in late}
        )
        r.flush = SimpleNamespace(**{key: Flush(filled[key], written[key], filled_sems[key]) for key in flushed})
        for copy in vars(r.late).values():
            copy.start()
        body(r)

    def spec_of(key):
        if key in specs:
            return specs[key]
        if key in in_hbm or key in late or key in flushed:
            return pl.BlockSpec(memory_space=pl.ANY)
        return pl.BlockSpec(memory_space=pltpu.SMEM if key in in_smem else pltpu.VMEM)

    arguments = {**inputs, **late}
    gives = {**outputs, **flushed}
    shapes = [jax.ShapeDtypeStruct(shape, dtype) for shape, dtype in gives.values()]
    moved = sum(v.size * v.dtype.itemsize for v in arguments.values())
    moved += sum(v.size * v.dtype.itemsize for v in shapes)
    extra = {} if grid is None else dict(grid=grid)
    params = dict(vmem_limit_bytes=VMEM_LIMIT)
    if collective is not None:
        params.update(collective_id=collective, has_side_effects=True)
    results = pl.pallas_call(
        kernel,
        out_shape=shapes,
        in_specs=[spec_of(key) for key in arguments],
        out_specs=[spec_of(key) for key in gives],
        scratch_shapes=list(scratch.values())
        + [pltpu.VMEM(v.shape, v.dtype) for v in late.values()]
        + [pltpu.SemaphoreType.DMA for _ in late]
        + [pltpu.VMEM(shape, dtype) for shape, dtype in flushed.values()]
        + [pltpu.SemaphoreType.DMA((pieces,)) for _ in flushed],
        compiler_params=pltpu.CompilerParams(**params),
        cost_estimate=pl.CostEstimate(flops=int(flops), bytes_accessed=int(moved), transcendentals=0),
        name=name,
        **extra,
    )(*arguments.values())
    return SimpleNamespace(**dict(zip(gives, results)))


def parity_matrix():
    row = lax.broadcasted_iota(jnp.int32, (2 * BLOCK, 2 * BLOCK), 0)
    col = lax.broadcasted_iota(jnp.int32, (2 * BLOCK, 2 * BLOCK), 1)
    source = 2 * (row % BLOCK) + row // BLOCK
    return jnp.where(col == source, 1.0, 0.0).astype(BF)


def head_lanes(count):
    lane = lax.broadcasted_iota(jnp.int32, (1, count * DH), 1)
    return [lane // DH == head for head in range(count)]


def head_flags(dilated, count):
    first = lax.axis_index(MP) * count
    return [jnp.logical_or(dilated[0] == first + head, dilated[1] == first + head) for head in range(count)]


def marked_lanes(dilated, count):
    marked = jnp.zeros((1, count * DH), jnp.int32)
    for flag, lanes in zip(head_flags(dilated, count), head_lanes(count)):
        marked = jnp.where(lanes, flag.astype(jnp.int32), marked)
    return marked > 0


def arrange_rows(natural, sort):
    groups = natural.shape[0] // (2 * BLOCK)
    parts = [
        dot(sort, natural[g * 2 * BLOCK : (g + 1) * 2 * BLOCK]).astype(BF) for g in range(groups)
    ]
    return jnp.concatenate([p[:BLOCK] for p in parts] + [p[BLOCK:] for p in parts], axis=0)


def restore_rows(arranged, sort):
    groups = arranged.shape[0] // (2 * BLOCK)
    half = groups * BLOCK
    parts = []
    for g in range(groups):
        pair = jnp.concatenate(
            [
                arranged[g * BLOCK : (g + 1) * BLOCK],
                arranged[half + g * BLOCK : half + (g + 1) * BLOCK],
            ],
            axis=0,
        )
        parts.append(dot_tn(sort, pair))
    return jnp.concatenate(parts, axis=0)


def soft_weights(query_block, key_block, lanes, allowed):
    raw = dot_nt(jnp.where(lanes, query_block, 0.0).astype(BF), key_block)
    scores = jnp.where(allowed, raw, MASK_FILL)
    top = jnp.max(scores, axis=1, keepdims=True)
    exponent = jnp.exp(scores - top)
    total = jnp.sum(exponent, axis=1, keepdims=True)
    return (exponent * (1.0 / total)).astype(BF)


def window_mask():
    row = lax.broadcasted_iota(jnp.int32, (BLOCK, 3 * BLOCK), 0)
    col = lax.broadcasted_iota(jnp.int32, (BLOCK, 3 * BLOCK), 1)
    return jnp.abs(row - col + BLOCK) <= WIN


def attend(query, pair, left, right, seg_query, seg_keys, dilated):
    rows, width = query.shape
    heads = width // DH
    blocks = rows // BLOCK
    keys = 3 * BLOCK
    slots = 2 * blocks

    def body(r):
        step = pl.program_id(0)

        @pl.when(step == 0)
        def _():
            marked = marked_lanes(r.dilated, heads)
            sort = parity_matrix()
            for which, held in ((0, r.keys), (1, r.values)):
                lanes = slice(which * width, (which + 1) * width)
                padded = jnp.concatenate([r.left[:, lanes], r.pair[:, lanes], r.right[:, lanes]], axis=0)
                middle = jnp.concatenate(
                    [
                        padded[BLOCK : (blocks + 1) * BLOCK],
                        padded[(blocks - 1) * BLOCK : (2 * blocks - 1) * BLOCK],
                    ],
                    axis=0,
                )
                held[...] = jnp.where(marked, arrange_rows(padded, sort), middle)
            scaled = (r.asked[...].astype(F32) * SCORE_SCALE).astype(BF)
            r.query[...] = jnp.where(marked, arrange_rows(scaled, sort), scaled)

        window = window_mask()
        first = step + 2 * (step >= blocks // 2)
        own = pl.ds(pl.multiple_of(step * BLOCK, BLOCK), BLOCK)
        near = pl.ds(pl.multiple_of(first * BLOCK, BLOCK), keys)
        key_block = r.keys[near, :]
        value_block = r.values[near, :]
        query_block = r.query[own, :]
        gathered = jnp.zeros((BLOCK, width), F32)
        flags = head_flags(r.dilated, heads)
        for head, lanes in enumerate(head_lanes(heads)):
            mine = jnp.where(flags[head], r.seg_query[own, 1:2], r.seg_query[own, 0:1])
            theirs = jnp.where(flags[head], r.seg_keys[1:2, near], r.seg_keys[0:1, near])
            soft = soft_weights(query_block, key_block, lanes, jnp.logical_and(window, mine == theirs))
            r.soft[head] = soft
            gathered = jnp.where(lanes, dot(soft, value_block), gathered)
        r.arranged[own, :] = gathered.astype(BF)

        @pl.when(step == blocks - 1)
        def _():
            arranged = r.arranged[...]
            natural = restore_rows(arranged, parity_matrix()).astype(BF)
            r.out[...] = jnp.where(marked_lanes(r.dilated, heads), natural, arranged)

    return run_kernel(
        body,
        "attend",
        dict(
            asked=query,
            pair=pair,
            left=left,
            right=right,
            seg_query=seg_query,
            seg_keys=seg_keys,
            dilated=dilated,
        ),
        dict(
            out=((rows, width), BF),
            arranged=((rows, width), BF),
            query=((rows, width), BF),
            keys=((slots * BLOCK, width), BF),
            values=((slots * BLOCK, width), BF),
            soft=((heads, rows, keys), BF),
        ),
        {},
        flops=4 * rows * keys * 256 * heads,
        grid=(blocks,),
        specs=dict(soft=pl.BlockSpec((heads, BLOCK, keys), lambda i: (0, i, 0))),
        in_smem=("dilated",),
    )


def attend_back(saved, grad_out, dilated, rim, mixed, count, collective):
    rows, width = grad_out.shape
    heads = width // DH
    blocks = rows // BLOCK
    keys = 3 * BLOCK
    slots = 2 * blocks if mixed else blocks + 2
    half = blocks // 2

    def order(i):
        return (i % 2) * half + i // 2

    def body(r):
        turn = pl.program_id(0)
        step = order(turn) if mixed else turn
        column = Column(count)
        first, last = column.index == 0, column.index == count - 1
        before = (lax.rem(column.index + count - 1, count), column.here)
        after = (lax.rem(column.index + 1, count), column.here)
        copy = copy_to(r.ready_left, r.from_right, r.sent.at[0], r.came.at[0], before)

        @pl.when(turn == 0)
        def _():
            barrier = pltpu.get_barrier_semaphore()

            @pl.when(jnp.logical_not(last))
            def _():
                pl.semaphore_signal(barrier, inc=1, device_id=after, device_id_type=MESH)

            grad = r.grad_out[...]
            if mixed:
                grad = jnp.where(marked_lanes(r.dilated, heads), arrange_rows(grad, parity_matrix()), grad)
            r.grad[...] = grad
            r.grad_keys[...] = jnp.zeros_like(r.grad_keys)
            r.grad_values[...] = jnp.zeros_like(r.grad_values)

            @pl.when(jnp.logical_not(first))
            def _():
                pl.semaphore_wait(barrier, 1)

        start = step + 2 * (step >= half) if mixed else step
        own = pl.ds(pl.multiple_of(step * BLOCK, BLOCK), BLOCK)
        near = pl.ds(pl.multiple_of(start * BLOCK, BLOCK), keys)
        key_block = r.keys[near, :]
        value_block = r.values[near, :]
        query_block = r.query[own, :]
        grad_block = r.grad[own, :]
        product = grad_block.astype(F32) * r.arranged[own, :].astype(F32)
        grad_query = jnp.zeros((BLOCK, width), F32)
        grad_key = jnp.zeros((keys, width), F32)
        grad_value = jnp.zeros((keys, width), F32)
        for head, lanes in enumerate(head_lanes(heads)):
            soft = r.soft[head]
            grad_head = jnp.where(lanes, grad_block, 0.0).astype(BF)
            row_dot = jnp.sum(jnp.where(lanes, product, 0.0), axis=1, keepdims=True)
            grad_soft = dot_nt(grad_head, value_block)
            grad_scores = (soft.astype(F32) * (grad_soft - row_dot)).astype(BF)
            grad_value += dot_tn(soft, grad_head)
            grad_key += dot_tn(grad_scores, jnp.where(lanes, query_block, 0.0).astype(BF))
            grad_query = jnp.where(lanes, dot(grad_scores, key_block), grad_query)
        r.grad_query[own, :] = (grad_query * SCORE_SCALE).astype(BF)
        r.grad_keys[near, :] += grad_key
        r.grad_values[near, :] += grad_value

        def natural_group(g, middle):
            both = []
            for held in (r.grad_keys, r.grad_values):
                plain = middle(held)
                pair = jnp.concatenate(
                    [
                        held[g * BLOCK : (g + 1) * BLOCK, :],
                        held[(blocks + g) * BLOCK : (blocks + g + 1) * BLOCK, :],
                    ],
                    axis=0,
                ).astype(BF)
                marked = marked_lanes(r.dilated, heads)
                both.append(jnp.where(marked, dot_tn(parity_matrix(), pair), plain).astype(BF))
            return jnp.concatenate(both, axis=1)

        edge = jnp.zeros((BLOCK, width), F32)

        @pl.when(turn == (1 if mixed else 0))
        def _():
            if mixed:
                r.ready_left[...] = natural_group(0, lambda held: jnp.concatenate([edge, held[:BLOCK, :]], axis=0))
            else:
                r.ready_left[...] = jnp.concatenate(
                    [r.grad_keys[:rim, :], r.grad_values[:rim, :]], axis=1
                ).astype(BF)

            @pl.when(jnp.logical_not(first))
            def _():
                copy.start()

        @pl.when(turn == blocks - 1)
        def _():
            if mixed:
                arranged = r.grad_query[...]
                natural = restore_rows(arranged, parity_matrix()).astype(BF)
                r.out_query[...] = jnp.where(marked_lanes(r.dilated, heads), natural, arranged)
                lap = 2 * BLOCK
                middle = blocks * BLOCK
                r.out_own[:lap, :] = natural_group(
                    1, lambda held: jnp.concatenate([held[BLOCK:lap, :], held[lap : lap + BLOCK, :] + held[middle : middle + BLOCK, :]], axis=0)
                )
                r.out_own[lap:, :] = natural_group(
                    2,
                    lambda held: jnp.concatenate(
                        [
                            held[lap + BLOCK : middle, :] + held[middle + BLOCK : middle + lap, :],
                            held[middle + lap : middle + lap + BLOCK, :],
                        ],
                        axis=0,
                    ),
                )
                r.out_right[...] = natural_group(
                    3, lambda held: jnp.concatenate([held[middle + lap + BLOCK :, :], edge], axis=0)
                )
            else:
                r.out_query[...] = r.grad_query[...]
                both = jnp.concatenate([r.grad_keys[rim:, :], r.grad_values[rim:, :]], axis=1).astype(BF)
                r.out_own[...] = both[:rows]
                r.out_right[...] = both[rows:]

            @pl.when(jnp.logical_not(last))
            def _():
                copy.wait_recv()
                tail = pl.ds(rows - rim, rim)
                r.out_own[tail, :] = (r.out_own[tail, :].astype(F32) + r.from_right[...].astype(F32)).astype(BF)

            @pl.when(jnp.logical_not(first))
            def _():
                copy.wait_send()

    soft_index = (lambda i: (0, order(i), 0)) if mixed else (lambda i: (0, i, 0))
    return run_kernel(
        body,
        "attend_back",
        dict(
            grad_out=grad_out,
            arranged=saved.arranged,
            query=saved.query,
            keys=saved.keys,
            values=saved.values,
            soft=saved.soft,
            dilated=dilated,
        ),
        dict(
            out_query=((rows, width), BF),
            out_own=((rows, 2 * width), BF),
            out_right=((rim, 2 * width), BF),
        ),
        dict(
            grad=pltpu.VMEM((rows, width), BF),
            grad_query=pltpu.VMEM((rows, width), BF),
            grad_keys=pltpu.VMEM((slots * BLOCK, width), F32),
            grad_values=pltpu.VMEM((slots * BLOCK, width), F32),
            ready_left=pltpu.VMEM((rim, 2 * width), BF),
            from_right=pltpu.VMEM((rim, 2 * width), BF),
            sent=pltpu.SemaphoreType.DMA((1,)),
            came=pltpu.SemaphoreType.DMA((1,)),
        ),
        collective=collective,
        flops=8 * rows * keys * 256 * heads,
        grid=(blocks,),
        specs=dict(soft=pl.BlockSpec((heads, BLOCK, keys), soft_index)),
        in_smem=("dilated",),
    )


class Partners:
    def __init__(self, count=0, shift=0):
        seq = lax.axis_index(SEQ)
        here = lax.axis_index(MP)
        self.core = lax.rem(here, 2)
        self.sibling = (seq, here + 1 - 2 * self.core)
        self.across = (seq, lax.rem(here + 2, 4))
        self.diagonal = (seq, lax.rem(here + 3 - 2 * self.core, 4))
        self.count, self.shift = count, shift

    def meet(self, column=None):
        barrier = pltpu.get_barrier_semaphore()
        others = [self.sibling, self.across, self.diagonal]
        if column is not None:
            others += [column.peer(k) for k in range(1, column.count)]
        for other in others:
            pl.semaphore_signal(barrier, inc=1, device_id=other, device_id_type=MESH)
        pl.semaphore_wait(barrier, len(others))

    def place(self, t):
        return lax.rem(t + self.shift, self.count) if self.shift else t

    def chunk(self, t):
        return pl.ds(pl.multiple_of(self.place(t) * CHUNK, CHUNK), CHUNK)

    def two_chunks(self, t):
        return pl.ds(pl.multiple_of(self.place(t - 1) * CHUNK, 2 * CHUNK), 2 * CHUNK)

    def own(self, t):
        return pl.ds(pl.multiple_of(self.place(t) * CHUNK + self.core * HALF, HALF), HALF)

    def other(self, t):
        return pl.ds(pl.multiple_of(self.place(t) * CHUNK + (1 - self.core) * HALF, HALF), HALF)

    def half(self, t):
        return pl.ds(pl.multiple_of(self.place(t) * HALF, HALF), HALF)


def copy_to(source, target, sent, arrived, device):
    return pltpu.make_async_remote_copy(
        src_ref=source, dst_ref=target, send_sem=sent, recv_sem=arrived, device_id=device, device_id_type=MESH
    )


def exchange_scratch(rows):
    count = rows // CHUNK
    return dict(
        part=pltpu.VMEM((rows, D), BF),
        near=pltpu.VMEM((rows // 2, D), BF),
        far=pltpu.VMEM((rows // 2, D), BF),
        core_sent=pltpu.SemaphoreType.DMA((count,)),
        core_came=pltpu.SemaphoreType.DMA((count,)),
        far_sent=pltpu.SemaphoreType.DMA((count,)),
        far_came=pltpu.SemaphoreType.DMA((count,)),
    )


def gather_scratch(rows, width=D, dtype=BF):
    count = rows // CHUNK
    return dict(
        full=pltpu.VMEM((rows, width), dtype),
        sent=pltpu.SemaphoreType.DMA((count,)),
        came=pltpu.SemaphoreType.DMA((count,)),
    )


class Exchange:
    def __init__(self, who, refs):
        self.who, self.r = who, refs

    def core_copy(self, t):
        who, r = self.who, self.r
        return copy_to(
            r.part.at[who.other(t), :], r.near.at[who.half(t), :], r.core_sent.at[t], r.core_came.at[t], who.sibling
        )

    def far_copy(self, t):
        who, r = self.who, self.r
        rows = who.half(t)
        return copy_to(r.near.at[rows, :], r.far.at[rows, :], r.far_sent.at[t], r.far_came.at[t], who.across)

    def give(self, t, part):
        self.r.part[self.who.chunk(t), :] = part.astype(BF)
        self.core_copy(t).start()

    def add(self, t):
        who, r = self.who, self.r
        self.core_copy(t).wait_recv()
        pair = r.part[who.own(t), :].astype(F32) + r.near[who.half(t), :].astype(F32)
        r.near[who.half(t), :] = pair.astype(BF)
        self.far_copy(t).start()

    def take(self, t):
        who, r = self.who, self.r
        self.far_copy(t).wait_recv()
        return r.near[who.half(t), :].astype(F32) + r.far[who.half(t), :].astype(F32)

    def finish(self, t):
        self.core_copy(t).wait_send()
        self.far_copy(t).wait_send()


class Gather:
    def __init__(self, who, refs):
        self.who, self.r = who, refs

    def copy(self, rows, t):
        r = self.r
        return copy_to(r.full.at[rows, :], r.full.at[rows, :], r.sent.at[t], r.came.at[t], self.who.sibling)

    def give(self, t, value):
        rows = self.who.own(t)
        self.r.full[rows, :] = value.astype(self.r.full.dtype)
        self.copy(rows, t).start()

    def take(self, t):
        self.wait(t)
        return self.r.full[self.who.chunk(t), :]

    def wait(self, t):
        self.copy(self.who.other(t), t).wait_recv()

    def finish(self, t):
        self.copy(self.who.own(t), t).wait_send()


class Column:
    def __init__(self, count):
        self.count = count
        self.lines = count // 2
        self.here = lax.axis_index(MP)
        self.index = lax.axis_index(SEQ)
        self.inner = lax.rem(self.index, 2)
        self.outer = lax.div(self.index, 2)

    def peer(self, k):
        return (lax.rem(self.index + k, self.count), self.here)

    def at(self, outer, inner):
        return (2 * outer + inner, self.here)

    def turn(self, k):
        return lax.rem(self.outer + k, self.lines)


def gather_sems(lines):
    return {
        key: pltpu.SemaphoreType.DMA((lines,)) for key in ("pair_sent", "pair_came", "up_sent", "down_sent", "line_came")
    }


class GatherBlocks:
    def __init__(self, column, refs):
        self.c, self.r = column, refs
        self.above = column.outer < column.lines - 1
        self.below = column.outer > 0

    def line_copy(self, source, step):
        c, r = self.c, self.r
        block = 2 * source + c.inner
        sent = r.up_sent if step > 0 else r.down_sent
        return copy_to(
            r.full.at[block], r.full.at[block], sent.at[source], r.line_came.at[source], c.at(c.outer + step, c.inner)
        )

    def pair_copy(self, source, inner):
        c, r = self.c, self.r
        block = 2 * source + inner
        return copy_to(
            r.full.at[block],
            r.full.at[block],
            r.pair_sent.at[source],
            r.pair_came.at[source],
            c.at(c.outer, 1 - c.inner),
        )

    def put(self, value):
        self.r.full[self.c.index] = value

    def start_line(self):
        c = self.c

        @pl.when(self.above)
        def _():
            self.line_copy(c.outer, 1).start()

        @pl.when(self.below)
        def _():
            self.line_copy(c.outer, -1).start()

    def start_pair(self):
        self.pair_copy(self.c.outer, self.c.inner).start()

    def relay(self, k):
        c = self.c

        @pl.when(c.outer >= k)
        def _():
            source = c.outer - k
            self.line_copy(source, 1).wait_recv()

            @pl.when(self.above)
            def _():
                self.line_copy(source, 1).start()

            self.hand_on(source)

        @pl.when(c.outer + k < c.lines)
        def _():
            source = c.outer + k
            self.line_copy(source, -1).wait_recv()

            @pl.when(self.below)
            def _():
                self.line_copy(source, -1).start()

            self.hand_on(source)

    def hand_on(self, source):
        self.pair_copy(source, self.c.inner).start()

    def arrive(self):
        for k in range(self.c.lines):
            self.pair_copy(k, 1 - self.c.inner).wait_recv()

    def finish(self):
        for k in range(self.c.lines):
            self.pair_copy(k, self.c.inner).wait_send()
        self.finish_line()

    def finish_line(self):
        c = self.c
        for k in range(c.lines):

            @pl.when(jnp.logical_and(self.above, c.outer >= k))
            def _(k=k):
                self.line_copy(k, 1).wait_send()

            @pl.when(jnp.logical_and(self.below, c.outer <= k))
            def _(k=k):
                self.line_copy(k, -1).wait_send()


class GatherPairs(GatherBlocks):
    def line_copy(self, source, step):
        c, r = self.c, self.r
        blocks = pl.ds(2 * source, 2)
        sent = r.up_sent if step > 0 else r.down_sent
        return copy_to(
            r.full.at[blocks], r.full.at[blocks], sent.at[source], r.line_came.at[source], c.at(c.outer + step, c.inner)
        )

    def begin(self):
        self.pair_copy(self.c.outer, 1 - self.c.inner).wait_recv()
        self.start_line()

    def hand_on(self, source):
        pass

    def finish(self):
        self.pair_copy(self.c.outer, self.c.inner).wait_send()
        self.finish_line()


def scatter_scratch(lines, block, size, held=True):
    scratch = {
        key: pltpu.SemaphoreType.DMA((lines + 1,))
        for key in ("pair_sent", "pair_came", "line_sent", "line_came", "own_came")
    }
    scratch.update(near=pltpu.VMEM((lines, block, size), BF), far=pltpu.VMEM((lines + 1, block, size), BF))
    if held:
        scratch["own"] = pltpu.VMEM((lines, block, size), BF)
    return scratch


class ScatterBlocks:
    def __init__(self, column, refs, total):
        self.c, self.r, self.total = column, refs, total
        self.above = column.outer < column.lines - 1
        self.below = column.outer > 0
        self.fetched = hasattr(refs, "own")
        order = []
        for k in range(column.lines // 2):
            order += [column.lines - 1 - k, k]
        self.order = order

    def pair_copy(self, outer):
        c, r = self.c, self.r
        return copy_to(
            r.grads.at[2 * outer + 1 - c.inner],
            r.near.at[outer],
            r.pair_sent.at[outer],
            r.pair_came.at[outer],
            c.at(c.outer, 1 - c.inner),
        )

    def own_copy(self, outer):
        c, r = self.c, self.r
        return pltpu.make_async_copy(r.grads.at[2 * outer + c.inner], r.own.at[outer], r.own_came.at[outer])

    def line_copy(self, target, step):
        c, r = self.c, self.r
        slot = target if step > 0 else jnp.where(c.outer - 1 == target, c.lines, target)
        return copy_to(
            r.near.at[target],
            r.far.at[slot],
            r.line_sent.at[target],
            r.line_came.at[slot],
            c.at(c.outer + step, c.inner),
        )

    def landing(self, slot, step):
        c, r = self.c, self.r
        return copy_to(
            r.near.at[c.outer], r.far.at[slot], r.line_sent.at[c.outer], r.line_came.at[slot], c.at(c.outer + step, c.inner)
        )

    def start(self):
        for outer in self.order:
            self.pair_copy(outer).start()
            if self.fetched:
                self.own_copy(outer).start()

    def pair_step(self, k):
        c, r = self.c, self.r
        for outer in self.order[2 * k : 2 * k + 2]:
            self.pair_copy(outer).wait_recv()
            if self.fetched:
                self.own_copy(outer).wait()
                own = r.own[outer]
            else:
                own = r.grads[2 * outer + c.inner]
            r.near[outer] = (own.astype(F32) + r.near[outer].astype(F32)).astype(BF)

    def line_step(self, wave):
        c, r = self.c, self.r
        from_top = c.lines - 1 - c.outer

        def pass_on(target, step, behind):
            @pl.when(behind)
            def _():
                self.landing(target, step).wait_recv()
                r.near[target] = (r.near[target].astype(F32) + r.far[target].astype(F32)).astype(BF)

            self.line_copy(target, step).start()

        @pl.when(c.outer <= wave)
        def _():
            pass_on(from_top + c.outer - wave + c.outer, 1, self.below)

        @pl.when(from_top <= wave)
        def _():
            pass_on(wave - from_top, -1, self.above)

    def close(self):
        c, r = self.c, self.r
        self.total[...] = r.near[c.outer].astype(F32)

        @pl.when(self.below)
        def _():
            self.landing(c.outer, 1).wait_recv()
            self.total[...] += r.far[c.outer].astype(F32)

        @pl.when(self.above)
        def _():
            self.landing(c.lines, -1).wait_recv()
            self.total[...] += r.far[c.lines].astype(F32)

    def finish(self):
        c = self.c
        for outer in self.order:
            self.pair_copy(outer).wait_send()
        for target in range(c.lines):

            @pl.when(c.outer < target)
            def _(target=target):
                self.line_copy(target, 1).wait_send()

            @pl.when(c.outer > target)
            def _(target=target):
                self.line_copy(target, -1).wait_send()

    def ticks(self, times):
        steps = [(times[0], lambda: self.pair_step(0)), (times[0], lambda: self.line_step(0))]
        steps += [(times[1], lambda: self.pair_step(1))]
        steps += [(times[k], lambda k=k: self.line_step(k)) for k in range(1, self.c.lines - 1)]
        steps += [(times[self.c.lines - 1], self.close)]
        return steps


def scatter_pairs_scratch(lines, block, size):
    scratch = {key: pltpu.SemaphoreType.DMA((lines + 1,)) for key in ("pair_sent", "pair_came", "line_sent", "line_came")}
    scratch.update(
        sums=pltpu.VMEM((2 * lines, block, size), BF),
        far=pltpu.VMEM((2 * lines + 2, block, size), BF),
        give=pltpu.VMEM((block, size), BF),
        get=pltpu.VMEM((block, size), BF),
        held=pltpu.SemaphoreType.DMA,
    )
    return scratch


class ScatterPairs:
    def __init__(self, column, refs, total):
        self.c, self.r, self.total = column, refs, total
        self.above = column.outer < column.lines - 1
        self.below = column.outer > 0
        self.fetch = pltpu.make_async_copy(refs.grads, refs.sums, refs.held)

    def line_copy(self, target, step):
        c, r = self.c, self.r
        slot = target if step > 0 else jnp.where(c.outer - 1 == target, c.lines, target)
        return copy_to(
            r.sums.at[pl.ds(2 * target, 2)],
            r.far.at[pl.ds(2 * slot, 2)],
            r.line_sent.at[target],
            r.line_came.at[slot],
            c.at(c.outer + step, c.inner),
        )

    def landing(self, slot, step):
        c, r = self.c, self.r
        return copy_to(
            r.sums.at[pl.ds(2 * c.outer, 2)],
            r.far.at[pl.ds(2 * slot, 2)],
            r.line_sent.at[c.outer],
            r.line_came.at[slot],
            c.at(c.outer + step, c.inner),
        )

    def pair_copy(self):
        c, r = self.c, self.r
        return copy_to(r.give, r.get, r.pair_sent.at[0], r.pair_came.at[0], c.at(c.outer, 1 - c.inner))

    def start(self):
        self.fetch.start()

    def line_step(self, wave):
        c, r = self.c, self.r
        from_top = c.lines - 1 - c.outer
        if wave == 0:
            self.fetch.wait()

        def pass_on(target, step, behind):
            @pl.when(behind)
            def _():
                self.landing(target, step).wait_recv()
                for k in range(2):
                    block = 2 * target + k
                    r.sums[block] = (r.sums[block].astype(F32) + r.far[block].astype(F32)).astype(BF)

            self.line_copy(target, step).start()

        @pl.when(c.outer <= wave)
        def _():
            pass_on(from_top + c.outer - wave + c.outer, 1, self.below)

        @pl.when(from_top <= wave)
        def _():
            pass_on(wave - from_top, -1, self.above)

    def close_line(self):
        c, r = self.c, self.r
        mine, other = 2 * c.outer + c.inner, 2 * c.outer + 1 - c.inner
        self.total[...] = r.sums[mine].astype(F32)

        @pl.when(self.below)
        def _():
            self.landing(c.outer, 1).wait_recv()
            self.total[...] += r.far[mine].astype(F32)
            r.sums[other] = (r.sums[other].astype(F32) + r.far[other].astype(F32)).astype(BF)

        @pl.when(self.above)
        def _():
            self.landing(c.lines, -1).wait_recv()
            self.total[...] += r.far[2 * c.lines + c.inner].astype(F32)
            r.sums[other] = (r.sums[other].astype(F32) + r.far[2 * c.lines + 1 - c.inner].astype(F32)).astype(BF)

        r.give[...] = r.sums[other]
        self.pair_copy().start()

    def close(self):
        self.pair_copy().wait_recv()
        self.total[...] += self.r.get[...].astype(F32)

    def finish(self):
        c = self.c
        self.pair_copy().wait_send()
        for target in range(c.lines):

            @pl.when(c.outer < target)
            def _(target=target):
                self.line_copy(target, 1).wait_send()

            @pl.when(c.outer > target)
            def _(target=target):
                self.line_copy(target, -1).wait_send()

    def ticks(self, times):
        steps = [(times[k], lambda k=k: self.line_step(k)) for k in range(self.c.lines - 1)]
        return steps + [(times[self.c.lines - 1], self.close_line), (times[self.c.lines], self.close)]


class Halo:
    def __init__(self, column, refs, source, rim, size):
        self.c, self.r, self.source, self.rim, self.size = column, refs, source, rim, size
        self.rows = source.shape[0]
        self.before = lax.rem(column.index + column.count - 1, column.count), column.here
        self.after = lax.rem(column.index + 1, column.count), column.here
        self.first, self.last = column.index == 0, column.index == column.count - 1

    def clear(self):
        @pl.when(self.first)
        def _():
            self.r.left[...] = jnp.zeros_like(self.r.left)

        @pl.when(self.last)
        def _():
            self.r.right[...] = jnp.zeros_like(self.r.right)

    def back_copy(self, t):
        rows = pl.ds(pl.multiple_of(t * self.size, self.size), self.size)
        return copy_to(
            self.source.at[rows, :], self.r.right.at[rows, :], self.r.back_sent.at[t], self.r.back_came.at[t], self.before
        )

    def ahead_copy(self, t):
        from_rows = pl.ds(pl.multiple_of(self.rows - self.rim + t * self.size, self.size), self.size)
        rows = pl.ds(pl.multiple_of(t * self.size, self.size), self.size)
        return copy_to(
            self.source.at[from_rows, :],
            self.r.left.at[rows, :],
            self.r.ahead_sent.at[t],
            self.r.ahead_came.at[t],
            self.after,
        )

    def send(self, t):
        count = self.rim // self.size
        offset = (self.rows - self.rim) // self.size

        @pl.when(jnp.logical_and(t < count, jnp.logical_not(self.first)))
        def _():
            self.back_copy(t).start()

        @pl.when(jnp.logical_and(t >= offset, jnp.logical_not(self.last)))
        def _():
            self.ahead_copy(t - offset).start()

    def arrive(self):
        for t in range(self.rim // self.size):

            @pl.when(jnp.logical_not(self.last))
            def _():
                self.back_copy(t).wait_recv()

            @pl.when(jnp.logical_not(self.first))
            def _():
                self.ahead_copy(t).wait_recv()

    def finish(self):
        for t in range(self.rim // self.size):

            @pl.when(jnp.logical_not(self.first))
            def _():
                self.back_copy(t).wait_send()

            @pl.when(jnp.logical_not(self.last))
            def _():
                self.ahead_copy(t).wait_send()


def halo_scratch(count):
    return {
        key: pltpu.SemaphoreType.DMA((count,)) for key in ("back_sent", "back_came", "ahead_sent", "ahead_came")
    }


def pick(r, prefix):
    start = prefix + "_"
    return SimpleNamespace(
        **{key[len(start) :]: value for key, value in vars(r).items() if key.startswith(start)}
    )


def prefixed(prefix, entries):
    return {prefix + "_" + key: value for key, value in entries.items()}


def run_stages(count, stages, ticks=()):
    last = max(delay for delay, _ in stages)

    def step(i, carry):
        for when in sorted({when for when, _ in ticks if when < count + last}):

            @pl.when(i == when)
            def _(when=when):
                for other, tick in ticks:
                    if other == when:
                        tick()

        for delay, stage in stages:

            @pl.when(jnp.logical_and(i >= delay, i < count + delay))
            def _(delay=delay, stage=stage):
                stage(i - delay)

        return carry

    lax.fori_loop(0, count + last, step, 0)
    for when, tick in sorted(ticks, key=lambda entry: entry[0]):
        if when >= count + last:
            tick()


def norm_forward(total, gain, shift):
    center = total - jnp.mean(total, axis=1, keepdims=True)
    spread = jnp.mean(center * center, axis=1, keepdims=True)
    inverse = lax.rsqrt(spread + NORM_EPSILON)
    unit = center * inverse
    return unit, inverse, unit * gain + shift


def norm_back(grad, unit, inverse, gain):
    grad_unit = grad * gain
    first = jnp.mean(grad_unit, axis=1, keepdims=True)
    second = jnp.mean(grad_unit * unit, axis=1, keepdims=True)
    return inverse * (grad_unit - first - unit * second)


def column_sum(value):
    return jnp.sum(value, axis=0, keepdims=True)


def split_two(value):
    high = value.astype(BF)
    return high, (value - high.astype(F32)).astype(BF)


def exact(value, product):
    high, rest = split_two(value)
    low = (value - high.astype(F32) - rest.astype(F32)).astype(BF)
    return product(high) + product(rest) + product(low)


def unturned(value, turn):
    high, rest = split_two(value)
    return dot_nt(high, turn) + dot_nt(rest, turn)


def wide(column):
    return jnp.broadcast_to(column, (column.shape[0], 128))


def forward_refs(rows, width, units):
    return dict(
        unit_one=((rows // 2, D), F32),
        unit_two=((rows // 2, D), F32),
        hidden=((rows, units), BF),
        slope=((rows, units), BF),
    )


def forward_small(rows):
    return dict(inverse_one=((rows // 2, 128), F32), inverse_two=((rows // 2, 128), F32))


def forward_stages(r, who, first, second, spread):
    def project(t):
        first.give(t, dot_nt(r.mixed[who.chunk(t), :], r.out_proj[...]))

    def middle(t):
        rows = who.own(t) if r.residual.shape[0] == r.mixed.shape[0] else who.half(t)
        total = r.residual[rows, :].astype(F32) + first.take(t) + r.shared[r.base + 0 : r.base + 1, :]
        unit, inverse, normed = norm_forward(total, r.shared[r.base + 1 : r.base + 2, :], r.shared[r.base + 2 : r.base + 3, :])
        r.unit_one[who.half(t), :] = unit
        r.inverse_one[who.half(t), :] = wide(inverse)
        r.normed[who.half(t), :] = normed
        spread.give(t, normed)

    def feed(t):
        pre = dot(spread.take(t), r.ffn_up[...]) + r.hidden_bias
        chance = 0.5 + 0.5 * lax.erf(pre * (0.5**0.5))
        hidden = (pre * chance).astype(BF)
        r.hidden[who.chunk(t), :] = hidden
        bell = jnp.exp(-0.5 * pre * pre) * 0.3989422804014327
        r.slope[who.chunk(t), :] = (chance + pre * bell).astype(BF)
        second.give(t, dot_nt(hidden, r.ffn_down[...]))

    def final(t):
        total = r.normed[who.half(t), :] + second.take(t) + r.shared[r.base + 3 : r.base + 4, :]
        unit, inverse, result = norm_forward(total, r.shared[r.base + 4 : r.base + 5, :], r.shared[r.base + 5 : r.base + 6, :])
        r.unit_two[who.half(t), :] = unit
        r.inverse_two[who.half(t), :] = wide(inverse)
        return unit, inverse, result

    return project, middle, feed, final


def backward_stages(r, who, ends, third, mids):
    def enter(t, grad, unit, inverse):
        grad_total = norm_back(grad, unit, inverse, r.shared[r.base + 4 : r.base + 5, :])
        r.vectors[3:4, :] += column_sum(grad_total)
        r.vectors[4:5, :] += column_sum(grad * unit)
        r.vectors[5:6, :] += column_sum(grad)
        r.kept[who.half(t), :] = grad_total
        ends.give(t, grad_total)

    def feed_back(t):
        rows = who.chunk(t)
        grad = ends.take(t)
        grad_pre = (dot(grad, r.ffn_down[...]) * r.slope[rows, :].astype(F32)).astype(BF)
        r.units[0:1, :] += column_sum(grad_pre.astype(F32))
        third.give(t, dot_nt(grad_pre, r.ffn_up[...]))
        r.grad_pre[pl.ds(pl.multiple_of(lax.rem(t, 2) * CHUNK, CHUNK), CHUNK), :] = grad_pre

        @pl.when(lax.rem(t, 2) == 1)
        def _():
            both = who.two_chunks(t)
            r.sum_up[...] += dot_tn(r.spread_full[both, :], r.grad_pre[...])
            r.sum_down[...] += dot_tn(ends.r.full[both, :], r.hidden[both, :])

    def leave(t):
        grad = r.kept[who.half(t), :] + third.take(t)
        unit = r.unit_one[who.half(t), :]
        grad_total = norm_back(grad, unit, r.inverse_one[who.half(t), 0:1], r.shared[r.base + 1 : r.base + 2, :])
        r.vectors[0:1, :] += column_sum(grad_total)
        r.vectors[1:2, :] += column_sum(grad * unit)
        r.vectors[2:3, :] += column_sum(grad)
        r.grad_one[who.half(t), :] = grad_total
        mids.give(t, grad_total)

    def project_back(t):
        rows = who.chunk(t)
        grad = mids.take(t)
        r.grad_mixed[rows, :] = dot(grad, r.out_proj[...]).astype(BF)

        @pl.when(lax.rem(t, 2) == 1)
        def _():
            both = who.two_chunks(t)
            r.sum_out[...] += dot_tn(mids.r.full[both, :], r.mixed[both, :])

    return enter, feed_back, leave, project_back


def clear(*refs):
    for ref in refs:
        ref[...] = jnp.zeros_like(ref)


def finish_all(count, parts):
    def step(t, carry):
        for part in parts:
            part.finish(t)
        return carry

    lax.fori_loop(0, count, step, 0)


def packed(ref):
    return jnp.concatenate([ref[k].astype(BF) for k in range(ref.shape[0])], axis=1)


def projection_bias(split, width):
    return jnp.concatenate([split[:, :width], jnp.zeros((1, width), F32), split[:, width : 2 * width]], axis=1)


def opening(activations, segments, owners, attn_weights, ffn_weights, split_biases, shared_vectors, count):
    rows = activations.shape[0]
    width, units = attn_weights.shape[3], ffn_weights.shape[3]
    heads = width // DH
    blocks = rows // BLOCK
    lines = count // 2
    block = D // count
    layers = split_biases.shape[0]

    def body(r):
        who = Partners()
        column = Column(count)
        who.meet(column)
        wide_attn = GatherBlocks(column, SimpleNamespace(full=r.full_attn, **vars(pick(r, "ga"))))
        wide_up = GatherBlocks(column, SimpleNamespace(full=r.full_up, **vars(pick(r, "gu"))))
        wide_down = GatherPairs(column, SimpleNamespace(full=r.full_down, **vars(pick(r, "gd"))))
        halo = Halo(column, SimpleNamespace(left=r.left, right=r.right, **vars(pick(r, "halo"))), r.pair, WIN, BLOCK)
        first, last = column.index == 0, column.index == count - 1
        to_before = copy_to(r.ids, r.ids_right, r.ids_sent.at[0], r.ids_came.at[0], halo.before)
        to_after = copy_to(r.ids, r.ids_left, r.ids_sent.at[1], r.ids_came.at[1], halo.after)
        wide_attn.put(packed(r.attn.at[0]))
        wide_attn.start_line()
        wide_attn.start_pair()
        r.ids[...] = r.segments[...].astype(F32)

        @pl.when(first)
        def _():
            r.ids_left[...] = jnp.zeros_like(r.ids_left)

        @pl.when(last)
        def _():
            r.ids_right[...] = jnp.zeros_like(r.ids_right)

        @pl.when(jnp.logical_not(first))
        def _():
            to_before.start()

        @pl.when(jnp.logical_not(last))
        def _():
            to_after.start()

        halo.clear()
        wide_down.put(r.ffn[0, 1].astype(BF))
        wide_down.start_pair()
        wide_up.put(r.ffn[0, 0].astype(BF))
        for slot in range(count):
            row = lax.broadcasted_iota(jnp.int32, (block, D), 0)
            col = lax.broadcasted_iota(jnp.int32, (block, D), 1)
            target = r.owners[slot] * block + row
            r.turn[slot * block : (slot + 1) * block, :] = jnp.where(col == target, 1.0, 0.0).astype(BF)

        def sort_chunk(t, carry):
            chunk = pl.ds(pl.multiple_of(t * BLOCK, BLOCK), BLOCK)
            r.low[chunk, :] = dot(r.activations[chunk, :], r.turn[...]).astype(BF)
            return carry

        lax.fori_loop(0, blocks, sort_chunk, 0)
        wide_attn.relay(1)
        padding = jnp.zeros((16 - 6 * layers, D), F32)
        stacked = [r.shared_vectors[k, layer : layer + 1, :] for layer in range(layers) for k in range(6)]
        stacked = jnp.concatenate(stacked + [padding], axis=0)
        r.shared[...] = exact(stacked, lambda part: dot(part, r.turn[...]))
        wide_attn.relay(2)
        wide_up.start_line()

        @pl.when(jnp.logical_not(last))
        def _():
            to_before.wait_recv()

        @pl.when(jnp.logical_not(first))
        def _():
            to_after.wait_recv()

        def flat(ref):
            return jnp.concatenate([ref[k : k + 1, :] for k in range(ref.shape[0])], axis=1)

        own_ids = flat(r.ids)
        padded = jnp.concatenate([flat(r.ids_left)[:, rows - 2 * WIN :], own_ids, flat(r.ids_right)[:, : 2 * WIN]], axis=1)
        r.id_row[...] = jnp.broadcast_to(padded, r.id_row.shape)
        sort = parity_matrix()
        lap = 2 * BLOCK
        sorted_ids = [
            dot_nt(r.id_row[:, g * lap : (g + 1) * lap].astype(BF), sort) for g in range(2 * blocks // 2)
        ]
        natural = jnp.concatenate(
            [padded[:, WIN : rows + WIN], padded[:, rows - WIN : 2 * rows - WIN]], axis=1
        )
        arranged = jnp.concatenate(
            [part[0:1, :BLOCK] for part in sorted_ids] + [part[0:1, BLOCK:] for part in sorted_ids], axis=1
        )
        r.seg_keys[0:1, :] = natural
        r.seg_keys[1:2, :] = arranged
        middle = sorted_ids[1:-1]
        own_arranged = jnp.concatenate(
            [part[0:1, :BLOCK] for part in middle] + [part[0:1, BLOCK:] for part in middle], axis=1
        )
        for which, row in ((0, own_ids), (1, own_arranged)):
            for k in range(rows // 128):
                square = jnp.broadcast_to(row[:, k * 128 : (k + 1) * 128], (128, 128))
                r.seg_query[k * 128 : (k + 1) * 128, which : which + 1] = square.T[:, 0:1]

        for k in range(3, lines):
            wide_attn.relay(k)
        wide_up.start_pair()
        wide_up.relay(1)
        wide_attn.arrive()
        r.proj[...] = r.full_attn[...].reshape(D, 4 * width)[:, : 3 * width]
        bias = projection_bias(r.split[0], width)

        def project(t):
            chunk = pl.ds(pl.multiple_of(t * BLOCK, BLOCK), BLOCK)
            value = dot(r.low[chunk, :], r.proj[...]) + bias
            r.query[chunk, :] = (value[:, :width].astype(BF).astype(F32) * SCORE_SCALE).astype(BF)
            pair = value[:, width:].astype(BF)
            r.pair[chunk, :] = pair
            inner = pl.ds(pl.multiple_of((t + 1) * BLOCK, BLOCK), BLOCK)
            r.keys[inner, :] = pair[:, :width]
            r.values[inner, :] = pair[:, width:]

        def outer_project(i, carry):
            t = i * (blocks - 1)
            project(t)
            halo.send(t)
            return carry

        def inner_project(i, carry):
            project(i)
            return carry

        lax.fori_loop(0, 2, outer_project, 0)
        wide_up.relay(2)
        wide_down.begin()
        lax.fori_loop(1, blocks - 1, inner_project, 0)
        for k in range(3, lines):
            wide_up.relay(k)

        def attend_block(step):
            own = pl.ds(pl.multiple_of(step * BLOCK, BLOCK), BLOCK)
            near = pl.ds(pl.multiple_of(step * BLOCK, BLOCK), 3 * BLOCK)
            key_block, value_block, query_block = r.keys[near, :], r.values[near, :], r.query[own, :]
            mine = r.seg_query[own, 0:1]
            theirs = r.id_row[0:1, pl.ds(pl.multiple_of(step * BLOCK + BLOCK, BLOCK), 3 * BLOCK)]
            allowed = jnp.logical_and(window_mask(), mine == theirs)
            gathered = jnp.zeros((BLOCK, width), F32)
            for head, lanes in enumerate(head_lanes(heads)):
                soft = soft_weights(query_block, key_block, lanes, allowed)
                r.soft[head, own, :] = soft
                gathered = jnp.where(lanes, dot(soft, value_block), gathered)
            r.out[own, :] = gathered.astype(BF)

        def inner_attend(i, carry):
            attend_block(i)
            return carry

        def outer_attend(i, carry):
            attend_block(i * (blocks - 1))
            return carry

        lax.fori_loop(1, blocks - 1, inner_attend, 0)
        wide_down.relay(1)
        halo.arrive()
        for part, start in ((r.left, 0), (r.right, (blocks + 1) * BLOCK)):
            r.keys[pl.ds(start, BLOCK), :] = part[:, :width]
            r.values[pl.ds(start, BLOCK), :] = part[:, width:]
        lax.fori_loop(0, 2, outer_attend, 0)
        for k in range(2, lines):
            wide_down.relay(k)
        wide_up.arrive()
        halo.finish()
        for engine in (wide_attn, wide_up, wide_down):
            engine.finish()

        @pl.when(jnp.logical_not(first))
        def _():
            to_before.wait_send()

        @pl.when(jnp.logical_not(last))
        def _():
            to_after.wait_send()

    scratch = dict(
        proj=pltpu.VMEM((D, 3 * width), BF),
        pair=pltpu.VMEM((rows, 2 * width), BF),
        left=pltpu.VMEM((WIN, 2 * width), BF),
        right=pltpu.VMEM((WIN, 2 * width), BF),
        ids=pltpu.VMEM((rows // 128, 128), F32),
        ids_left=pltpu.VMEM((rows // 128, 128), F32),
        ids_right=pltpu.VMEM((rows // 128, 128), F32),
        ids_sent=pltpu.SemaphoreType.DMA((2,)),
        ids_came=pltpu.SemaphoreType.DMA((2,)),
        id_row=pltpu.VMEM((8, rows + 4 * WIN), F32),
    )
    scratch.update(prefixed("ga", gather_sems(lines)))
    scratch.update(prefixed("gu", gather_sems(lines)))
    scratch.update(prefixed("gd", gather_sems(lines)))
    scratch.update(prefixed("halo", halo_scratch(1)))
    return run_kernel(
        body,
        "opening",
        dict(
            activations=activations,
            segments=segments.reshape(rows // 128, 128),
            owners=owners,
            attn=attn_weights,
            ffn=ffn_weights,
            split=split_biases,
            shared_vectors=shared_vectors.transpose(1, 0, 2),
        ),
        dict(
            full_attn=((count, block, 4 * width), BF),
            full_up=((count, block, units), BF),
            full_down=((count, block, units), BF),
            low=((rows, D), BF),
            turn=((D, D), BF),
            shared=((16, D), F32),
            seg_query=((rows, 2), F32),
            seg_keys=((8, 2 * rows), F32),
            out=((rows, width), BF),
            query=((rows, width), BF),
            keys=((rows + 2 * BLOCK, width), BF),
            values=((rows + 2 * BLOCK, width), BF),
            soft=((heads, rows, 3 * BLOCK), BF),
        ),
        scratch,
        collective=5,
        flops=2 * rows * D * (D + 3 * width),
        in_smem=("owners",),
    )


def middle_forward(mixed, attn, ffn_up, ffn_down, residual, shared, split_biases, attn_weights, ffn_weights, count):
    rows, width = mixed.shape
    units = ffn_up.shape[1]
    chunks = rows // CHUNK
    lines = count // 2
    block = D // count

    def body(r):
        who = Partners()
        r.base = 0
        first, second = Exchange(who, pick(r, "first")), Exchange(who, pick(r, "second"))
        spread = Gather(who, SimpleNamespace(full=r.spread_full, sent=r.spread_sent, came=r.spread_came))
        last = Gather(who, SimpleNamespace(full=r.last_full, sent=r.last_sent, came=r.last_came))
        column = Column(count)
        who.meet(column)
        wide_attn = GatherBlocks(column, SimpleNamespace(full=r.full_attn, **vars(pick(r, "ga"))))
        wide_up = GatherBlocks(column, SimpleNamespace(full=r.full_up, **vars(pick(r, "gu"))))
        wide_down = GatherPairs(column, SimpleNamespace(full=r.full_down, **vars(pick(r, "gd"))))
        halo = Halo(column, SimpleNamespace(left=r.left, right=r.right, **vars(pick(r, "halo"))), r.pair, 2 * WIN, CHUNK)
        wide_attn.put(packed(r.next_attn.at[1]))
        wide_attn.start_line()
        wide_attn.start_pair()
        wide_down.put(r.next_ffn[1, 1].astype(BF))
        wide_down.start_pair()
        wide_up.put(r.next_ffn[1, 0].astype(BF))
        halo.clear()
        r.out_proj[...] = r.attn[:, 3 * width :]
        r.hidden_bias = r.split[0][:, 2 * width :]
        next_bias = projection_bias(r.split[1], width)

        def unpack():
            wide_attn.arrive()
            r.next_proj[...] = r.full_attn[...].reshape(D, 4 * width)[:, : 3 * width]

        ticks = [(3, r.late.residual.wait), (4, r.late.ffn_up.wait), (4, r.late.ffn_down.wait), (chunks, unpack)]
        ticks += [(when, lambda k=k: wide_attn.relay(k + 1)) for k, when in enumerate(GATHER_TIMES[0])]
        ticks += [(GATHER_TIMES[1][0], wide_up.start_line), (GATHER_TIMES[1][1], wide_up.start_pair)]
        ticks += [(when, lambda k=k: wide_up.relay(k + 1)) for k, when in enumerate(GATHER_TIMES[2])]
        ticks += [(GATHER_TIMES[3][0], wide_down.begin)]
        ticks += [(when, lambda k=k: wide_down.relay(k + 1)) for k, when in enumerate(GATHER_TIMES[3][1:])]
        project, middle, feed, final = forward_stages(r, who, first, second, spread)

        def middle_out(t):
            middle(t)
            r.flush.unit_one.copy(who.half(t), t).start()

        def feed_out(t):
            feed(t)
            for flush in (r.flush.hidden, r.flush.slope, r.flush.spread_full):
                flush.copy(who.chunk(t), t).start()

        def close(t):
            _, _, result = final(t)
            r.result[who.half(t), :] = result
            for flush in (r.flush.unit_two, r.flush.result):
                flush.copy(who.half(t), t).start()
            last.give(t, result)

        def next_project(t):
            value = (dot(last.take(t), r.next_proj[...]) + next_bias).astype(BF)
            r.query[who.chunk(t), :] = value[:, :width]
            r.pair[who.chunk(t), :] = value[:, width:]
            halo.send(t)
            r.flush.last_full.copy(who.chunk(t), t).start()

        run_stages(
            chunks,
            [
                (5, second.add),
                (1, first.add),
                (7, close),
                (3, middle_out),
                (8, next_project),
                (4, feed_out),
                (0, project),
            ],
            ticks,
        )
        finish_all(chunks, (first, second, spread, last))
        halo.arrive()
        wide_up.arrive()
        halo.finish()
        for engine in (wide_attn, wide_up, wide_down):
            engine.finish()

        def written(t, carry):
            for flush in (r.flush.hidden, r.flush.slope, r.flush.spread_full, r.flush.last_full):
                flush.copy(who.chunk(t), t).wait()
            for flush in (r.flush.unit_one, r.flush.unit_two, r.flush.result):
                flush.copy(who.half(t), t).wait()
            return carry

        lax.fori_loop(0, chunks, written, 0)

    outputs = forward_small(rows)
    outputs.update(
        query=((rows, width), BF),
        pair=((rows, 2 * width), BF),
        full_attn=((count, block, 4 * width), BF),
        full_up=((count, block, units), BF),
        full_down=((count, block, units), BF),
        left=((2 * WIN, 2 * width), BF),
        right=((2 * WIN, 2 * width), BF),
    )
    flushed = forward_refs(rows, width, units)
    flushed.update(spread_full=((rows, D), BF), last_full=((rows, D), BF), result=((rows // 2, D), F32))
    scratch = dict(
        normed=pltpu.VMEM((rows // 2, D), F32),
        out_proj=pltpu.VMEM((D, width), BF),
        next_proj=pltpu.VMEM((D, 3 * width), BF),
    )
    scratch.update(prefixed("first", exchange_scratch(rows)))
    scratch.update(prefixed("second", exchange_scratch(rows)))
    for key in ("spread", "last"):
        for part in ("sent", "came"):
            scratch[key + "_" + part] = pltpu.SemaphoreType.DMA((chunks,))
    for key in ("ga", "gu", "gd"):
        scratch.update(prefixed(key, gather_sems(lines)))
    scratch.update(prefixed("halo", halo_scratch(2 * WIN // CHUNK)))
    return run_kernel(
        body,
        "middle_forward",
        dict(
            mixed=mixed,
            attn=attn,
            shared=shared,
            split=split_biases,
            next_attn=attn_weights,
            next_ffn=ffn_weights,
        ),
        outputs,
        scratch,
        collective=1,
        flops=2 * rows * D * (4 * width + 2 * units),
        late=dict(residual=residual, ffn_up=ffn_up, ffn_down=ffn_down),
        flushed=flushed,
        pieces=chunks,
    )


def turning(mixed, attn, ffn_up, ffn_down, residual, shared, split_biases, cotangent, turn):
    rows, width = mixed.shape
    units = ffn_up.shape[1]
    chunks = rows // CHUNK

    def body(r):
        who = Partners()
        r.base = 6
        first, second = Exchange(who, pick(r, "first")), Exchange(who, pick(r, "second"))
        third = Exchange(who, pick(r, "third"))
        spread = Gather(who, pick(r, "spread"))
        ends, mids = Gather(who, pick(r, "ends")), Gather(who, pick(r, "mids"))
        out = Gather(who, SimpleNamespace(full=r.output, sent=r.out_sent, came=r.out_came))
        who.meet()
        r.out_proj[...] = r.attn[:, 3 * width :]
        r.hidden_bias = r.split[1][:, 2 * width :]
        clear(r.vectors, r.units, r.sum_up, r.sum_down, r.sum_out)
        project, middle, feed, final = forward_stages(r, who, first, second, spread)
        enter, feed_back, leave, project_back = backward_stages(r, who, ends, third, mids)

        ticks = [(3, r.late.residual.wait), (4, r.late.ffn_up.wait), (4, r.late.ffn_down.wait)]
        ticks += [(7, r.late.cotangent.wait), (7, r.late.turn.wait)]

        def close(t):
            unit, inverse, result = final(t)
            grad = dot(r.cotangent[who.own(t), :], r.turn[...])
            enter(t, grad, unit, inverse)
            out.give(t, unturned(result, r.turn[...]))

        run_stages(
            chunks,
            [
                (9, third.add),
                (5, second.add),
                (1, first.add),
                (11, leave),
                (7, close),
                (3, middle),
                (12, project_back),
                (8, feed_back),
                (4, feed),
                (0, project),
            ],
            ticks,
        )

        def arrive(t, carry):
            out.wait(t)
            return carry

        lax.fori_loop(0, chunks, arrive, 0)
        finish_all(chunks, (first, second, third, spread, ends, mids, out))
        r.up[...] = r.sum_up[...].astype(BF)
        r.down[...] = r.sum_down[...].astype(BF)
        r.proj[...] = r.sum_out[...].astype(BF)

    outputs = dict(
        output=((rows, D), F32),
        up=((D, units), BF),
        down=((D, units), BF),
        proj=((D, width), BF),
        grad_one=((rows // 2, D), F32),
        grad_mixed=((rows, width), BF),
        vectors=((8, D), F32),
        units=((8, units), F32),
    )
    scratch = dict(
        normed=pltpu.VMEM((rows // 2, D), F32),
        kept=pltpu.VMEM((rows // 2, D), F32),
        grad_pre=pltpu.VMEM((2 * CHUNK, units), BF),
        out_proj=pltpu.VMEM((D, width), BF),
        sum_up=pltpu.VMEM((D, units), F32),
        sum_down=pltpu.VMEM((D, units), F32),
        sum_out=pltpu.VMEM((D, width), F32),
        out_sent=pltpu.SemaphoreType.DMA((chunks,)),
        out_came=pltpu.SemaphoreType.DMA((chunks,)),
    )
    for key, (shape, dtype) in {**forward_refs(rows, width, units), **forward_small(rows)}.items():
        scratch[key] = pltpu.VMEM(shape, dtype)
    for key in ("first", "second", "third"):
        scratch.update(prefixed(key, exchange_scratch(rows)))
    for key in ("spread", "ends", "mids"):
        scratch.update(prefixed(key, gather_scratch(rows)))
    return run_kernel(
        body,
        "turning",
        dict(
            mixed=mixed,
            attn=attn,
            shared=shared,
            split=split_biases,
        ),
        outputs,
        scratch,
        collective=2,
        flops=2 * rows * D * (3 * width + 6 * units),
        late=dict(residual=residual, ffn_up=ffn_up, ffn_down=ffn_down, cotangent=cotangent, turn=turn),
    )


def projection_back_stage(r, who, column, exchange):
    rows, width = r.grad_query.shape
    rim = r.out_right.shape[0]
    first, last = column.index == 0, column.index == column.count - 1
    after = (lax.rem(column.index + 1, column.count), column.here)
    copy = copy_to(r.out_right, r.from_left, r.halo_sent.at[0], r.halo_came.at[0], after)

    def begin():
        r.grad_pair[...] = r.grad_own[...]

        @pl.when(jnp.logical_not(last))
        def _():
            copy.start()

    def absorb():
        @pl.when(jnp.logical_not(first))
        def _():
            copy.wait_recv()
            where = pl.ds(0, rim)
            total = r.grad_pair[where, :].astype(F32) + r.from_left[...].astype(F32)
            r.grad_pair[where, :] = total.astype(BF)

    def end():
        @pl.when(jnp.logical_not(last))
        def _():
            copy.wait_send()

    def stage(k):
        both = who.two_chunks(2 * k + 1)
        parts = jnp.concatenate([r.grad_query[both, :], r.grad_pair[both, :]], axis=1)
        exchange.r.part[both, :] = dot_nt(parts, r.next_attn[:, : 3 * width]).astype(BF)
        for t in (2 * k, 2 * k + 1):
            exchange.core_copy(t).start()
        r.sum_three[...] += dot_tn(r.low[both, :], parts)
        r.biases[0:1, :] += column_sum(parts.astype(F32))

    half = rows // CHUNK // 2
    steps = [(0 if k < half // 2 else half, k) for k in range(half)]
    ticks = [(half, absorb)] + [(first_time + k % (half // 2), lambda k=k: stage(k)) for first_time, k in steps]
    return begin, end, ticks


def projection_back_scratch(rows, rim, width):
    return dict(
        grad_pair=pltpu.VMEM((rows, 2 * width), BF),
        from_left=pltpu.VMEM((rim, 2 * width), BF),
        halo_sent=pltpu.SemaphoreType.DMA((1,)),
        halo_came=pltpu.SemaphoreType.DMA((1,)),
        sum_three=pltpu.VMEM((D, 3 * width), F32),
    )


def scatter_three(column, r, totals):
    return (
        ScatterPairs(column, SimpleNamespace(grads=r.above_up, **vars(pick(r, "ru"))), totals[0]),
        ScatterBlocks(column, SimpleNamespace(grads=r.above_down, **vars(pick(r, "rd"))), totals[1]),
        ScatterBlocks(column, SimpleNamespace(grads=r.packed, **vars(pick(r, "ra"))), totals[2]),
    )


def scatter_three_scratch(count, width, units):
    lines, block = count // 2, D // count
    scratch = dict(packed=pltpu.VMEM((count, block, 4 * width), BF))
    scratch.update(prefixed("ru", scatter_pairs_scratch(lines, block, units)))
    scratch.update(prefixed("rd", scatter_scratch(lines, block, units)))
    scratch.update(prefixed("ra", scatter_scratch(lines, block, 4 * width, held=False)))
    return scratch


def pack_attention(r):
    both = jnp.concatenate([r.sum_three[...].astype(BF), r.above_proj[...]], axis=1)
    r.packed[...] = both.reshape(r.packed.shape)


def middle_backward(back, next_attn, grad_above, low, saved, mixed, attn, ffn_up, ffn_down, shared, above, count):
    rows, width = mixed.shape
    units = ffn_up.shape[1]
    chunks = rows // CHUNK
    block = D // count
    rim = back.out_right.shape[0]

    def body(r):
        who = Partners(chunks, chunks // 2)
        r.base = 0
        zeroth, third = Exchange(who, pick(r, "zeroth")), Exchange(who, pick(r, "third"))
        ends, mids = Gather(who, pick(r, "ends")), Gather(who, pick(r, "mids"))
        column = Column(count)
        who.meet(column)
        up, down, three = scatter_three(column, r, (r.up_total, r.down_total, r.attn_total))
        begin, end, back_ticks = projection_back_stage(r, who, column, zeroth)
        begin()
        up.start()
        down.start()

        def start_three():
            pack_attention(r)
            three.start()

        ticks = [tick for engine, times in zip((up, down, three), BACK_TIMES) for tick in engine.ticks(times)]
        ticks += [(chunks // 2 + 2, start_three)]
        ticks += [(3, r.late.unit_two.wait), (3, r.late.grad_above.wait), (4, r.late.ffn_up.wait)]
        ticks += [(4, r.late.ffn_down.wait), (4, r.late.slope.wait), (4, r.late.hidden.wait)]
        ticks += [(4, r.late.spread_full.wait), (7, r.late.unit_one.wait), (8, r.late.mixed.wait)]
        ticks = back_ticks + ticks
        r.out_proj[...] = r.attn[:, 3 * width :]
        clear(r.vectors, r.units, r.biases, r.sum_up, r.sum_down, r.sum_out, r.sum_three)
        enter, feed_back, leave, project_back = backward_stages(r, who, ends, third, mids)

        def start(t):
            half = who.half(t)
            enter(t, r.grad_above[half, :] + zeroth.take(t), r.unit_two[half, :], r.inverse_two[half, 0:1])

        run_stages(
            chunks,
            [
                (5, third.add),
                (1, zeroth.add),
                (7, leave),
                (3, start),
                (8, project_back),
                (4, feed_back),
            ],
            ticks,
        )
        finish_all(chunks, (zeroth, third, ends, mids))
        end()
        r.up[...] = r.sum_up[...].astype(BF)
        r.down[...] = r.sum_down[...].astype(BF)
        r.proj[...] = r.sum_out[...].astype(BF)
        for engine in (up, down, three):
            engine.finish()

    outputs = dict(
        up=((D, units), BF),
        down=((D, units), BF),
        proj=((D, width), BF),
        grad_one=((rows // 2, D), F32),
        grad_mixed=((rows, width), BF),
        vectors=((8, D), F32),
        units=((8, units), F32),
        biases=((8, 3 * width), F32),
        up_total=((block, units), F32),
        down_total=((block, units), F32),
        attn_total=((block, 4 * width), F32),
    )
    scratch = dict(
        kept=pltpu.VMEM((rows // 2, D), F32),
        grad_pre=pltpu.VMEM((2 * CHUNK, units), BF),
        out_proj=pltpu.VMEM((D, width), BF),
        sum_up=pltpu.VMEM((D, units), F32),
        sum_down=pltpu.VMEM((D, units), F32),
        sum_out=pltpu.VMEM((D, width), F32),
    )
    scratch.update(projection_back_scratch(rows, rim, width))
    scratch.update(scatter_three_scratch(count, width, units))
    for key in ("zeroth", "third"):
        scratch.update(prefixed(key, exchange_scratch(rows)))
    for key in ("ends", "mids"):
        scratch.update(prefixed(key, gather_scratch(rows)))
    return run_kernel(
        body,
        "middle_backward",
        dict(
            grad_query=back.out_query,
            grad_own=back.out_own,
            out_right=back.out_right,
            next_attn=next_attn,
            low=low,
            inverse_one=saved.inverse_one,
            inverse_two=saved.inverse_two,
            attn=attn,
            shared=shared,
            above_up=above.up.reshape(count, block, units),
            above_down=above.down.reshape(count, block, units),
            above_proj=above.proj,
        ),
        outputs,
        scratch,
        collective=3,
        flops=2 * rows * D * (8 * width + 4 * units),
        in_hbm=("above_up", "above_down"),
        late=dict(
            unit_two=saved.unit_two,
            grad_above=grad_above,
            ffn_down=ffn_down,
            slope=saved.slope,
            ffn_up=ffn_up,
            hidden=saved.hidden,
            spread_full=saved.spread_full,
            unit_one=saved.unit_one,
            mixed=mixed,
        ),
    )


class SmallSum:
    def __init__(self, who, column, refs):
        self.who, self.c, self.r = who, column, refs

    def copy(self, slot, source, device):
        r = self.r
        return copy_to(r.kept.at[source], r.came.at[slot], r.sent_sem.at[slot], r.came_sem.at[slot], device)

    def core_copy(self):
        return self.copy(0, 0, self.who.sibling)

    def pair_copy(self):
        return self.copy(1, 1, self.c.at(self.c.outer, 1 - self.c.inner))

    def line_copy(self, target, slot):
        c, r = self.c, self.r
        return copy_to(
            r.kept.at[2], r.came.at[2 + slot], r.sent_sem.at[2 + target], r.came_sem.at[2 + slot], c.at(target, c.inner)
        )

    def second(self, both):
        r = self.r
        self.core_copy().wait_recv()
        row = lax.broadcasted_iota(jnp.int32, r.kept.shape[1:], 0)
        r.kept[1] = r.kept[0] + jnp.where(row < both, r.came[0], 0.0)
        self.pair_copy().start()

    def third(self):
        r, c = self.r, self.c
        self.pair_copy().wait_recv()
        r.kept[2] = r.kept[1] + r.came[1]
        for k in range(1, c.lines):
            self.line_copy(c.turn(k), c.outer).start()
        r.came[2 + c.outer] = r.kept[2]

    def result(self):
        r, c = self.r, self.c
        for k in range(1, c.lines):
            source = c.turn(k)
            self.line_copy(source, source).wait_recv()
        return sum(r.came[2 + k] for k in range(c.lines))

    def finish(self):
        c = self.c
        self.core_copy().wait_send()
        self.pair_copy().wait_send()
        for k in range(1, c.lines):
            self.line_copy(c.turn(k), c.outer).wait_send()


def small_scratch(lines, shape):
    return dict(
        kept=pltpu.VMEM((3,) + shape, F32),
        came=pltpu.VMEM((2 + lines,) + shape, F32),
        sent_sem=pltpu.SemaphoreType.DMA((2 + lines,)),
        came_sem=pltpu.SemaphoreType.DMA((2 + lines,)),
    )


class NormSum:
    def __init__(self, who, column, refs):
        self.who, self.c, self.r = who, column, refs

    def mp_copy(self, device, target, slot):
        r = self.r
        return copy_to(r.mp_came.at[slot], r.mp_came.at[slot], r.mp_sent.at[target], r.mp_sem.at[slot], device)

    def seq_copy(self, device, target, slot):
        r = self.r
        return copy_to(r.seq_came.at[slot], r.seq_came.at[slot], r.seq_sent.at[target], r.seq_sem.at[slot], device)

    def run(self, value):
        who, c, r = self.who, self.c, self.r
        here = c.here
        r.mp_came[here] = jnp.full((8, 128), 1.0, F32) * value
        for k in range(1, 4):
            target = lax.rem(here + k, 4)
            self.mp_copy((c.index, target), target, here).start()
        for k in range(1, 4):
            source = lax.rem(here + k, 4)
            self.mp_copy((c.index, source), source, source).wait_recv()
        r.seq_came[c.index] = sum(r.mp_came[k] for k in range(4))
        for k in range(1, c.count):
            target = lax.rem(c.index + k, c.count)
            self.seq_copy((target, here), target, c.index).start()
        for k in range(1, c.count):
            source = lax.rem(c.index + k, c.count)
            self.seq_copy((source, here), source, source).wait_recv()
        total = sum(r.seq_came[k] for k in range(c.count))
        for k in range(1, 4):
            target = lax.rem(here + k, 4)
            self.mp_copy((c.index, target), target, here).wait_send()
        for k in range(1, c.count):
            target = lax.rem(c.index + k, c.count)
            self.seq_copy((target, here), target, c.index).wait_send()
        return total


def norm_scratch(count):
    return dict(
        mp_came=pltpu.VMEM((4, 8, 128), F32),
        mp_sent=pltpu.SemaphoreType.DMA((4,)),
        mp_sem=pltpu.SemaphoreType.DMA((4,)),
        seq_came=pltpu.VMEM((count, 8, 128), F32),
        seq_sent=pltpu.SemaphoreType.DMA((count,)),
        seq_sem=pltpu.SemaphoreType.DMA((count,)),
    )


def squares(ref):
    value = ref[...]
    return jnp.sum(value * value)


def ending(back, next_attn, grad_above, low, turn, above, top, count):
    rows, width = back.out_query.shape
    chunks = rows // CHUNK
    lines, block = count // 2, D // count
    units = above.units.shape[1]
    rim = back.out_right.shape[0]

    def body(r):
        who = Partners(chunks, chunks // 2)
        zeroth = Exchange(who, pick(r, "zeroth"))
        out = Gather(who, SimpleNamespace(full=r.output, sent=r.out_sent, came=r.out_came))
        column = Column(count)
        who.meet(column)
        up, down, three = scatter_three(column, r, (r.ffn_grads.at[0], r.ffn_grads.at[1], r.attn_grads.at[0]))
        small = SmallSum(who, column, pick(r, "small"))
        begin, end, back_ticks = projection_back_stage(r, who, column, zeroth)
        begin()
        up.start()
        down.start()

        def start_three():
            pack_attention(r)
            three.start()
            r.small_kept[0, 0:6, :] = r.vectors_low[0:6, :]
            r.small_kept[0, 6:12, :] = r.vectors_top[0:6, :]
            r.small_kept[0, 12:13, :] = r.units_low[0:1, :]
            r.small_kept[0, 13:14, :] = r.units_top[0:1, :]
            pieces = []
            for ref in (r.biases, r.biases_top):
                pieces += [ref[0:1, :width], ref[0:1, 2 * width :]]
            r.small_kept[0, 14:15, :] = jnp.concatenate(pieces, axis=1)
            r.small_kept[0, 15:16, :] = jnp.zeros((1, D), F32)
            small.core_copy().start()

        ticks = [tick for engine, times in zip((up, down, three), END_TIMES) for tick in engine.ticks(times)]
        ticks += [(chunks // 2 + 2, start_three), (3, r.late.grad_above.wait), (3, r.late.turn.wait)]
        ticks += [(chunks // 2 + 4, lambda: small.second(12)), (chunks // 2 + 6, small.third)]
        ticks = back_ticks + ticks
        clear(r.biases, r.sum_three)

        def close(t):
            out.give(t, unturned(r.grad_above[who.half(t), :] + zeroth.take(t), r.turn[...]))

        run_stages(chunks, [(1, zeroth.add), (3, close)], ticks)
        vectors = small.result()
        r.vectors[...] = vectors
        r.ffn_grads[2] = r.up_top[...]
        r.ffn_grads[3] = r.down_top[...]
        r.attn_grads[1] = r.attn_top[...]
        row = lax.broadcasted_iota(jnp.int32, (16, D), 0)
        squared = vectors * vectors
        split = jnp.sum(jnp.where(row >= 12, squared, 0.0))
        shared = jnp.sum(jnp.where(row < 12, squared, 0.0))
        first_seq = column.index == 0
        first_both = jnp.logical_and(first_seq, column.here == 0)
        value = squares(r.ffn_grads) + squares(r.attn_grads)
        value = value + jnp.where(first_seq, split, 0.0) + jnp.where(first_both, shared, 0.0)
        total = NormSum(who, column, pick(r, "norm")).run(value)
        r.norm[...] = jnp.sqrt(total)

        def arrive(t, carry):
            out.wait(t)
            return carry

        lax.fori_loop(0, chunks, arrive, 0)
        finish_all(chunks, (zeroth, out))
        end()
        for engine in (up, down, three, small):
            engine.finish()

    outputs = dict(
        output=((rows, D), F32),
        ffn_grads=((4, block, units), F32),
        attn_grads=((2, block, 4 * width), F32),
        vectors=((16, D), F32),
        norm=((8, 128), F32),
    )
    scratch = dict(
        biases=pltpu.VMEM((8, 3 * width), F32),
        out_sent=pltpu.SemaphoreType.DMA((chunks,)),
        out_came=pltpu.SemaphoreType.DMA((chunks,)),
    )
    scratch.update(projection_back_scratch(rows, rim, width))
    scratch.update(scatter_three_scratch(count, width, units))
    scratch.update(prefixed("zeroth", exchange_scratch(rows)))
    scratch.update(prefixed("small", small_scratch(lines, (16, D))))
    scratch.update(prefixed("norm", norm_scratch(count)))
    return run_kernel(
        body,
        "ending",
        dict(
            grad_query=back.out_query,
            grad_own=back.out_own,
            out_right=back.out_right,
            next_attn=next_attn,
            low=low,
            above_up=above.up.reshape(count, block, units),
            above_down=above.down.reshape(count, block, units),
            above_proj=above.proj,
            up_top=above.up_total,
            down_top=above.down_total,
            attn_top=above.attn_total,
            vectors_low=above.vectors,
            vectors_top=top.vectors,
            units_low=above.units,
            units_top=top.units,
            biases_top=above.biases,
        ),
        outputs,
        scratch,
        collective=4,
        flops=2 * rows * D * 6 * width,
        in_hbm=("above_up", "above_down"),
        late=dict(grad_above=grad_above, turn=turn),
    )


def moments(grad, first, second):
    first_new = BETA_FIRST * first + (1.0 - BETA_FIRST) * grad
    second_new = BETA_SECOND * second + (1.0 - BETA_SECOND) * grad * grad
    size = jnp.sqrt(second_new / (1.0 - BETA_SECOND**STEP)) + ADAM_EPSILON
    return first_new, second_new, first_new / (1.0 - BETA_FIRST**STEP) / size


def update(end, turn, attn, ffn, split, shared):
    block, units = ffn[0].shape[2:]
    width = attn[0].shape[3]
    rates = [0.5 * D ** (-0.5)] * 3 + [0.5 * (WIN / D) ** 0.5]
    names = ("weights", "first", "second", "average", "basis")

    def matrix(grad, weight, first, second, average, basis, rate):
        basis = basis.astype(BF)
        turned = dot(grad.astype(BF), basis)
        first_new, second_new, direction = moments(turned, first, second)
        back = dot_nt(direction.astype(BF), basis)
        weight_new = weight - rate * (back + DECAY_RATE * weight)
        return weight_new, first_new, second_new, AVERAGE_RATE * average + (1.0 - AVERAGE_RATE) * weight_new

    def body(r):
        step = pl.program_id(0)
        factor = CLIP_LEVEL / jnp.maximum(r.norm[0:1, 0:1], CLIP_LEVEL)
        rate = jnp.where(step % 2 == 0, 0.5 * D ** (-0.5), 0.5 * FF ** (-0.5))
        results = matrix(
            factor * r.ffn_grads[...],
            r.ffn_weights[...],
            r.ffn_first[...],
            r.ffn_second[...],
            r.ffn_average[...],
            r.ffn_basis[...],
            rate,
        )
        for key, value in zip(names, results):
            getattr(r, "ffn_" + key + "_new")[...] = value

        for at in range(4):

            @pl.when(step == at)
            def _(at=at):
                layer = at // 2
                for which in (2 * (at % 2), 2 * (at % 2) + 1):
                    grad = factor * r.attn_grads[layer, :, which * width : (which + 1) * width]
                    weight, first, second, average = matrix(
                        grad,
                        r.attn_weights[layer, which],
                        r.attn_first[layer, which],
                        r.attn_second[layer, which],
                        r.attn_average[layer, which],
                        r.attn_basis[layer, which, 0, 0],
                        rates[which],
                    )
                    r.attn_weights_new[layer, which] = weight
                    r.attn_first_new[layer, which] = first
                    r.attn_average_new[layer, which] = average
                    if which < 3:
                        r.attn_second_new[layer, which] = second
                    else:
                        r.projection_second[layer] = second

        @pl.when(step == 0)
        def _():
            r.norm_out[0, 0] = jnp.max(r.norm[0:1, :])
            real = exact(r.vectors[...], lambda part: dot_nt(part, r.turn[...]))
            for layer in range(2):
                tail = r.vectors[14:15, layer * 2 * width : (layer + 1) * 2 * width]
                split_grad = jnp.concatenate([tail, r.vectors[12 + layer : 13 + layer, :]], axis=1)
                grad = factor * split_grad
                first_new, second_new, direction = moments(grad, r.split_first[layer], r.split_second[layer])
                r.split_old_new[layer] = r.split_old[layer] - VECTOR_RATE * direction
                r.split_first_new[layer] = first_new
                r.split_second_new[layer] = second_new
            for k in range(6):
                grad = factor * jnp.concatenate([real[k : k + 1], real[6 + k : 7 + k]], axis=0)
                first_new, second_new, direction = moments(grad, r.shared_first[k], r.shared_second[k])
                r.shared_old_new[k] = r.shared_old[k] - VECTOR_RATE * direction
                r.shared_first_new[k] = first_new
                r.shared_second_new[k] = second_new

    inputs = dict(
        ffn_grads=end.ffn_grads, attn_grads=end.attn_grads, vectors=end.vectors, norm=end.norm, turn=turn
    )
    outputs, specs = {}, {}
    specs["ffn_grads"] = pl.BlockSpec((None, block, units), lambda i: (i, 0, 0))
    matrix_spec = pl.BlockSpec((None, None, block, units), lambda i: (i // 2, i % 2, 0, 0))
    for key, array in zip(names, ffn):
        inputs["ffn_" + key] = array
        specs["ffn_" + key] = matrix_spec
    specs["ffn_basis"] = pl.BlockSpec((None, None, None, None, units, units), lambda i: (i // 2, i % 2, 0, 0, 0, 0))
    for key, array in zip(names, attn):
        inputs["attn_" + key] = array
    for prefix, group in (("split", split), ("shared", shared)):
        for key, array in zip(("old", "first", "second"), group):
            inputs[prefix + "_" + key] = array
    for key in ("weights", "first", "second", "average"):
        outputs["ffn_" + key + "_new"] = (ffn[0].shape, F32)
        specs["ffn_" + key + "_new"] = matrix_spec
        outputs["attn_" + key + "_new"] = (attn[0].shape, F32)
    outputs["attn_second_new"] = ((2, 3, block, width), F32)
    outputs["projection_second"] = ((2, block, width), F32)
    for prefix, group in (("split", split), ("shared", shared)):
        for key in ("old", "first", "second"):
            outputs[prefix + "_" + key + "_new"] = (group[0].shape, F32)
    outputs["norm_out"] = ((1, 1), F32)
    return run_kernel(
        body,
        "update",
        inputs,
        outputs,
        {},
        flops=4 * block * units * units * 4,
        grid=(4,),
        specs=specs,
        in_smem=("norm_out",),
    )


def direct(
    activations,
    cotangent,
    segments,
    dilated_heads,
    owners,
    attn_weights,
    attn_first,
    attn_second,
    attn_average,
    attn_basis,
    ffn_weights,
    ffn_first,
    ffn_second,
    ffn_average,
    ffn_basis,
    split_biases,
    split_first,
    split_second,
    shared_vectors,
    shared_first,
    shared_second,
):
    count = lax.axis_size(SEQ)
    near = opening(
        activations, segments, owners, attn_weights, ffn_weights, split_biases, shared_vectors, count
    )
    near.arranged = near.out
    attn_zero, up_zero, down_zero = (
        full.reshape(D, -1) for full in (near.full_attn, near.full_up, near.full_down)
    )
    mid = middle_forward(
        near.out,
        attn_zero,
        up_zero,
        down_zero,
        near.low,
        near.shared,
        split_biases,
        attn_weights,
        ffn_weights,
        count,
    )
    attn_one, up_one, down_one = (full.reshape(D, -1) for full in (mid.full_attn, mid.full_up, mid.full_down))
    far = attend(mid.query, mid.pair, mid.left, mid.right, near.seg_query, near.seg_keys, dilated_heads)
    top = turning(
        far.out, attn_one, up_one, down_one, mid.result, near.shared, split_biases, cotangent, near.turn
    )
    far_back = attend_back(far, top.grad_mixed, dilated_heads, 2 * WIN, True, count, 6)
    low = middle_backward(
        far_back,
        attn_one,
        top.grad_one,
        mid.last_full,
        mid,
        near.out,
        attn_zero,
        up_zero,
        down_zero,
        near.shared,
        top,
        count,
    )
    near_back = attend_back(near, low.grad_mixed, dilated_heads, WIN, False, count, 7)
    end = ending(near_back, attn_zero, low.grad_one, near.low, near.turn, low, top, count)
    new = update(
        end,
        near.turn,
        (attn_weights, attn_first, attn_second, attn_average, attn_basis),
        (ffn_weights, ffn_first, ffn_second, ffn_average, ffn_basis),
        (split_biases, split_first, split_second),
        tuple(array.transpose(1, 0, 2) for array in (shared_vectors, shared_first, shared_second)),
    )
    return (
        top.output,
        end.output,
        new.attn_weights_new,
        new.attn_first_new,
        new.attn_second_new,
        new.projection_second,
        new.attn_average_new,
        new.ffn_weights_new,
        new.ffn_first_new,
        new.ffn_second_new,
        new.ffn_average_new,
        new.split_old_new,
        new.split_first_new,
        new.split_second_new,
        new.shared_old_new.transpose(1, 0, 2),
        new.shared_first_new.transpose(1, 0, 2),
        new.shared_second_new.transpose(1, 0, 2),
        new.norm_out.reshape(()),
    )


def with_halo(cells, sides, width):
    for axis, dim in sides:
        count = lax.axis_size(axis)
        ends = count - 1
        head = lax.slice_in_dim(cells, 0, width, axis=dim)
        tail = lax.slice_in_dim(cells, cells.shape[dim] - width, cells.shape[dim], axis=dim)
        cells = jnp.concatenate(
            [
                lax.ppermute(tail, axis, [(i, (i + 1) % count) for i in range(ends)]),
                cells,
                lax.ppermute(head, axis, [((i + 1) % count, i) for i in range(ends)]),
            ],
            axis=dim,
        )
    return cells


def from_behind(block, axis, distance):
    devices = range(lax.axis_size(axis))
    route = [(i - distance, i) for i in devices if i - distance in devices]
    return lax.ppermute(block, axis, route)


def normalize_layer(values, gain, shift):
    center = values - jnp.mean(values, axis=-1, keepdims=True)
    spread = jnp.mean(center * center, axis=-1, keepdims=True)
    return center * lax.rsqrt(spread + NORM_EPSILON) * gain + shift


def head_masks(offsets, dilated):
    near = jnp.abs(offsets) <= WIN
    far = jnp.logical_and(jnp.abs(offsets) <= 2 * WIN, offsets % 2 == 0)
    return jnp.where(dilated[:, None, None], far[None, :, :], near[None, :, :])


def join_heads(term):
    return lax.psum(term.astype(jnp.bfloat16), MP).astype(jnp.float32)


def join_grads(term):
    return lax.psum(term, MP)


def fetch_rims(pair, rim_width):
    return with_halo(pair, ((SEQ, 0),), rim_width)


def masked_scores(query_block, key_block, seg_query, seg_keys, dilated, rim_width):
    block_rows = query_block.shape[0]
    key_rows = key_block.shape[0]
    offsets = (
        jnp.arange(block_rows, dtype=jnp.int32)[:, None]
        - jnp.arange(key_rows, dtype=jnp.int32)[None, :]
        + rim_width
    )
    allowed = jnp.logical_and(
        head_masks(offsets, dilated), (seg_query[:, None] == seg_keys[None, :])[None, :, :]
    )
    raw = jnp.einsum(
        "qhd,khd->hqk", query_block, key_block, preferred_element_type=jnp.float32
    ) * DH ** (-0.5)
    return jnp.where(allowed, raw, MASK_FILL)


def plain_attend(query, key_pad, value_pad, seg_own, seg_near, dilated, rim_width):
    row_count = query.shape[0]
    block_rows = min(512, row_count)
    key_rows = block_rows + 2 * rim_width

    def one_block(first_row):
        query_block = lax.dynamic_slice_in_dim(query, first_row, block_rows, 0)
        key_block = lax.dynamic_slice_in_dim(key_pad, first_row, key_rows, 0)
        value_block = lax.dynamic_slice_in_dim(value_pad, first_row, key_rows, 0)
        scores = masked_scores(
            query_block,
            key_block,
            lax.dynamic_slice_in_dim(seg_own, first_row, block_rows, 0),
            lax.dynamic_slice_in_dim(seg_near, first_row, key_rows, 0),
            dilated,
            rim_width,
        )
        row_max = jnp.max(scores, axis=2, keepdims=True)
        exponent = jnp.exp(scores - row_max)
        row_total = jnp.sum(exponent, axis=2, keepdims=True)
        softmax = (exponent / row_total).astype(jnp.bfloat16)
        mixed_block = jnp.einsum(
            "hqk,khd->qhd", softmax, value_block, preferred_element_type=jnp.float32
        )
        return (mixed_block, (row_max + jnp.log(row_total))[:, :, 0])

    starts = jnp.arange(row_count // block_rows, dtype=jnp.int32) * block_rows
    mixed_heads, log_totals = lax.map(one_block, starts)
    return (mixed_heads.reshape(row_count, -1), log_totals)


def plain_attend_back(query, padded, log_totals, grad_mixed, seg_own, seg_near, dilated, rim_width):
    row_count, head_count, _ = query.shape
    head_width = head_count * DH
    block_rows = min(512, row_count)
    key_rows = block_rows + 2 * rim_width
    key_pad = padded[:, :head_width].reshape(-1, head_count, DH)
    value_pad = padded[:, head_width:].reshape(-1, head_count, DH)
    grad_heads = grad_mixed.reshape(row_count, head_count, DH)
    score_scale = DH ** (-0.5)

    def one_step(carry, inputs):
        first_row, totals_block = inputs
        query_block = lax.dynamic_slice_in_dim(query, first_row, block_rows, 0)
        key_block = lax.dynamic_slice_in_dim(key_pad, first_row, key_rows, 0)
        value_block = lax.dynamic_slice_in_dim(value_pad, first_row, key_rows, 0)
        grad_block = lax.dynamic_slice_in_dim(grad_heads, first_row, block_rows, 0)
        scores = masked_scores(
            query_block,
            key_block,
            lax.dynamic_slice_in_dim(seg_own, first_row, block_rows, 0),
            lax.dynamic_slice_in_dim(seg_near, first_row, key_rows, 0),
            dilated,
            rim_width,
        )
        softmax = jnp.exp(scores - totals_block[:, :, None])
        grad_value = jnp.einsum(
            "hqk,qhd->khd",
            softmax.astype(jnp.bfloat16),
            grad_block,
            preferred_element_type=jnp.float32,
        )
        grad_soft = jnp.einsum(
            "qhd,khd->hqk", grad_block, value_block, preferred_element_type=jnp.float32
        )
        row_dot = jnp.sum(grad_soft * softmax, axis=2, keepdims=True)
        grad_scores = (softmax * (grad_soft - row_dot)).astype(jnp.bfloat16)
        grad_query = (
            jnp.einsum("hqk,khd->qhd", grad_scores, key_block, preferred_element_type=jnp.float32)
            * score_scale
        )
        grad_key = (
            jnp.einsum("hqk,qhd->khd", grad_scores, query_block, preferred_element_type=jnp.float32)
            * score_scale
        )
        update = jnp.concatenate(
            [grad_key.reshape(key_rows, head_width), grad_value.reshape(key_rows, head_width)],
            axis=1,
        )
        current = lax.dynamic_slice_in_dim(carry, first_row, key_rows, 0)
        carry = lax.dynamic_update_slice_in_dim(carry, current + update, first_row, 0)
        return (carry, grad_query.reshape(block_rows, head_width))

    starts = jnp.arange(row_count // block_rows, dtype=jnp.int32) * block_rows
    initial = jnp.zeros((row_count + 2 * rim_width, 2 * head_width), jnp.float32)
    grad_pad, grad_query = lax.scan(one_step, initial, (starts, log_totals))
    from_above = from_behind(grad_pad[:rim_width], SEQ, -1)
    from_below = from_behind(grad_pad[row_count + rim_width :], SEQ, 1)
    grad_pair = grad_pad[rim_width : row_count + rim_width]
    grad_pair = (
        grad_pair
        + jnp.pad(from_below, ((0, row_count - rim_width), (0, 0)))
        + jnp.pad(from_above, ((row_count - rim_width, 0), (0, 0)))
    )
    return (grad_query.reshape(row_count, head_width), grad_pair)


def layer_forward(inputs, attn, ffn, shared, split, seg_own, seg_pad, dilated, rim_width):
    head_width = attn.shape[2]
    row_count = inputs.shape[0]
    inputs_low = inputs.astype(jnp.bfloat16)
    biases = jnp.stack(
        [
            split[0, :head_width],
            jnp.zeros((head_width,), jnp.float32),
            split[0, head_width : 2 * head_width],
        ]
    )
    projected = (
        jnp.einsum("td,mdc->tmc", inputs_low, attn[:3], preferred_element_type=jnp.float32)
        + biases[None]
    ).astype(jnp.bfloat16)
    query = projected[:, 0].reshape(row_count, -1, DH)
    padded = fetch_rims(jnp.concatenate([projected[:, 1], projected[:, 2]], axis=1), rim_width)
    key_pad = padded[:, :head_width].reshape(-1, head_width // DH, DH)
    value_pad = padded[:, head_width:].reshape(-1, head_width // DH, DH)
    seg_near = lax.slice_in_dim(
        seg_pad, 2 * WIN - rim_width, 2 * WIN + row_count + rim_width, axis=0
    )
    mixed_heads, log_totals = plain_attend(
        query, key_pad, value_pad, seg_own, seg_near, dilated, rim_width
    )
    mixed_heads = mixed_heads.astype(jnp.bfloat16)
    attn_sum = (
        inputs
        + join_heads(
            dot_nt(mixed_heads, attn[3])
        )
        + shared[0]
    )
    normed = normalize_layer(attn_sum, shared[1], shared[2])
    normed_low = normed.astype(jnp.bfloat16)
    pre_gelu = (
        jnp.dot(normed_low, ffn[0], preferred_element_type=jnp.float32) + split[0, 2 * head_width :]
    )
    hidden = jax.nn.gelu(pre_gelu, approximate=False).astype(jnp.bfloat16)
    ffn_sum = (
        normed
        + join_heads(dot_nt(hidden, ffn[1]))
        + shared[3]
    )
    result = normalize_layer(ffn_sum, shared[4], shared[5])
    return (
        result,
        (
            inputs_low,
            query,
            padded,
            log_totals,
            mixed_heads,
            attn_sum,
            normed_low,
            pre_gelu,
            hidden,
            ffn_sum,
        ),
    )


def layer_backward(grad_out, saved, attn, ffn, shared, seg_own, seg_pad, dilated, rim_width):
    (
        inputs_low,
        query,
        padded,
        log_totals,
        mixed_heads,
        attn_sum,
        normed_low,
        pre_gelu,
        hidden,
        ffn_sum,
    ) = saved
    head_width = attn.shape[2]
    row_count = inputs_low.shape[0]
    seg_near = lax.slice_in_dim(
        seg_pad, 2 * WIN - rim_width, 2 * WIN + row_count + rim_width, axis=0
    )
    _, pull_out = jax.vjp(normalize_layer, ffn_sum, shared[4], shared[5])
    grad_ffn_sum, grad_gain_two, grad_shift_two = pull_out(grad_out)
    grad_branch = grad_ffn_sum.astype(jnp.bfloat16)
    grad_down = dot_tn(grad_branch, hidden)
    grad_hidden = jnp.dot(grad_branch, ffn[1], preferred_element_type=jnp.float32)
    _, pull_gelu = jax.vjp(lambda value: jax.nn.gelu(value, approximate=False), pre_gelu)
    grad_pre = pull_gelu(grad_hidden)[0].astype(jnp.bfloat16)
    grad_up = dot_tn(normed_low, grad_pre)
    grad_normed = grad_ffn_sum + join_grads(
        dot_nt(grad_pre, ffn[0])
    )
    _, pull_mid = jax.vjp(normalize_layer, attn_sum, shared[1], shared[2])
    grad_attn_sum, grad_gain_one, grad_shift_one = pull_mid(grad_normed)
    grad_attn_out = grad_attn_sum.astype(jnp.bfloat16)
    grad_out_proj = dot_tn(grad_attn_out, mixed_heads)
    grad_mixed = jnp.dot(grad_attn_out, attn[3], preferred_element_type=jnp.float32).astype(
        jnp.bfloat16
    )
    grad_query, grad_pair = plain_attend_back(
        query, padded, log_totals, grad_mixed, seg_own, seg_near, dilated, rim_width
    )
    grad_proj = jnp.stack(
        [grad_query, grad_pair[:, :head_width], grad_pair[:, head_width:]], axis=1
    ).astype(jnp.bfloat16)
    grad_in_proj = jnp.einsum(
        "td,tmc->mdc", inputs_low, grad_proj, preferred_element_type=jnp.float32
    )
    grad_inputs = grad_attn_sum + join_grads(
        jnp.einsum("tmc,mdc->td", grad_proj, attn[:3], preferred_element_type=jnp.float32)
    )
    proj_sums = jnp.sum(grad_proj.astype(jnp.float32), axis=0)
    split_grad = jnp.concatenate(
        [proj_sums[0], proj_sums[2], jnp.sum(grad_pre.astype(jnp.float32), axis=0)]
    )
    shared_grad = jnp.stack(
        [
            jnp.sum(grad_attn_sum, axis=0),
            grad_gain_one,
            grad_shift_one,
            jnp.sum(grad_ffn_sum, axis=0),
            grad_gain_two,
            grad_shift_two,
        ]
    )
    attn_grad = jnp.concatenate([grad_in_proj, grad_out_proj[None]], axis=0)
    ffn_grad = jnp.stack([grad_up, grad_down])
    return (grad_inputs, attn_grad, ffn_grad, shared_grad, split_grad)


def from_slots(gathered, owners, slot_count):
    layer_count, matrix_count, row_count, col_count = gathered.shape
    blocks = gathered.reshape(
        layer_count, matrix_count, slot_count, row_count // slot_count, col_count
    )
    return jnp.take(blocks, owners, axis=2).reshape(gathered.shape)


def to_slots(grads, inverse, slot_count):
    matrix_count, row_count, col_count = grads.shape
    blocks = grads.reshape(matrix_count, slot_count, row_count // slot_count, col_count)
    return jnp.take(blocks, inverse, axis=1).reshape(grads.shape)


def rotate_update(weight, grad_now, first, second, running_average, basis, rates):
    turn = basis[:, :, 0, 0]
    turned = jnp.einsum("lmre,lmec->lmrc", grad_now, turn, precision=HIGHEST_PRECISION)
    first_new = BETA_FIRST * first + (1.0 - BETA_FIRST) * turned
    second_new = BETA_SECOND * second + (1.0 - BETA_SECOND) * turned * turned
    direction = (
        first_new
        / (1.0 - BETA_FIRST**STEP)
        / (jnp.sqrt(second_new / (1.0 - BETA_SECOND**STEP)) + ADAM_EPSILON)
    )
    back = jnp.einsum("lmrc,lmec->lmre", direction, turn, precision=HIGHEST_PRECISION)
    weight_new = weight - rates[None, :, None, None] * (back + DECAY_RATE * weight)
    average_new = AVERAGE_RATE * running_average + (1.0 - AVERAGE_RATE) * weight_new
    return (weight_new, first_new, second_new, average_new)


def vector_update(current, grad_now, first, second):
    first_new = BETA_FIRST * first + (1.0 - BETA_FIRST) * grad_now
    second_new = BETA_SECOND * second + (1.0 - BETA_SECOND) * grad_now * grad_now
    direction = (
        first_new
        / (1.0 - BETA_FIRST**STEP)
        / (jnp.sqrt(second_new / (1.0 - BETA_SECOND**STEP)) + ADAM_EPSILON)
    )
    return (current - VECTOR_RATE * direction, first_new, second_new)


def with_collectives(
    activations,
    cotangent,
    segments,
    dilated_heads,
    owners,
    attn_weights,
    attn_first,
    attn_second,
    attn_average,
    attn_basis,
    ffn_weights,
    ffn_first,
    ffn_second,
    ffn_average,
    ffn_basis,
    split_biases,
    split_first,
    split_second,
    shared_vectors,
    shared_first,
    shared_second,
):
    slot_count = lax.axis_size(SEQ)
    layer_count = attn_weights.shape[0]
    attn_full, ffn_full = (
        lax.all_gather(attn_weights.astype(jnp.bfloat16), SEQ, axis=2, tiled=True),
        lax.all_gather(ffn_weights.astype(jnp.bfloat16), SEQ, axis=2, tiled=True),
    )
    attn_full = from_slots(attn_full, owners, slot_count)
    ffn_full = from_slots(ffn_full, owners, slot_count)
    seg_pad = with_halo(segments, ((SEQ, 0),), 2 * WIN)
    head_width = attn_full.shape[3]
    head_count = head_width // DH
    heads_here = lax.axis_index(MP) * head_count + jnp.arange(head_count, dtype=jnp.int32)
    head_flags = jnp.any(heads_here[:, None] == dilated_heads[None, :], axis=1)
    current = activations.astype(jnp.float32)
    saved_list = []
    for layer_index in range(layer_count):
        dilated = jnp.logical_and(head_flags, layer_index % 2 == 1)
        rim_width = 2 * WIN if layer_index % 2 == 1 else WIN
        current, saved = layer_forward(
            current,
            attn_full[layer_index],
            ffn_full[layer_index],
            shared_vectors[layer_index],
            split_biases[layer_index],
            segments,
            seg_pad,
            dilated,
            rim_width,
        )
        saved_list.append(saved)
    slot_range = jnp.arange(slot_count, dtype=jnp.int32)
    inverse = jnp.sum(
        jnp.where(owners[None, :] == slot_range[:, None], slot_range[None, :], 0), axis=1
    )
    grad_now = cotangent.astype(jnp.float32)
    attn_list = [None] * layer_count
    ffn_list = [None] * layer_count
    shared_list = [None] * layer_count
    split_list = [None] * layer_count
    for layer_index in range(layer_count - 1, -1, -1):
        dilated = jnp.logical_and(head_flags, layer_index % 2 == 1)
        rim_width = 2 * WIN if layer_index % 2 == 1 else WIN
        grad_now, attn_grad, ffn_grad, shared_grad, split_grad = layer_backward(
            grad_now,
            saved_list[layer_index],
            attn_full[layer_index],
            ffn_full[layer_index],
            shared_vectors[layer_index],
            segments,
            seg_pad,
            dilated,
            rim_width,
        )
        attn_grad = to_slots(attn_grad, inverse, slot_count)
        ffn_grad = to_slots(ffn_grad, inverse, slot_count)
        attn_list[layer_index] = attn_grad
        ffn_list[layer_index] = ffn_grad
        shared_list[layer_index] = shared_grad
        split_list[layer_index] = split_grad[None, :]
    attn_grads = jnp.stack(attn_list)
    ffn_grads = jnp.stack(ffn_list)
    attn_grads, ffn_grads = (
        lax.psum_scatter(attn_grads, SEQ, scatter_dimension=2, tiled=True),
        lax.psum_scatter(ffn_grads, SEQ, scatter_dimension=2, tiled=True),
    )
    shared_grads, split_grads = lax.psum((jnp.stack(shared_list), jnp.stack(split_list)), SEQ)
    first_seq = lax.axis_index(SEQ) == 0
    first_both = jnp.logical_and(first_seq, lax.axis_index(MP) == 0)
    local_sum = jnp.sum(attn_grads * attn_grads) + jnp.sum(ffn_grads * ffn_grads)
    local_sum = (
        local_sum
        + jnp.where(first_seq, jnp.sum(split_grads * split_grads), 0.0)
        + jnp.where(first_both, jnp.sum(shared_grads * shared_grads), 0.0)
    )
    grad_norm = jnp.sqrt(lax.psum(local_sum, (SEQ, MP)))
    factor = CLIP_LEVEL / jnp.maximum(grad_norm, CLIP_LEVEL)
    attn_rates = jnp.array([0.5 * D ** (-0.5)] * 3 + [0.5 * (WIN / D) ** 0.5], jnp.float32)
    ffn_rates = jnp.array([0.5 * D ** (-0.5), 0.5 * FF ** (-0.5)], jnp.float32)
    attn_out = rotate_update(
        attn_weights,
        factor * attn_grads,
        attn_first,
        attn_second,
        attn_average,
        attn_basis,
        attn_rates,
    )
    ffn_out = rotate_update(
        ffn_weights, factor * ffn_grads, ffn_first, ffn_second, ffn_average, ffn_basis, ffn_rates
    )
    split_out = vector_update(split_biases, factor * split_grads, split_first, split_second)
    shared_out = vector_update(shared_vectors, factor * shared_grads, shared_first, shared_second)
    return (
        current,
        grad_now,
        attn_out[0],
        attn_out[1],
        attn_out[2][:, :3],
        attn_out[2][:, 3],
        attn_out[3],
        ffn_out[0],
        ffn_out[1],
        ffn_out[2],
        ffn_out[3],
        split_out[0],
        split_out[1],
        split_out[2],
        shared_out[0],
        shared_out[1],
        shared_out[2],
        grad_norm,
    )


def solution(mesh):
    placed = (
        P(SEQ, None),
        P(SEQ, None),
        P(SEQ),
        P(),
        P(),
        P(None, None, SEQ, MP),
        P(None, None, SEQ, MP),
        P(None, None, SEQ, MP),
        P(None, None, SEQ, MP),
        P(None, None, SEQ, MP, None, None),
        P(None, None, SEQ, MP),
        P(None, None, SEQ, MP),
        P(None, None, SEQ, MP),
        P(None, None, SEQ, MP),
        P(None, None, SEQ, MP, None, None),
        P(None, MP, None),
        P(None, MP, None),
        P(None, MP, None),
        P(),
        P(),
        P(),
    )
    count = mesh.shape[SEQ]
    fits = count % 4 == 0 and (D // count) % 16 == 0 and mesh.shape[MP] == 4
    return jax.shard_map(
        direct if fits else with_collectives,
        mesh=mesh,
        in_specs=placed,
        out_specs=(
            P(SEQ, None),
            P(SEQ, None),
            P(None, None, SEQ, MP),
            P(None, None, SEQ, MP),
            P(None, None, SEQ, MP),
            P(None, SEQ, MP),
            P(None, None, SEQ, MP),
            P(None, None, SEQ, MP),
            P(None, None, SEQ, MP),
            P(None, None, SEQ, MP),
            P(None, None, SEQ, MP),
            P(None, MP, None),
            P(None, MP, None),
            P(None, MP, None),
            P(),
            P(),
            P(),
            P(),
        ),
        check_vma=False,
    )
```

```python
from types import SimpleNamespace

import jax
import jax.numpy as jnp
from jax import lax
from jax.experimental import pallas as pl
from jax.experimental.pallas import tpu as pltpu
from jax.sharding import PartitionSpec as P

D = 768
DH = 64
FF = 3072
WIN = 256
STEP = 10

HIGHEST_PRECISION = lax.Precision.HIGHEST
NORM_EPSILON = 1e-05
MASK_FILL = -1e30
CLIP_LEVEL = 1.0
BETA_FIRST = 0.5
BETA_SECOND = 0.5
ADAM_EPSILON = 1e-08
DECAY_RATE = 0.01
AVERAGE_RATE = 0.7
VECTOR_RATE = 0.3

BF = jnp.bfloat16
SEQ, MP = "seq", "mp"
F32 = jnp.float32
MESH = pl.DeviceIdType.MESH
BLOCK = 256
CHUNK = 128
WIDE_CHUNK = 256
VMEM_LIMIT = 56 * 1024 * 1024
SCORE_SCALE = DH ** (-0.5)

GATHER_TIMES = ((2, 4, 5), (3, 5), (6, 7, 9), (7, 10, 13, 16))
BACK_TIMES = ((1, 4, 7, 10, 12), (6, 8, 10, 12), (10, 13, 15, 17))
END_TIMES = ((1, 4, 7, 10, 13), (5, 8, 10, 12), (11, 14, 15, 16))


def dot(left, right):
    return jnp.dot(left, right, preferred_element_type=F32)


def dot_nt(left, right):
    return lax.dot_general(left, right, (((1,), (1,)), ((), ())), preferred_element_type=F32)


def dot_tn(left, right):
    return lax.dot_general(left, right, (((0,), (0,)), ((), ())), preferred_element_type=F32)


class Flush:
    def __init__(self, held, out, sems):
        self.held, self.out, self.sems = held, out, sems

    def copy(self, rows, t):
        return pltpu.make_async_copy(self.held.at[rows, :], self.out.at[rows, :], self.sems.at[t])


def run_kernel(
    body,
    name,
    inputs,
    outputs,
    scratch,
    collective=None,
    flops=0,
    grid=None,
    specs=None,
    in_smem=(),
    in_hbm=(),
    late=None,
    flushed=None,
    pieces=0,
):
    specs, late, flushed = specs or {}, late or {}, flushed or {}

    def kernel(*refs):
        refs = list(refs)

        def take(keys):
            got = refs[: len(keys)]
            del refs[: len(keys)]
            return dict(zip(keys, got))

        given, distant, made, written, held = (take(keys) for keys in (inputs, late, outputs, flushed, scratch))
        fetched, fetched_sems, filled, filled_sems = (take(keys) for keys in (late, late, flushed, flushed))
        r = SimpleNamespace(**given, **made, **held, **fetched, **filled)
        r.late = SimpleNamespace(
            **{key: pltpu.make_async_copy(distant[key], fetched[key], fetched_sems[key]) for key in late}
        )
        r.flush = SimpleNamespace(**{key: Flush(filled[key], written[key], filled_sems[key]) for key in flushed})
        for copy in vars(r.late).values():
            copy.start()
        body(r)

    def spec_of(key):
        if key in specs:
            return specs[key]
        if key in in_hbm or key in late or key in flushed:
            return pl.BlockSpec(memory_space=pl.ANY)
        return pl.BlockSpec(memory_space=pltpu.SMEM if key in in_smem else pltpu.VMEM)

    arguments = {**inputs, **late}
    gives = {**outputs, **flushed}
    shapes = [jax.ShapeDtypeStruct(shape, dtype) for shape, dtype in gives.values()]
    moved = sum(v.size * v.dtype.itemsize for v in arguments.values())
    moved += sum(v.size * v.dtype.itemsize for v in shapes)
    extra = {} if grid is None else dict(grid=grid)
    params = dict(vmem_limit_bytes=VMEM_LIMIT)
    if collective is not None:
        params.update(collective_id=collective, has_side_effects=True)
    results = pl.pallas_call(
        kernel,
        out_shape=shapes,
        in_specs=[spec_of(key) for key in arguments],
        out_specs=[spec_of(key) for key in gives],
        scratch_shapes=list(scratch.values())
        + [pltpu.VMEM(v.shape, v.dtype) for v in late.values()]
        + [pltpu.SemaphoreType.DMA for _ in late]
        + [pltpu.VMEM(shape, dtype) for shape, dtype in flushed.values()]
        + [pltpu.SemaphoreType.DMA((pieces,)) for _ in flushed],
        compiler_params=pltpu.CompilerParams(**params),
        cost_estimate=pl.CostEstimate(flops=int(flops), bytes_accessed=int(moved), transcendentals=0),
        name=name,
        **extra,
    )(*arguments.values())
    return SimpleNamespace(**dict(zip(gives, results)))


def parity_matrix():
    row = lax.broadcasted_iota(jnp.int32, (2 * BLOCK, 2 * BLOCK), 0)
    col = lax.broadcasted_iota(jnp.int32, (2 * BLOCK, 2 * BLOCK), 1)
    source = 2 * (row % BLOCK) + row // BLOCK
    return jnp.where(col == source, 1.0, 0.0).astype(BF)


def head_lanes(count):
    lane = lax.broadcasted_iota(jnp.int32, (1, count * DH), 1)
    return [lane // DH == head for head in range(count)]


def head_flags(dilated, count):
    first = lax.axis_index(MP) * count
    return [jnp.logical_or(dilated[0] == first + head, dilated[1] == first + head) for head in range(count)]


def marked_lanes(dilated, count):
    marked = jnp.zeros((1, count * DH), jnp.int32)
    for flag, lanes in zip(head_flags(dilated, count), head_lanes(count)):
        marked = jnp.where(lanes, flag.astype(jnp.int32), marked)
    return marked > 0


def sorted_groups(natural, sort):
    groups = natural.shape[0] // (2 * BLOCK)
    return [dot(sort, natural[g * 2 * BLOCK : (g + 1) * 2 * BLOCK]).astype(BF) for g in range(groups)]


def arrange_rows(natural, sort):
    return jnp.concatenate(sorted_groups(natural, sort), axis=0)


def split_rows(natural, sort):
    parts = sorted_groups(natural, sort)
    return jnp.concatenate([p[:BLOCK] for p in parts] + [p[BLOCK:] for p in parts], axis=0)


def soft_weights(query_block, key_block, lanes, allowed):
    raw = dot_nt(jnp.where(lanes, query_block, 0.0).astype(BF), key_block)
    scores = jnp.where(allowed, raw, MASK_FILL)
    top = jnp.max(scores, axis=1, keepdims=True)
    exponent = jnp.exp(scores - top)
    total = jnp.sum(exponent, axis=1, keepdims=True)
    return (exponent * (1.0 / total)).astype(BF)


def window_mask():
    row = lax.broadcasted_iota(jnp.int32, (BLOCK, 3 * BLOCK), 0)
    col = lax.broadcasted_iota(jnp.int32, (BLOCK, 3 * BLOCK), 1)
    return jnp.abs(row - col + BLOCK) <= WIN


def key_starts(step, mixed):
    natural = pl.ds(pl.multiple_of(step * BLOCK, BLOCK), 3 * BLOCK)
    if not mixed:
        return natural, natural
    first = (step % 2) * 4 + step // 2
    return natural, pl.ds(pl.multiple_of(first * BLOCK, BLOCK), 3 * BLOCK)


class HeadExchange:
    def __init__(self, who, source, gathered, sent, came):
        self.who, self.source, self.gathered, self.sent, self.came = who, source, gathered, sent, came
        here = lax.axis_index(MP)
        self.here = here
        self.devices = who.sibling, who.across, who.diagonal

    def copy(self, kind, t, slot):
        who = self.who
        rows = who.own(t) if kind == 1 else who.other(t)
        return copy_to(
            self.source.at[rows, :],
            self.gathered.at[slot, who.half(t), :],
            self.sent.at[kind, t],
            self.came.at[kind, t],
            self.devices[kind],
        )

    def give(self, t):
        self.gathered[self.here, self.who.half(t), :] = self.source[self.who.own(t), :]
        for kind in range(3):
            self.copy(kind, t, self.here).start()

    def take(self, t):
        for kind in range(3):
            self.copy(kind, t, self.devices[kind][1]).wait_recv()

    def finish(self, t):
        for kind in range(3):
            self.copy(kind, t, self.here).wait_send()


def attend(query, pair, left, right, seg_query, seg_keys, dilated):
    rows, width = query.shape
    heads = width // DH
    blocks = rows // BLOCK
    keys = 3 * BLOCK
    slots = 2 * blocks
    chunks = rows // WIDE_CHUNK

    def body(r):
        step = pl.program_id(0)
        who = Partners(size=WIDE_CHUNK)
        exchange = HeadExchange(who, r.out, r.landed, r.sent, r.came)

        @pl.when(step == 0)
        def _():
            who.call()
            marked = marked_lanes(r.dilated, heads)
            sort = parity_matrix()
            for which, held in ((0, r.keys), (1, r.values)):
                lanes = slice(which * width, (which + 1) * width)
                padded = jnp.concatenate([r.left[:, lanes], r.pair[:, lanes], r.right[:, lanes]], axis=0)
                natural = jnp.concatenate([padded[BLOCK : (blocks + 3) * BLOCK], padded[: 2 * BLOCK]], axis=0)
                held[...] = jnp.where(marked, split_rows(padded, sort), natural)
            scaled = (r.asked[...].astype(F32) * SCORE_SCALE).astype(BF)
            r.query[...] = jnp.where(marked, arrange_rows(scaled, sort), scaled)

        window = window_mask()
        natural, dilated_near = key_starts(step, True)
        own = pl.ds(pl.multiple_of(step * BLOCK, BLOCK), BLOCK)
        marked = marked_lanes(r.dilated, heads)
        key_block = jnp.where(marked, r.keys[dilated_near, :], r.keys[natural, :])
        value_block = jnp.where(marked, r.values[dilated_near, :], r.values[natural, :])
        query_block = r.query[own, :]
        gathered = jnp.zeros((BLOCK, width), F32)
        flags = head_flags(r.dilated, heads)
        for head, lanes in enumerate(head_lanes(heads)):
            mine = jnp.where(flags[head], r.seg_query[own, 1:2], r.seg_query[own, 0:1])
            theirs = jnp.where(flags[head], r.seg_keys[1:2, dilated_near], r.seg_keys[0:1, natural])
            soft = soft_weights(query_block, key_block, lanes, jnp.logical_and(window, mine == theirs))
            r.soft[head] = soft
            gathered = jnp.where(lanes, dot(soft, value_block), gathered)
        r.arranged[own, :] = gathered.astype(BF)

        for group in range(blocks // 2):

            @pl.when(step == 2 * group + 1)
            def _(group=group):
                part = slice(group * 2 * BLOCK, (group + 1) * 2 * BLOCK)
                arranged = r.arranged[part, :]
                restored = dot_tn(parity_matrix(), arranged).astype(BF)
                r.out[part, :] = jnp.where(marked, restored, arranged)
                if group == 0:
                    who.gather()
                    for t in range(chunks // 2):
                        exchange.give(t)

        @pl.when(step == blocks - 1)
        def _():
            for t in range(chunks // 2):
                exchange.take(t)
                exchange.finish(t)
            r.first[...] = r.landed[...]

    return run_kernel(
        body,
        "attend",
        dict(
            asked=query,
            pair=pair,
            left=left,
            right=right,
            seg_query=seg_query,
            seg_keys=seg_keys,
            dilated=dilated,
        ),
        dict(
            out=((rows, width), BF),
            first=((4, rows // 4, width), BF),
            arranged=((rows, width), BF),
            query=((rows, width), BF),
            keys=((slots * BLOCK, width), BF),
            values=((slots * BLOCK, width), BF),
            soft=((heads, rows, keys), BF),
        ),
        dict(
            landed=pltpu.VMEM((4, rows // 4, width), BF),
            sent=pltpu.SemaphoreType.DMA((3, chunks // 2)),
            came=pltpu.SemaphoreType.DMA((3, chunks // 2)),
        ),
        collective=8,
        flops=4 * rows * keys * 256 * heads,
        grid=(blocks,),
        specs=dict(soft=pl.BlockSpec((heads, BLOCK, keys), lambda i: (0, i, 0))),
        in_smem=("dilated",),
    )


def attend_back(saved, grad_out, dilated, rim, mixed, count, collective):
    rows, width = grad_out.shape
    heads = width // DH
    blocks = rows // BLOCK
    keys = 3 * BLOCK
    slots = 2 * blocks if mixed else blocks + 2

    def body(r):
        step = pl.program_id(0)
        column = Column(count)
        first, last = column.index == 0, column.index == count - 1
        before = (lax.rem(column.index + count - 1, count), column.here)
        after = (lax.rem(column.index + 1, count), column.here)
        copy = copy_to(r.ready_left, r.from_right, r.sent.at[0], r.came.at[0], before)

        @pl.when(step == 0)
        def _():
            barrier = pltpu.get_barrier_semaphore()

            @pl.when(jnp.logical_not(last))
            def _():
                pl.semaphore_signal(barrier, inc=1, device_id=after, device_id_type=MESH)

            grad = r.grad_out[...]
            if mixed:
                grad = jnp.where(marked_lanes(r.dilated, heads), arrange_rows(grad, parity_matrix()), grad)
            r.grad[...] = grad
            r.grad_keys[...] = jnp.zeros_like(r.grad_keys)
            r.grad_values[...] = jnp.zeros_like(r.grad_values)

        natural, dilated_near = key_starts(step, mixed)
        own = pl.ds(pl.multiple_of(step * BLOCK, BLOCK), BLOCK)
        marked = marked_lanes(r.dilated, heads)
        key_block, value_block = r.keys[natural, :], r.values[natural, :]
        if mixed:
            key_block = jnp.where(marked, r.keys[dilated_near, :], key_block)
            value_block = jnp.where(marked, r.values[dilated_near, :], value_block)
        query_block = r.query[own, :]
        grad_block = r.grad[own, :]
        product = grad_block.astype(F32) * r.arranged[own, :].astype(F32)
        grad_query = jnp.zeros((BLOCK, width), F32)
        grad_key = jnp.zeros((keys, width), F32)
        grad_value = jnp.zeros((keys, width), F32)
        for head, lanes in enumerate(head_lanes(heads)):
            soft = r.soft[head]
            grad_head = jnp.where(lanes, grad_block, 0.0).astype(BF)
            row_dot = jnp.sum(jnp.where(lanes, product, 0.0), axis=1, keepdims=True)
            grad_soft = dot_nt(grad_head, value_block)
            grad_scores = (soft.astype(F32) * (grad_soft - row_dot)).astype(BF)
            grad_value += dot_tn(soft, grad_head)
            grad_key += dot_tn(grad_scores, jnp.where(lanes, query_block, 0.0).astype(BF))
            grad_query = jnp.where(lanes, dot(grad_scores, key_block), grad_query)
        r.grad_query[own, :] = (grad_query * SCORE_SCALE).astype(BF)
        if mixed:
            for held, grad in ((r.grad_keys, grad_key), (r.grad_values, grad_value)):
                held[dilated_near, :] += jnp.where(marked, grad, 0.0)
                held[natural, :] += jnp.where(marked, 0.0, grad)
        else:
            r.grad_keys[natural, :] += grad_key
            r.grad_values[natural, :] += grad_value

        def natural_group(g, middle):
            both = []
            for held in (r.grad_keys, r.grad_values):
                plain = middle(held)
                pair = jnp.concatenate(
                    [
                        held[g * BLOCK : (g + 1) * BLOCK, :],
                        held[(blocks + g) * BLOCK : (blocks + g + 1) * BLOCK, :],
                    ],
                    axis=0,
                ).astype(BF)
                both.append(jnp.where(marked, dot_tn(parity_matrix(), pair), plain).astype(BF))
            return jnp.concatenate(both, axis=1)

        edge = jnp.zeros((BLOCK, width), F32)

        @pl.when(step == (1 if mixed else 0))
        def _():
            if mixed:
                r.ready_left[...] = natural_group(0, lambda held: jnp.concatenate([edge, held[:BLOCK, :]], axis=0))
            else:
                r.ready_left[...] = jnp.concatenate(
                    [r.grad_keys[:rim, :], r.grad_values[:rim, :]], axis=1
                ).astype(BF)

            @pl.when(jnp.logical_not(first))
            def _():
                pl.semaphore_wait(pltpu.get_barrier_semaphore(), 1)
                copy.start()

        @pl.when(step == blocks - 1)
        def _():
            if mixed:
                for g in range(blocks // 2):
                    part = slice(g * 2 * BLOCK, (g + 1) * 2 * BLOCK)
                    arranged = r.grad_query[part, :]
                    restored = dot_tn(parity_matrix(), arranged).astype(BF)
                    r.out_query[part, :] = jnp.where(marked, restored, arranged)
                lap = 2 * BLOCK
                r.out_own[:lap, :] = natural_group(1, lambda held: held[BLOCK : 3 * BLOCK, :])
                r.out_own[lap:, :] = natural_group(2, lambda held: held[3 * BLOCK : 5 * BLOCK, :])
                r.out_right[...] = natural_group(
                    3, lambda held: jnp.concatenate([held[5 * BLOCK : 6 * BLOCK, :], edge], axis=0)
                )
            else:
                r.out_query[...] = r.grad_query[...]
                both = jnp.concatenate([r.grad_keys[rim:, :], r.grad_values[rim:, :]], axis=1).astype(BF)
                r.out_own[...] = both[:rows]
                r.out_right[...] = both[rows:]

            @pl.when(jnp.logical_not(last))
            def _():
                copy.wait_recv()
                tail = pl.ds(rows - rim, rim)
                r.out_own[tail, :] = (r.out_own[tail, :].astype(F32) + r.from_right[...].astype(F32)).astype(BF)

            @pl.when(jnp.logical_not(first))
            def _():
                copy.wait_send()

    return run_kernel(
        body,
        "attend_back",
        dict(
            grad_out=grad_out,
            arranged=saved.arranged,
            query=saved.query,
            keys=saved.keys,
            values=saved.values,
            soft=saved.soft,
            dilated=dilated,
        ),
        dict(
            out_query=((rows, width), BF),
            out_own=((rows, 2 * width), BF),
            out_right=((rim, 2 * width), BF),
        ),
        dict(
            grad=pltpu.VMEM((rows, width), BF),
            grad_query=pltpu.VMEM((rows, width), BF),
            grad_keys=pltpu.VMEM((slots * BLOCK, width), F32),
            grad_values=pltpu.VMEM((slots * BLOCK, width), F32),
            ready_left=pltpu.VMEM((rim, 2 * width), BF),
            from_right=pltpu.VMEM((rim, 2 * width), BF),
            sent=pltpu.SemaphoreType.DMA((1,)),
            came=pltpu.SemaphoreType.DMA((1,)),
        ),
        collective=collective,
        flops=8 * rows * keys * 256 * heads,
        grid=(blocks,),
        specs=dict(soft=pl.BlockSpec((heads, BLOCK, keys), lambda i: (0, i, 0))),
        in_smem=("dilated",),
    )


class Partners:
    def __init__(self, count=0, shift=0, size=CHUNK):
        seq = lax.axis_index(SEQ)
        here = lax.axis_index(MP)
        self.core = lax.rem(here, 2)
        self.sibling = (seq, here + 1 - 2 * self.core)
        self.across = (seq, lax.rem(here + 2, 4))
        self.diagonal = (seq, lax.rem(here + 3 - 2 * self.core, 4))
        self.count, self.shift, self.size = count, shift, size

    def others(self, column):
        found = [self.sibling, self.across, self.diagonal]
        if column is not None:
            found += [column.peer(k) for k in range(1, column.count)]
        return found

    def call(self, column=None):
        barrier = pltpu.get_barrier_semaphore()
        for other in self.others(column):
            pl.semaphore_signal(barrier, inc=1, device_id=other, device_id_type=MESH)

    def gather(self, column=None):
        pl.semaphore_wait(pltpu.get_barrier_semaphore(), len(self.others(column)))

    def meet(self, column=None):
        self.call(column)
        self.gather(column)

    def place(self, t):
        return lax.rem(t + self.shift, self.count) if self.shift else t

    def chunk(self, t):
        return pl.ds(pl.multiple_of(self.place(t) * self.size, self.size), self.size)

    def two_chunks(self, t):
        return pl.ds(pl.multiple_of(self.place(t - 1) * self.size, 2 * self.size), 2 * self.size)

    def part(self, t, core):
        half = self.size // 2
        return pl.ds(pl.multiple_of(self.place(t) * self.size + core * half, half), half)

    def own(self, t):
        return self.part(t, self.core)

    def other(self, t):
        return self.part(t, 1 - self.core)

    def half(self, t):
        half = self.size // 2
        return pl.ds(pl.multiple_of(self.place(t) * half, half), half)


def copy_to(source, target, sent, arrived, device):
    return pltpu.make_async_remote_copy(
        src_ref=source, dst_ref=target, send_sem=sent, recv_sem=arrived, device_id=device, device_id_type=MESH
    )


def exchange_scratch(rows):
    count = rows // CHUNK
    return dict(
        part=pltpu.VMEM((rows, D), BF),
        near=pltpu.VMEM((rows // 2, D), BF),
        far=pltpu.VMEM((rows // 2, D), BF),
        core_sent=pltpu.SemaphoreType.DMA((count,)),
        core_came=pltpu.SemaphoreType.DMA((count,)),
        far_sent=pltpu.SemaphoreType.DMA((count,)),
        far_came=pltpu.SemaphoreType.DMA((count,)),
    )


def gather_scratch(rows, width=D, dtype=BF):
    count = rows // CHUNK
    return dict(
        full=pltpu.VMEM((rows, width), dtype),
        sent=pltpu.SemaphoreType.DMA((count,)),
        came=pltpu.SemaphoreType.DMA((count,)),
    )


class Exchange:
    def __init__(self, who, refs):
        self.who, self.r = who, refs

    def core_copy(self, t):
        who, r = self.who, self.r
        return copy_to(
            r.part.at[who.other(t), :], r.near.at[who.half(t), :], r.core_sent.at[t], r.core_came.at[t], who.sibling
        )

    def far_copy(self, t):
        who, r = self.who, self.r
        rows = who.half(t)
        return copy_to(r.near.at[rows, :], r.far.at[rows, :], r.far_sent.at[t], r.far_came.at[t], who.across)

    def give(self, t, part):
        self.r.part[self.who.chunk(t), :] = part.astype(BF)
        self.core_copy(t).start()

    def add(self, t):
        who, r = self.who, self.r
        self.core_copy(t).wait_recv()
        pair = r.part[who.own(t), :].astype(F32) + r.near[who.half(t), :].astype(F32)
        r.near[who.half(t), :] = pair.astype(BF)
        self.far_copy(t).start()

    def take(self, t):
        who, r = self.who, self.r
        self.far_copy(t).wait_recv()
        return r.near[who.half(t), :].astype(F32) + r.far[who.half(t), :].astype(F32)

    def finish(self, t):
        self.core_copy(t).wait_send()
        self.far_copy(t).wait_send()


class Gather:
    def __init__(self, who, refs):
        self.who, self.r = who, refs

    def copy(self, rows, t):
        r = self.r
        return copy_to(r.full.at[rows, :], r.full.at[rows, :], r.sent.at[t], r.came.at[t], self.who.sibling)

    def give(self, t, value):
        rows = self.who.own(t)
        self.r.full[rows, :] = value.astype(self.r.full.dtype)
        self.copy(rows, t).start()

    def take(self, t):
        self.wait(t)
        return self.r.full[self.who.chunk(t), :]

    def wait(self, t):
        self.copy(self.who.other(t), t).wait_recv()

    def finish(self, t):
        self.copy(self.who.own(t), t).wait_send()


class Column:
    def __init__(self, count):
        self.count = count
        self.lines = count // 2
        self.here = lax.axis_index(MP)
        self.index = lax.axis_index(SEQ)
        self.inner = lax.rem(self.index, 2)
        self.outer = lax.div(self.index, 2)

    def peer(self, k):
        return (lax.rem(self.index + k, self.count), self.here)

    def at(self, outer, inner):
        return (2 * outer + inner, self.here)

    def turn(self, k):
        return lax.rem(self.outer + k, self.lines)


def gather_sems(lines):
    return {
        key: pltpu.SemaphoreType.DMA((lines,)) for key in ("pair_sent", "pair_came", "up_sent", "down_sent", "line_came")
    }


class GatherBlocks:
    def __init__(self, column, refs):
        self.c, self.r = column, refs
        self.above = column.outer < column.lines - 1
        self.below = column.outer > 0

    def line_copy(self, source, step):
        c, r = self.c, self.r
        block = 2 * source + c.inner
        sent = r.up_sent if step > 0 else r.down_sent
        return copy_to(
            r.full.at[block], r.full.at[block], sent.at[source], r.line_came.at[source], c.at(c.outer + step, c.inner)
        )

    def pair_copy(self, source, inner):
        c, r = self.c, self.r
        block = 2 * source + inner
        return copy_to(
            r.full.at[block],
            r.full.at[block],
            r.pair_sent.at[source],
            r.pair_came.at[source],
            c.at(c.outer, 1 - c.inner),
        )

    def put(self, value):
        self.r.full[self.c.index] = value

    def start_line(self):
        c = self.c

        @pl.when(self.above)
        def _():
            self.line_copy(c.outer, 1).start()

        @pl.when(self.below)
        def _():
            self.line_copy(c.outer, -1).start()

    def start_pair(self):
        self.pair_copy(self.c.outer, self.c.inner).start()

    def relay(self, k):
        c = self.c

        @pl.when(c.outer >= k)
        def _():
            source = c.outer - k
            self.line_copy(source, 1).wait_recv()

            @pl.when(self.above)
            def _():
                self.line_copy(source, 1).start()

            self.hand_on(source)

        @pl.when(c.outer + k < c.lines)
        def _():
            source = c.outer + k
            self.line_copy(source, -1).wait_recv()

            @pl.when(self.below)
            def _():
                self.line_copy(source, -1).start()

            self.hand_on(source)

    def hand_on(self, source):
        self.pair_copy(source, self.c.inner).start()

    def arrive(self):
        for k in range(self.c.lines):
            self.pair_copy(k, 1 - self.c.inner).wait_recv()

    def finish(self):
        for k in range(self.c.lines):
            self.pair_copy(k, self.c.inner).wait_send()
        self.finish_line()

    def finish_line(self):
        c = self.c
        for k in range(c.lines):

            @pl.when(jnp.logical_and(self.above, c.outer >= k))
            def _(k=k):
                self.line_copy(k, 1).wait_send()

            @pl.when(jnp.logical_and(self.below, c.outer <= k))
            def _(k=k):
                self.line_copy(k, -1).wait_send()


class GatherPairs(GatherBlocks):
    def line_copy(self, source, step):
        c, r = self.c, self.r
        blocks = pl.ds(2 * source, 2)
        sent = r.up_sent if step > 0 else r.down_sent
        return copy_to(
            r.full.at[blocks], r.full.at[blocks], sent.at[source], r.line_came.at[source], c.at(c.outer + step, c.inner)
        )

    def begin(self):
        self.pair_copy(self.c.outer, 1 - self.c.inner).wait_recv()
        self.start_line()

    def hand_on(self, source):
        pass

    def finish(self):
        self.pair_copy(self.c.outer, self.c.inner).wait_send()
        self.finish_line()


def scatter_scratch(lines, block, size, held=True):
    scratch = {
        key: pltpu.SemaphoreType.DMA((lines + 1,))
        for key in ("pair_sent", "pair_came", "line_sent", "line_came", "own_came")
    }
    scratch.update(near=pltpu.VMEM((lines, block, size), BF), far=pltpu.VMEM((lines + 1, block, size), BF))
    if held:
        scratch["own"] = pltpu.VMEM((lines, block, size), BF)
    return scratch


class ScatterBlocks:
    def __init__(self, column, refs, total):
        self.c, self.r, self.total = column, refs, total
        self.above = column.outer < column.lines - 1
        self.below = column.outer > 0
        self.fetched = hasattr(refs, "own")
        order = []
        for k in range(column.lines // 2):
            order += [column.lines - 1 - k, k]
        self.order = order

    def pair_copy(self, outer):
        c, r = self.c, self.r
        return copy_to(
            r.grads.at[2 * outer + 1 - c.inner],
            r.near.at[outer],
            r.pair_sent.at[outer],
            r.pair_came.at[outer],
            c.at(c.outer, 1 - c.inner),
        )

    def own_copy(self, outer):
        c, r = self.c, self.r
        return pltpu.make_async_copy(r.grads.at[2 * outer + c.inner], r.own.at[outer], r.own_came.at[outer])

    def line_copy(self, target, step):
        c, r = self.c, self.r
        slot = target if step > 0 else jnp.where(c.outer - 1 == target, c.lines, target)
        return copy_to(
            r.near.at[target],
            r.far.at[slot],
            r.line_sent.at[target],
            r.line_came.at[slot],
            c.at(c.outer + step, c.inner),
        )

    def landing(self, slot, step):
        c, r = self.c, self.r
        return copy_to(
            r.near.at[c.outer], r.far.at[slot], r.line_sent.at[c.outer], r.line_came.at[slot], c.at(c.outer + step, c.inner)
        )

    def start(self):
        for outer in self.order:
            self.pair_copy(outer).start()
            if self.fetched:
                self.own_copy(outer).start()

    def pair_step(self, k):
        c, r = self.c, self.r
        for outer in self.order[2 * k : 2 * k + 2]:
            self.pair_copy(outer).wait_recv()
            if self.fetched:
                self.own_copy(outer).wait()
                own = r.own[outer]
            else:
                own = r.grads[2 * outer + c.inner]
            r.near[outer] = (own.astype(F32) + r.near[outer].astype(F32)).astype(BF)

    def line_step(self, wave):
        c, r = self.c, self.r
        from_top = c.lines - 1 - c.outer

        def pass_on(target, step, behind):
            @pl.when(behind)
            def _():
                self.landing(target, step).wait_recv()
                r.near[target] = (r.near[target].astype(F32) + r.far[target].astype(F32)).astype(BF)

            self.line_copy(target, step).start()

        @pl.when(c.outer <= wave)
        def _():
            pass_on(from_top + c.outer - wave + c.outer, 1, self.below)

        @pl.when(from_top <= wave)
        def _():
            pass_on(wave - from_top, -1, self.above)

    def close(self):
        c, r = self.c, self.r
        self.total[...] = r.near[c.outer].astype(F32)

        @pl.when(self.below)
        def _():
            self.landing(c.outer, 1).wait_recv()
            self.total[...] += r.far[c.outer].astype(F32)

        @pl.when(self.above)
        def _():
            self.landing(c.lines, -1).wait_recv()
            self.total[...] += r.far[c.lines].astype(F32)

    def finish(self):
        c = self.c
        for outer in self.order:
            self.pair_copy(outer).wait_send()
        for target in range(c.lines):

            @pl.when(c.outer < target)
            def _(target=target):
                self.line_copy(target, 1).wait_send()

            @pl.when(c.outer > target)
            def _(target=target):
                self.line_copy(target, -1).wait_send()

    def ticks(self, times):
        steps = [(times[0], lambda: self.pair_step(0)), (times[0], lambda: self.line_step(0))]
        steps += [(times[1], lambda: self.pair_step(1))]
        steps += [(times[k], lambda k=k: self.line_step(k)) for k in range(1, self.c.lines - 1)]
        steps += [(times[self.c.lines - 1], self.close)]
        return steps


def scatter_pairs_scratch(lines, block, size):
    scratch = {key: pltpu.SemaphoreType.DMA((lines + 1,)) for key in ("pair_sent", "pair_came", "line_sent", "line_came")}
    scratch.update(
        sums=pltpu.VMEM((2 * lines, block, size), BF),
        far=pltpu.VMEM((2 * lines + 2, block, size), BF),
        give=pltpu.VMEM((block, size), BF),
        get=pltpu.VMEM((block, size), BF),
        held=pltpu.SemaphoreType.DMA,
    )
    return scratch


class ScatterPairs:
    def __init__(self, column, refs, total):
        self.c, self.r, self.total = column, refs, total
        self.above = column.outer < column.lines - 1
        self.below = column.outer > 0
        self.fetch = pltpu.make_async_copy(refs.grads, refs.sums, refs.held)

    def line_copy(self, target, step):
        c, r = self.c, self.r
        slot = target if step > 0 else jnp.where(c.outer - 1 == target, c.lines, target)
        return copy_to(
            r.sums.at[pl.ds(2 * target, 2)],
            r.far.at[pl.ds(2 * slot, 2)],
            r.line_sent.at[target],
            r.line_came.at[slot],
            c.at(c.outer + step, c.inner),
        )

    def landing(self, slot, step):
        c, r = self.c, self.r
        return copy_to(
            r.sums.at[pl.ds(2 * c.outer, 2)],
            r.far.at[pl.ds(2 * slot, 2)],
            r.line_sent.at[c.outer],
            r.line_came.at[slot],
            c.at(c.outer + step, c.inner),
        )

    def pair_copy(self):
        c, r = self.c, self.r
        return copy_to(r.give, r.get, r.pair_sent.at[0], r.pair_came.at[0], c.at(c.outer, 1 - c.inner))

    def start(self):
        self.fetch.start()

    def line_step(self, wave):
        c, r = self.c, self.r
        from_top = c.lines - 1 - c.outer
        if wave == 0:
            self.fetch.wait()

        def pass_on(target, step, behind):
            @pl.when(behind)
            def _():
                self.landing(target, step).wait_recv()
                for k in range(2):
                    block = 2 * target + k
                    r.sums[block] = (r.sums[block].astype(F32) + r.far[block].astype(F32)).astype(BF)

            self.line_copy(target, step).start()

        @pl.when(c.outer <= wave)
        def _():
            pass_on(from_top + c.outer - wave + c.outer, 1, self.below)

        @pl.when(from_top <= wave)
        def _():
            pass_on(wave - from_top, -1, self.above)

    def close_line(self):
        c, r = self.c, self.r
        mine, other = 2 * c.outer + c.inner, 2 * c.outer + 1 - c.inner
        self.total[...] = r.sums[mine].astype(F32)

        @pl.when(self.below)
        def _():
            self.landing(c.outer, 1).wait_recv()
            self.total[...] += r.far[mine].astype(F32)
            r.sums[other] = (r.sums[other].astype(F32) + r.far[other].astype(F32)).astype(BF)

        @pl.when(self.above)
        def _():
            self.landing(c.lines, -1).wait_recv()
            self.total[...] += r.far[2 * c.lines + c.inner].astype(F32)
            r.sums[other] = (r.sums[other].astype(F32) + r.far[2 * c.lines + 1 - c.inner].astype(F32)).astype(BF)

        r.give[...] = r.sums[other]
        self.pair_copy().start()

    def close(self):
        self.pair_copy().wait_recv()
        self.total[...] += self.r.get[...].astype(F32)

    def finish(self):
        c = self.c
        self.pair_copy().wait_send()
        for target in range(c.lines):

            @pl.when(c.outer < target)
            def _(target=target):
                self.line_copy(target, 1).wait_send()

            @pl.when(c.outer > target)
            def _(target=target):
                self.line_copy(target, -1).wait_send()

    def ticks(self, times):
        steps = [(times[k], lambda k=k: self.line_step(k)) for k in range(self.c.lines - 1)]
        return steps + [(times[self.c.lines - 1], self.close_line), (times[self.c.lines], self.close)]


class Halo:
    def __init__(self, column, refs, source, rim, size):
        self.c, self.r, self.source, self.rim, self.size = column, refs, source, rim, size
        self.rows = source.shape[0]
        self.before = lax.rem(column.index + column.count - 1, column.count), column.here
        self.after = lax.rem(column.index + 1, column.count), column.here
        self.first, self.last = column.index == 0, column.index == column.count - 1

    def clear(self):
        @pl.when(self.first)
        def _():
            self.r.left[...] = jnp.zeros_like(self.r.left)

        @pl.when(self.last)
        def _():
            self.r.right[...] = jnp.zeros_like(self.r.right)

    def back_copy(self, t):
        rows = pl.ds(pl.multiple_of(t * self.size, self.size), self.size)
        return copy_to(
            self.source.at[rows, :], self.r.right.at[rows, :], self.r.back_sent.at[t], self.r.back_came.at[t], self.before
        )

    def ahead_copy(self, t):
        from_rows = pl.ds(pl.multiple_of(self.rows - self.rim + t * self.size, self.size), self.size)
        rows = pl.ds(pl.multiple_of(t * self.size, self.size), self.size)
        return copy_to(
            self.source.at[from_rows, :],
            self.r.left.at[rows, :],
            self.r.ahead_sent.at[t],
            self.r.ahead_came.at[t],
            self.after,
        )

    def send(self, t):
        count = self.rim // self.size
        offset = (self.rows - self.rim) // self.size

        @pl.when(jnp.logical_and(t < count, jnp.logical_not(self.first)))
        def _():
            self.back_copy(t).start()

        @pl.when(jnp.logical_and(t >= offset, jnp.logical_not(self.last)))
        def _():
            self.ahead_copy(t - offset).start()

    def arrive(self):
        for t in range(self.rim // self.size):

            @pl.when(jnp.logical_not(self.last))
            def _():
                self.back_copy(t).wait_recv()

            @pl.when(jnp.logical_not(self.first))
            def _():
                self.ahead_copy(t).wait_recv()

    def finish(self):
        for t in range(self.rim // self.size):

            @pl.when(jnp.logical_not(self.first))
            def _():
                self.back_copy(t).wait_send()

            @pl.when(jnp.logical_not(self.last))
            def _():
                self.ahead_copy(t).wait_send()


def halo_scratch(count):
    return {
        key: pltpu.SemaphoreType.DMA((count,)) for key in ("back_sent", "back_came", "ahead_sent", "ahead_came")
    }


def pick(r, prefix):
    start = prefix + "_"
    return SimpleNamespace(
        **{key[len(start) :]: value for key, value in vars(r).items() if key.startswith(start)}
    )


def prefixed(prefix, entries):
    return {prefix + "_" + key: value for key, value in entries.items()}


def run_stages(count, stages, ticks=()):
    last = max(delay for delay, _ in stages)

    def step(i, carry):
        for when in sorted({when for when, _ in ticks if when < count + last}):

            @pl.when(i == when)
            def _(when=when):
                for other, tick in ticks:
                    if other == when:
                        tick()

        for delay, stage in stages:

            @pl.when(jnp.logical_and(i >= delay, i < count + delay))
            def _(delay=delay, stage=stage):
                stage(i - delay)

        return carry

    lax.fori_loop(0, count + last, step, 0)
    for when, tick in sorted(ticks, key=lambda entry: entry[0]):
        if when >= count + last:
            tick()


def norm_forward(total, gain, shift):
    center = total - jnp.mean(total, axis=1, keepdims=True)
    spread = jnp.mean(center * center, axis=1, keepdims=True)
    inverse = lax.rsqrt(spread + NORM_EPSILON)
    unit = center * inverse
    return unit, inverse, unit * gain + shift


def norm_back(grad, unit, inverse, gain):
    grad_unit = grad * gain
    first = jnp.mean(grad_unit, axis=1, keepdims=True)
    second = jnp.mean(grad_unit * unit, axis=1, keepdims=True)
    return inverse * (grad_unit - first - unit * second)


def column_sum(value):
    return jnp.sum(value, axis=0, keepdims=True)


def split_two(value):
    high = value.astype(BF)
    return high, (value - high.astype(F32)).astype(BF)


def exact(value, product):
    high, rest = split_two(value)
    low = (value - high.astype(F32) - rest.astype(F32)).astype(BF)
    return product(high) + product(rest) + product(low)


def wide(column):
    return jnp.broadcast_to(column, (column.shape[0], 128))


def forward_refs(rows, width, units):
    return dict(
        unit_one=((rows // 2, D), F32),
        unit_two=((rows // 2, D), F32),
        hidden=((rows, units), BF),
        slope=((rows, units), BF),
    )


def forward_small(rows):
    return dict(inverse_one=((rows // 2, 128), F32), inverse_two=((rows // 2, 128), F32))


def forward_stages(r, who, projected, second, spread):
    def middle(t):
        rows = who.own(t) if r.residual.shape[0] == r.mixed.shape[0] else who.half(t)
        total = r.residual[rows, :].astype(F32) + projected(t) + r.shared[r.base + 0 : r.base + 1, :]
        unit, inverse, normed = norm_forward(total, r.shared[r.base + 1 : r.base + 2, :], r.shared[r.base + 2 : r.base + 3, :])
        r.unit_one[who.half(t), :] = unit
        r.inverse_one[who.half(t), :] = wide(inverse)
        r.normed[who.half(t), :] = normed
        spread.give(t, normed)

    def feed(t):
        pre = dot(spread.take(t), r.ffn_up[...]) + r.hidden_bias
        chance = 0.5 + 0.5 * lax.erf(pre * (0.5**0.5))
        hidden = (pre * chance).astype(BF)
        r.hidden[who.chunk(t), :] = hidden
        bell = jnp.exp(-0.5 * pre * pre) * 0.3989422804014327
        r.slope[who.chunk(t), :] = (chance + pre * bell).astype(BF)
        second.give(t, dot_nt(hidden, r.ffn_down[...]))

    def final(t):
        total = r.normed[who.half(t), :] + second.take(t) + r.shared[r.base + 3 : r.base + 4, :]
        unit, inverse, result = norm_forward(total, r.shared[r.base + 4 : r.base + 5, :], r.shared[r.base + 5 : r.base + 6, :])
        r.unit_two[who.half(t), :] = unit
        r.inverse_two[who.half(t), :] = wide(inverse)
        return unit, inverse, result

    return middle, feed, final


def backward_stages(r, who, ends, third, mids):
    def enter(t, grad, unit, inverse):
        grad_total = norm_back(grad, unit, inverse, r.shared[r.base + 4 : r.base + 5, :])
        r.vectors[3:4, :] += column_sum(grad_total)
        r.vectors[4:5, :] += column_sum(grad * unit)
        r.vectors[5:6, :] += column_sum(grad)
        r.kept[who.half(t), :] = grad_total
        ends.give(t, grad_total)

    def feed_back(t):
        rows = who.chunk(t)
        grad = ends.take(t)
        grad_pre = (dot(grad, r.ffn_down[...]) * r.slope[rows, :].astype(F32)).astype(BF)
        r.units[0:1, :] += column_sum(grad_pre.astype(F32))
        third.give(t, dot_nt(grad_pre, r.ffn_up[...]))
        r.grad_pre[pl.ds(pl.multiple_of(lax.rem(t, 2) * who.size, who.size), who.size), :] = grad_pre

        @pl.when(lax.rem(t, 2) == 1)
        def _():
            both = who.two_chunks(t)
            r.sum_up[...] += dot_tn(r.spread_full[both, :], r.grad_pre[...])
            r.sum_down[...] += dot_tn(ends.r.full[both, :], r.hidden[both, :])

    def leave(t):
        grad = r.kept[who.half(t), :] + third.take(t)
        unit = r.unit_one[who.half(t), :]
        grad_total = norm_back(grad, unit, r.inverse_one[who.half(t), 0:1], r.shared[r.base + 1 : r.base + 2, :])
        r.vectors[0:1, :] += column_sum(grad_total)
        r.vectors[1:2, :] += column_sum(grad * unit)
        r.vectors[2:3, :] += column_sum(grad)
        if r.grad_one is not None:
            r.grad_one[who.half(t), :] = grad_total
        mids.give(t, grad_total)

    def project_back(t):
        rows = who.chunk(t)
        grad = mids.take(t)
        r.grad_mixed[rows, :] = dot(grad, r.out_proj[...]).astype(BF)

        @pl.when(lax.rem(t, 2) == 1)
        def _():
            both = who.two_chunks(t)
            r.sum_out[...] += dot_tn(mids.r.full[both, :], r.mixed[both, :])

    return enter, feed_back, leave, project_back


def clear(*refs):
    for ref in refs:
        ref[...] = jnp.zeros_like(ref)


def finish_all(count, parts):
    def step(t, carry):
        for part in parts:
            part.finish(t)
        return carry

    lax.fori_loop(0, count, step, 0)


def packed(ref):
    return jnp.concatenate([ref[k].astype(BF) for k in range(ref.shape[0])], axis=1)


def projection_bias(split, width):
    return jnp.concatenate([split[:, :width], jnp.zeros((1, width), F32), split[:, width : 2 * width]], axis=1)


def opening(activations, segments, owners, attn_weights, ffn_weights, split_biases, shared_vectors, count):
    rows = activations.shape[0]
    width, units = attn_weights.shape[3], ffn_weights.shape[3]
    heads = width // DH
    blocks = rows // BLOCK
    lines = count // 2
    block = D // count
    layers = split_biases.shape[0]

    def body(r):
        who = Partners()
        column = Column(count)
        who.meet(column)
        wide_attn = GatherBlocks(column, SimpleNamespace(full=r.full_attn, **vars(pick(r, "ga"))))
        wide_up = GatherBlocks(column, SimpleNamespace(full=r.full_up, **vars(pick(r, "gu"))))
        wide_down = GatherPairs(column, SimpleNamespace(full=r.full_down, **vars(pick(r, "gd"))))
        halo = Halo(column, SimpleNamespace(left=r.left, right=r.right, **vars(pick(r, "halo"))), r.pair, WIN, BLOCK)
        first, last = column.index == 0, column.index == count - 1
        to_before = copy_to(r.ids, r.ids_right, r.ids_sent.at[0], r.ids_came.at[0], halo.before)
        to_after = copy_to(r.ids, r.ids_left, r.ids_sent.at[1], r.ids_came.at[1], halo.after)
        wide_attn.put(packed(r.attn.at[0]))
        wide_attn.start_line()
        wide_attn.start_pair()
        r.ids[...] = r.segments[...].astype(F32)

        @pl.when(first)
        def _():
            r.ids_left[...] = jnp.zeros_like(r.ids_left)

        @pl.when(last)
        def _():
            r.ids_right[...] = jnp.zeros_like(r.ids_right)

        @pl.when(jnp.logical_not(first))
        def _():
            to_before.start()

        @pl.when(jnp.logical_not(last))
        def _():
            to_after.start()

        halo.clear()
        wide_down.put(r.ffn[0, 1].astype(BF))
        wide_down.start_pair()
        wide_up.put(r.ffn[0, 0].astype(BF))
        for slot in range(count):
            row = lax.broadcasted_iota(jnp.int32, (block, D), 0)
            col = lax.broadcasted_iota(jnp.int32, (block, D), 1)
            target = r.owners[slot] * block + row
            r.turn[slot * block : (slot + 1) * block, :] = jnp.where(col == target, 1.0, 0.0).astype(BF)

        def sort_chunk(t, carry):
            chunk = pl.ds(pl.multiple_of(t * BLOCK, BLOCK), BLOCK)
            r.low[chunk, :] = dot(r.activations[chunk, :], r.turn[...]).astype(BF)
            return carry

        lax.fori_loop(0, blocks, sort_chunk, 0)
        wide_attn.relay(1)
        padding = jnp.zeros((16 - 6 * layers, D), F32)
        stacked = [r.shared_vectors[k, layer : layer + 1, :] for layer in range(layers) for k in range(6)]
        stacked = jnp.concatenate(stacked + [padding], axis=0)
        r.shared[...] = exact(stacked, lambda part: dot(part, r.turn[...]))
        wide_attn.relay(2)
        wide_up.start_line()

        @pl.when(jnp.logical_not(last))
        def _():
            to_before.wait_recv()

        @pl.when(jnp.logical_not(first))
        def _():
            to_after.wait_recv()

        def flat(ref):
            return jnp.concatenate([ref[k : k + 1, :] for k in range(ref.shape[0])], axis=1)

        own_ids = flat(r.ids)
        padded = jnp.concatenate([flat(r.ids_left)[:, rows - 2 * WIN :], own_ids, flat(r.ids_right)[:, : 2 * WIN]], axis=1)
        r.id_row[...] = jnp.broadcast_to(padded, r.id_row.shape)
        sort = parity_matrix()
        lap = 2 * BLOCK
        sorted_ids = [
            dot_nt(r.id_row[:, g * lap : (g + 1) * lap].astype(BF), sort) for g in range(2 * blocks // 2)
        ]
        natural = jnp.concatenate([padded[:, WIN : rows + 3 * WIN], padded[:, : 2 * WIN]], axis=1)
        arranged = jnp.concatenate(
            [part[0:1, :BLOCK] for part in sorted_ids] + [part[0:1, BLOCK:] for part in sorted_ids], axis=1
        )
        r.seg_keys[0:1, :] = natural
        r.seg_keys[1:2, :] = arranged
        middle = sorted_ids[1:-1]
        own_arranged = jnp.concatenate([part[0:1, :] for part in middle], axis=1)
        for which, row in ((0, own_ids), (1, own_arranged)):
            for k in range(rows // 128):
                square = jnp.broadcast_to(row[:, k * 128 : (k + 1) * 128], (128, 128))
                r.seg_query[k * 128 : (k + 1) * 128, which : which + 1] = square.T[:, 0:1]

        for k in range(3, lines):
            wide_attn.relay(k)
        wide_up.start_pair()
        wide_up.relay(1)
        wide_attn.arrive()
        r.proj[...] = r.full_attn[...].reshape(D, 4 * width)[:, : 3 * width]
        bias = projection_bias(r.split[0], width)

        def project(t):
            chunk = pl.ds(pl.multiple_of(t * BLOCK, BLOCK), BLOCK)
            value = dot(r.low[chunk, :], r.proj[...]) + bias
            r.query[chunk, :] = (value[:, :width].astype(BF).astype(F32) * SCORE_SCALE).astype(BF)
            pair = value[:, width:].astype(BF)
            r.pair[chunk, :] = pair
            inner = pl.ds(pl.multiple_of((t + 1) * BLOCK, BLOCK), BLOCK)
            r.keys[inner, :] = pair[:, :width]
            r.values[inner, :] = pair[:, width:]

        def outer_project(i, carry):
            t = i * (blocks - 1)
            project(t)
            halo.send(t)
            return carry

        def inner_project(i, carry):
            project(i)
            return carry

        lax.fori_loop(0, 2, outer_project, 0)
        wide_up.relay(2)
        wide_down.begin()
        lax.fori_loop(1, blocks - 1, inner_project, 0)
        for k in range(3, lines):
            wide_up.relay(k)

        def attend_block(step):
            own = pl.ds(pl.multiple_of(step * BLOCK, BLOCK), BLOCK)
            near = pl.ds(pl.multiple_of(step * BLOCK, BLOCK), 3 * BLOCK)
            key_block, value_block, query_block = r.keys[near, :], r.values[near, :], r.query[own, :]
            mine = r.seg_query[own, 0:1]
            theirs = r.id_row[0:1, pl.ds(pl.multiple_of(step * BLOCK + BLOCK, BLOCK), 3 * BLOCK)]
            allowed = jnp.logical_and(window_mask(), mine == theirs)
            gathered = jnp.zeros((BLOCK, width), F32)
            for head, lanes in enumerate(head_lanes(heads)):
                soft = soft_weights(query_block, key_block, lanes, allowed)
                r.soft[head, own, :] = soft
                gathered = jnp.where(lanes, dot(soft, value_block), gathered)
            r.out[own, :] = gathered.astype(BF)

        def inner_attend(i, carry):
            attend_block(i)
            return carry

        def outer_attend(i, carry):
            attend_block(i * (blocks - 1))
            return carry

        lax.fori_loop(1, blocks - 1, inner_attend, 0)
        wide_down.relay(1)
        halo.arrive()
        for part, start in ((r.left, 0), (r.right, (blocks + 1) * BLOCK)):
            r.keys[pl.ds(start, BLOCK), :] = part[:, :width]
            r.values[pl.ds(start, BLOCK), :] = part[:, width:]
        lax.fori_loop(0, 2, outer_attend, 0)
        for k in range(2, lines):
            wide_down.relay(k)
        wide_up.arrive()
        halo.finish()
        for engine in (wide_attn, wide_up, wide_down):
            engine.finish()

        @pl.when(jnp.logical_not(first))
        def _():
            to_before.wait_send()

        @pl.when(jnp.logical_not(last))
        def _():
            to_after.wait_send()

    scratch = dict(
        proj=pltpu.VMEM((D, 3 * width), BF),
        pair=pltpu.VMEM((rows, 2 * width), BF),
        left=pltpu.VMEM((WIN, 2 * width), BF),
        right=pltpu.VMEM((WIN, 2 * width), BF),
        ids=pltpu.VMEM((rows // 128, 128), F32),
        ids_left=pltpu.VMEM((rows // 128, 128), F32),
        ids_right=pltpu.VMEM((rows // 128, 128), F32),
        ids_sent=pltpu.SemaphoreType.DMA((2,)),
        ids_came=pltpu.SemaphoreType.DMA((2,)),
        id_row=pltpu.VMEM((8, rows + 4 * WIN), F32),
    )
    scratch.update(prefixed("ga", gather_sems(lines)))
    scratch.update(prefixed("gu", gather_sems(lines)))
    scratch.update(prefixed("gd", gather_sems(lines)))
    scratch.update(prefixed("halo", halo_scratch(1)))
    return run_kernel(
        body,
        "opening",
        dict(
            activations=activations,
            segments=segments.reshape(rows // 128, 128),
            owners=owners,
            attn=attn_weights,
            ffn=ffn_weights,
            split=split_biases,
            shared_vectors=shared_vectors.transpose(1, 0, 2),
        ),
        dict(
            full_attn=((count, block, 4 * width), BF),
            full_up=((count, block, units), BF),
            full_down=((count, block, units), BF),
            low=((rows, D), BF),
            turn=((D, D), BF),
            shared=((16, D), F32),
            seg_query=((rows, 2), F32),
            seg_keys=((8, 2 * rows), F32),
            out=((rows, width), BF),
            query=((rows, width), BF),
            keys=((rows + 2 * BLOCK, width), BF),
            values=((rows + 2 * BLOCK, width), BF),
            soft=((heads, rows, 3 * BLOCK), BF),
        ),
        scratch,
        collective=5,
        flops=2 * rows * D * (D + 3 * width),
        in_smem=("owners",),
    )


def middle_forward(mixed, attn, ffn_up, ffn_down, residual, shared, split_biases, attn_weights, ffn_weights, count):
    rows, width = mixed.shape
    units = ffn_up.shape[1]
    chunks = rows // CHUNK
    lines = count // 2
    block = D // count

    def body(r):
        who = Partners()
        r.base = 0
        first, second = Exchange(who, pick(r, "first")), Exchange(who, pick(r, "second"))
        spread = Gather(who, SimpleNamespace(full=r.spread_full, sent=r.spread_sent, came=r.spread_came))
        last = Gather(who, SimpleNamespace(full=r.last_full, sent=r.last_sent, came=r.last_came))
        column = Column(count)
        who.meet(column)
        wide_attn = GatherBlocks(column, SimpleNamespace(full=r.full_attn, **vars(pick(r, "ga"))))
        wide_up = GatherBlocks(column, SimpleNamespace(full=r.full_up, **vars(pick(r, "gu"))))
        wide_down = GatherPairs(column, SimpleNamespace(full=r.full_down, **vars(pick(r, "gd"))))
        halo = Halo(column, SimpleNamespace(left=r.left, right=r.right, **vars(pick(r, "halo"))), r.pair, 2 * WIN, CHUNK)
        wide_attn.put(packed(r.next_attn.at[1]))
        wide_attn.start_line()
        wide_attn.start_pair()
        wide_down.put(r.next_ffn[1, 1].astype(BF))
        wide_down.start_pair()
        wide_up.put(r.next_ffn[1, 0].astype(BF))
        halo.clear()
        r.out_proj[...] = r.attn[:, 3 * width :]
        r.hidden_bias = r.split[0][:, 2 * width :]
        next_bias = projection_bias(r.split[1], width)

        def share(kind, slot):
            device = who.across if kind == 1 else who.sibling
            return copy_to(
                r.next_out.at[slot], r.next_out.at[slot], r.share_sent.at[kind], r.share_came.at[kind], device
            )

        def hand_on():
            share(1, who.across[1]).wait_recv()
            share(2, who.across[1]).start()

        def unpack():
            wide_attn.arrive()
            packed_attn = r.full_attn[...].reshape(D, 4 * width)
            r.next_proj[...] = packed_attn[:, : 3 * width]
            r.next_out[column.here] = packed_attn[:, 3 * width :].astype(F32).T.astype(BF)
            share(0, column.here).start()
            share(1, column.here).start()

        ticks = [(3, r.late.residual.wait), (4, r.late.ffn_up.wait), (4, r.late.ffn_down.wait), (chunks, unpack), (chunks + 6, hand_on)]
        ticks += [(when, lambda k=k: wide_attn.relay(k + 1)) for k, when in enumerate(GATHER_TIMES[0])]
        ticks += [(GATHER_TIMES[1][0], wide_up.start_line), (GATHER_TIMES[1][1], wide_up.start_pair)]
        ticks += [(when, lambda k=k: wide_up.relay(k + 1)) for k, when in enumerate(GATHER_TIMES[2])]
        ticks += [(GATHER_TIMES[3][0], wide_down.begin)]
        ticks += [(when, lambda k=k: wide_down.relay(k + 1)) for k, when in enumerate(GATHER_TIMES[3][1:])]
        middle, feed, final = forward_stages(r, who, first.take, second, spread)

        def project(t):
            first.give(t, dot_nt(r.mixed[who.chunk(t), :], r.out_proj[...]))

        def middle_out(t):
            middle(t)
            r.flush.unit_one.copy(who.half(t), t).start()

        def feed_out(t):
            feed(t)
            for flush in (r.flush.hidden, r.flush.slope, r.flush.spread_full):
                flush.copy(who.chunk(t), t).start()

        def close(t):
            _, _, result = final(t)
            r.flush.unit_two.copy(who.half(t), t).start()
            last.give(t, result)

        def next_project(t):
            value = (dot(last.take(t), r.next_proj[...]) + next_bias).astype(BF)
            r.query[who.chunk(t), :] = value[:, :width]
            r.pair[who.chunk(t), :] = value[:, width:]
            halo.send(t)
            r.flush.last_full.copy(who.chunk(t), t).start()

        run_stages(
            chunks,
            [
                (5, second.add),
                (1, first.add),
                (7, close),
                (3, middle_out),
                (8, next_project),
                (4, feed_out),
                (0, project),
            ],
            ticks,
        )
        finish_all(chunks, (first, second, spread, last))
        halo.arrive()
        share(0, who.sibling[1]).wait_recv()
        share(2, who.diagonal[1]).wait_recv()
        for kind, slot in enumerate((column.here, column.here, who.across[1])):
            share(kind, slot).wait_send()
        wide_up.arrive()
        halo.finish()
        for engine in (wide_attn, wide_up, wide_down):
            engine.finish()

        def written(t, carry):
            for flush in (r.flush.hidden, r.flush.slope, r.flush.spread_full, r.flush.last_full):
                flush.copy(who.chunk(t), t).wait()
            for flush in (r.flush.unit_one, r.flush.unit_two):
                flush.copy(who.half(t), t).wait()
            return carry

        lax.fori_loop(0, chunks, written, 0)

    outputs = forward_small(rows)
    outputs.update(
        query=((rows, width), BF),
        pair=((rows, 2 * width), BF),
        full_attn=((count, block, 4 * width), BF),
        next_out=((4, width, D), BF),
        full_up=((count, block, units), BF),
        full_down=((count, block, units), BF),
        left=((2 * WIN, 2 * width), BF),
        right=((2 * WIN, 2 * width), BF),
    )
    flushed = forward_refs(rows, width, units)
    flushed.update(spread_full=((rows, D), BF), last_full=((rows, D), BF))
    scratch = dict(
        normed=pltpu.VMEM((rows // 2, D), F32),
        out_proj=pltpu.VMEM((D, width), BF),
        next_proj=pltpu.VMEM((D, 3 * width), BF),
        share_sent=pltpu.SemaphoreType.DMA((3,)),
        share_came=pltpu.SemaphoreType.DMA((3,)),
    )
    scratch.update(prefixed("first", exchange_scratch(rows)))
    scratch.update(prefixed("second", exchange_scratch(rows)))
    for key in ("spread", "last"):
        for part in ("sent", "came"):
            scratch[key + "_" + part] = pltpu.SemaphoreType.DMA((chunks,))
    for key in ("ga", "gu", "gd"):
        scratch.update(prefixed(key, gather_sems(lines)))
    scratch.update(prefixed("halo", halo_scratch(2 * WIN // CHUNK)))
    return run_kernel(
        body,
        "middle_forward",
        dict(
            mixed=mixed,
            attn=attn,
            shared=shared,
            split=split_biases,
            next_attn=attn_weights,
            next_ffn=ffn_weights,
        ),
        outputs,
        scratch,
        collective=1,
        flops=2 * rows * D * (4 * width + 2 * units),
        late=dict(residual=residual, ffn_up=ffn_up, ffn_down=ffn_down),
        flushed=flushed,
        pieces=chunks,
    )


def turning(mixed, first_mixed, out_proj, attn, ffn_up, ffn_down, residual, shared, split_biases, cotangent, turn):
    rows, width = mixed.shape
    units = ffn_up.shape[1]
    chunks = rows // WIDE_CHUNK

    def body(r):
        who = Partners(size=WIDE_CHUNK)
        r.base, r.grad_one = 6, None
        second, third = Exchange(who, pick(r, "second")), Exchange(who, pick(r, "third"))
        heads = HeadExchange(who, r.mixed, r.gathered, r.heads_sent, r.heads_came)
        spread = Gather(who, pick(r, "spread"))
        ends = Gather(who, pick(r, "ends"))
        mids = Gather(who, SimpleNamespace(full=r.grad_low, sent=r.mids_sent, came=r.mids_came))
        out = Gather(who, SimpleNamespace(full=r.output, sent=r.out_sent, came=r.out_came))
        who.meet()
        for t in range(chunks // 2, chunks):
            heads.give(t)
        r.gathered[:, : rows // 4, :] = r.first_mixed[...]
        r.out_proj[...] = r.attn[:, 3 * width :]
        r.hidden_bias = r.split[1][:, 2 * width :]
        clear(r.vectors, r.units, r.sum_up, r.sum_down, r.sum_out)

        def projected(t):
            @pl.when(t >= chunks // 2)
            def _():
                heads.take(t)

            mine = jnp.concatenate([r.gathered[k, who.half(t), :] for k in range(4)], axis=1)
            return dot(mine, r.full_out[...].reshape(D, D))

        middle, feed, final = forward_stages(r, who, projected, second, spread)
        enter, feed_back, leave, project_back = backward_stages(r, who, ends, third, mids)

        ticks = [(0, r.late.residual.wait), (1, r.late.ffn_up.wait), (1, r.late.ffn_down.wait)]
        ticks += [(4, r.late.cotangent.wait), (4, r.late.turn.wait)]

        def close(t):
            unit, inverse, result = final(t)
            grad = dot(r.cotangent[who.own(t), :], r.turn[...])
            enter(t, grad, unit, inverse)
            out.give(t, result)

        run_stages(
            chunks,
            [
                (6, third.add),
                (2, second.add),
                (8, leave),
                (4, close),
                (0, middle),
                (9, project_back),
                (5, feed_back),
                (1, feed),
            ],
            ticks,
        )

        def arrive(t, carry):
            out.wait(t)
            return carry

        lax.fori_loop(0, chunks, arrive, 0)
        finish_all(chunks, (second, third, spread, ends, mids, out))
        for t in range(chunks // 2, chunks):
            heads.finish(t)
        r.up[...] = r.sum_up[...].astype(BF)
        r.down[...] = r.sum_down[...].astype(BF)
        r.proj[...] = r.sum_out[...].astype(BF)

    outputs = dict(
        output=((rows, D), BF),
        up=((D, units), BF),
        down=((D, units), BF),
        proj=((D, width), BF),
        grad_low=((rows, D), BF),
        grad_mixed=((rows, width), BF),
        vectors=((8, D), F32),
        units=((8, units), F32),
    )
    scratch = dict(
        normed=pltpu.VMEM((rows // 2, D), F32),
        kept=pltpu.VMEM((rows // 2, D), F32),
        grad_pre=pltpu.VMEM((2 * WIDE_CHUNK, units), BF),
        out_proj=pltpu.VMEM((D, width), BF),
        gathered=pltpu.VMEM((4, rows // 2, width), BF),
        heads_sent=pltpu.SemaphoreType.DMA((3, chunks)),
        heads_came=pltpu.SemaphoreType.DMA((3, chunks)),
        sum_up=pltpu.VMEM((D, units), F32),
        sum_down=pltpu.VMEM((D, units), F32),
        sum_out=pltpu.VMEM((D, width), F32),
        mids_sent=pltpu.SemaphoreType.DMA((chunks,)),
        mids_came=pltpu.SemaphoreType.DMA((chunks,)),
        out_sent=pltpu.SemaphoreType.DMA((chunks,)),
        out_came=pltpu.SemaphoreType.DMA((chunks,)),
    )
    for key, (shape, dtype) in {**forward_refs(rows, width, units), **forward_small(rows)}.items():
        scratch[key] = pltpu.VMEM(shape, dtype)
    for key in ("second", "third"):
        scratch.update(prefixed(key, exchange_scratch(rows)))
    for key in ("spread", "ends"):
        scratch.update(prefixed(key, gather_scratch(rows)))
    return run_kernel(
        body,
        "turning",
        dict(
            mixed=mixed,
            first_mixed=first_mixed,
            full_out=out_proj,
            attn=attn,
            shared=shared,
            split=split_biases,
        ),
        outputs,
        scratch,
        collective=2,
        flops=2 * rows * D * (3 * width + 6 * units),
        late=dict(residual=residual, ffn_up=ffn_up, ffn_down=ffn_down, cotangent=cotangent, turn=turn),
    )


def projection_back_stage(r, who, column, exchange):
    rows, width = r.grad_query.shape
    rim = r.out_right.shape[0]
    first, last = column.index == 0, column.index == column.count - 1
    after = (lax.rem(column.index + 1, column.count), column.here)
    copy = copy_to(r.out_right, r.from_left, r.halo_sent.at[0], r.halo_came.at[0], after)

    def begin():
        r.grad_pair[...] = r.grad_own[...]

        @pl.when(jnp.logical_not(last))
        def _():
            copy.start()

    def absorb():
        @pl.when(jnp.logical_not(first))
        def _():
            copy.wait_recv()
            where = pl.ds(0, rim)
            total = r.grad_pair[where, :].astype(F32) + r.from_left[...].astype(F32)
            r.grad_pair[where, :] = total.astype(BF)

    def end():
        @pl.when(jnp.logical_not(last))
        def _():
            copy.wait_send()

    def stage(k):
        both = who.two_chunks(2 * k + 1)
        parts = jnp.concatenate([r.grad_query[both, :], r.grad_pair[both, :]], axis=1)
        exchange.r.part[both, :] = dot_nt(parts, r.next_attn[:, : 3 * width]).astype(BF)
        for t in (2 * k, 2 * k + 1):
            exchange.core_copy(t).start()
        r.sum_three[...] += dot_tn(r.low[both, :], parts)
        r.biases[0:1, :] += column_sum(parts.astype(F32))

    half = rows // CHUNK // 2
    steps = [(0 if k < half // 2 else half, k) for k in range(half)]
    ticks = [(half, absorb)] + [(first_time + k % (half // 2), lambda k=k: stage(k)) for first_time, k in steps]
    return begin, end, ticks


def projection_back_scratch(rows, rim, width):
    return dict(
        grad_pair=pltpu.VMEM((rows, 2 * width), BF),
        from_left=pltpu.VMEM((rim, 2 * width), BF),
        halo_sent=pltpu.SemaphoreType.DMA((1,)),
        halo_came=pltpu.SemaphoreType.DMA((1,)),
        sum_three=pltpu.VMEM((D, 3 * width), F32),
    )


def scatter_three(column, r, totals):
    return (
        ScatterPairs(column, SimpleNamespace(grads=r.above_up, **vars(pick(r, "ru"))), totals[0]),
        ScatterBlocks(column, SimpleNamespace(grads=r.above_down, **vars(pick(r, "rd"))), totals[1]),
        ScatterBlocks(column, SimpleNamespace(grads=r.packed, **vars(pick(r, "ra"))), totals[2]),
    )


def scatter_three_scratch(count, width, units):
    lines, block = count // 2, D // count
    scratch = dict(packed=pltpu.VMEM((count, block, 4 * width), BF))
    scratch.update(prefixed("ru", scatter_pairs_scratch(lines, block, units)))
    scratch.update(prefixed("rd", scatter_scratch(lines, block, units)))
    scratch.update(prefixed("ra", scatter_scratch(lines, block, 4 * width, held=False)))
    return scratch


def pack_attention(r):
    both = jnp.concatenate([r.sum_three[...].astype(BF), r.above_proj[...]], axis=1)
    r.packed[...] = both.reshape(r.packed.shape)


def middle_backward(back, next_attn, grad_above, low, saved, mixed, attn, ffn_up, ffn_down, shared, above, count):
    rows, width = mixed.shape
    units = ffn_up.shape[1]
    chunks = rows // CHUNK
    block = D // count
    rim = back.out_right.shape[0]

    def body(r):
        who = Partners(chunks, chunks // 2)
        r.base = 0
        zeroth, third = Exchange(who, pick(r, "zeroth")), Exchange(who, pick(r, "third"))
        ends, mids = Gather(who, pick(r, "ends")), Gather(who, pick(r, "mids"))
        column = Column(count)
        who.meet(column)
        up, down, three = scatter_three(column, r, (r.up_total, r.down_total, r.attn_total))
        begin, end, back_ticks = projection_back_stage(r, who, column, zeroth)
        begin()
        up.start()
        down.start()

        def start_three():
            pack_attention(r)
            three.start()

        ticks = [tick for engine, times in zip((up, down, three), BACK_TIMES) for tick in engine.ticks(times)]
        ticks += [(chunks // 2 + 2, start_three)]
        ticks += [(3, r.late.unit_two.wait), (3, r.late.grad_above.wait), (4, r.late.ffn_up.wait)]
        ticks += [(4, r.late.ffn_down.wait), (4, r.late.slope.wait), (4, r.late.hidden.wait)]
        ticks += [(4, r.late.spread_full.wait), (7, r.late.unit_one.wait), (8, r.late.mixed.wait)]
        ticks = back_ticks + ticks
        r.out_proj[...] = r.attn[:, 3 * width :]
        clear(r.vectors, r.units, r.biases, r.sum_up, r.sum_down, r.sum_out, r.sum_three)
        enter, feed_back, leave, project_back = backward_stages(r, who, ends, third, mids)

        def start(t):
            half = who.half(t)
            enter(t, r.grad_above[who.own(t), :].astype(F32) + zeroth.take(t), r.unit_two[half, :], r.inverse_two[half, 0:1])

        run_stages(
            chunks,
            [
                (5, third.add),
                (1, zeroth.add),
                (7, leave),
                (3, start),
                (8, project_back),
                (4, feed_back),
            ],
            ticks,
        )
        finish_all(chunks, (zeroth, third, ends, mids))
        end()
        r.up[...] = r.sum_up[...].astype(BF)
        r.down[...] = r.sum_down[...].astype(BF)
        r.proj[...] = r.sum_out[...].astype(BF)
        for engine in (up, down, three):
            engine.finish()

    outputs = dict(
        up=((D, units), BF),
        down=((D, units), BF),
        proj=((D, width), BF),
        grad_one=((rows // 2, D), F32),
        grad_mixed=((rows, width), BF),
        vectors=((8, D), F32),
        units=((8, units), F32),
        biases=((8, 3 * width), F32),
        up_total=((block, units), F32),
        down_total=((block, units), F32),
        attn_total=((block, 4 * width), F32),
    )
    scratch = dict(
        kept=pltpu.VMEM((rows // 2, D), F32),
        grad_pre=pltpu.VMEM((2 * CHUNK, units), BF),
        out_proj=pltpu.VMEM((D, width), BF),
        sum_up=pltpu.VMEM((D, units), F32),
        sum_down=pltpu.VMEM((D, units), F32),
        sum_out=pltpu.VMEM((D, width), F32),
    )
    scratch.update(projection_back_scratch(rows, rim, width))
    scratch.update(scatter_three_scratch(count, width, units))
    for key in ("zeroth", "third"):
        scratch.update(prefixed(key, exchange_scratch(rows)))
    for key in ("ends", "mids"):
        scratch.update(prefixed(key, gather_scratch(rows)))
    return run_kernel(
        body,
        "middle_backward",
        dict(
            grad_query=back.out_query,
            grad_own=back.out_own,
            out_right=back.out_right,
            next_attn=next_attn,
            low=low,
            inverse_one=saved.inverse_one,
            inverse_two=saved.inverse_two,
            attn=attn,
            shared=shared,
            above_up=above.up.reshape(count, block, units),
            above_down=above.down.reshape(count, block, units),
            above_proj=above.proj,
        ),
        outputs,
        scratch,
        collective=3,
        flops=2 * rows * D * (8 * width + 4 * units),
        in_hbm=("above_up", "above_down"),
        late=dict(
            unit_two=saved.unit_two,
            grad_above=grad_above,
            ffn_down=ffn_down,
            slope=saved.slope,
            ffn_up=ffn_up,
            hidden=saved.hidden,
            spread_full=saved.spread_full,
            unit_one=saved.unit_one,
            mixed=mixed,
        ),
    )


class SmallSum:
    def __init__(self, who, column, refs):
        self.who, self.c, self.r = who, column, refs

    def copy(self, slot, source, device):
        r = self.r
        return copy_to(r.kept.at[source], r.came.at[slot], r.sent_sem.at[slot], r.came_sem.at[slot], device)

    def core_copy(self):
        return self.copy(0, 0, self.who.sibling)

    def pair_copy(self):
        return self.copy(1, 1, self.c.at(self.c.outer, 1 - self.c.inner))

    def line_copy(self, target, slot):
        c, r = self.c, self.r
        return copy_to(
            r.kept.at[2], r.came.at[2 + slot], r.sent_sem.at[2 + target], r.came_sem.at[2 + slot], c.at(target, c.inner)
        )

    def second(self, both):
        r = self.r
        self.core_copy().wait_recv()
        row = lax.broadcasted_iota(jnp.int32, r.kept.shape[1:], 0)
        r.kept[1] = r.kept[0] + jnp.where(row < both, r.came[0], 0.0)
        self.pair_copy().start()

    def third(self):
        r, c = self.r, self.c
        self.pair_copy().wait_recv()
        r.kept[2] = r.kept[1] + r.came[1]
        for k in range(1, c.lines):
            self.line_copy(c.turn(k), c.outer).start()
        r.came[2 + c.outer] = r.kept[2]

    def result(self):
        r, c = self.r, self.c
        for k in range(1, c.lines):
            source = c.turn(k)
            self.line_copy(source, source).wait_recv()
        return sum(r.came[2 + k] for k in range(c.lines))

    def finish(self):
        c = self.c
        self.core_copy().wait_send()
        self.pair_copy().wait_send()
        for k in range(1, c.lines):
            self.line_copy(c.turn(k), c.outer).wait_send()


def small_scratch(lines, shape):
    return dict(
        kept=pltpu.VMEM((3,) + shape, F32),
        came=pltpu.VMEM((2 + lines,) + shape, F32),
        sent_sem=pltpu.SemaphoreType.DMA((2 + lines,)),
        came_sem=pltpu.SemaphoreType.DMA((2 + lines,)),
    )


class NormSum:
    def __init__(self, who, column, refs):
        self.who, self.c, self.r = who, column, refs

    def mp_copy(self, device, target, slot):
        r = self.r
        return copy_to(r.mp_came.at[slot], r.mp_came.at[slot], r.mp_sent.at[target], r.mp_sem.at[slot], device)

    def seq_copy(self, device, target, slot):
        r = self.r
        return copy_to(r.seq_came.at[slot], r.seq_came.at[slot], r.seq_sent.at[target], r.seq_sem.at[slot], device)

    def run(self, value):
        who, c, r = self.who, self.c, self.r
        here = c.here
        r.mp_came[here] = jnp.full((8, 128), 1.0, F32) * value
        for k in range(1, 4):
            target = lax.rem(here + k, 4)
            self.mp_copy((c.index, target), target, here).start()
        for k in range(1, 4):
            source = lax.rem(here + k, 4)
            self.mp_copy((c.index, source), source, source).wait_recv()
        r.seq_came[c.index] = sum(r.mp_came[k] for k in range(4))
        for k in range(1, c.count):
            target = lax.rem(c.index + k, c.count)
            self.seq_copy((target, here), target, c.index).start()
        for k in range(1, c.count):
            source = lax.rem(c.index + k, c.count)
            self.seq_copy((source, here), source, source).wait_recv()
        total = sum(r.seq_came[k] for k in range(c.count))
        for k in range(1, 4):
            target = lax.rem(here + k, 4)
            self.mp_copy((c.index, target), target, here).wait_send()
        for k in range(1, c.count):
            target = lax.rem(c.index + k, c.count)
            self.seq_copy((target, here), target, c.index).wait_send()
        return total


def norm_scratch(count):
    return dict(
        mp_came=pltpu.VMEM((4, 8, 128), F32),
        mp_sent=pltpu.SemaphoreType.DMA((4,)),
        mp_sem=pltpu.SemaphoreType.DMA((4,)),
        seq_came=pltpu.VMEM((count, 8, 128), F32),
        seq_sent=pltpu.SemaphoreType.DMA((count,)),
        seq_sem=pltpu.SemaphoreType.DMA((count,)),
    )


def squares(ref):
    value = ref[...]
    return jnp.sum(value * value)


def ending(back, next_attn, grad_above, low, above, top, count):
    rows, width = back.out_query.shape
    chunks = rows // CHUNK
    lines, block = count // 2, D // count
    units = above.units.shape[1]
    rim = back.out_right.shape[0]

    def body(r):
        who = Partners(chunks, chunks // 2)
        zeroth = Exchange(who, pick(r, "zeroth"))
        out = Gather(who, SimpleNamespace(full=r.output, sent=r.out_sent, came=r.out_came))
        column = Column(count)
        who.meet(column)
        up, down, three = scatter_three(column, r, (r.ffn_grads.at[0], r.ffn_grads.at[1], r.attn_grads.at[0]))
        small = SmallSum(who, column, pick(r, "small"))
        begin, end, back_ticks = projection_back_stage(r, who, column, zeroth)
        begin()
        up.start()
        down.start()

        def start_three():
            pack_attention(r)
            three.start()
            r.small_kept[0, 0:6, :] = r.vectors_low[0:6, :]
            r.small_kept[0, 6:12, :] = r.vectors_top[0:6, :]
            r.small_kept[0, 12:13, :] = r.units_low[0:1, :]
            r.small_kept[0, 13:14, :] = r.units_top[0:1, :]
            pieces = []
            for ref in (r.biases, r.biases_top):
                pieces += [ref[0:1, :width], ref[0:1, 2 * width :]]
            r.small_kept[0, 14:15, :] = jnp.concatenate(pieces, axis=1)
            r.small_kept[0, 15:16, :] = jnp.zeros((1, D), F32)
            small.core_copy().start()

        ticks = [tick for engine, times in zip((up, down, three), END_TIMES) for tick in engine.ticks(times)]
        ticks += [(chunks // 2 + 2, start_three), (3, r.late.grad_above.wait)]
        ticks += [(chunks // 2 + 4, lambda: small.second(12)), (chunks // 2 + 6, small.third)]
        ticks = back_ticks + ticks
        clear(r.biases, r.sum_three)

        def close(t):
            out.give(t, r.grad_above[who.half(t), :] + zeroth.take(t))

        run_stages(chunks, [(1, zeroth.add), (3, close)], ticks)
        vectors = small.result()
        r.vectors[...] = vectors
        r.ffn_grads[2] = r.up_top[...]
        r.ffn_grads[3] = r.down_top[...]
        r.attn_grads[1] = r.attn_top[...]
        row = lax.broadcasted_iota(jnp.int32, (16, D), 0)
        squared = vectors * vectors
        split = jnp.sum(jnp.where(row >= 12, squared, 0.0))
        shared = jnp.sum(jnp.where(row < 12, squared, 0.0))
        first_seq = column.index == 0
        first_both = jnp.logical_and(first_seq, column.here == 0)
        value = squares(r.ffn_grads) + squares(r.attn_grads)
        value = value + jnp.where(first_seq, split, 0.0) + jnp.where(first_both, shared, 0.0)
        total = NormSum(who, column, pick(r, "norm")).run(value)
        r.norm[...] = jnp.sqrt(total)

        def arrive(t, carry):
            out.wait(t)
            return carry

        lax.fori_loop(0, chunks, arrive, 0)
        finish_all(chunks, (zeroth, out))
        end()
        for engine in (up, down, three, small):
            engine.finish()

    outputs = dict(
        output=((rows, D), BF),
        ffn_grads=((4, block, units), F32),
        attn_grads=((2, block, 4 * width), F32),
        vectors=((16, D), F32),
        norm=((8, 128), F32),
    )
    scratch = dict(
        biases=pltpu.VMEM((8, 3 * width), F32),
        out_sent=pltpu.SemaphoreType.DMA((chunks,)),
        out_came=pltpu.SemaphoreType.DMA((chunks,)),
    )
    scratch.update(projection_back_scratch(rows, rim, width))
    scratch.update(scatter_three_scratch(count, width, units))
    scratch.update(prefixed("zeroth", exchange_scratch(rows)))
    scratch.update(prefixed("small", small_scratch(lines, (16, D))))
    scratch.update(prefixed("norm", norm_scratch(count)))
    return run_kernel(
        body,
        "ending",
        dict(
            grad_query=back.out_query,
            grad_own=back.out_own,
            out_right=back.out_right,
            next_attn=next_attn,
            low=low,
            above_up=above.up.reshape(count, block, units),
            above_down=above.down.reshape(count, block, units),
            above_proj=above.proj,
            up_top=above.up_total,
            down_top=above.down_total,
            attn_top=above.attn_total,
            vectors_low=above.vectors,
            vectors_top=top.vectors,
            units_low=above.units,
            units_top=top.units,
            biases_top=above.biases,
        ),
        outputs,
        scratch,
        collective=4,
        flops=2 * rows * D * 6 * width,
        in_hbm=("above_up", "above_down"),
        late=dict(grad_above=grad_above),
    )


def moments(grad, first, second):
    first_new = BETA_FIRST * first + (1.0 - BETA_FIRST) * grad
    second_new = BETA_SECOND * second + (1.0 - BETA_SECOND) * grad * grad
    size = jnp.sqrt(second_new / (1.0 - BETA_SECOND**STEP)) + ADAM_EPSILON
    return first_new, second_new, first_new / (1.0 - BETA_FIRST**STEP) / size


def update(result, end, turn, attn, ffn, split, shared):
    block, units = ffn[0].shape[2:]
    width = attn[0].shape[3]
    rates = [0.5 * D ** (-0.5)] * 3 + [0.5 * (WIN / D) ** 0.5]
    names = ("weights", "first", "second", "average", "basis")

    def matrix(grad, weight, first, second, average, basis, rate):
        basis = basis.astype(BF)
        turned = dot(grad.astype(BF), basis)
        first_new, second_new, direction = moments(turned, first, second)
        back = dot_nt(direction.astype(BF), basis)
        weight_new = weight - rate * (back + DECAY_RATE * weight)
        return weight_new, first_new, second_new, AVERAGE_RATE * average + (1.0 - AVERAGE_RATE) * weight_new

    def body(r):
        step = pl.program_id(0)
        factor = CLIP_LEVEL / jnp.maximum(r.norm[0:1, 0:1], CLIP_LEVEL)
        r.result_real[...] = dot_nt(r.result[...], r.turn[...])
        r.grad_real[...] = dot_nt(r.grad[...], r.turn[...])
        rate = jnp.where(step % 2 == 0, 0.5 * D ** (-0.5), 0.5 * FF ** (-0.5))
        results = matrix(
            factor * r.ffn_grads[...],
            r.ffn_weights[...],
            r.ffn_first[...],
            r.ffn_second[...],
            r.ffn_average[...],
            r.ffn_basis[...],
            rate,
        )
        for key, value in zip(names, results):
            getattr(r, "ffn_" + key + "_new")[...] = value

        for at in range(4):

            @pl.when(step == at)
            def _(at=at):
                layer = at // 2
                for which in (2 * (at % 2), 2 * (at % 2) + 1):
                    grad = factor * r.attn_grads[layer, :, which * width : (which + 1) * width]
                    weight, first, second, average = matrix(
                        grad,
                        r.attn_weights[layer, which],
                        r.attn_first[layer, which],
                        r.attn_second[layer, which],
                        r.attn_average[layer, which],
                        r.attn_basis[layer, which, 0, 0],
                        rates[which],
                    )
                    r.attn_weights_new[layer, which] = weight
                    r.attn_first_new[layer, which] = first
                    r.attn_average_new[layer, which] = average
                    if which < 3:
                        r.attn_second_new[layer, which] = second
                    else:
                        r.projection_second[layer] = second

        @pl.when(step == 0)
        def _():
            r.norm_out[0, 0] = jnp.max(r.norm[0:1, :])
            real = exact(r.vectors[...], lambda part: dot_nt(part, r.turn[...]))
            for layer in range(2):
                tail = r.vectors[14:15, layer * 2 * width : (layer + 1) * 2 * width]
                split_grad = jnp.concatenate([tail, r.vectors[12 + layer : 13 + layer, :]], axis=1)
                grad = factor * split_grad
                first_new, second_new, direction = moments(grad, r.split_first[layer], r.split_second[layer])
                r.split_old_new[layer] = r.split_old[layer] - VECTOR_RATE * direction
                r.split_first_new[layer] = first_new
                r.split_second_new[layer] = second_new
            for k in range(6):
                grad = factor * jnp.concatenate([real[k : k + 1], real[6 + k : 7 + k]], axis=0)
                first_new, second_new, direction = moments(grad, r.shared_first[k], r.shared_second[k])
                r.shared_old_new[k] = r.shared_old[k] - VECTOR_RATE * direction
                r.shared_first_new[k] = first_new
                r.shared_second_new[k] = second_new

    inputs = dict(
        ffn_grads=end.ffn_grads, attn_grads=end.attn_grads, vectors=end.vectors, norm=end.norm, turn=turn
    )
    rows = result.shape[0]
    inputs.update(result=result, grad=end.output)
    outputs = dict(result_real=((rows, D), F32), grad_real=((rows, D), F32))
    row_spec = pl.BlockSpec((rows // 4, D), lambda i: (i, 0))
    specs = dict(result=row_spec, grad=row_spec, result_real=row_spec, grad_real=row_spec)
    specs["ffn_grads"] = pl.BlockSpec((None, block, units), lambda i: (i, 0, 0))
    matrix_spec = pl.BlockSpec((None, None, block, units), lambda i: (i // 2, i % 2, 0, 0))
    for key, array in zip(names, ffn):
        inputs["ffn_" + key] = array
        specs["ffn_" + key] = matrix_spec
    specs["ffn_basis"] = pl.BlockSpec((None, None, None, None, units, units), lambda i: (i // 2, i % 2, 0, 0, 0, 0))
    for key, array in zip(names, attn):
        inputs["attn_" + key] = array
    for prefix, group in (("split", split), ("shared", shared)):
        for key, array in zip(("old", "first", "second"), group):
            inputs[prefix + "_" + key] = array
    for key in ("weights", "first", "second", "average"):
        outputs["ffn_" + key + "_new"] = (ffn[0].shape, F32)
        specs["ffn_" + key + "_new"] = matrix_spec
        outputs["attn_" + key + "_new"] = (attn[0].shape, F32)
    outputs["attn_second_new"] = ((2, 3, block, width), F32)
    outputs["projection_second"] = ((2, block, width), F32)
    for prefix, group in (("split", split), ("shared", shared)):
        for key in ("old", "first", "second"):
            outputs[prefix + "_" + key + "_new"] = (group[0].shape, F32)
    outputs["norm_out"] = ((1, 1), F32)
    return run_kernel(
        body,
        "update",
        inputs,
        outputs,
        {},
        flops=4 * block * units * units * 4,
        grid=(4,),
        specs=specs,
        in_smem=("norm_out",),
    )


def direct(
    activations,
    cotangent,
    segments,
    dilated_heads,
    owners,
    attn_weights,
    attn_first,
    attn_second,
    attn_average,
    attn_basis,
    ffn_weights,
    ffn_first,
    ffn_second,
    ffn_average,
    ffn_basis,
    split_biases,
    split_first,
    split_second,
    shared_vectors,
    shared_first,
    shared_second,
):
    count = lax.axis_size(SEQ)
    near = opening(
        activations, segments, owners, attn_weights, ffn_weights, split_biases, shared_vectors, count
    )
    near.arranged = near.out
    attn_zero, up_zero, down_zero = (
        full.reshape(D, -1) for full in (near.full_attn, near.full_up, near.full_down)
    )
    mid = middle_forward(
        near.out,
        attn_zero,
        up_zero,
        down_zero,
        near.low,
        near.shared,
        split_biases,
        attn_weights,
        ffn_weights,
        count,
    )
    attn_one, up_one, down_one = (full.reshape(D, -1) for full in (mid.full_attn, mid.full_up, mid.full_down))
    far = attend(mid.query, mid.pair, mid.left, mid.right, near.seg_query, near.seg_keys, dilated_heads)
    top = turning(
        far.out, far.first, mid.next_out, attn_one, up_one, down_one, mid.last_full, near.shared, split_biases, cotangent, near.turn
    )
    far_back = attend_back(far, top.grad_mixed, dilated_heads, 2 * WIN, True, count, 6)
    low = middle_backward(
        far_back,
        attn_one,
        top.grad_low,
        mid.last_full,
        mid,
        near.out,
        attn_zero,
        up_zero,
        down_zero,
        near.shared,
        top,
        count,
    )
    near_back = attend_back(near, low.grad_mixed, dilated_heads, WIN, False, count, 7)
    end = ending(near_back, attn_zero, low.grad_one, near.low, low, top, count)
    new = update(
        top.output,
        end,
        near.turn,
        (attn_weights, attn_first, attn_second, attn_average, attn_basis),
        (ffn_weights, ffn_first, ffn_second, ffn_average, ffn_basis),
        (split_biases, split_first, split_second),
        tuple(array.transpose(1, 0, 2) for array in (shared_vectors, shared_first, shared_second)),
    )
    return (
        new.result_real,
        new.grad_real,
        new.attn_weights_new,
        new.attn_first_new,
        new.attn_second_new,
        new.projection_second,
        new.attn_average_new,
        new.ffn_weights_new,
        new.ffn_first_new,
        new.ffn_second_new,
        new.ffn_average_new,
        new.split_old_new,
        new.split_first_new,
        new.split_second_new,
        new.shared_old_new.transpose(1, 0, 2),
        new.shared_first_new.transpose(1, 0, 2),
        new.shared_second_new.transpose(1, 0, 2),
        new.norm_out.reshape(()),
    )


def with_halo(cells, sides, width):
    for axis, dim in sides:
        count = lax.axis_size(axis)
        ends = count - 1
        head = lax.slice_in_dim(cells, 0, width, axis=dim)
        tail = lax.slice_in_dim(cells, cells.shape[dim] - width, cells.shape[dim], axis=dim)
        cells = jnp.concatenate(
            [
                lax.ppermute(tail, axis, [(i, (i + 1) % count) for i in range(ends)]),
                cells,
                lax.ppermute(head, axis, [((i + 1) % count, i) for i in range(ends)]),
            ],
            axis=dim,
        )
    return cells


def from_behind(block, axis, distance):
    devices = range(lax.axis_size(axis))
    route = [(i - distance, i) for i in devices if i - distance in devices]
    return lax.ppermute(block, axis, route)


def normalize_layer(values, gain, shift):
    center = values - jnp.mean(values, axis=-1, keepdims=True)
    spread = jnp.mean(center * center, axis=-1, keepdims=True)
    return center * lax.rsqrt(spread + NORM_EPSILON) * gain + shift


def head_masks(offsets, dilated):
    near = jnp.abs(offsets) <= WIN
    far = jnp.logical_and(jnp.abs(offsets) <= 2 * WIN, offsets % 2 == 0)
    return jnp.where(dilated[:, None, None], far[None, :, :], near[None, :, :])


def join_heads(term):
    return lax.psum(term.astype(jnp.bfloat16), MP).astype(jnp.float32)


def join_grads(term):
    return lax.psum(term, MP)


def fetch_rims(pair, rim_width):
    return with_halo(pair, ((SEQ, 0),), rim_width)


def masked_scores(query_block, key_block, seg_query, seg_keys, dilated, rim_width):
    block_rows = query_block.shape[0]
    key_rows = key_block.shape[0]
    offsets = (
        jnp.arange(block_rows, dtype=jnp.int32)[:, None]
        - jnp.arange(key_rows, dtype=jnp.int32)[None, :]
        + rim_width
    )
    allowed = jnp.logical_and(
        head_masks(offsets, dilated), (seg_query[:, None] == seg_keys[None, :])[None, :, :]
    )
    raw = jnp.einsum(
        "qhd,khd->hqk", query_block, key_block, preferred_element_type=jnp.float32
    ) * DH ** (-0.5)
    return jnp.where(allowed, raw, MASK_FILL)


def plain_attend(query, key_pad, value_pad, seg_own, seg_near, dilated, rim_width):
    row_count = query.shape[0]
    block_rows = min(512, row_count)
    key_rows = block_rows + 2 * rim_width

    def one_block(first_row):
        query_block = lax.dynamic_slice_in_dim(query, first_row, block_rows, 0)
        key_block = lax.dynamic_slice_in_dim(key_pad, first_row, key_rows, 0)
        value_block = lax.dynamic_slice_in_dim(value_pad, first_row, key_rows, 0)
        scores = masked_scores(
            query_block,
            key_block,
            lax.dynamic_slice_in_dim(seg_own, first_row, block_rows, 0),
            lax.dynamic_slice_in_dim(seg_near, first_row, key_rows, 0),
            dilated,
            rim_width,
        )
        row_max = jnp.max(scores, axis=2, keepdims=True)
        exponent = jnp.exp(scores - row_max)
        row_total = jnp.sum(exponent, axis=2, keepdims=True)
        softmax = (exponent / row_total).astype(jnp.bfloat16)
        mixed_block = jnp.einsum(
            "hqk,khd->qhd", softmax, value_block, preferred_element_type=jnp.float32
        )
        return (mixed_block, (row_max + jnp.log(row_total))[:, :, 0])

    starts = jnp.arange(row_count // block_rows, dtype=jnp.int32) * block_rows
    mixed_heads, log_totals = lax.map(one_block, starts)
    return (mixed_heads.reshape(row_count, -1), log_totals)


def plain_attend_back(query, padded, log_totals, grad_mixed, seg_own, seg_near, dilated, rim_width):
    row_count, head_count, _ = query.shape
    head_width = head_count * DH
    block_rows = min(512, row_count)
    key_rows = block_rows + 2 * rim_width
    key_pad = padded[:, :head_width].reshape(-1, head_count, DH)
    value_pad = padded[:, head_width:].reshape(-1, head_count, DH)
    grad_heads = grad_mixed.reshape(row_count, head_count, DH)
    score_scale = DH ** (-0.5)

    def one_step(carry, inputs):
        first_row, totals_block = inputs
        query_block = lax.dynamic_slice_in_dim(query, first_row, block_rows, 0)
        key_block = lax.dynamic_slice_in_dim(key_pad, first_row, key_rows, 0)
        value_block = lax.dynamic_slice_in_dim(value_pad, first_row, key_rows, 0)
        grad_block = lax.dynamic_slice_in_dim(grad_heads, first_row, block_rows, 0)
        scores = masked_scores(
            query_block,
            key_block,
            lax.dynamic_slice_in_dim(seg_own, first_row, block_rows, 0),
            lax.dynamic_slice_in_dim(seg_near, first_row, key_rows, 0),
            dilated,
            rim_width,
        )
        softmax = jnp.exp(scores - totals_block[:, :, None])
        grad_value = jnp.einsum(
            "hqk,qhd->khd",
            softmax.astype(jnp.bfloat16),
            grad_block,
            preferred_element_type=jnp.float32,
        )
        grad_soft = jnp.einsum(
            "qhd,khd->hqk", grad_block, value_block, preferred_element_type=jnp.float32
        )
        row_dot = jnp.sum(grad_soft * softmax, axis=2, keepdims=True)
        grad_scores = (softmax * (grad_soft - row_dot)).astype(jnp.bfloat16)
        grad_query = (
            jnp.einsum("hqk,khd->qhd", grad_scores, key_block, preferred_element_type=jnp.float32)
            * score_scale
        )
        grad_key = (
            jnp.einsum("hqk,qhd->khd", grad_scores, query_block, preferred_element_type=jnp.float32)
            * score_scale
        )
        update = jnp.concatenate(
            [grad_key.reshape(key_rows, head_width), grad_value.reshape(key_rows, head_width)],
            axis=1,
        )
        current = lax.dynamic_slice_in_dim(carry, first_row, key_rows, 0)
        carry = lax.dynamic_update_slice_in_dim(carry, current + update, first_row, 0)
        return (carry, grad_query.reshape(block_rows, head_width))

    starts = jnp.arange(row_count // block_rows, dtype=jnp.int32) * block_rows
    initial = jnp.zeros((row_count + 2 * rim_width, 2 * head_width), jnp.float32)
    grad_pad, grad_query = lax.scan(one_step, initial, (starts, log_totals))
    from_above = from_behind(grad_pad[:rim_width], SEQ, -1)
    from_below = from_behind(grad_pad[row_count + rim_width :], SEQ, 1)
    grad_pair = grad_pad[rim_width : row_count + rim_width]
    grad_pair = (
        grad_pair
        + jnp.pad(from_below, ((0, row_count - rim_width), (0, 0)))
        + jnp.pad(from_above, ((row_count - rim_width, 0), (0, 0)))
    )
    return (grad_query.reshape(row_count, head_width), grad_pair)


def layer_forward(inputs, attn, ffn, shared, split, seg_own, seg_pad, dilated, rim_width):
    head_width = attn.shape[2]
    row_count = inputs.shape[0]
    inputs_low = inputs.astype(jnp.bfloat16)
    biases = jnp.stack(
        [
            split[0, :head_width],
            jnp.zeros((head_width,), jnp.float32),
            split[0, head_width : 2 * head_width],
        ]
    )
    projected = (
        jnp.einsum("td,mdc->tmc", inputs_low, attn[:3], preferred_element_type=jnp.float32)
        + biases[None]
    ).astype(jnp.bfloat16)
    query = projected[:, 0].reshape(row_count, -1, DH)
    padded = fetch_rims(jnp.concatenate([projected[:, 1], projected[:, 2]], axis=1), rim_width)
    key_pad = padded[:, :head_width].reshape(-1, head_width // DH, DH)
    value_pad = padded[:, head_width:].reshape(-1, head_width // DH, DH)
    seg_near = lax.slice_in_dim(
        seg_pad, 2 * WIN - rim_width, 2 * WIN + row_count + rim_width, axis=0
    )
    mixed_heads, log_totals = plain_attend(
        query, key_pad, value_pad, seg_own, seg_near, dilated, rim_width
    )
    mixed_heads = mixed_heads.astype(jnp.bfloat16)
    attn_sum = (
        inputs
        + join_heads(
            dot_nt(mixed_heads, attn[3])
        )
        + shared[0]
    )
    normed = normalize_layer(attn_sum, shared[1], shared[2])
    normed_low = normed.astype(jnp.bfloat16)
    pre_gelu = (
        jnp.dot(normed_low, ffn[0], preferred_element_type=jnp.float32) + split[0, 2 * head_width :]
    )
    hidden = jax.nn.gelu(pre_gelu, approximate=False).astype(jnp.bfloat16)
    ffn_sum = (
        normed
        + join_heads(dot_nt(hidden, ffn[1]))
        + shared[3]
    )
    result = normalize_layer(ffn_sum, shared[4], shared[5])
    return (
        result,
        (
            inputs_low,
            query,
            padded,
            log_totals,
            mixed_heads,
            attn_sum,
            normed_low,
            pre_gelu,
            hidden,
            ffn_sum,
        ),
    )


def layer_backward(grad_out, saved, attn, ffn, shared, seg_own, seg_pad, dilated, rim_width):
    (
        inputs_low,
        query,
        padded,
        log_totals,
        mixed_heads,
        attn_sum,
        normed_low,
        pre_gelu,
        hidden,
        ffn_sum,
    ) = saved
    head_width = attn.shape[2]
    row_count = inputs_low.shape[0]
    seg_near = lax.slice_in_dim(
        seg_pad, 2 * WIN - rim_width, 2 * WIN + row_count + rim_width, axis=0
    )
    _, pull_out = jax.vjp(normalize_layer, ffn_sum, shared[4], shared[5])
    grad_ffn_sum, grad_gain_two, grad_shift_two = pull_out(grad_out)
    grad_branch = grad_ffn_sum.astype(jnp.bfloat16)
    grad_down = dot_tn(grad_branch, hidden)
    grad_hidden = jnp.dot(grad_branch, ffn[1], preferred_element_type=jnp.float32)
    _, pull_gelu = jax.vjp(lambda value: jax.nn.gelu(value, approximate=False), pre_gelu)
    grad_pre = pull_gelu(grad_hidden)[0].astype(jnp.bfloat16)
    grad_up = dot_tn(normed_low, grad_pre)
    grad_normed = grad_ffn_sum + join_grads(
        dot_nt(grad_pre, ffn[0])
    )
    _, pull_mid = jax.vjp(normalize_layer, attn_sum, shared[1], shared[2])
    grad_attn_sum, grad_gain_one, grad_shift_one = pull_mid(grad_normed)
    grad_attn_out = grad_attn_sum.astype(jnp.bfloat16)
    grad_out_proj = dot_tn(grad_attn_out, mixed_heads)
    grad_mixed = jnp.dot(grad_attn_out, attn[3], preferred_element_type=jnp.float32).astype(
        jnp.bfloat16
    )
    grad_query, grad_pair = plain_attend_back(
        query, padded, log_totals, grad_mixed, seg_own, seg_near, dilated, rim_width
    )
    grad_proj = jnp.stack(
        [grad_query, grad_pair[:, :head_width], grad_pair[:, head_width:]], axis=1
    ).astype(jnp.bfloat16)
    grad_in_proj = jnp.einsum(
        "td,tmc->mdc", inputs_low, grad_proj, preferred_element_type=jnp.float32
    )
    grad_inputs = grad_attn_sum + join_grads(
        jnp.einsum("tmc,mdc->td", grad_proj, attn[:3], preferred_element_type=jnp.float32)
    )
    proj_sums = jnp.sum(grad_proj.astype(jnp.float32), axis=0)
    split_grad = jnp.concatenate(
        [proj_sums[0], proj_sums[2], jnp.sum(grad_pre.astype(jnp.float32), axis=0)]
    )
    shared_grad = jnp.stack(
        [
            jnp.sum(grad_attn_sum, axis=0),
            grad_gain_one,
            grad_shift_one,
            jnp.sum(grad_ffn_sum, axis=0),
            grad_gain_two,
            grad_shift_two,
        ]
    )
    attn_grad = jnp.concatenate([grad_in_proj, grad_out_proj[None]], axis=0)
    ffn_grad = jnp.stack([grad_up, grad_down])
    return (grad_inputs, attn_grad, ffn_grad, shared_grad, split_grad)


def from_slots(gathered, owners, slot_count):
    layer_count, matrix_count, row_count, col_count = gathered.shape
    blocks = gathered.reshape(
        layer_count, matrix_count, slot_count, row_count // slot_count, col_count
    )
    return jnp.take(blocks, owners, axis=2).reshape(gathered.shape)


def to_slots(grads, inverse, slot_count):
    matrix_count, row_count, col_count = grads.shape
    blocks = grads.reshape(matrix_count, slot_count, row_count // slot_count, col_count)
    return jnp.take(blocks, inverse, axis=1).reshape(grads.shape)


def rotate_update(weight, grad_now, first, second, running_average, basis, rates):
    turn = basis[:, :, 0, 0]
    turned = jnp.einsum("lmre,lmec->lmrc", grad_now, turn, precision=HIGHEST_PRECISION)
    first_new = BETA_FIRST * first + (1.0 - BETA_FIRST) * turned
    second_new = BETA_SECOND * second + (1.0 - BETA_SECOND) * turned * turned
    direction = (
        first_new
        / (1.0 - BETA_FIRST**STEP)
        / (jnp.sqrt(second_new / (1.0 - BETA_SECOND**STEP)) + ADAM_EPSILON)
    )
    back = jnp.einsum("lmrc,lmec->lmre", direction, turn, precision=HIGHEST_PRECISION)
    weight_new = weight - rates[None, :, None, None] * (back + DECAY_RATE * weight)
    average_new = AVERAGE_RATE * running_average + (1.0 - AVERAGE_RATE) * weight_new
    return (weight_new, first_new, second_new, average_new)


def vector_update(current, grad_now, first, second):
    first_new = BETA_FIRST * first + (1.0 - BETA_FIRST) * grad_now
    second_new = BETA_SECOND * second + (1.0 - BETA_SECOND) * grad_now * grad_now
    direction = (
        first_new
        / (1.0 - BETA_FIRST**STEP)
        / (jnp.sqrt(second_new / (1.0 - BETA_SECOND**STEP)) + ADAM_EPSILON)
    )
    return (current - VECTOR_RATE * direction, first_new, second_new)


def with_collectives(
    activations,
    cotangent,
    segments,
    dilated_heads,
    owners,
    attn_weights,
    attn_first,
    attn_second,
    attn_average,
    attn_basis,
    ffn_weights,
    ffn_first,
    ffn_second,
    ffn_average,
    ffn_basis,
    split_biases,
    split_first,
    split_second,
    shared_vectors,
    shared_first,
    shared_second,
):
    slot_count = lax.axis_size(SEQ)
    layer_count = attn_weights.shape[0]
    attn_full, ffn_full = (
        lax.all_gather(attn_weights.astype(jnp.bfloat16), SEQ, axis=2, tiled=True),
        lax.all_gather(ffn_weights.astype(jnp.bfloat16), SEQ, axis=2, tiled=True),
    )
    attn_full = from_slots(attn_full, owners, slot_count)
    ffn_full = from_slots(ffn_full, owners, slot_count)
    seg_pad = with_halo(segments, ((SEQ, 0),), 2 * WIN)
    head_width = attn_full.shape[3]
    head_count = head_width // DH
    heads_here = lax.axis_index(MP) * head_count + jnp.arange(head_count, dtype=jnp.int32)
    head_flags = jnp.any(heads_here[:, None] == dilated_heads[None, :], axis=1)
    current = activations.astype(jnp.float32)
    saved_list = []
    for layer_index in range(layer_count):
        dilated = jnp.logical_and(head_flags, layer_index % 2 == 1)
        rim_width = 2 * WIN if layer_index % 2 == 1 else WIN
        current, saved = layer_forward(
            current,
            attn_full[layer_index],
            ffn_full[layer_index],
            shared_vectors[layer_index],
            split_biases[layer_index],
            segments,
            seg_pad,
            dilated,
            rim_width,
        )
        saved_list.append(saved)
    slot_range = jnp.arange(slot_count, dtype=jnp.int32)
    inverse = jnp.sum(
        jnp.where(owners[None, :] == slot_range[:, None], slot_range[None, :], 0), axis=1
    )
    grad_now = cotangent.astype(jnp.float32)
    attn_list = [None] * layer_count
    ffn_list = [None] * layer_count
    shared_list = [None] * layer_count
    split_list = [None] * layer_count
    for layer_index in range(layer_count - 1, -1, -1):
        dilated = jnp.logical_and(head_flags, layer_index % 2 == 1)
        rim_width = 2 * WIN if layer_index % 2 == 1 else WIN
        grad_now, attn_grad, ffn_grad, shared_grad, split_grad = layer_backward(
            grad_now,
            saved_list[layer_index],
            attn_full[layer_index],
            ffn_full[layer_index],
            shared_vectors[layer_index],
            segments,
            seg_pad,
            dilated,
            rim_width,
        )
        attn_grad = to_slots(attn_grad, inverse, slot_count)
        ffn_grad = to_slots(ffn_grad, inverse, slot_count)
        attn_list[layer_index] = attn_grad
        ffn_list[layer_index] = ffn_grad
        shared_list[layer_index] = shared_grad
        split_list[layer_index] = split_grad[None, :]
    attn_grads = jnp.stack(attn_list)
    ffn_grads = jnp.stack(ffn_list)
    attn_grads, ffn_grads = (
        lax.psum_scatter(attn_grads, SEQ, scatter_dimension=2, tiled=True),
        lax.psum_scatter(ffn_grads, SEQ, scatter_dimension=2, tiled=True),
    )
    shared_grads, split_grads = lax.psum((jnp.stack(shared_list), jnp.stack(split_list)), SEQ)
    first_seq = lax.axis_index(SEQ) == 0
    first_both = jnp.logical_and(first_seq, lax.axis_index(MP) == 0)
    local_sum = jnp.sum(attn_grads * attn_grads) + jnp.sum(ffn_grads * ffn_grads)
    local_sum = (
        local_sum
        + jnp.where(first_seq, jnp.sum(split_grads * split_grads), 0.0)
        + jnp.where(first_both, jnp.sum(shared_grads * shared_grads), 0.0)
    )
    grad_norm = jnp.sqrt(lax.psum(local_sum, (SEQ, MP)))
    factor = CLIP_LEVEL / jnp.maximum(grad_norm, CLIP_LEVEL)
    attn_rates = jnp.array([0.5 * D ** (-0.5)] * 3 + [0.5 * (WIN / D) ** 0.5], jnp.float32)
    ffn_rates = jnp.array([0.5 * D ** (-0.5), 0.5 * FF ** (-0.5)], jnp.float32)
    attn_out = rotate_update(
        attn_weights,
        factor * attn_grads,
        attn_first,
        attn_second,
        attn_average,
        attn_basis,
        attn_rates,
    )
    ffn_out = rotate_update(
        ffn_weights, factor * ffn_grads, ffn_first, ffn_second, ffn_average, ffn_basis, ffn_rates
    )
    split_out = vector_update(split_biases, factor * split_grads, split_first, split_second)
    shared_out = vector_update(shared_vectors, factor * shared_grads, shared_first, shared_second)
    return (
        current,
        grad_now,
        attn_out[0],
        attn_out[1],
        attn_out[2][:, :3],
        attn_out[2][:, 3],
        attn_out[3],
        ffn_out[0],
        ffn_out[1],
        ffn_out[2],
        ffn_out[3],
        split_out[0],
        split_out[1],
        split_out[2],
        shared_out[0],
        shared_out[1],
        shared_out[2],
        grad_norm,
    )


def solution(mesh):
    placed = (
        P(SEQ, None),
        P(SEQ, None),
        P(SEQ),
        P(),
        P(),
        P(None, None, SEQ, MP),
        P(None, None, SEQ, MP),
        P(None, None, SEQ, MP),
        P(None, None, SEQ, MP),
        P(None, None, SEQ, MP, None, None),
        P(None, None, SEQ, MP),
        P(None, None, SEQ, MP),
        P(None, None, SEQ, MP),
        P(None, None, SEQ, MP),
        P(None, None, SEQ, MP, None, None),
        P(None, MP, None),
        P(None, MP, None),
        P(None, MP, None),
        P(),
        P(),
        P(),
    )
    count = mesh.shape[SEQ]
    fits = count % 4 == 0 and (D // count) % 16 == 0 and mesh.shape[MP] == 4
    return jax.shard_map(
        direct if fits else with_collectives,
        mesh=mesh,
        in_specs=placed,
        out_specs=(
            P(SEQ, None),
            P(SEQ, None),
            P(None, None, SEQ, MP),
            P(None, None, SEQ, MP),
            P(None, None, SEQ, MP),
            P(None, SEQ, MP),
            P(None, None, SEQ, MP),
            P(None, None, SEQ, MP),
            P(None, None, SEQ, MP),
            P(None, None, SEQ, MP),
            P(None, None, SEQ, MP),
            P(None, MP, None),
            P(None, MP, None),
            P(None, MP, None),
            P(),
            P(),
            P(),
            P(),
        ),
        check_vma=False,
    )
```

```python
from types import SimpleNamespace

import jax
import jax.numpy as jnp
from jax import lax
from jax.experimental import pallas as pl
from jax.experimental.pallas import tpu as pltpu
from jax.sharding import PartitionSpec as P

D = 768
DH = 64
FF = 3072
WIN = 256
STEP = 10

HIGHEST_PRECISION = lax.Precision.HIGHEST
NORM_EPSILON = 1e-05
MASK_FILL = -1e30
CLIP_LEVEL = 1.0
BETA_FIRST = 0.5
BETA_SECOND = 0.5
ADAM_EPSILON = 1e-08
DECAY_RATE = 0.01
AVERAGE_RATE = 0.7
VECTOR_RATE = 0.3

BF = jnp.bfloat16
SEQ, MP = "seq", "mp"
F32 = jnp.float32
MESH = pl.DeviceIdType.MESH
BLOCK = 256
CHUNK = 128
WIDE_CHUNK = 256
VMEM_LIMIT = 56 * 1024 * 1024
SCORE_SCALE = DH ** (-0.5)

GATHER_TIMES = ((2, 3, 5), (3, 5), (6, 7, 9), (7, 10, 13, 16))
BACK_TIMES = ((1, 4, 7, 10, 12), (6, 8, 10, 12), (10, 13, 15, 17))
END_TIMES = ((1, 4, 7, 10, 13), (5, 8, 10, 12), (11, 14, 15, 16))
SMALL_TIMES = (8, 10)


def dot(left, right):
    return jnp.dot(left, right, preferred_element_type=F32)


def dot_nt(left, right):
    return lax.dot_general(left, right, (((1,), (1,)), ((), ())), preferred_element_type=F32)


def dot_tn(left, right):
    return lax.dot_general(left, right, (((0,), (0,)), ((), ())), preferred_element_type=F32)


class Flush:
    def __init__(self, held, out, sems):
        self.held, self.out, self.sems = held, out, sems

    def copy(self, rows, t):
        return pltpu.make_async_copy(self.held.at[rows, :], self.out.at[rows, :], self.sems.at[t])


def run_kernel(
    body,
    name,
    inputs,
    outputs,
    scratch,
    collective=None,
    flops=0,
    grid=None,
    specs=None,
    in_smem=(),
    in_hbm=(),
    late=None,
    flushed=None,
    whole=None,
    pieces=0,
):
    specs, late, flushed, whole = specs or {}, late or {}, flushed or {}, whole or {}

    def kernel(*refs):
        refs = list(refs)

        def take(keys):
            got = refs[: len(keys)]
            del refs[: len(keys)]
            return dict(zip(keys, got))

        given, distant, made, written, far, held = (
            take(keys) for keys in (inputs, late, outputs, flushed, whole, scratch)
        )
        fetched, fetched_sems, filled, filled_sems = (take(keys) for keys in (late, late, flushed, flushed))
        kept, kept_sems = take(whole), take(whole)
        r = SimpleNamespace(**given, **made, **held, **fetched, **filled, **kept)
        if whole:
            *first, last = whole
            r.flush_whole = SimpleNamespace(
                **{key: pltpu.make_async_copy(kept[key], far[key], kept_sems[key].at[0]) for key in first}
            )
            r.soft_hbm, r.soft_sem = far[last], kept_sems[last]
        r.late = SimpleNamespace(
            **{key: pltpu.make_async_copy(distant[key], fetched[key], fetched_sems[key]) for key in late}
        )
        r.flush = SimpleNamespace(**{key: Flush(filled[key], written[key], filled_sems[key]) for key in flushed})
        for copy in vars(r.late).values():
            copy.start()
        body(r)

    def spec_of(key):
        if key in specs:
            return specs[key]
        if key in in_hbm or key in late or key in flushed or key in whole:
            return pl.BlockSpec(memory_space=pl.ANY)
        return pl.BlockSpec(memory_space=pltpu.SMEM if key in in_smem else pltpu.VMEM)

    arguments = {**inputs, **late}
    gives = {**outputs, **flushed, **whole}
    shapes = [jax.ShapeDtypeStruct(shape, dtype) for shape, dtype in gives.values()]
    moved = sum(v.size * v.dtype.itemsize for v in arguments.values())
    moved += sum(v.size * v.dtype.itemsize for v in shapes)
    extra = {} if grid is None else dict(grid=grid)
    params = dict(vmem_limit_bytes=VMEM_LIMIT)
    if collective is not None:
        params.update(collective_id=collective, has_side_effects=True)
    results = pl.pallas_call(
        kernel,
        out_shape=shapes,
        in_specs=[spec_of(key) for key in arguments],
        out_specs=[spec_of(key) for key in gives],
        scratch_shapes=list(scratch.values())
        + [pltpu.VMEM(v.shape, v.dtype) for v in late.values()]
        + [pltpu.SemaphoreType.DMA for _ in late]
        + [pltpu.VMEM(shape, dtype) for shape, dtype in flushed.values()]
        + [pltpu.SemaphoreType.DMA((pieces,)) for _ in flushed]
        + [pltpu.VMEM(shape, dtype) for shape, dtype in whole.values()]
        + [pltpu.SemaphoreType.DMA((pieces,)) for _ in whole],
        compiler_params=pltpu.CompilerParams(**params),
        cost_estimate=pl.CostEstimate(flops=int(flops), bytes_accessed=int(moved), transcendentals=0),
        name=name,
        **extra,
    )(*arguments.values())
    return SimpleNamespace(**dict(zip(gives, results)))


def parity_matrix():
    row = lax.broadcasted_iota(jnp.int32, (2 * BLOCK, 2 * BLOCK), 0)
    col = lax.broadcasted_iota(jnp.int32, (2 * BLOCK, 2 * BLOCK), 1)
    source = 2 * (row % BLOCK) + row // BLOCK
    return jnp.where(col == source, 1.0, 0.0).astype(BF)


def head_lanes(count):
    lane = lax.broadcasted_iota(jnp.int32, (1, count * DH), 1)
    return [lane // DH == head for head in range(count)]


def head_flags(dilated, count):
    first = lax.axis_index(MP) * count
    return [jnp.logical_or(dilated[0] == first + head, dilated[1] == first + head) for head in range(count)]


def marked_lanes(dilated, count):
    marked = jnp.zeros((1, count * DH), jnp.int32)
    for flag, lanes in zip(head_flags(dilated, count), head_lanes(count)):
        marked = jnp.where(lanes, flag.astype(jnp.int32), marked)
    return marked > 0


def sorted_groups(natural, sort):
    groups = natural.shape[0] // (2 * BLOCK)
    return [dot(sort, natural[g * 2 * BLOCK : (g + 1) * 2 * BLOCK]).astype(BF) for g in range(groups)]


def arrange_rows(natural, sort):
    return jnp.concatenate(sorted_groups(natural, sort), axis=0)


def split_rows(natural, sort):
    parts = sorted_groups(natural, sort)
    return jnp.concatenate([p[:BLOCK] for p in parts] + [p[BLOCK:] for p in parts], axis=0)


def soft_weights(query_block, key_block, lanes, allowed):
    raw = dot_nt(jnp.where(lanes, query_block, 0.0).astype(BF), key_block)
    scores = jnp.where(allowed, raw, MASK_FILL)
    top = jnp.max(scores, axis=1, keepdims=True)
    exponent = jnp.exp(scores - top)
    total = jnp.sum(exponent, axis=1, keepdims=True)
    return (exponent * (1.0 / total)).astype(BF)


def window_mask():
    row = lax.broadcasted_iota(jnp.int32, (BLOCK, 3 * BLOCK), 0)
    col = lax.broadcasted_iota(jnp.int32, (BLOCK, 3 * BLOCK), 1)
    return jnp.abs(row - col + BLOCK) <= WIN


class OutShare:
    def __init__(self, who, refs):
        self.who, self.r, self.here = who, refs, lax.axis_index(MP)

    def copy(self, kind, slot):
        r = self.r
        device = self.who.across if kind == 1 else self.who.sibling
        return copy_to(r.full.at[slot], r.full.at[slot], r.sent.at[kind], r.came.at[kind], device)

    def begin(self, own):
        self.r.full[self.here] = own.astype(F32).T.astype(BF)
        self.copy(0, self.here).start()
        self.copy(1, self.here).start()

    def hand_on(self):
        self.copy(1, self.who.across[1]).wait_recv()
        self.copy(2, self.who.across[1]).start()

    def finish(self):
        self.copy(0, self.who.sibling[1]).wait_recv()
        self.copy(2, self.who.diagonal[1]).wait_recv()
        for kind, slot in enumerate((self.here, self.here, self.who.across[1])):
            self.copy(kind, slot).wait_send()


def share_scratch():
    return dict(share_sent=pltpu.SemaphoreType.DMA((3,)), share_came=pltpu.SemaphoreType.DMA((3,)))


def key_starts(step, mixed):
    natural = pl.ds(pl.multiple_of(step * BLOCK, BLOCK), 3 * BLOCK)
    if not mixed:
        return natural, natural
    first = (step % 2) * 4 + step // 2
    return natural, pl.ds(pl.multiple_of(first * BLOCK, BLOCK), 3 * BLOCK)


class HeadExchange:
    def __init__(self, who, source, gathered, sent, came):
        self.who, self.source, self.gathered, self.sent, self.came = who, source, gathered, sent, came
        here = lax.axis_index(MP)
        self.here = here
        self.devices = who.sibling, who.across, who.diagonal

    def copy(self, kind, t, slot):
        who = self.who
        rows = who.own(t) if kind == 1 else who.other(t)
        return copy_to(
            self.source.at[rows, :],
            self.gathered.at[slot, who.half(t), :],
            self.sent.at[kind, t],
            self.came.at[kind, t],
            self.devices[kind],
        )

    def give(self, t):
        self.gathered[self.here, self.who.half(t), :] = self.source[self.who.own(t), :]
        for kind in range(3):
            self.copy(kind, t, self.here).start()

    def take(self, t):
        for kind in range(3):
            self.copy(kind, t, self.devices[kind][1]).wait_recv()

    def finish(self, t):
        for kind in range(3):
            self.copy(kind, t, self.here).wait_send()


def attend(query, pair, left, right, seg_query, seg_keys, dilated):
    rows, width = query.shape
    heads = width // DH
    blocks = rows // BLOCK
    keys = 3 * BLOCK
    slots = 2 * blocks
    chunks = rows // WIDE_CHUNK

    def body(r):
        step = pl.program_id(0)
        who = Partners(size=WIDE_CHUNK)
        exchange = HeadExchange(who, r.out, r.landed, r.sent, r.came)

        @pl.when(step == 0)
        def _():
            who.call()
            marked = marked_lanes(r.dilated, heads)
            sort = parity_matrix()
            for which, held in ((0, r.keys), (1, r.values)):
                lanes = slice(which * width, (which + 1) * width)
                padded = jnp.concatenate([r.left[:, lanes], r.pair[:, lanes], r.right[:, lanes]], axis=0)
                natural = jnp.concatenate([padded[BLOCK : (blocks + 3) * BLOCK], padded[: 2 * BLOCK]], axis=0)
                held[...] = jnp.where(marked, split_rows(padded, sort), natural)
            scaled = (r.asked[...].astype(F32) * SCORE_SCALE).astype(BF)
            r.query[...] = jnp.where(marked, arrange_rows(scaled, sort), scaled)

        window = window_mask()
        natural, dilated_near = key_starts(step, True)
        own = pl.ds(pl.multiple_of(step * BLOCK, BLOCK), BLOCK)
        marked = marked_lanes(r.dilated, heads)
        key_block = jnp.where(marked, r.keys[dilated_near, :], r.keys[natural, :])
        value_block = jnp.where(marked, r.values[dilated_near, :], r.values[natural, :])
        query_block = r.query[own, :]
        gathered = jnp.zeros((BLOCK, width), F32)
        flags = head_flags(r.dilated, heads)
        for head, lanes in enumerate(head_lanes(heads)):
            mine = jnp.where(flags[head], r.seg_query[own, 1:2], r.seg_query[own, 0:1])
            theirs = jnp.where(flags[head], r.seg_keys[1:2, dilated_near], r.seg_keys[0:1, natural])
            soft = soft_weights(query_block, key_block, lanes, jnp.logical_and(window, mine == theirs))
            r.soft[head] = soft
            gathered = jnp.where(lanes, dot(soft, value_block), gathered)
        r.arranged[own, :] = gathered.astype(BF)

        for group in range(blocks // 2):

            @pl.when(step == 2 * group + 1)
            def _(group=group):
                part = slice(group * 2 * BLOCK, (group + 1) * 2 * BLOCK)
                arranged = r.arranged[part, :]
                restored = dot_tn(parity_matrix(), arranged).astype(BF)
                r.out[part, :] = jnp.where(marked, restored, arranged)
                if group == 0:
                    who.gather()
                    for t in range(chunks // 2):
                        exchange.give(t)

        @pl.when(step == blocks - 1)
        def _():
            for t in range(chunks // 2):
                exchange.take(t)
                exchange.finish(t)
            r.first[...] = r.landed[...]

    return run_kernel(
        body,
        "attend",
        dict(
            asked=query,
            pair=pair,
            left=left,
            right=right,
            seg_query=seg_query,
            seg_keys=seg_keys,
            dilated=dilated,
        ),
        dict(
            out=((rows, width), BF),
            first=((4, rows // 4, width), BF),
            arranged=((rows, width), BF),
            query=((rows, width), BF),
            keys=((slots * BLOCK, width), BF),
            values=((slots * BLOCK, width), BF),
            soft=((heads, rows, keys), BF),
        ),
        dict(
            landed=pltpu.VMEM((4, rows // 4, width), BF),
            sent=pltpu.SemaphoreType.DMA((3, chunks // 2)),
            came=pltpu.SemaphoreType.DMA((3, chunks // 2)),
        ),
        collective=8,
        flops=4 * rows * keys * 256 * heads,
        grid=(blocks,),
        specs=dict(soft=pl.BlockSpec((heads, BLOCK, keys), lambda i: (0, i, 0))),
        in_smem=("dilated",),
    )


def attend_back(saved, grad_out, dilated, rim, mixed, count, collective):
    rows, width = grad_out.shape
    heads = width // DH
    blocks = rows // BLOCK
    keys = 3 * BLOCK
    slots = 2 * blocks if mixed else blocks + 2

    def body(r):
        step = pl.program_id(0)
        column = Column(count)
        first, last = column.index == 0, column.index == count - 1
        before = (lax.rem(column.index + count - 1, count), column.here)
        after = (lax.rem(column.index + 1, count), column.here)
        copy = copy_to(r.ready_left, r.from_right, r.sent.at[0], r.came.at[0], before)

        @pl.when(step == 0)
        def _():
            barrier = pltpu.get_barrier_semaphore()

            @pl.when(jnp.logical_not(last))
            def _():
                pl.semaphore_signal(barrier, inc=1, device_id=after, device_id_type=MESH)

            grad = r.grad_out[...]
            if mixed:
                grad = jnp.where(marked_lanes(r.dilated, heads), arrange_rows(grad, parity_matrix()), grad)
            r.grad[...] = grad
            r.grad_keys[...] = jnp.zeros_like(r.grad_keys)
            r.grad_values[...] = jnp.zeros_like(r.grad_values)

        natural, dilated_near = key_starts(step, mixed)
        own = pl.ds(pl.multiple_of(step * BLOCK, BLOCK), BLOCK)
        marked = marked_lanes(r.dilated, heads)
        key_block, value_block = r.keys[natural, :], r.values[natural, :]
        if mixed:
            key_block = jnp.where(marked, r.keys[dilated_near, :], key_block)
            value_block = jnp.where(marked, r.values[dilated_near, :], value_block)
        query_block = r.query[own, :]
        grad_block = r.grad[own, :]
        product = grad_block.astype(F32) * r.arranged[own, :].astype(F32)
        grad_query = jnp.zeros((BLOCK, width), F32)
        grad_key = jnp.zeros((keys, width), F32)
        grad_value = jnp.zeros((keys, width), F32)
        for head, lanes in enumerate(head_lanes(heads)):
            soft = r.soft[head]
            grad_head = jnp.where(lanes, grad_block, 0.0).astype(BF)
            row_dot = jnp.sum(jnp.where(lanes, product, 0.0), axis=1, keepdims=True)
            grad_soft = dot_nt(grad_head, value_block)
            grad_scores = (soft.astype(F32) * (grad_soft - row_dot)).astype(BF)
            grad_value += dot_tn(soft, grad_head)
            grad_key += dot_tn(grad_scores, jnp.where(lanes, query_block, 0.0).astype(BF))
            grad_query = jnp.where(lanes, dot(grad_scores, key_block), grad_query)
        r.grad_query[own, :] = (grad_query * SCORE_SCALE).astype(BF)
        if mixed:
            for held, grad in ((r.grad_keys, grad_key), (r.grad_values, grad_value)):
                held[dilated_near, :] += jnp.where(marked, grad, 0.0)
                held[natural, :] += jnp.where(marked, 0.0, grad)
        else:
            r.grad_keys[natural, :] += grad_key
            r.grad_values[natural, :] += grad_value

        def natural_group(g, middle):
            both = []
            for held in (r.grad_keys, r.grad_values):
                plain = middle(held)
                pair = jnp.concatenate(
                    [
                        held[g * BLOCK : (g + 1) * BLOCK, :],
                        held[(blocks + g) * BLOCK : (blocks + g + 1) * BLOCK, :],
                    ],
                    axis=0,
                ).astype(BF)
                both.append(jnp.where(marked, dot_tn(parity_matrix(), pair), plain).astype(BF))
            return jnp.concatenate(both, axis=1)

        edge = jnp.zeros((BLOCK, width), F32)

        @pl.when(step == (1 if mixed else 0))
        def _():
            if mixed:
                r.ready_left[...] = natural_group(0, lambda held: jnp.concatenate([edge, held[:BLOCK, :]], axis=0))
            else:
                r.ready_left[...] = jnp.concatenate(
                    [r.grad_keys[:rim, :], r.grad_values[:rim, :]], axis=1
                ).astype(BF)

            @pl.when(jnp.logical_not(first))
            def _():
                pl.semaphore_wait(pltpu.get_barrier_semaphore(), 1)
                copy.start()

        @pl.when(step == blocks - 1)
        def _():
            if mixed:
                for g in range(blocks // 2):
                    part = slice(g * 2 * BLOCK, (g + 1) * 2 * BLOCK)
                    arranged = r.grad_query[part, :]
                    restored = dot_tn(parity_matrix(), arranged).astype(BF)
                    r.out_query[part, :] = jnp.where(marked, restored, arranged)
                lap = 2 * BLOCK
                r.out_own[:lap, :] = natural_group(1, lambda held: held[BLOCK : 3 * BLOCK, :])
                r.out_own[lap:, :] = natural_group(2, lambda held: held[3 * BLOCK : 5 * BLOCK, :])
                r.out_right[...] = natural_group(
                    3, lambda held: jnp.concatenate([held[5 * BLOCK : 6 * BLOCK, :], edge], axis=0)
                )
            else:
                r.out_query[...] = r.grad_query[...]
                both = jnp.concatenate([r.grad_keys[rim:, :], r.grad_values[rim:, :]], axis=1).astype(BF)
                r.out_own[...] = both[:rows]
                r.out_right[...] = both[rows:]

            @pl.when(jnp.logical_not(last))
            def _():
                copy.wait_recv()
                tail = pl.ds(rows - rim, rim)
                r.out_own[tail, :] = (r.out_own[tail, :].astype(F32) + r.from_right[...].astype(F32)).astype(BF)

            @pl.when(jnp.logical_not(first))
            def _():
                copy.wait_send()

    return run_kernel(
        body,
        "attend_back",
        dict(
            grad_out=grad_out,
            arranged=saved.arranged,
            query=saved.query,
            keys=saved.keys,
            values=saved.values,
            soft=saved.soft,
            dilated=dilated,
        ),
        dict(
            out_query=((rows, width), BF),
            out_own=((rows, 2 * width), BF),
            out_right=((rim, 2 * width), BF),
        ),
        dict(
            grad=pltpu.VMEM((rows, width), BF),
            grad_query=pltpu.VMEM((rows, width), BF),
            grad_keys=pltpu.VMEM((slots * BLOCK, width), F32),
            grad_values=pltpu.VMEM((slots * BLOCK, width), F32),
            ready_left=pltpu.VMEM((rim, 2 * width), BF),
            from_right=pltpu.VMEM((rim, 2 * width), BF),
            sent=pltpu.SemaphoreType.DMA((1,)),
            came=pltpu.SemaphoreType.DMA((1,)),
        ),
        collective=collective,
        flops=8 * rows * keys * 256 * heads,
        grid=(blocks,),
        specs=dict(soft=pl.BlockSpec((heads, BLOCK, keys), lambda i: (0, i, 0))),
        in_smem=("dilated",),
    )


class Partners:
    def __init__(self, count=0, shift=0, size=CHUNK):
        seq = lax.axis_index(SEQ)
        here = lax.axis_index(MP)
        self.core = lax.rem(here, 2)
        self.sibling = (seq, here + 1 - 2 * self.core)
        self.across = (seq, lax.rem(here + 2, 4))
        self.diagonal = (seq, lax.rem(here + 3 - 2 * self.core, 4))
        self.count, self.shift, self.size = count, shift, size

    def others(self, column):
        found = [self.sibling, self.across, self.diagonal]
        if column is not None:
            found += [column.peer(k) for k in range(1, column.count)]
        return found

    def call(self, column=None):
        barrier = pltpu.get_barrier_semaphore()
        for other in self.others(column):
            pl.semaphore_signal(barrier, inc=1, device_id=other, device_id_type=MESH)

    def gather(self, column=None):
        pl.semaphore_wait(pltpu.get_barrier_semaphore(), len(self.others(column)))

    def meet(self, column=None):
        self.call(column)
        self.gather(column)

    def place(self, t):
        return lax.rem(t + self.shift, self.count) if self.shift else t

    def chunk(self, t):
        return pl.ds(pl.multiple_of(self.place(t) * self.size, self.size), self.size)

    def two_chunks(self, t):
        return pl.ds(pl.multiple_of(self.place(t - 1) * self.size, 2 * self.size), 2 * self.size)

    def part(self, t, core):
        half = self.size // 2
        return pl.ds(pl.multiple_of(self.place(t) * self.size + core * half, half), half)

    def own(self, t):
        return self.part(t, self.core)

    def other(self, t):
        return self.part(t, 1 - self.core)

    def half(self, t):
        half = self.size // 2
        return pl.ds(pl.multiple_of(self.place(t) * half, half), half)


def copy_to(source, target, sent, arrived, device):
    return pltpu.make_async_remote_copy(
        src_ref=source, dst_ref=target, send_sem=sent, recv_sem=arrived, device_id=device, device_id_type=MESH
    )


def exchange_scratch(rows):
    count = rows // CHUNK
    return dict(
        part=pltpu.VMEM((rows, D), BF),
        near=pltpu.VMEM((rows // 2, D), BF),
        far=pltpu.VMEM((rows // 2, D), BF),
        core_sent=pltpu.SemaphoreType.DMA((count,)),
        core_came=pltpu.SemaphoreType.DMA((count,)),
        far_sent=pltpu.SemaphoreType.DMA((count,)),
        far_came=pltpu.SemaphoreType.DMA((count,)),
    )


def gather_scratch(rows, width=D, dtype=BF):
    count = rows // CHUNK
    return dict(
        full=pltpu.VMEM((rows, width), dtype),
        sent=pltpu.SemaphoreType.DMA((count,)),
        came=pltpu.SemaphoreType.DMA((count,)),
    )


class Exchange:
    def __init__(self, who, refs):
        self.who, self.r = who, refs

    def core_copy(self, t):
        who, r = self.who, self.r
        return copy_to(
            r.part.at[who.other(t), :], r.near.at[who.half(t), :], r.core_sent.at[t], r.core_came.at[t], who.sibling
        )

    def far_copy(self, t):
        who, r = self.who, self.r
        rows = who.half(t)
        return copy_to(r.near.at[rows, :], r.far.at[rows, :], r.far_sent.at[t], r.far_came.at[t], who.across)

    def give(self, t, part):
        self.r.part[self.who.chunk(t), :] = part.astype(BF)
        self.core_copy(t).start()

    def add(self, t):
        who, r = self.who, self.r
        self.core_copy(t).wait_recv()
        pair = r.part[who.own(t), :].astype(F32) + r.near[who.half(t), :].astype(F32)
        r.near[who.half(t), :] = pair.astype(BF)
        self.far_copy(t).start()

    def take(self, t):
        who, r = self.who, self.r
        self.far_copy(t).wait_recv()
        return r.near[who.half(t), :].astype(F32) + r.far[who.half(t), :].astype(F32)

    def finish(self, t):
        self.core_copy(t).wait_send()
        self.far_copy(t).wait_send()


class Gather:
    def __init__(self, who, refs):
        self.who, self.r = who, refs

    def copy(self, rows, t):
        r = self.r
        return copy_to(r.full.at[rows, :], r.full.at[rows, :], r.sent.at[t], r.came.at[t], self.who.sibling)

    def give(self, t, value):
        rows = self.who.own(t)
        self.r.full[rows, :] = value.astype(self.r.full.dtype)
        self.copy(rows, t).start()

    def take(self, t):
        self.wait(t)
        return self.r.full[self.who.chunk(t), :]

    def wait(self, t):
        self.copy(self.who.other(t), t).wait_recv()

    def finish(self, t):
        self.copy(self.who.own(t), t).wait_send()


class Column:
    def __init__(self, count):
        self.count = count
        self.lines = count // 2
        self.here = lax.axis_index(MP)
        self.index = lax.axis_index(SEQ)
        self.inner = lax.rem(self.index, 2)
        self.outer = lax.div(self.index, 2)

    def peer(self, k):
        return (lax.rem(self.index + k, self.count), self.here)

    def at(self, outer, inner):
        return (2 * outer + inner, self.here)

    def turn(self, k):
        return lax.rem(self.outer + k, self.lines)


def gather_sems(lines):
    return {
        key: pltpu.SemaphoreType.DMA((lines,)) for key in ("pair_sent", "pair_came", "up_sent", "down_sent", "line_came")
    }


class GatherBlocks:
    def __init__(self, column, refs):
        self.c, self.r = column, refs
        self.above = column.outer < column.lines - 1
        self.below = column.outer > 0

    def line_copy(self, source, step):
        c, r = self.c, self.r
        block = 2 * source + c.inner
        sent = r.up_sent if step > 0 else r.down_sent
        return copy_to(
            r.full.at[block], r.full.at[block], sent.at[source], r.line_came.at[source], c.at(c.outer + step, c.inner)
        )

    def pair_copy(self, source, inner):
        c, r = self.c, self.r
        block = 2 * source + inner
        return copy_to(
            r.full.at[block],
            r.full.at[block],
            r.pair_sent.at[source],
            r.pair_came.at[source],
            c.at(c.outer, 1 - c.inner),
        )

    def put(self, value):
        self.r.full[self.c.index] = value

    def start_line(self):
        c = self.c

        @pl.when(self.above)
        def _():
            self.line_copy(c.outer, 1).start()

        @pl.when(self.below)
        def _():
            self.line_copy(c.outer, -1).start()

    def start_pair(self):
        self.pair_copy(self.c.outer, self.c.inner).start()

    def relay(self, k):
        c = self.c

        @pl.when(c.outer >= k)
        def _():
            source = c.outer - k
            self.line_copy(source, 1).wait_recv()

            @pl.when(self.above)
            def _():
                self.line_copy(source, 1).start()

            self.hand_on(source)

        @pl.when(c.outer + k < c.lines)
        def _():
            source = c.outer + k
            self.line_copy(source, -1).wait_recv()

            @pl.when(self.below)
            def _():
                self.line_copy(source, -1).start()

            self.hand_on(source)

    def hand_on(self, source):
        self.pair_copy(source, self.c.inner).start()

    def arrive(self):
        for k in range(self.c.lines):
            self.pair_copy(k, 1 - self.c.inner).wait_recv()

    def finish(self):
        for k in range(self.c.lines):
            self.pair_copy(k, self.c.inner).wait_send()
        self.finish_line()

    def finish_line(self):
        c = self.c
        for k in range(c.lines):

            @pl.when(jnp.logical_and(self.above, c.outer >= k))
            def _(k=k):
                self.line_copy(k, 1).wait_send()

            @pl.when(jnp.logical_and(self.below, c.outer <= k))
            def _(k=k):
                self.line_copy(k, -1).wait_send()


class GatherPairs(GatherBlocks):
    def line_copy(self, source, step):
        c, r = self.c, self.r
        blocks = pl.ds(2 * source, 2)
        sent = r.up_sent if step > 0 else r.down_sent
        return copy_to(
            r.full.at[blocks], r.full.at[blocks], sent.at[source], r.line_came.at[source], c.at(c.outer + step, c.inner)
        )

    def begin(self):
        self.pair_copy(self.c.outer, 1 - self.c.inner).wait_recv()
        self.start_line()

    def hand_on(self, source):
        pass

    def finish(self):
        self.pair_copy(self.c.outer, self.c.inner).wait_send()
        self.finish_line()


def scatter_scratch(lines, block, size, held=True):
    scratch = {
        key: pltpu.SemaphoreType.DMA((lines + 1,))
        for key in ("pair_sent", "pair_came", "line_sent", "line_came", "own_came")
    }
    scratch.update(near=pltpu.VMEM((lines, block, size), BF), far=pltpu.VMEM((lines + 1, block, size), BF))
    if held:
        scratch["own"] = pltpu.VMEM((lines, block, size), BF)
    return scratch


class ScatterBlocks:
    def __init__(self, column, refs, total):
        self.c, self.r, self.total = column, refs, total
        self.above = column.outer < column.lines - 1
        self.below = column.outer > 0
        self.fetched = hasattr(refs, "own")
        order = []
        for k in range(column.lines // 2):
            order += [column.lines - 1 - k, k]
        self.order = order

    def pair_copy(self, outer):
        c, r = self.c, self.r
        return copy_to(
            r.grads.at[2 * outer + 1 - c.inner],
            r.near.at[outer],
            r.pair_sent.at[outer],
            r.pair_came.at[outer],
            c.at(c.outer, 1 - c.inner),
        )

    def own_copy(self, outer):
        c, r = self.c, self.r
        return pltpu.make_async_copy(r.grads.at[2 * outer + c.inner], r.own.at[outer], r.own_came.at[outer])

    def line_copy(self, target, step):
        c, r = self.c, self.r
        slot = target if step > 0 else jnp.where(c.outer - 1 == target, c.lines, target)
        return copy_to(
            r.near.at[target],
            r.far.at[slot],
            r.line_sent.at[target],
            r.line_came.at[slot],
            c.at(c.outer + step, c.inner),
        )

    def landing(self, slot, step):
        c, r = self.c, self.r
        return copy_to(
            r.near.at[c.outer], r.far.at[slot], r.line_sent.at[c.outer], r.line_came.at[slot], c.at(c.outer + step, c.inner)
        )

    def start(self):
        for outer in self.order:
            self.pair_copy(outer).start()
            if self.fetched:
                self.own_copy(outer).start()

    def pair_step(self, k):
        c, r = self.c, self.r
        for outer in self.order[2 * k : 2 * k + 2]:
            self.pair_copy(outer).wait_recv()
            if self.fetched:
                self.own_copy(outer).wait()
                own = r.own[outer]
            else:
                own = r.grads[2 * outer + c.inner]
            r.near[outer] = (own.astype(F32) + r.near[outer].astype(F32)).astype(BF)

    def line_step(self, wave):
        c, r = self.c, self.r
        from_top = c.lines - 1 - c.outer

        def pass_on(target, step, behind):
            @pl.when(behind)
            def _():
                self.landing(target, step).wait_recv()
                r.near[target] = (r.near[target].astype(F32) + r.far[target].astype(F32)).astype(BF)

            self.line_copy(target, step).start()

        @pl.when(c.outer <= wave)
        def _():
            pass_on(from_top + c.outer - wave + c.outer, 1, self.below)

        @pl.when(from_top <= wave)
        def _():
            pass_on(wave - from_top, -1, self.above)

    def close(self):
        c, r = self.c, self.r
        self.total[...] = r.near[c.outer].astype(F32)

        @pl.when(self.below)
        def _():
            self.landing(c.outer, 1).wait_recv()
            self.total[...] += r.far[c.outer].astype(F32)

        @pl.when(self.above)
        def _():
            self.landing(c.lines, -1).wait_recv()
            self.total[...] += r.far[c.lines].astype(F32)

    def finish(self):
        c = self.c
        for outer in self.order:
            self.pair_copy(outer).wait_send()
        for target in range(c.lines):

            @pl.when(c.outer < target)
            def _(target=target):
                self.line_copy(target, 1).wait_send()

            @pl.when(c.outer > target)
            def _(target=target):
                self.line_copy(target, -1).wait_send()

    def ticks(self, times):
        steps = [(times[0], lambda: self.pair_step(0)), (times[0], lambda: self.line_step(0))]
        steps += [(times[1], lambda: self.pair_step(1))]
        steps += [(times[k], lambda k=k: self.line_step(k)) for k in range(1, self.c.lines - 1)]
        steps += [(times[self.c.lines - 1], self.close)]
        return steps


def scatter_pairs_scratch(lines, block, size):
    scratch = {key: pltpu.SemaphoreType.DMA((lines + 1,)) for key in ("pair_sent", "pair_came", "line_sent", "line_came")}
    scratch.update(
        sums=pltpu.VMEM((2 * lines, block, size), BF),
        far=pltpu.VMEM((2 * lines + 2, block, size), BF),
        give=pltpu.VMEM((block, size), BF),
        get=pltpu.VMEM((block, size), BF),
        held=pltpu.SemaphoreType.DMA,
    )
    return scratch


class ScatterPairs:
    def __init__(self, column, refs, total):
        self.c, self.r, self.total = column, refs, total
        self.above = column.outer < column.lines - 1
        self.below = column.outer > 0
        self.fetch = pltpu.make_async_copy(refs.grads, refs.sums, refs.held)

    def line_copy(self, target, step):
        c, r = self.c, self.r
        slot = target if step > 0 else jnp.where(c.outer - 1 == target, c.lines, target)
        return copy_to(
            r.sums.at[pl.ds(2 * target, 2)],
            r.far.at[pl.ds(2 * slot, 2)],
            r.line_sent.at[target],
            r.line_came.at[slot],
            c.at(c.outer + step, c.inner),
        )

    def landing(self, slot, step):
        c, r = self.c, self.r
        return copy_to(
            r.sums.at[pl.ds(2 * c.outer, 2)],
            r.far.at[pl.ds(2 * slot, 2)],
            r.line_sent.at[c.outer],
            r.line_came.at[slot],
            c.at(c.outer + step, c.inner),
        )

    def pair_copy(self):
        c, r = self.c, self.r
        return copy_to(r.give, r.get, r.pair_sent.at[0], r.pair_came.at[0], c.at(c.outer, 1 - c.inner))

    def start(self):
        self.fetch.start()

    def line_step(self, wave):
        c, r = self.c, self.r
        from_top = c.lines - 1 - c.outer
        if wave == 0:
            self.fetch.wait()

        def pass_on(target, step, behind):
            @pl.when(behind)
            def _():
                self.landing(target, step).wait_recv()
                for k in range(2):
                    block = 2 * target + k
                    r.sums[block] = (r.sums[block].astype(F32) + r.far[block].astype(F32)).astype(BF)

            self.line_copy(target, step).start()

        @pl.when(c.outer <= wave)
        def _():
            pass_on(from_top + c.outer - wave + c.outer, 1, self.below)

        @pl.when(from_top <= wave)
        def _():
            pass_on(wave - from_top, -1, self.above)

    def close_line(self):
        c, r = self.c, self.r
        mine, other = 2 * c.outer + c.inner, 2 * c.outer + 1 - c.inner
        self.total[...] = r.sums[mine].astype(F32)

        @pl.when(self.below)
        def _():
            self.landing(c.outer, 1).wait_recv()
            self.total[...] += r.far[mine].astype(F32)
            r.sums[other] = (r.sums[other].astype(F32) + r.far[other].astype(F32)).astype(BF)

        @pl.when(self.above)
        def _():
            self.landing(c.lines, -1).wait_recv()
            self.total[...] += r.far[2 * c.lines + c.inner].astype(F32)
            r.sums[other] = (r.sums[other].astype(F32) + r.far[2 * c.lines + 1 - c.inner].astype(F32)).astype(BF)

        r.give[...] = r.sums[other]
        self.pair_copy().start()

    def close(self):
        self.pair_copy().wait_recv()
        self.total[...] += self.r.get[...].astype(F32)

    def finish(self):
        c = self.c
        self.pair_copy().wait_send()
        for target in range(c.lines):

            @pl.when(c.outer < target)
            def _(target=target):
                self.line_copy(target, 1).wait_send()

            @pl.when(c.outer > target)
            def _(target=target):
                self.line_copy(target, -1).wait_send()

    def ticks(self, times):
        steps = [(times[k], lambda k=k: self.line_step(k)) for k in range(self.c.lines - 1)]
        return steps + [(times[self.c.lines - 1], self.close_line), (times[self.c.lines], self.close)]


class Halo:
    def __init__(self, column, refs, source, rim, size):
        self.c, self.r, self.source, self.rim, self.size = column, refs, source, rim, size
        self.rows = source.shape[0]
        self.before = lax.rem(column.index + column.count - 1, column.count), column.here
        self.after = lax.rem(column.index + 1, column.count), column.here
        self.first, self.last = column.index == 0, column.index == column.count - 1

    def clear(self):
        @pl.when(self.first)
        def _():
            self.r.left[...] = jnp.zeros_like(self.r.left)

        @pl.when(self.last)
        def _():
            self.r.right[...] = jnp.zeros_like(self.r.right)

    def back_copy(self, t):
        rows = pl.ds(pl.multiple_of(t * self.size, self.size), self.size)
        return copy_to(
            self.source.at[rows, :], self.r.right.at[rows, :], self.r.back_sent.at[t], self.r.back_came.at[t], self.before
        )

    def ahead_copy(self, t):
        from_rows = pl.ds(pl.multiple_of(self.rows - self.rim + t * self.size, self.size), self.size)
        rows = pl.ds(pl.multiple_of(t * self.size, self.size), self.size)
        return copy_to(
            self.source.at[from_rows, :],
            self.r.left.at[rows, :],
            self.r.ahead_sent.at[t],
            self.r.ahead_came.at[t],
            self.after,
        )

    def send(self, t):
        count = self.rim // self.size
        offset = (self.rows - self.rim) // self.size

        @pl.when(jnp.logical_and(t < count, jnp.logical_not(self.first)))
        def _():
            self.back_copy(t).start()

        @pl.when(jnp.logical_and(t >= offset, jnp.logical_not(self.last)))
        def _():
            self.ahead_copy(t - offset).start()

    def arrive(self):
        for t in range(self.rim // self.size):

            @pl.when(jnp.logical_not(self.last))
            def _():
                self.back_copy(t).wait_recv()

            @pl.when(jnp.logical_not(self.first))
            def _():
                self.ahead_copy(t).wait_recv()

    def finish(self):
        for t in range(self.rim // self.size):

            @pl.when(jnp.logical_not(self.first))
            def _():
                self.back_copy(t).wait_send()

            @pl.when(jnp.logical_not(self.last))
            def _():
                self.ahead_copy(t).wait_send()


def halo_scratch(count):
    return {
        key: pltpu.SemaphoreType.DMA((count,)) for key in ("back_sent", "back_came", "ahead_sent", "ahead_came")
    }


def pick(r, prefix):
    start = prefix + "_"
    return SimpleNamespace(
        **{key[len(start) :]: value for key, value in vars(r).items() if key.startswith(start)}
    )


def prefixed(prefix, entries):
    return {prefix + "_" + key: value for key, value in entries.items()}


def run_stages(count, stages, ticks=()):
    last = max(delay for delay, _ in stages)

    def step(i, carry):
        for when in sorted({when for when, _ in ticks if when < count + last}):

            @pl.when(i == when)
            def _(when=when):
                for other, tick in ticks:
                    if other == when:
                        tick()

        for delay, stage in stages:

            @pl.when(jnp.logical_and(i >= delay, i < count + delay))
            def _(delay=delay, stage=stage):
                stage(i - delay)

        return carry

    lax.fori_loop(0, count + last, step, 0)
    for when, tick in sorted(ticks, key=lambda entry: entry[0]):
        if when >= count + last:
            tick()


def norm_forward(total, gain, shift):
    center = total - jnp.mean(total, axis=1, keepdims=True)
    spread = jnp.mean(center * center, axis=1, keepdims=True)
    inverse = lax.rsqrt(spread + NORM_EPSILON)
    unit = center * inverse
    return unit, inverse, unit * gain + shift


def norm_back(grad, unit, inverse, gain):
    grad_unit = grad * gain
    first = jnp.mean(grad_unit, axis=1, keepdims=True)
    second = jnp.mean(grad_unit * unit, axis=1, keepdims=True)
    return inverse * (grad_unit - first - unit * second)


def column_sum(value):
    return jnp.sum(value, axis=0, keepdims=True)


def split_two(value):
    high = value.astype(BF)
    return high, (value - high.astype(F32)).astype(BF)


def exact(value, product):
    high, rest = split_two(value)
    low = (value - high.astype(F32) - rest.astype(F32)).astype(BF)
    return product(high) + product(rest) + product(low)


def wide(column):
    return jnp.broadcast_to(column, (column.shape[0], 128))


def forward_refs(rows, width, units):
    return dict(
        unit_one=((rows // 2, D), F32),
        unit_two=((rows // 2, D), F32),
        hidden=((rows, units), BF),
        slope=((rows, units), BF),
    )


def forward_small(rows):
    return dict(inverse_one=((rows // 2, 128), F32), inverse_two=((rows // 2, 128), F32))


def forward_stages(r, who, projected, second, spread):
    def middle(t):
        total = r.residual[who.own(t), :].astype(F32) + projected(t) + r.shared[r.base + 0 : r.base + 1, :]
        unit, inverse, normed = norm_forward(total, r.shared[r.base + 1 : r.base + 2, :], r.shared[r.base + 2 : r.base + 3, :])
        r.unit_one[who.half(t), :] = unit
        r.inverse_one[who.half(t), :] = wide(inverse)
        r.normed[who.half(t), :] = normed
        spread.give(t, normed)

    def feed(t):
        pre = dot(spread.take(t), r.ffn_up[...]) + r.hidden_bias
        chance = 0.5 + 0.5 * lax.erf(pre * (0.5**0.5))
        hidden = (pre * chance).astype(BF)
        r.hidden[who.chunk(t), :] = hidden
        bell = jnp.exp(-0.5 * pre * pre) * 0.3989422804014327
        r.slope[who.chunk(t), :] = (chance + pre * bell).astype(BF)
        second.give(t, dot_nt(hidden, r.ffn_down[...]))

    def final(t):
        total = r.normed[who.half(t), :] + second.take(t) + r.shared[r.base + 3 : r.base + 4, :]
        unit, inverse, result = norm_forward(total, r.shared[r.base + 4 : r.base + 5, :], r.shared[r.base + 5 : r.base + 6, :])
        r.unit_two[who.half(t), :] = unit
        r.inverse_two[who.half(t), :] = wide(inverse)
        return unit, inverse, result

    return middle, feed, final


def backward_stages(r, who, ends, third, mids):
    def enter(t, grad, unit, inverse):
        grad_total = norm_back(grad, unit, inverse, r.shared[r.base + 4 : r.base + 5, :])
        r.vectors[3:4, :] += column_sum(grad_total)
        r.vectors[4:5, :] += column_sum(grad * unit)
        r.vectors[5:6, :] += column_sum(grad)
        r.kept[who.half(t), :] = grad_total
        ends.give(t, grad_total)

    def feed_back(t):
        rows = who.chunk(t)
        grad = ends.take(t)
        grad_pre = (dot(grad, r.ffn_down[...]) * r.slope[rows, :].astype(F32)).astype(BF)
        r.units[0:1, :] += column_sum(grad_pre.astype(F32))
        third.give(t, dot_nt(grad_pre, r.ffn_up[...]))
        r.grad_pre[pl.ds(pl.multiple_of(lax.rem(t, 2) * who.size, who.size), who.size), :] = grad_pre

        @pl.when(lax.rem(t, 2) == 1)
        def _():
            both = who.two_chunks(t)
            r.sum_up[...] += dot_tn(r.spread_full[both, :], r.grad_pre[...])
            r.sum_down[...] += dot_tn(ends.r.full[both, :], r.hidden[both, :])

    def leave(t):
        grad = r.kept[who.half(t), :] + third.take(t)
        unit = r.unit_one[who.half(t), :]
        grad_total = norm_back(grad, unit, r.inverse_one[who.half(t), 0:1], r.shared[r.base + 1 : r.base + 2, :])
        r.vectors[0:1, :] += column_sum(grad_total)
        r.vectors[1:2, :] += column_sum(grad * unit)
        r.vectors[2:3, :] += column_sum(grad)
        if r.grad_one is not None:
            r.grad_one[who.half(t), :] = grad_total
        mids.give(t, grad_total)

    def project_back(t):
        rows = who.chunk(t)
        grad = mids.take(t)
        r.grad_mixed[rows, :] = dot(grad, r.out_proj[...]).astype(BF)

        @pl.when(lax.rem(t, 2) == 1)
        def _():
            both = who.two_chunks(t)
            r.sum_out[...] += dot_tn(mids.r.full[both, :], r.mixed[both, :])

    return enter, feed_back, leave, project_back


def clear(*refs):
    for ref in refs:
        ref[...] = jnp.zeros_like(ref)


def finish_all(count, parts):
    def step(t, carry):
        for part in parts:
            part.finish(t)
        return carry

    lax.fori_loop(0, count, step, 0)


def packed(ref):
    return jnp.concatenate([ref[k].astype(BF) for k in range(ref.shape[0])], axis=1)


def projection_bias(split, width):
    return jnp.concatenate([split[:, :width], jnp.zeros((1, width), F32), split[:, width : 2 * width]], axis=1)


def opening(activations, segments, owners, attn_weights, ffn_weights, split_biases, shared_vectors, count):
    rows = activations.shape[0]
    width, units = attn_weights.shape[3], ffn_weights.shape[3]
    heads = width // DH
    blocks = rows // BLOCK
    lines = count // 2
    block = D // count
    layers = split_biases.shape[0]

    def body(r):
        who = Partners()
        column = Column(count)
        who.meet(column)
        wide_attn = GatherBlocks(column, SimpleNamespace(full=r.full_attn, **vars(pick(r, "ga"))))
        wide_up = GatherBlocks(column, SimpleNamespace(full=r.full_up, **vars(pick(r, "gu"))))
        wide_down = GatherPairs(column, SimpleNamespace(full=r.full_down, **vars(pick(r, "gd"))))
        halo = Halo(column, SimpleNamespace(left=r.left, right=r.right, **vars(pick(r, "halo"))), r.pair, WIN, BLOCK)
        first, last = column.index == 0, column.index == count - 1
        to_before = copy_to(r.ids, r.ids_right, r.ids_sent.at[0], r.ids_came.at[0], halo.before)
        to_after = copy_to(r.ids, r.ids_left, r.ids_sent.at[1], r.ids_came.at[1], halo.after)
        r.late.attn.wait()
        wide_attn.put(packed(r.attn.at[0]))
        wide_attn.start_line()
        wide_attn.start_pair()
        r.ids[...] = r.segments[...].astype(F32)

        @pl.when(first)
        def _():
            r.ids_left[...] = jnp.zeros_like(r.ids_left)

        @pl.when(last)
        def _():
            r.ids_right[...] = jnp.zeros_like(r.ids_right)

        @pl.when(jnp.logical_not(first))
        def _():
            to_before.start()

        @pl.when(jnp.logical_not(last))
        def _():
            to_after.start()

        halo.clear()
        r.late.ffn.wait()
        wide_down.put(r.ffn[0, 1].astype(BF))
        wide_down.start_pair()
        wide_up.put(r.ffn[0, 0].astype(BF))
        for slot in range(count):
            row = lax.broadcasted_iota(jnp.int32, (block, D), 0)
            col = lax.broadcasted_iota(jnp.int32, (block, D), 1)
            target = r.owners[slot] * block + row
            r.turn[slot * block : (slot + 1) * block, :] = jnp.where(col == target, 1.0, 0.0).astype(BF)

        def sort_chunk(t, carry):
            chunk = pl.ds(pl.multiple_of(t * BLOCK, BLOCK), BLOCK)
            r.low[chunk, :] = dot(r.activations[chunk, :], r.turn[...]).astype(BF)
            return carry

        r.flush_whole.turn.start()
        r.late.activations.wait()
        lax.fori_loop(0, blocks, sort_chunk, 0)
        r.flush_whole.low.start()
        wide_attn.relay(1)
        padding = jnp.zeros((16 - 6 * layers, D), F32)
        stacked = [r.shared_vectors[k, layer : layer + 1, :] for layer in range(layers) for k in range(6)]
        stacked = jnp.concatenate(stacked + [padding], axis=0)
        r.shared[...] = exact(stacked, lambda part: dot(part, r.turn[...]))
        wide_attn.relay(2)
        wide_up.start_line()

        @pl.when(jnp.logical_not(last))
        def _():
            to_before.wait_recv()

        @pl.when(jnp.logical_not(first))
        def _():
            to_after.wait_recv()

        def flat(ref):
            return jnp.concatenate([ref[k : k + 1, :] for k in range(ref.shape[0])], axis=1)

        own_ids = flat(r.ids)
        padded = jnp.concatenate([flat(r.ids_left)[:, rows - 2 * WIN :], own_ids, flat(r.ids_right)[:, : 2 * WIN]], axis=1)
        r.id_row[...] = jnp.broadcast_to(padded, r.id_row.shape)
        sort = parity_matrix()
        lap = 2 * BLOCK
        sorted_ids = [
            dot_nt(r.id_row[:, g * lap : (g + 1) * lap].astype(BF), sort) for g in range(2 * blocks // 2)
        ]
        natural = jnp.concatenate([padded[:, WIN : rows + 3 * WIN], padded[:, : 2 * WIN]], axis=1)
        arranged = jnp.concatenate(
            [part[0:1, :BLOCK] for part in sorted_ids] + [part[0:1, BLOCK:] for part in sorted_ids], axis=1
        )
        r.seg_keys[0:1, :] = natural
        r.seg_keys[1:2, :] = arranged
        middle = sorted_ids[1:-1]
        own_arranged = jnp.concatenate([part[0:1, :] for part in middle], axis=1)
        for which, row in ((0, own_ids), (1, own_arranged)):
            for k in range(rows // 128):
                square = jnp.broadcast_to(row[:, k * 128 : (k + 1) * 128], (128, 128))
                r.seg_query[k * 128 : (k + 1) * 128, which : which + 1] = square.T[:, 0:1]

        for k in range(3, lines):
            wide_attn.relay(k)
        wide_up.start_pair()
        wide_up.relay(1)
        wide_attn.arrive()
        r.flush_whole.full_attn.start()
        whole_attn = r.full_attn[...].reshape(D, 4 * width)
        r.proj[...] = whole_attn[:, : 3 * width]
        share = OutShare(who, SimpleNamespace(full=r.full_out, sent=r.share_sent, came=r.share_came))
        share.begin(whole_attn[:, 3 * width :])
        exchange = HeadExchange(who, r.out, r.gathered, r.heads_sent, r.heads_came)
        bias = projection_bias(r.split[0], width)

        def project(t):
            chunk = pl.ds(pl.multiple_of(t * BLOCK, BLOCK), BLOCK)
            value = dot(r.low[chunk, :], r.proj[...]) + bias
            r.query[chunk, :] = (value[:, :width].astype(BF).astype(F32) * SCORE_SCALE).astype(BF)
            pair = value[:, width:].astype(BF)
            r.pair[chunk, :] = pair
            inner = pl.ds(pl.multiple_of((t + 1) * BLOCK, BLOCK), BLOCK)
            r.keys[inner, :] = pair[:, :width]
            r.values[inner, :] = pair[:, width:]

        def outer_project(i, carry):
            t = i * (blocks - 1)
            project(t)
            halo.send(t)
            return carry

        def inner_project(i, carry):
            project(i)
            return carry

        lax.fori_loop(0, 2, outer_project, 0)
        wide_up.relay(2)
        wide_down.begin()
        lax.fori_loop(1, blocks - 1, inner_project, 0)
        for k in range(3, lines):
            wide_up.relay(k)

        def written(step):
            rows_of = pl.ds(pl.multiple_of(step * BLOCK, BLOCK), BLOCK)
            return pltpu.make_async_copy(r.soft.at[:, rows_of, :], r.soft_hbm.at[:, rows_of, :], r.soft_sem.at[step])

        def attend_block(step):
            own = pl.ds(pl.multiple_of(step * BLOCK, BLOCK), BLOCK)
            near = pl.ds(pl.multiple_of(step * BLOCK, BLOCK), 3 * BLOCK)
            key_block, value_block, query_block = r.keys[near, :], r.values[near, :], r.query[own, :]
            mine = r.seg_query[own, 0:1]
            theirs = r.id_row[0:1, pl.ds(pl.multiple_of(step * BLOCK + BLOCK, BLOCK), 3 * BLOCK)]
            allowed = jnp.logical_and(window_mask(), mine == theirs)
            gathered = jnp.zeros((BLOCK, width), F32)
            for head, lanes in enumerate(head_lanes(heads)):
                soft = soft_weights(query_block, key_block, lanes, allowed)
                r.soft[head, own, :] = soft
                gathered = jnp.where(lanes, dot(soft, value_block), gathered)
            r.out[own, :] = gathered.astype(BF)
            written(step).start()
            for k in range(BLOCK // CHUNK):
                exchange.give(BLOCK // CHUNK * step + k)

        def inner_attend(i, carry):
            attend_block(i)
            return carry

        def outer_attend(i, carry):
            attend_block(i * (blocks - 1))
            return carry

        lax.fori_loop(1, blocks - 1, inner_attend, 0)
        wide_down.relay(1)
        share.hand_on()
        halo.arrive()
        for part, start in ((r.left, 0), (r.right, (blocks + 1) * BLOCK)):
            r.keys[pl.ds(start, BLOCK), :] = part[:, :width]
            r.values[pl.ds(start, BLOCK), :] = part[:, width:]
        lax.fori_loop(0, 2, outer_attend, 0)
        for k in range(2, lines):
            wide_down.relay(k)
        wide_up.arrive()

        def exchanged(t, carry):
            exchange.take(t)
            exchange.finish(t)
            return carry

        lax.fori_loop(0, rows // CHUNK, exchanged, 0)
        share.finish()
        for step in range(blocks):
            written(step).wait()
        for copy in vars(r.flush_whole).values():
            copy.wait()
        halo.finish()
        for engine in (wide_attn, wide_up, wide_down):
            engine.finish()

        @pl.when(jnp.logical_not(first))
        def _():
            to_before.wait_send()

        @pl.when(jnp.logical_not(last))
        def _():
            to_after.wait_send()

    scratch = dict(
        proj=pltpu.VMEM((D, 3 * width), BF),
        pair=pltpu.VMEM((rows, 2 * width), BF),
        left=pltpu.VMEM((WIN, 2 * width), BF),
        right=pltpu.VMEM((WIN, 2 * width), BF),
        ids=pltpu.VMEM((rows // 128, 128), F32),
        ids_left=pltpu.VMEM((rows // 128, 128), F32),
        ids_right=pltpu.VMEM((rows // 128, 128), F32),
        ids_sent=pltpu.SemaphoreType.DMA((2,)),
        ids_came=pltpu.SemaphoreType.DMA((2,)),
        id_row=pltpu.VMEM((8, rows + 4 * WIN), F32),
    )
    scratch.update(
        heads_sent=pltpu.SemaphoreType.DMA((3, rows // CHUNK)),
        heads_came=pltpu.SemaphoreType.DMA((3, rows // CHUNK)),
        **share_scratch(),
    )
    scratch.update(prefixed("ga", gather_sems(lines)))
    scratch.update(prefixed("gu", gather_sems(lines)))
    scratch.update(prefixed("gd", gather_sems(lines)))
    scratch.update(prefixed("halo", halo_scratch(1)))
    return run_kernel(
        body,
        "opening",
        dict(
            segments=segments.reshape(rows // 128, 128),
            owners=owners,
            split=split_biases,
            shared_vectors=shared_vectors.transpose(1, 0, 2),
        ),
        dict(
            full_up=((count, block, units), BF),
            full_down=((count, block, units), BF),
            shared=((16, D), F32),
            seg_query=((rows, 2), F32),
            seg_keys=((8, 2 * rows), F32),
            out=((rows, width), BF),
            gathered=((4, rows // 2, width), BF),
            full_out=((4, width, D), BF),
            query=((rows, width), BF),
            keys=((rows + 2 * BLOCK, width), BF),
            values=((rows + 2 * BLOCK, width), BF),
        ),
        scratch,
        collective=5,
        flops=2 * rows * D * (D + 3 * width),
        in_smem=("owners",),
        late=dict(attn=attn_weights, ffn=ffn_weights, activations=activations),
        whole=dict(
            full_attn=((count, block, 4 * width), BF),
            low=((rows, D), BF),
            turn=((D, D), BF),
            soft=((heads, rows, 3 * BLOCK), BF),
        ),
        pieces=blocks,
    )


def middle_forward(gathered, full_out, ffn_up, ffn_down, residual, shared, split_biases, attn_weights, ffn_weights, count):
    rows, width = 2 * gathered.shape[1], gathered.shape[2]
    units = ffn_up.shape[1]
    chunks = rows // CHUNK
    lines = count // 2
    block = D // count

    def body(r):
        who = Partners()
        r.base = 0
        second = Exchange(who, pick(r, "second"))
        spread = Gather(who, SimpleNamespace(full=r.spread_full, sent=r.spread_sent, came=r.spread_came))
        last = Gather(who, SimpleNamespace(full=r.last_full, sent=r.last_sent, came=r.last_came))
        column = Column(count)
        who.meet(column)
        wide_attn = GatherBlocks(column, SimpleNamespace(full=r.full_attn, **vars(pick(r, "ga"))))
        wide_up = GatherBlocks(column, SimpleNamespace(full=r.full_up, **vars(pick(r, "gu"))))
        wide_down = GatherPairs(column, SimpleNamespace(full=r.full_down, **vars(pick(r, "gd"))))
        share = OutShare(who, SimpleNamespace(full=r.next_out, sent=r.share_sent, came=r.share_came))
        halo = Halo(column, SimpleNamespace(left=r.left, right=r.right, **vars(pick(r, "halo"))), r.pair, 2 * WIN, CHUNK)
        r.late.next_attn.wait()
        wide_attn.put(packed(r.next_attn.at[1]))
        wide_attn.start_line()
        wide_attn.start_pair()
        r.late.next_ffn.wait()
        wide_down.put(r.next_ffn[1, 1].astype(BF))
        wide_down.start_pair()
        wide_up.put(r.next_ffn[1, 0].astype(BF))
        halo.clear()
        r.late.full_out.wait()
        r.late.gathered.wait()
        r.hidden_bias = r.split[0][:, 2 * width :]
        next_bias = projection_bias(r.split[1], width)

        def unpack():
            wide_attn.arrive()
            packed_attn = r.full_attn[...].reshape(D, 4 * width)
            r.next_proj[...] = packed_attn[:, : 3 * width]
            share.begin(packed_attn[:, 3 * width :])

        ticks = [(0, r.late.residual.wait), (1, r.late.ffn_up.wait), (1, r.late.ffn_down.wait), (chunks, unpack), (chunks + 6, share.hand_on)]
        ticks += [(when, lambda k=k: wide_attn.relay(k + 1)) for k, when in enumerate(GATHER_TIMES[0])]
        ticks += [(GATHER_TIMES[1][0], wide_up.start_line), (GATHER_TIMES[1][1], wide_up.start_pair)]
        ticks += [(when, lambda k=k: wide_up.relay(k + 1)) for k, when in enumerate(GATHER_TIMES[2])]
        ticks += [(GATHER_TIMES[3][0], wide_down.begin)]
        ticks += [(when, lambda k=k: wide_down.relay(k + 1)) for k, when in enumerate(GATHER_TIMES[3][1:])]

        def projected(t):
            mine = jnp.concatenate([r.gathered[k, who.half(t), :] for k in range(4)], axis=1)
            return dot(mine, r.full_out[...].reshape(D, D))

        middle, feed, final = forward_stages(r, who, projected, second, spread)

        def middle_out(t):
            middle(t)
            r.flush.unit_one.copy(who.half(t), t).start()

        def feed_out(t):
            feed(t)
            for flush in (r.flush.hidden, r.flush.slope, r.flush.spread_full):
                flush.copy(who.chunk(t), t).start()

        def close(t):
            _, _, result = final(t)
            r.flush.unit_two.copy(who.half(t), t).start()
            last.give(t, result)

        def next_project(t):
            value = (dot(last.take(t), r.next_proj[...]) + next_bias).astype(BF)
            r.query[who.chunk(t), :] = value[:, :width]
            r.pair[who.chunk(t), :] = value[:, width:]
            halo.send(t)
            r.flush.last_full.copy(who.chunk(t), t).start()

        run_stages(
            chunks,
            [
                (2, second.add),
                (4, close),
                (0, middle_out),
                (8, next_project),
                (1, feed_out),
            ],
            ticks,
        )
        finish_all(chunks, (second, spread, last))
        halo.arrive()
        share.finish()
        wide_up.arrive()
        halo.finish()
        for engine in (wide_attn, wide_up, wide_down):
            engine.finish()

        def written(t, carry):
            for flush in (r.flush.hidden, r.flush.slope, r.flush.spread_full, r.flush.last_full):
                flush.copy(who.chunk(t), t).wait()
            for flush in (r.flush.unit_one, r.flush.unit_two):
                flush.copy(who.half(t), t).wait()
            return carry

        lax.fori_loop(0, chunks, written, 0)

    outputs = forward_small(rows)
    outputs.update(
        query=((rows, width), BF),
        pair=((rows, 2 * width), BF),
        full_attn=((count, block, 4 * width), BF),
        next_out=((4, width, D), BF),
        full_up=((count, block, units), BF),
        full_down=((count, block, units), BF),
        left=((2 * WIN, 2 * width), BF),
        right=((2 * WIN, 2 * width), BF),
    )
    flushed = forward_refs(rows, width, units)
    flushed.update(spread_full=((rows, D), BF), last_full=((rows, D), BF))
    scratch = dict(
        normed=pltpu.VMEM((rows // 2, D), F32),
        next_proj=pltpu.VMEM((D, 3 * width), BF),
        **share_scratch(),
    )
    scratch.update(prefixed("second", exchange_scratch(rows)))
    for key in ("spread", "last"):
        for part in ("sent", "came"):
            scratch[key + "_" + part] = pltpu.SemaphoreType.DMA((chunks,))
    for key in ("ga", "gu", "gd"):
        scratch.update(prefixed(key, gather_sems(lines)))
    scratch.update(prefixed("halo", halo_scratch(2 * WIN // CHUNK)))
    return run_kernel(
        body,
        "middle_forward",
        dict(shared=shared, split=split_biases),
        outputs,
        scratch,
        collective=1,
        flops=2 * rows * D * (4 * width + 2 * units),
        late=dict(
            next_attn=attn_weights,
            next_ffn=ffn_weights,
            full_out=full_out,
            gathered=gathered,
            residual=residual,
            ffn_up=ffn_up,
            ffn_down=ffn_down,
        ),
        flushed=flushed,
        pieces=chunks,
    )


def turning(mixed, first_mixed, out_proj, attn, ffn_up, ffn_down, residual, shared, split_biases, cotangent, turn):
    rows, width = mixed.shape
    units = ffn_up.shape[1]
    chunks = rows // WIDE_CHUNK

    def body(r):
        who = Partners(size=WIDE_CHUNK)
        r.base, r.grad_one = 6, None
        second, third = Exchange(who, pick(r, "second")), Exchange(who, pick(r, "third"))
        heads = HeadExchange(who, r.mixed, r.gathered, r.heads_sent, r.heads_came)
        spread = Gather(who, pick(r, "spread"))
        ends = Gather(who, pick(r, "ends"))
        mids = Gather(who, SimpleNamespace(full=r.grad_low, sent=r.mids_sent, came=r.mids_came))
        out = Gather(who, SimpleNamespace(full=r.output, sent=r.out_sent, came=r.out_came))
        who.meet()
        r.late.mixed.wait()
        for t in range(chunks // 2, chunks):
            heads.give(t)
        r.late.first_mixed.wait()
        r.gathered[:, : rows // 4, :] = r.first_mixed[...]
        r.late.full_out.wait()
        r.late.attn.wait()
        r.out_proj[...] = r.attn[:, 3 * width :]
        r.hidden_bias = r.split[1][:, 2 * width :]
        clear(r.vectors, r.units, r.sum_up, r.sum_down, r.sum_out)

        def projected(t):
            @pl.when(t >= chunks // 2)
            def _():
                heads.take(t)

            mine = jnp.concatenate([r.gathered[k, who.half(t), :] for k in range(4)], axis=1)
            return dot(mine, r.full_out[...].reshape(D, D))

        middle, feed, final = forward_stages(r, who, projected, second, spread)
        enter, feed_back, leave, project_back = backward_stages(r, who, ends, third, mids)

        ticks = [(0, r.late.residual.wait), (1, r.late.ffn_up.wait), (1, r.late.ffn_down.wait)]
        ticks += [(4, r.late.cotangent.wait), (4, r.late.turn.wait)]

        def close(t):
            unit, inverse, result = final(t)
            grad = dot(r.cotangent[who.own(t), :], r.turn[...])
            enter(t, grad, unit, inverse)
            out.give(t, result)

        run_stages(
            chunks,
            [
                (6, third.add),
                (2, second.add),
                (8, leave),
                (4, close),
                (0, middle),
                (9, project_back),
                (5, feed_back),
                (1, feed),
            ],
            ticks,
        )

        def arrive(t, carry):
            out.wait(t)
            return carry

        lax.fori_loop(0, chunks, arrive, 0)
        finish_all(chunks, (second, third, spread, ends, mids, out))
        for t in range(chunks // 2, chunks):
            heads.finish(t)
        r.up[...] = r.sum_up[...].astype(BF)
        r.down[...] = r.sum_down[...].astype(BF)
        r.proj[...] = r.sum_out[...].astype(BF)

    outputs = dict(
        output=((rows, D), BF),
        up=((D, units), BF),
        down=((D, units), BF),
        proj=((D, width), BF),
        grad_low=((rows, D), BF),
        grad_mixed=((rows, width), BF),
        vectors=((8, D), F32),
        units=((8, units), F32),
    )
    scratch = dict(
        normed=pltpu.VMEM((rows // 2, D), F32),
        kept=pltpu.VMEM((rows // 2, D), F32),
        grad_pre=pltpu.VMEM((2 * WIDE_CHUNK, units), BF),
        out_proj=pltpu.VMEM((D, width), BF),
        gathered=pltpu.VMEM((4, rows // 2, width), BF),
        heads_sent=pltpu.SemaphoreType.DMA((3, chunks)),
        heads_came=pltpu.SemaphoreType.DMA((3, chunks)),
        sum_up=pltpu.VMEM((D, units), F32),
        sum_down=pltpu.VMEM((D, units), F32),
        sum_out=pltpu.VMEM((D, width), F32),
        mids_sent=pltpu.SemaphoreType.DMA((chunks,)),
        mids_came=pltpu.SemaphoreType.DMA((chunks,)),
        out_sent=pltpu.SemaphoreType.DMA((chunks,)),
        out_came=pltpu.SemaphoreType.DMA((chunks,)),
    )
    for key, (shape, dtype) in {**forward_refs(rows, width, units), **forward_small(rows)}.items():
        scratch[key] = pltpu.VMEM(shape, dtype)
    for key in ("second", "third"):
        scratch.update(prefixed(key, exchange_scratch(rows)))
    for key in ("spread", "ends"):
        scratch.update(prefixed(key, gather_scratch(rows)))
    return run_kernel(
        body,
        "turning",
        dict(
            shared=shared,
            split=split_biases,
        ),
        outputs,
        scratch,
        collective=2,
        flops=2 * rows * D * (3 * width + 6 * units),
        late=dict(
            mixed=mixed,
            first_mixed=first_mixed,
            full_out=out_proj,
            attn=attn,
            residual=residual,
            ffn_up=ffn_up,
            ffn_down=ffn_down,
            cotangent=cotangent,
            turn=turn,
        ),
    )


def projection_back_stage(r, who, column, exchange):
    rows, width = r.grad_query.shape
    rim = r.out_right.shape[0]
    first, last = column.index == 0, column.index == column.count - 1
    after = (lax.rem(column.index + 1, column.count), column.here)
    copy = copy_to(r.out_right, r.from_left, r.halo_sent.at[0], r.halo_came.at[0], after)

    def begin():
        r.grad_pair[...] = r.grad_own[...]

        @pl.when(jnp.logical_not(last))
        def _():
            copy.start()

    def absorb():
        @pl.when(jnp.logical_not(first))
        def _():
            copy.wait_recv()
            where = pl.ds(0, rim)
            total = r.grad_pair[where, :].astype(F32) + r.from_left[...].astype(F32)
            r.grad_pair[where, :] = total.astype(BF)

    def end():
        @pl.when(jnp.logical_not(last))
        def _():
            copy.wait_send()

    def stage(k):
        both = who.two_chunks(2 * k + 1)
        parts = jnp.concatenate([r.grad_query[both, :], r.grad_pair[both, :]], axis=1)
        exchange.r.part[both, :] = dot_nt(parts, r.next_attn[:, : 3 * width]).astype(BF)
        for t in (2 * k, 2 * k + 1):
            exchange.core_copy(t).start()
        r.sum_three[...] += dot_tn(r.low[both, :], parts)
        r.biases[0:1, :] += column_sum(parts.astype(F32))

    half = rows // CHUNK // 2
    steps = [(0 if k < half // 2 else half, k) for k in range(half)]
    ticks = [(half, absorb)] + [(first_time + k % (half // 2), lambda k=k: stage(k)) for first_time, k in steps]
    return begin, end, ticks


def projection_back_scratch(rows, rim, width):
    return dict(
        grad_pair=pltpu.VMEM((rows, 2 * width), BF),
        from_left=pltpu.VMEM((rim, 2 * width), BF),
        halo_sent=pltpu.SemaphoreType.DMA((1,)),
        halo_came=pltpu.SemaphoreType.DMA((1,)),
        sum_three=pltpu.VMEM((D, 3 * width), F32),
    )


def scatter_three(column, r, totals):
    return (
        ScatterPairs(column, SimpleNamespace(grads=r.above_up, **vars(pick(r, "ru"))), totals[0]),
        ScatterBlocks(column, SimpleNamespace(grads=r.above_down, **vars(pick(r, "rd"))), totals[1]),
        ScatterBlocks(column, SimpleNamespace(grads=r.packed, **vars(pick(r, "ra"))), totals[2]),
    )


def scatter_three_scratch(count, width, units):
    lines, block = count // 2, D // count
    scratch = dict(packed=pltpu.VMEM((count, block, 4 * width), BF))
    scratch.update(prefixed("ru", scatter_pairs_scratch(lines, block, units)))
    scratch.update(prefixed("rd", scatter_scratch(lines, block, units)))
    scratch.update(prefixed("ra", scatter_scratch(lines, block, 4 * width, held=False)))
    return scratch


def pack_attention(r):
    both = jnp.concatenate([r.sum_three[...].astype(BF), r.above_proj[...]], axis=1)
    r.packed[...] = both.reshape(r.packed.shape)


def middle_backward(back, next_attn, grad_above, low, saved, mixed, attn, ffn_up, ffn_down, shared, above, count):
    rows, width = mixed.shape
    units = ffn_up.shape[1]
    chunks = rows // CHUNK
    block = D // count
    rim = back.out_right.shape[0]

    def body(r):
        who = Partners(chunks, chunks // 2)
        r.base = 0
        zeroth, third = Exchange(who, pick(r, "zeroth")), Exchange(who, pick(r, "third"))
        ends, mids = Gather(who, pick(r, "ends")), Gather(who, pick(r, "mids"))
        column = Column(count)
        who.meet(column)
        up, down, three = scatter_three(column, r, (r.up_total, r.down_total, r.attn_total))
        begin, end, back_ticks = projection_back_stage(r, who, column, zeroth)
        for copy in (r.late.out_right, r.late.grad_own, r.late.grad_query, r.late.next_attn, r.late.low):
            copy.wait()
        begin()
        up.start()
        down.start()

        def start_three():
            pack_attention(r)
            three.start()

        ticks = [tick for engine, times in zip((up, down, three), BACK_TIMES) for tick in engine.ticks(times)]
        ticks += [(chunks // 2 + 2, start_three)]
        ticks += [(3, r.late.unit_two.wait), (3, r.late.grad_above.wait), (4, r.late.ffn_up.wait)]
        ticks += [(4, r.late.ffn_down.wait), (4, r.late.slope.wait), (4, r.late.hidden.wait)]
        ticks += [(4, r.late.spread_full.wait), (7, r.late.unit_one.wait), (8, r.late.mixed.wait)]
        ticks = back_ticks + ticks
        r.late.attn.wait()
        r.out_proj[...] = r.attn[:, 3 * width :]
        clear(r.vectors, r.units, r.biases, r.sum_up, r.sum_down, r.sum_out, r.sum_three)
        enter, feed_back, leave, project_back = backward_stages(r, who, ends, third, mids)

        def start(t):
            half = who.half(t)
            enter(t, r.grad_above[who.own(t), :].astype(F32) + zeroth.take(t), r.unit_two[half, :], r.inverse_two[half, 0:1])

        run_stages(
            chunks,
            [
                (5, third.add),
                (1, zeroth.add),
                (7, leave),
                (3, start),
                (8, project_back),
                (4, feed_back),
            ],
            ticks,
        )
        finish_all(chunks, (zeroth, third, ends, mids))
        end()
        r.up[...] = r.sum_up[...].astype(BF)
        r.down[...] = r.sum_down[...].astype(BF)
        r.proj[...] = r.sum_out[...].astype(BF)
        for engine in (up, down, three):
            engine.finish()

    outputs = dict(
        up=((D, units), BF),
        down=((D, units), BF),
        proj=((D, width), BF),
        grad_one=((rows // 2, D), F32),
        grad_mixed=((rows, width), BF),
        vectors=((8, D), F32),
        units=((8, units), F32),
        biases=((8, 3 * width), F32),
        up_total=((block, units), F32),
        down_total=((block, units), F32),
        attn_total=((block, 4 * width), F32),
    )
    scratch = dict(
        kept=pltpu.VMEM((rows // 2, D), F32),
        grad_pre=pltpu.VMEM((2 * CHUNK, units), BF),
        out_proj=pltpu.VMEM((D, width), BF),
        sum_up=pltpu.VMEM((D, units), F32),
        sum_down=pltpu.VMEM((D, units), F32),
        sum_out=pltpu.VMEM((D, width), F32),
    )
    scratch.update(projection_back_scratch(rows, rim, width))
    scratch.update(scatter_three_scratch(count, width, units))
    for key in ("zeroth", "third"):
        scratch.update(prefixed(key, exchange_scratch(rows)))
    for key in ("ends", "mids"):
        scratch.update(prefixed(key, gather_scratch(rows)))
    return run_kernel(
        body,
        "middle_backward",
        dict(
            inverse_one=saved.inverse_one,
            inverse_two=saved.inverse_two,
            shared=shared,
            above_up=above.up.reshape(count, block, units),
            above_down=above.down.reshape(count, block, units),
            above_proj=above.proj,
        ),
        outputs,
        scratch,
        collective=3,
        flops=2 * rows * D * (8 * width + 4 * units),
        in_hbm=("above_up", "above_down"),
        late=dict(
            out_right=back.out_right,
            grad_own=back.out_own,
            grad_query=back.out_query,
            next_attn=next_attn,
            low=low,
            attn=attn,
            unit_two=saved.unit_two,
            grad_above=grad_above,
            ffn_down=ffn_down,
            slope=saved.slope,
            ffn_up=ffn_up,
            hidden=saved.hidden,
            spread_full=saved.spread_full,
            unit_one=saved.unit_one,
            mixed=mixed,
        ),
    )


class SmallSum:
    def __init__(self, who, column, refs):
        self.who, self.c, self.r = who, column, refs

    def copy(self, slot, source, device):
        r = self.r
        return copy_to(r.kept.at[source], r.came.at[slot], r.sent_sem.at[slot], r.came_sem.at[slot], device)

    def core_copy(self):
        return self.copy(0, 0, self.who.sibling)

    def pair_copy(self):
        return self.copy(1, 1, self.c.at(self.c.outer, 1 - self.c.inner))

    def line_copy(self, target, slot):
        c, r = self.c, self.r
        return copy_to(
            r.kept.at[2], r.came.at[2 + slot], r.sent_sem.at[2 + target], r.came_sem.at[2 + slot], c.at(target, c.inner)
        )

    def second(self, both):
        r = self.r
        self.core_copy().wait_recv()
        row = lax.broadcasted_iota(jnp.int32, r.kept.shape[1:], 0)
        r.kept[1] = r.kept[0] + jnp.where(row < both, r.came[0], 0.0)
        self.pair_copy().start()

    def third(self):
        r, c = self.r, self.c
        self.pair_copy().wait_recv()
        r.kept[2] = r.kept[1] + r.came[1]
        for k in range(1, c.lines):
            self.line_copy(c.turn(k), c.outer).start()
        r.came[2 + c.outer] = r.kept[2]

    def result(self):
        r, c = self.r, self.c
        for k in range(1, c.lines):
            source = c.turn(k)
            self.line_copy(source, source).wait_recv()
        return sum(r.came[2 + k] for k in range(c.lines))

    def finish(self):
        c = self.c
        self.core_copy().wait_send()
        self.pair_copy().wait_send()
        for k in range(1, c.lines):
            self.line_copy(c.turn(k), c.outer).wait_send()


def small_scratch(lines, shape):
    return dict(
        kept=pltpu.VMEM((3,) + shape, F32),
        came=pltpu.VMEM((2 + lines,) + shape, F32),
        sent_sem=pltpu.SemaphoreType.DMA((2 + lines,)),
        came_sem=pltpu.SemaphoreType.DMA((2 + lines,)),
    )


class NormSum:
    def __init__(self, who, column, refs):
        self.who, self.c, self.r = who, column, refs

    def mp_copy(self, device, target, slot):
        r = self.r
        return copy_to(r.mp_came.at[slot], r.mp_came.at[slot], r.mp_sent.at[target], r.mp_sem.at[slot], device)

    def seq_copy(self, device, target, slot):
        r = self.r
        return copy_to(r.seq_came.at[slot], r.seq_came.at[slot], r.seq_sent.at[target], r.seq_sem.at[slot], device)

    def run(self, value):
        who, c, r = self.who, self.c, self.r
        here = c.here
        r.mp_came[here] = jnp.full((8, 128), 1.0, F32) * value
        for k in range(1, 4):
            target = lax.rem(here + k, 4)
            self.mp_copy((c.index, target), target, here).start()
        for k in range(1, 4):
            source = lax.rem(here + k, 4)
            self.mp_copy((c.index, source), source, source).wait_recv()
        r.seq_came[c.index] = sum(r.mp_came[k] for k in range(4))
        for k in range(1, c.count):
            target = lax.rem(c.index + k, c.count)
            self.seq_copy((target, here), target, c.index).start()
        for k in range(1, c.count):
            source = lax.rem(c.index + k, c.count)
            self.seq_copy((source, here), source, source).wait_recv()
        total = sum(r.seq_came[k] for k in range(c.count))
        for k in range(1, 4):
            target = lax.rem(here + k, 4)
            self.mp_copy((c.index, target), target, here).wait_send()
        for k in range(1, c.count):
            target = lax.rem(c.index + k, c.count)
            self.seq_copy((target, here), target, c.index).wait_send()
        return total


def norm_scratch(count):
    return dict(
        mp_came=pltpu.VMEM((4, 8, 128), F32),
        mp_sent=pltpu.SemaphoreType.DMA((4,)),
        mp_sem=pltpu.SemaphoreType.DMA((4,)),
        seq_came=pltpu.VMEM((count, 8, 128), F32),
        seq_sent=pltpu.SemaphoreType.DMA((count,)),
        seq_sem=pltpu.SemaphoreType.DMA((count,)),
    )


def squares(ref):
    value = ref[...]
    return jnp.sum(value * value)


def ending(back, next_attn, grad_above, low, above, top, count):
    rows, width = back.out_query.shape
    chunks = rows // CHUNK
    lines, block = count // 2, D // count
    units = above.units.shape[1]
    rim = back.out_right.shape[0]

    def body(r):
        who = Partners(chunks, chunks // 2)
        zeroth = Exchange(who, pick(r, "zeroth"))
        out = Gather(who, SimpleNamespace(full=r.output, sent=r.out_sent, came=r.out_came))
        column = Column(count)
        who.meet(column)
        up, down, three = scatter_three(column, r, (r.ffn_grads.at[0], r.ffn_grads.at[1], r.attn_grads.at[0]))
        small = SmallSum(who, column, pick(r, "small"))
        begin, end, back_ticks = projection_back_stage(r, who, column, zeroth)
        for copy in (r.late.out_right, r.late.grad_own, r.late.grad_query, r.late.next_attn, r.late.low):
            copy.wait()
        begin()
        up.start()
        down.start()

        def start_three():
            pack_attention(r)
            three.start()
            r.small_kept[0, 0:6, :] = r.vectors_low[0:6, :]
            r.small_kept[0, 6:12, :] = r.vectors_top[0:6, :]
            r.small_kept[0, 12:13, :] = r.units_low[0:1, :]
            r.small_kept[0, 13:14, :] = r.units_top[0:1, :]
            pieces = []
            for ref in (r.biases, r.biases_top):
                pieces += [ref[0:1, :width], ref[0:1, 2 * width :]]
            r.small_kept[0, 14:15, :] = jnp.concatenate(pieces, axis=1)
            r.small_kept[0, 15:16, :] = jnp.zeros((1, D), F32)
            small.core_copy().start()

        ticks = [tick for engine, times in zip((up, down, three), END_TIMES) for tick in engine.ticks(times)]
        ticks += [(chunks // 2 + 2, start_three), (3, r.late.grad_above.wait)]
        ticks += [(SMALL_TIMES[0], lambda: small.second(12)), (SMALL_TIMES[1], small.third)]
        ticks = back_ticks + ticks
        clear(r.biases, r.sum_three)

        def close(t):
            out.give(t, r.grad_above[who.half(t), :] + zeroth.take(t))

        run_stages(chunks, [(1, zeroth.add), (3, close)], ticks)
        vectors = small.result()
        r.vectors[...] = vectors
        r.ffn_grads[2] = r.up_top[...]
        r.ffn_grads[3] = r.down_top[...]
        r.attn_grads[1] = r.attn_top[...]
        row = lax.broadcasted_iota(jnp.int32, (16, D), 0)
        squared = vectors * vectors
        split = jnp.sum(jnp.where(row >= 12, squared, 0.0))
        shared = jnp.sum(jnp.where(row < 12, squared, 0.0))
        first_seq = column.index == 0
        first_both = jnp.logical_and(first_seq, column.here == 0)
        value = squares(r.ffn_grads) + squares(r.attn_grads)
        value = value + jnp.where(first_seq, split, 0.0) + jnp.where(first_both, shared, 0.0)
        total = NormSum(who, column, pick(r, "norm")).run(value)
        r.norm[...] = jnp.sqrt(total)

        def arrive(t, carry):
            out.wait(t)
            return carry

        lax.fori_loop(0, chunks, arrive, 0)
        finish_all(chunks, (zeroth, out))
        end()
        for engine in (up, down, three, small):
            engine.finish()

    outputs = dict(
        output=((rows, D), BF),
        ffn_grads=((4, block, units), F32),
        attn_grads=((2, block, 4 * width), F32),
        vectors=((16, D), F32),
        norm=((8, 128), F32),
    )
    scratch = dict(
        biases=pltpu.VMEM((8, 3 * width), F32),
        out_sent=pltpu.SemaphoreType.DMA((chunks,)),
        out_came=pltpu.SemaphoreType.DMA((chunks,)),
    )
    scratch.update(projection_back_scratch(rows, rim, width))
    scratch.update(scatter_three_scratch(count, width, units))
    scratch.update(prefixed("zeroth", exchange_scratch(rows)))
    scratch.update(prefixed("small", small_scratch(lines, (16, D))))
    scratch.update(prefixed("norm", norm_scratch(count)))
    return run_kernel(
        body,
        "ending",
        dict(
            above_up=above.up.reshape(count, block, units),
            above_down=above.down.reshape(count, block, units),
            above_proj=above.proj,
            up_top=above.up_total,
            down_top=above.down_total,
            attn_top=above.attn_total,
            vectors_low=above.vectors,
            vectors_top=top.vectors,
            units_low=above.units,
            units_top=top.units,
            biases_top=above.biases,
        ),
        outputs,
        scratch,
        collective=4,
        flops=2 * rows * D * 6 * width,
        in_hbm=("above_up", "above_down"),
        late=dict(
            out_right=back.out_right,
            grad_own=back.out_own,
            grad_query=back.out_query,
            next_attn=next_attn,
            low=low,
            grad_above=grad_above,
        ),
    )


def moments(grad, first, second):
    first_new = BETA_FIRST * first + (1.0 - BETA_FIRST) * grad
    second_new = BETA_SECOND * second + (1.0 - BETA_SECOND) * grad * grad
    size = jnp.sqrt(second_new / (1.0 - BETA_SECOND**STEP)) + ADAM_EPSILON
    return first_new, second_new, first_new / (1.0 - BETA_FIRST**STEP) / size


def update(result, end, turn, attn, ffn, split, shared):
    block, units = ffn[0].shape[2:]
    width = attn[0].shape[3]
    rates = [0.5 * D ** (-0.5)] * 3 + [0.5 * (WIN / D) ** 0.5]
    names = ("weights", "first", "second", "average", "basis")

    def matrix(grad, weight, first, second, average, basis, rate):
        basis = basis.astype(BF)
        turned = dot(grad.astype(BF), basis)
        first_new, second_new, direction = moments(turned, first, second)
        back = dot_nt(direction.astype(BF), basis)
        weight_new = weight - rate * (back + DECAY_RATE * weight)
        return weight_new, first_new, second_new, AVERAGE_RATE * average + (1.0 - AVERAGE_RATE) * weight_new

    def body(r):
        step = pl.program_id(0)
        factor = CLIP_LEVEL / jnp.maximum(r.norm[0:1, 0:1], CLIP_LEVEL)
        r.result_real[...] = dot_nt(r.result[...], r.turn[...])
        r.grad_real[...] = dot_nt(r.grad[...], r.turn[...])
        rate = jnp.where(step % 2 == 0, 0.5 * D ** (-0.5), 0.5 * FF ** (-0.5))
        results = matrix(
            factor * r.ffn_grads[...],
            r.ffn_weights[...],
            r.ffn_first[...],
            r.ffn_second[...],
            r.ffn_average[...],
            r.ffn_basis[...],
            rate,
        )
        for key, value in zip(names, results):
            getattr(r, "ffn_" + key + "_new")[...] = value

        for at in range(4):

            @pl.when(step == at)
            def _(at=at):
                layer = at // 2
                for which in (2 * (at % 2), 2 * (at % 2) + 1):
                    grad = factor * r.attn_grads[layer, :, which * width : (which + 1) * width]
                    weight, first, second, average = matrix(
                        grad,
                        r.attn_weights[layer, which],
                        r.attn_first[layer, which],
                        r.attn_second[layer, which],
                        r.attn_average[layer, which],
                        r.attn_basis[layer, which, 0, 0],
                        rates[which],
                    )
                    r.attn_weights_new[layer, which] = weight
                    r.attn_first_new[layer, which] = first
                    r.attn_average_new[layer, which] = average
                    if which < 3:
                        r.attn_second_new[layer, which] = second
                    else:
                        r.projection_second[layer] = second

        @pl.when(step == 0)
        def _():
            r.norm_out[0, 0] = jnp.max(r.norm[0:1, :])
            real = exact(r.vectors[...], lambda part: dot_nt(part, r.turn[...]))
            for layer in range(2):
                tail = r.vectors[14:15, layer * 2 * width : (layer + 1) * 2 * width]
                split_grad = jnp.concatenate([tail, r.vectors[12 + layer : 13 + layer, :]], axis=1)
                grad = factor * split_grad
                first_new, second_new, direction = moments(grad, r.split_first[layer], r.split_second[layer])
                r.split_old_new[layer] = r.split_old[layer] - VECTOR_RATE * direction
                r.split_first_new[layer] = first_new
                r.split_second_new[layer] = second_new
            for k in range(6):
                grad = factor * jnp.concatenate([real[k : k + 1], real[6 + k : 7 + k]], axis=0)
                first_new, second_new, direction = moments(grad, r.shared_first[k], r.shared_second[k])
                r.shared_old_new[k] = r.shared_old[k] - VECTOR_RATE * direction
                r.shared_first_new[k] = first_new
                r.shared_second_new[k] = second_new

    inputs = dict(
        ffn_grads=end.ffn_grads, attn_grads=end.attn_grads, vectors=end.vectors, norm=end.norm, turn=turn
    )
    rows = result.shape[0]
    inputs.update(result=result, grad=end.output)
    outputs = dict(result_real=((rows, D), F32), grad_real=((rows, D), F32))
    row_spec = pl.BlockSpec((rows // 4, D), lambda i: (i, 0))
    specs = dict(result=row_spec, grad=row_spec, result_real=row_spec, grad_real=row_spec)
    specs["ffn_grads"] = pl.BlockSpec((None, block, units), lambda i: (i, 0, 0))
    matrix_spec = pl.BlockSpec((None, None, block, units), lambda i: (i // 2, i % 2, 0, 0))
    for key, array in zip(names, ffn):
        inputs["ffn_" + key] = array
        specs["ffn_" + key] = matrix_spec
    specs["ffn_basis"] = pl.BlockSpec((None, None, None, None, units, units), lambda i: (i // 2, i % 2, 0, 0, 0, 0))
    for key, array in zip(names, attn):
        inputs["attn_" + key] = array
    for prefix, group in (("split", split), ("shared", shared)):
        for key, array in zip(("old", "first", "second"), group):
            inputs[prefix + "_" + key] = array
    for key in ("weights", "first", "second", "average"):
        outputs["ffn_" + key + "_new"] = (ffn[0].shape, F32)
        specs["ffn_" + key + "_new"] = matrix_spec
        outputs["attn_" + key + "_new"] = (attn[0].shape, F32)
    outputs["attn_second_new"] = ((2, 3, block, width), F32)
    outputs["projection_second"] = ((2, block, width), F32)
    for prefix, group in (("split", split), ("shared", shared)):
        for key in ("old", "first", "second"):
            outputs[prefix + "_" + key + "_new"] = (group[0].shape, F32)
    outputs["norm_out"] = ((1, 1), F32)
    return run_kernel(
        body,
        "update",
        inputs,
        outputs,
        {},
        flops=4 * block * units * units * 4,
        grid=(4,),
        specs=specs,
        in_smem=("norm_out",),
    )


def direct(
    activations,
    cotangent,
    segments,
    dilated_heads,
    owners,
    attn_weights,
    attn_first,
    attn_second,
    attn_average,
    attn_basis,
    ffn_weights,
    ffn_first,
    ffn_second,
    ffn_average,
    ffn_basis,
    split_biases,
    split_first,
    split_second,
    shared_vectors,
    shared_first,
    shared_second,
):
    count = lax.axis_size(SEQ)
    near = opening(
        activations, segments, owners, attn_weights, ffn_weights, split_biases, shared_vectors, count
    )
    near.arranged = near.out
    attn_zero, up_zero, down_zero = (
        full.reshape(D, -1) for full in (near.full_attn, near.full_up, near.full_down)
    )
    mid = middle_forward(
        near.gathered,
        near.full_out,
        up_zero,
        down_zero,
        near.low,
        near.shared,
        split_biases,
        attn_weights,
        ffn_weights,
        count,
    )
    far = attend(
        mid.query,
        mid.pair,
        mid.left,
        mid.right,
        near.seg_query,
        near.seg_keys,
        dilated_heads,
    )
    attn_one, up_one, down_one = (full.reshape(D, -1) for full in (mid.full_attn, mid.full_up, mid.full_down))
    top = turning(
        far.out, far.first, mid.next_out, attn_one, up_one, down_one, mid.last_full, near.shared, split_biases, cotangent, near.turn
    )
    far_back = attend_back(far, top.grad_mixed, dilated_heads, 2 * WIN, True, count, 6)
    low = middle_backward(
        far_back,
        attn_one,
        top.grad_low,
        mid.last_full,
        mid,
        near.out,
        attn_zero,
        up_zero,
        down_zero,
        near.shared,
        top,
        count,
    )
    near_back = attend_back(near, low.grad_mixed, dilated_heads, WIN, False, count, 7)
    end = ending(near_back, attn_zero, low.grad_one, near.low, low, top, count)
    new = update(
        top.output,
        end,
        near.turn,
        (attn_weights, attn_first, attn_second, attn_average, attn_basis),
        (ffn_weights, ffn_first, ffn_second, ffn_average, ffn_basis),
        (split_biases, split_first, split_second),
        tuple(array.transpose(1, 0, 2) for array in (shared_vectors, shared_first, shared_second)),
    )
    return (
        new.result_real,
        new.grad_real,
        new.attn_weights_new,
        new.attn_first_new,
        new.attn_second_new,
        new.projection_second,
        new.attn_average_new,
        new.ffn_weights_new,
        new.ffn_first_new,
        new.ffn_second_new,
        new.ffn_average_new,
        new.split_old_new,
        new.split_first_new,
        new.split_second_new,
        new.shared_old_new.transpose(1, 0, 2),
        new.shared_first_new.transpose(1, 0, 2),
        new.shared_second_new.transpose(1, 0, 2),
        new.norm_out.reshape(()),
    )


def with_halo(cells, sides, width):
    for axis, dim in sides:
        count = lax.axis_size(axis)
        ends = count - 1
        head = lax.slice_in_dim(cells, 0, width, axis=dim)
        tail = lax.slice_in_dim(cells, cells.shape[dim] - width, cells.shape[dim], axis=dim)
        cells = jnp.concatenate(
            [
                lax.ppermute(tail, axis, [(i, (i + 1) % count) for i in range(ends)]),
                cells,
                lax.ppermute(head, axis, [((i + 1) % count, i) for i in range(ends)]),
            ],
            axis=dim,
        )
    return cells


def from_behind(block, axis, distance):
    devices = range(lax.axis_size(axis))
    route = [(i - distance, i) for i in devices if i - distance in devices]
    return lax.ppermute(block, axis, route)


def normalize_layer(values, gain, shift):
    center = values - jnp.mean(values, axis=-1, keepdims=True)
    spread = jnp.mean(center * center, axis=-1, keepdims=True)
    return center * lax.rsqrt(spread + NORM_EPSILON) * gain + shift


def head_masks(offsets, dilated):
    near = jnp.abs(offsets) <= WIN
    far = jnp.logical_and(jnp.abs(offsets) <= 2 * WIN, offsets % 2 == 0)
    return jnp.where(dilated[:, None, None], far[None, :, :], near[None, :, :])


def join_heads(term):
    return lax.psum(term.astype(jnp.bfloat16), MP).astype(jnp.float32)


def join_grads(term):
    return lax.psum(term, MP)


def fetch_rims(pair, rim_width):
    return with_halo(pair, ((SEQ, 0),), rim_width)


def masked_scores(query_block, key_block, seg_query, seg_keys, dilated, rim_width):
    block_rows = query_block.shape[0]
    key_rows = key_block.shape[0]
    offsets = (
        jnp.arange(block_rows, dtype=jnp.int32)[:, None]
        - jnp.arange(key_rows, dtype=jnp.int32)[None, :]
        + rim_width
    )
    allowed = jnp.logical_and(
        head_masks(offsets, dilated), (seg_query[:, None] == seg_keys[None, :])[None, :, :]
    )
    raw = jnp.einsum(
        "qhd,khd->hqk", query_block, key_block, preferred_element_type=jnp.float32
    ) * DH ** (-0.5)
    return jnp.where(allowed, raw, MASK_FILL)


def plain_attend(query, key_pad, value_pad, seg_own, seg_near, dilated, rim_width):
    row_count = query.shape[0]
    block_rows = min(512, row_count)
    key_rows = block_rows + 2 * rim_width

    def one_block(first_row):
        query_block = lax.dynamic_slice_in_dim(query, first_row, block_rows, 0)
        key_block = lax.dynamic_slice_in_dim(key_pad, first_row, key_rows, 0)
        value_block = lax.dynamic_slice_in_dim(value_pad, first_row, key_rows, 0)
        scores = masked_scores(
            query_block,
            key_block,
            lax.dynamic_slice_in_dim(seg_own, first_row, block_rows, 0),
            lax.dynamic_slice_in_dim(seg_near, first_row, key_rows, 0),
            dilated,
            rim_width,
        )
        row_max = jnp.max(scores, axis=2, keepdims=True)
        exponent = jnp.exp(scores - row_max)
        row_total = jnp.sum(exponent, axis=2, keepdims=True)
        softmax = (exponent / row_total).astype(jnp.bfloat16)
        mixed_block = jnp.einsum(
            "hqk,khd->qhd", softmax, value_block, preferred_element_type=jnp.float32
        )
        return (mixed_block, (row_max + jnp.log(row_total))[:, :, 0])

    starts = jnp.arange(row_count // block_rows, dtype=jnp.int32) * block_rows
    mixed_heads, log_totals = lax.map(one_block, starts)
    return (mixed_heads.reshape(row_count, -1), log_totals)


def plain_attend_back(query, padded, log_totals, grad_mixed, seg_own, seg_near, dilated, rim_width):
    row_count, head_count, _ = query.shape
    head_width = head_count * DH
    block_rows = min(512, row_count)
    key_rows = block_rows + 2 * rim_width
    key_pad = padded[:, :head_width].reshape(-1, head_count, DH)
    value_pad = padded[:, head_width:].reshape(-1, head_count, DH)
    grad_heads = grad_mixed.reshape(row_count, head_count, DH)
    score_scale = DH ** (-0.5)

    def one_step(carry, inputs):
        first_row, totals_block = inputs
        query_block = lax.dynamic_slice_in_dim(query, first_row, block_rows, 0)
        key_block = lax.dynamic_slice_in_dim(key_pad, first_row, key_rows, 0)
        value_block = lax.dynamic_slice_in_dim(value_pad, first_row, key_rows, 0)
        grad_block = lax.dynamic_slice_in_dim(grad_heads, first_row, block_rows, 0)
        scores = masked_scores(
            query_block,
            key_block,
            lax.dynamic_slice_in_dim(seg_own, first_row, block_rows, 0),
            lax.dynamic_slice_in_dim(seg_near, first_row, key_rows, 0),
            dilated,
            rim_width,
        )
        softmax = jnp.exp(scores - totals_block[:, :, None])
        grad_value = jnp.einsum(
            "hqk,qhd->khd",
            softmax.astype(jnp.bfloat16),
            grad_block,
            preferred_element_type=jnp.float32,
        )
        grad_soft = jnp.einsum(
            "qhd,khd->hqk", grad_block, value_block, preferred_element_type=jnp.float32
        )
        row_dot = jnp.sum(grad_soft * softmax, axis=2, keepdims=True)
        grad_scores = (softmax * (grad_soft - row_dot)).astype(jnp.bfloat16)
        grad_query = (
            jnp.einsum("hqk,khd->qhd", grad_scores, key_block, preferred_element_type=jnp.float32)
            * score_scale
        )
        grad_key = (
            jnp.einsum("hqk,qhd->khd", grad_scores, query_block, preferred_element_type=jnp.float32)
            * score_scale
        )
        update = jnp.concatenate(
            [grad_key.reshape(key_rows, head_width), grad_value.reshape(key_rows, head_width)],
            axis=1,
        )
        current = lax.dynamic_slice_in_dim(carry, first_row, key_rows, 0)
        carry = lax.dynamic_update_slice_in_dim(carry, current + update, first_row, 0)
        return (carry, grad_query.reshape(block_rows, head_width))

    starts = jnp.arange(row_count // block_rows, dtype=jnp.int32) * block_rows
    initial = jnp.zeros((row_count + 2 * rim_width, 2 * head_width), jnp.float32)
    grad_pad, grad_query = lax.scan(one_step, initial, (starts, log_totals))
    from_above = from_behind(grad_pad[:rim_width], SEQ, -1)
    from_below = from_behind(grad_pad[row_count + rim_width :], SEQ, 1)
    grad_pair = grad_pad[rim_width : row_count + rim_width]
    grad_pair = (
        grad_pair
        + jnp.pad(from_below, ((0, row_count - rim_width), (0, 0)))
        + jnp.pad(from_above, ((row_count - rim_width, 0), (0, 0)))
    )
    return (grad_query.reshape(row_count, head_width), grad_pair)


def layer_forward(inputs, attn, ffn, shared, split, seg_own, seg_pad, dilated, rim_width):
    head_width = attn.shape[2]
    row_count = inputs.shape[0]
    inputs_low = inputs.astype(jnp.bfloat16)
    biases = jnp.stack(
        [
            split[0, :head_width],
            jnp.zeros((head_width,), jnp.float32),
            split[0, head_width : 2 * head_width],
        ]
    )
    projected = (
        jnp.einsum("td,mdc->tmc", inputs_low, attn[:3], preferred_element_type=jnp.float32)
        + biases[None]
    ).astype(jnp.bfloat16)
    query = projected[:, 0].reshape(row_count, -1, DH)
    padded = fetch_rims(jnp.concatenate([projected[:, 1], projected[:, 2]], axis=1), rim_width)
    key_pad = padded[:, :head_width].reshape(-1, head_width // DH, DH)
    value_pad = padded[:, head_width:].reshape(-1, head_width // DH, DH)
    seg_near = lax.slice_in_dim(
        seg_pad, 2 * WIN - rim_width, 2 * WIN + row_count + rim_width, axis=0
    )
    mixed_heads, log_totals = plain_attend(
        query, key_pad, value_pad, seg_own, seg_near, dilated, rim_width
    )
    mixed_heads = mixed_heads.astype(jnp.bfloat16)
    attn_sum = (
        inputs
        + join_heads(
            dot_nt(mixed_heads, attn[3])
        )
        + shared[0]
    )
    normed = normalize_layer(attn_sum, shared[1], shared[2])
    normed_low = normed.astype(jnp.bfloat16)
    pre_gelu = (
        jnp.dot(normed_low, ffn[0], preferred_element_type=jnp.float32) + split[0, 2 * head_width :]
    )
    hidden = jax.nn.gelu(pre_gelu, approximate=False).astype(jnp.bfloat16)
    ffn_sum = (
        normed
        + join_heads(dot_nt(hidden, ffn[1]))
        + shared[3]
    )
    result = normalize_layer(ffn_sum, shared[4], shared[5])
    return (
        result,
        (
            inputs_low,
            query,
            padded,
            log_totals,
            mixed_heads,
            attn_sum,
            normed_low,
            pre_gelu,
            hidden,
            ffn_sum,
        ),
    )


def layer_backward(grad_out, saved, attn, ffn, shared, seg_own, seg_pad, dilated, rim_width):
    (
        inputs_low,
        query,
        padded,
        log_totals,
        mixed_heads,
        attn_sum,
        normed_low,
        pre_gelu,
        hidden,
        ffn_sum,
    ) = saved
    head_width = attn.shape[2]
    row_count = inputs_low.shape[0]
    seg_near = lax.slice_in_dim(
        seg_pad, 2 * WIN - rim_width, 2 * WIN + row_count + rim_width, axis=0
    )
    _, pull_out = jax.vjp(normalize_layer, ffn_sum, shared[4], shared[5])
    grad_ffn_sum, grad_gain_two, grad_shift_two = pull_out(grad_out)
    grad_branch = grad_ffn_sum.astype(jnp.bfloat16)
    grad_down = dot_tn(grad_branch, hidden)
    grad_hidden = jnp.dot(grad_branch, ffn[1], preferred_element_type=jnp.float32)
    _, pull_gelu = jax.vjp(lambda value: jax.nn.gelu(value, approximate=False), pre_gelu)
    grad_pre = pull_gelu(grad_hidden)[0].astype(jnp.bfloat16)
    grad_up = dot_tn(normed_low, grad_pre)
    grad_normed = grad_ffn_sum + join_grads(
        dot_nt(grad_pre, ffn[0])
    )
    _, pull_mid = jax.vjp(normalize_layer, attn_sum, shared[1], shared[2])
    grad_attn_sum, grad_gain_one, grad_shift_one = pull_mid(grad_normed)
    grad_attn_out = grad_attn_sum.astype(jnp.bfloat16)
    grad_out_proj = dot_tn(grad_attn_out, mixed_heads)
    grad_mixed = jnp.dot(grad_attn_out, attn[3], preferred_element_type=jnp.float32).astype(
        jnp.bfloat16
    )
    grad_query, grad_pair = plain_attend_back(
        query, padded, log_totals, grad_mixed, seg_own, seg_near, dilated, rim_width
    )
    grad_proj = jnp.stack(
        [grad_query, grad_pair[:, :head_width], grad_pair[:, head_width:]], axis=1
    ).astype(jnp.bfloat16)
    grad_in_proj = jnp.einsum(
        "td,tmc->mdc", inputs_low, grad_proj, preferred_element_type=jnp.float32
    )
    grad_inputs = grad_attn_sum + join_grads(
        jnp.einsum("tmc,mdc->td", grad_proj, attn[:3], preferred_element_type=jnp.float32)
    )
    proj_sums = jnp.sum(grad_proj.astype(jnp.float32), axis=0)
    split_grad = jnp.concatenate(
        [proj_sums[0], proj_sums[2], jnp.sum(grad_pre.astype(jnp.float32), axis=0)]
    )
    shared_grad = jnp.stack(
        [
            jnp.sum(grad_attn_sum, axis=0),
            grad_gain_one,
            grad_shift_one,
            jnp.sum(grad_ffn_sum, axis=0),
            grad_gain_two,
            grad_shift_two,
        ]
    )
    attn_grad = jnp.concatenate([grad_in_proj, grad_out_proj[None]], axis=0)
    ffn_grad = jnp.stack([grad_up, grad_down])
    return (grad_inputs, attn_grad, ffn_grad, shared_grad, split_grad)


def from_slots(gathered, owners, slot_count):
    layer_count, matrix_count, row_count, col_count = gathered.shape
    blocks = gathered.reshape(
        layer_count, matrix_count, slot_count, row_count // slot_count, col_count
    )
    return jnp.take(blocks, owners, axis=2).reshape(gathered.shape)


def to_slots(grads, inverse, slot_count):
    matrix_count, row_count, col_count = grads.shape
    blocks = grads.reshape(matrix_count, slot_count, row_count // slot_count, col_count)
    return jnp.take(blocks, inverse, axis=1).reshape(grads.shape)


def rotate_update(weight, grad_now, first, second, running_average, basis, rates):
    turn = basis[:, :, 0, 0]
    turned = jnp.einsum("lmre,lmec->lmrc", grad_now, turn, precision=HIGHEST_PRECISION)
    first_new = BETA_FIRST * first + (1.0 - BETA_FIRST) * turned
    second_new = BETA_SECOND * second + (1.0 - BETA_SECOND) * turned * turned
    direction = (
        first_new
        / (1.0 - BETA_FIRST**STEP)
        / (jnp.sqrt(second_new / (1.0 - BETA_SECOND**STEP)) + ADAM_EPSILON)
    )
    back = jnp.einsum("lmrc,lmec->lmre", direction, turn, precision=HIGHEST_PRECISION)
    weight_new = weight - rates[None, :, None, None] * (back + DECAY_RATE * weight)
    average_new = AVERAGE_RATE * running_average + (1.0 - AVERAGE_RATE) * weight_new
    return (weight_new, first_new, second_new, average_new)


def vector_update(current, grad_now, first, second):
    first_new = BETA_FIRST * first + (1.0 - BETA_FIRST) * grad_now
    second_new = BETA_SECOND * second + (1.0 - BETA_SECOND) * grad_now * grad_now
    direction = (
        first_new
        / (1.0 - BETA_FIRST**STEP)
        / (jnp.sqrt(second_new / (1.0 - BETA_SECOND**STEP)) + ADAM_EPSILON)
    )
    return (current - VECTOR_RATE * direction, first_new, second_new)


def with_collectives(
    activations,
    cotangent,
    segments,
    dilated_heads,
    owners,
    attn_weights,
    attn_first,
    attn_second,
    attn_average,
    attn_basis,
    ffn_weights,
    ffn_first,
    ffn_second,
    ffn_average,
    ffn_basis,
    split_biases,
    split_first,
    split_second,
    shared_vectors,
    shared_first,
    shared_second,
):
    slot_count = lax.axis_size(SEQ)
    layer_count = attn_weights.shape[0]
    attn_full, ffn_full = (
        lax.all_gather(attn_weights.astype(jnp.bfloat16), SEQ, axis=2, tiled=True),
        lax.all_gather(ffn_weights.astype(jnp.bfloat16), SEQ, axis=2, tiled=True),
    )
    attn_full = from_slots(attn_full, owners, slot_count)
    ffn_full = from_slots(ffn_full, owners, slot_count)
    seg_pad = with_halo(segments, ((SEQ, 0),), 2 * WIN)
    head_width = attn_full.shape[3]
    head_count = head_width // DH
    heads_here = lax.axis_index(MP) * head_count + jnp.arange(head_count, dtype=jnp.int32)
    head_flags = jnp.any(heads_here[:, None] == dilated_heads[None, :], axis=1)
    current = activations.astype(jnp.float32)
    saved_list = []
    for layer_index in range(layer_count):
        dilated = jnp.logical_and(head_flags, layer_index % 2 == 1)
        rim_width = 2 * WIN if layer_index % 2 == 1 else WIN
        current, saved = layer_forward(
            current,
            attn_full[layer_index],
            ffn_full[layer_index],
            shared_vectors[layer_index],
            split_biases[layer_index],
            segments,
            seg_pad,
            dilated,
            rim_width,
        )
        saved_list.append(saved)
    slot_range = jnp.arange(slot_count, dtype=jnp.int32)
    inverse = jnp.sum(
        jnp.where(owners[None, :] == slot_range[:, None], slot_range[None, :], 0), axis=1
    )
    grad_now = cotangent.astype(jnp.float32)
    attn_list = [None] * layer_count
    ffn_list = [None] * layer_count
    shared_list = [None] * layer_count
    split_list = [None] * layer_count
    for layer_index in range(layer_count - 1, -1, -1):
        dilated = jnp.logical_and(head_flags, layer_index % 2 == 1)
        rim_width = 2 * WIN if layer_index % 2 == 1 else WIN
        grad_now, attn_grad, ffn_grad, shared_grad, split_grad = layer_backward(
            grad_now,
            saved_list[layer_index],
            attn_full[layer_index],
            ffn_full[layer_index],
            shared_vectors[layer_index],
            segments,
            seg_pad,
            dilated,
            rim_width,
        )
        attn_grad = to_slots(attn_grad, inverse, slot_count)
        ffn_grad = to_slots(ffn_grad, inverse, slot_count)
        attn_list[layer_index] = attn_grad
        ffn_list[layer_index] = ffn_grad
        shared_list[layer_index] = shared_grad
        split_list[layer_index] = split_grad[None, :]
    attn_grads = jnp.stack(attn_list)
    ffn_grads = jnp.stack(ffn_list)
    attn_grads, ffn_grads = (
        lax.psum_scatter(attn_grads, SEQ, scatter_dimension=2, tiled=True),
        lax.psum_scatter(ffn_grads, SEQ, scatter_dimension=2, tiled=True),
    )
    shared_grads, split_grads = lax.psum((jnp.stack(shared_list), jnp.stack(split_list)), SEQ)
    first_seq = lax.axis_index(SEQ) == 0
    first_both = jnp.logical_and(first_seq, lax.axis_index(MP) == 0)
    local_sum = jnp.sum(attn_grads * attn_grads) + jnp.sum(ffn_grads * ffn_grads)
    local_sum = (
        local_sum
        + jnp.where(first_seq, jnp.sum(split_grads * split_grads), 0.0)
        + jnp.where(first_both, jnp.sum(shared_grads * shared_grads), 0.0)
    )
    grad_norm = jnp.sqrt(lax.psum(local_sum, (SEQ, MP)))
    factor = CLIP_LEVEL / jnp.maximum(grad_norm, CLIP_LEVEL)
    attn_rates = jnp.array([0.5 * D ** (-0.5)] * 3 + [0.5 * (WIN / D) ** 0.5], jnp.float32)
    ffn_rates = jnp.array([0.5 * D ** (-0.5), 0.5 * FF ** (-0.5)], jnp.float32)
    attn_out = rotate_update(
        attn_weights,
        factor * attn_grads,
        attn_first,
        attn_second,
        attn_average,
        attn_basis,
        attn_rates,
    )
    ffn_out = rotate_update(
        ffn_weights, factor * ffn_grads, ffn_first, ffn_second, ffn_average, ffn_basis, ffn_rates
    )
    split_out = vector_update(split_biases, factor * split_grads, split_first, split_second)
    shared_out = vector_update(shared_vectors, factor * shared_grads, shared_first, shared_second)
    return (
        current,
        grad_now,
        attn_out[0],
        attn_out[1],
        attn_out[2][:, :3],
        attn_out[2][:, 3],
        attn_out[3],
        ffn_out[0],
        ffn_out[1],
        ffn_out[2],
        ffn_out[3],
        split_out[0],
        split_out[1],
        split_out[2],
        shared_out[0],
        shared_out[1],
        shared_out[2],
        grad_norm,
    )


def solution(mesh):
    placed = (
        P(SEQ, None),
        P(SEQ, None),
        P(SEQ),
        P(),
        P(),
        P(None, None, SEQ, MP),
        P(None, None, SEQ, MP),
        P(None, None, SEQ, MP),
        P(None, None, SEQ, MP),
        P(None, None, SEQ, MP, None, None),
        P(None, None, SEQ, MP),
        P(None, None, SEQ, MP),
        P(None, None, SEQ, MP),
        P(None, None, SEQ, MP),
        P(None, None, SEQ, MP, None, None),
        P(None, MP, None),
        P(None, MP, None),
        P(None, MP, None),
        P(),
        P(),
        P(),
    )
    count = mesh.shape[SEQ]
    fits = count % 4 == 0 and (D // count) % 16 == 0 and mesh.shape[MP] == 4
    return jax.shard_map(
        direct if fits else with_collectives,
        mesh=mesh,
        in_specs=placed,
        out_specs=(
            P(SEQ, None),
            P(SEQ, None),
            P(None, None, SEQ, MP),
            P(None, None, SEQ, MP),
            P(None, None, SEQ, MP),
            P(None, SEQ, MP),
            P(None, None, SEQ, MP),
            P(None, None, SEQ, MP),
            P(None, None, SEQ, MP),
            P(None, None, SEQ, MP),
            P(None, None, SEQ, MP),
            P(None, MP, None),
            P(None, MP, None),
            P(None, MP, None),
            P(),
            P(),
            P(),
            P(),
        ),
        check_vma=False,
    )
```

```python
from types import SimpleNamespace

import jax
import jax.numpy as jnp
from jax import lax
from jax.experimental import pallas as pl
from jax.experimental.pallas import tpu as pltpu
from jax.sharding import PartitionSpec as P

D = 768
DH = 64
FF = 3072
WIN = 256
STEP = 10

HIGHEST_PRECISION = lax.Precision.HIGHEST
NORM_EPSILON = 1e-05
MASK_FILL = -1e30
CLIP_LEVEL = 1.0
BETA_FIRST = 0.5
BETA_SECOND = 0.5
ADAM_EPSILON = 1e-08
DECAY_RATE = 0.01
AVERAGE_RATE = 0.7
VECTOR_RATE = 0.3

BF = jnp.bfloat16
SEQ, MP = "seq", "mp"
F32 = jnp.float32
MESH = pl.DeviceIdType.MESH
BLOCK = 256
CHUNK = 128
WIDE_CHUNK = 256
VMEM_LIMIT = 56 * 1024 * 1024
SCORE_SCALE = DH ** (-0.5)

GATHER_TIMES = ((2, 3, 5), (3, 5), (6, 7, 9), (7, 10, 13, 16))
BACK_TIMES = ((1, 4, 7, 10, 12), (6, 8, 10, 12), (9, 12, 14, 16))
END_TIMES = ((1, 4, 7, 10, 13), (5, 8, 10, 12), (11, 14, 15, 16))
SMALL_TIMES = (7, 12)


def dot(left, right):
    return jnp.dot(left, right, preferred_element_type=F32)


def dot_nt(left, right):
    return lax.dot_general(left, right, (((1,), (1,)), ((), ())), preferred_element_type=F32)


def dot_tn(left, right):
    return lax.dot_general(left, right, (((0,), (0,)), ((), ())), preferred_element_type=F32)


class Flush:
    def __init__(self, held, out, sems):
        self.held, self.out, self.sems = held, out, sems

    def copy(self, rows, t):
        return pltpu.make_async_copy(self.held.at[rows, :], self.out.at[rows, :], self.sems.at[t])


def run_kernel(
    body,
    name,
    inputs,
    outputs,
    scratch,
    collective=None,
    flops=0,
    grid=None,
    specs=None,
    in_smem=(),
    in_hbm=(),
    late=None,
    flushed=None,
    whole=None,
    pieces=0,
):
    specs, late, flushed, whole = specs or {}, late or {}, flushed or {}, whole or {}

    def kernel(*refs):
        refs = list(refs)

        def take(keys):
            got = refs[: len(keys)]
            del refs[: len(keys)]
            return dict(zip(keys, got))

        given, distant, made, written, far, held = (
            take(keys) for keys in (inputs, late, outputs, flushed, whole, scratch)
        )
        fetched, fetched_sems, filled, filled_sems = (take(keys) for keys in (late, late, flushed, flushed))
        kept, kept_sems = take(whole), take(whole)
        r = SimpleNamespace(**given, **made, **held, **fetched, **filled, **kept)
        if whole:
            *first, last = whole
            r.flush_whole = SimpleNamespace(
                **{key: pltpu.make_async_copy(kept[key], far[key], kept_sems[key].at[0]) for key in first}
            )
            r.soft_hbm, r.soft_sem = far[last], kept_sems[last]
        r.late = SimpleNamespace(
            **{key: pltpu.make_async_copy(distant[key], fetched[key], fetched_sems[key]) for key in late}
        )
        r.flush = SimpleNamespace(**{key: Flush(filled[key], written[key], filled_sems[key]) for key in flushed})
        for copy in vars(r.late).values():
            copy.start()
        body(r)

    def spec_of(key):
        if key in specs:
            return specs[key]
        if key in in_hbm or key in late or key in flushed or key in whole:
            return pl.BlockSpec(memory_space=pl.ANY)
        return pl.BlockSpec(memory_space=pltpu.SMEM if key in in_smem else pltpu.VMEM)

    arguments = {**inputs, **late}
    gives = {**outputs, **flushed, **whole}
    shapes = [jax.ShapeDtypeStruct(shape, dtype) for shape, dtype in gives.values()]
    moved = sum(v.size * v.dtype.itemsize for v in arguments.values())
    moved += sum(v.size * v.dtype.itemsize for v in shapes)
    extra = {} if grid is None else dict(grid=grid)
    params = dict(vmem_limit_bytes=VMEM_LIMIT)
    if collective is not None:
        params.update(collective_id=collective, has_side_effects=True)
    results = pl.pallas_call(
        kernel,
        out_shape=shapes,
        in_specs=[spec_of(key) for key in arguments],
        out_specs=[spec_of(key) for key in gives],
        scratch_shapes=list(scratch.values())
        + [pltpu.VMEM(v.shape, v.dtype) for v in late.values()]
        + [pltpu.SemaphoreType.DMA for _ in late]
        + [pltpu.VMEM(shape, dtype) for shape, dtype in flushed.values()]
        + [pltpu.SemaphoreType.DMA((pieces,)) for _ in flushed]
        + [pltpu.VMEM(shape, dtype) for shape, dtype in whole.values()]
        + [pltpu.SemaphoreType.DMA((pieces,)) for _ in whole],
        compiler_params=pltpu.CompilerParams(**params),
        cost_estimate=pl.CostEstimate(flops=int(flops), bytes_accessed=int(moved), transcendentals=0),
        name=name,
        **extra,
    )(*arguments.values())
    return SimpleNamespace(**dict(zip(gives, results)))


def parity_matrix():
    row = lax.broadcasted_iota(jnp.int32, (2 * BLOCK, 2 * BLOCK), 0)
    col = lax.broadcasted_iota(jnp.int32, (2 * BLOCK, 2 * BLOCK), 1)
    source = 2 * (row % BLOCK) + row // BLOCK
    return jnp.where(col == source, 1.0, 0.0).astype(BF)


def head_lanes(count):
    lane = lax.broadcasted_iota(jnp.int32, (1, count * DH), 1)
    return [lane // DH == head for head in range(count)]


def head_flags(dilated, count):
    first = lax.axis_index(MP) * count
    return [jnp.logical_or(dilated[0] == first + head, dilated[1] == first + head) for head in range(count)]


def marked_lanes(dilated, count):
    marked = jnp.zeros((1, count * DH), jnp.int32)
    for flag, lanes in zip(head_flags(dilated, count), head_lanes(count)):
        marked = jnp.where(lanes, flag.astype(jnp.int32), marked)
    return marked > 0


def sorted_groups(natural, sort):
    groups = natural.shape[0] // (2 * BLOCK)
    return [dot(sort, natural[g * 2 * BLOCK : (g + 1) * 2 * BLOCK]).astype(BF) for g in range(groups)]


def arrange_rows(natural, sort):
    return jnp.concatenate(sorted_groups(natural, sort), axis=0)


def split_rows(natural, sort):
    parts = sorted_groups(natural, sort)
    return jnp.concatenate([p[:BLOCK] for p in parts] + [p[BLOCK:] for p in parts], axis=0)


def soft_weights(query_block, key_block, lanes, allowed):
    raw = dot_nt(jnp.where(lanes, query_block, 0.0).astype(BF), key_block)
    scores = jnp.where(allowed, raw, MASK_FILL)
    top = jnp.max(scores, axis=1, keepdims=True)
    exponent = jnp.exp(scores - top)
    total = jnp.sum(exponent, axis=1, keepdims=True)
    return (exponent * (1.0 / total)).astype(BF)


def window_mask():
    row = lax.broadcasted_iota(jnp.int32, (BLOCK, 3 * BLOCK), 0)
    col = lax.broadcasted_iota(jnp.int32, (BLOCK, 3 * BLOCK), 1)
    return jnp.abs(row - col + BLOCK) <= WIN


class OutShare:
    def __init__(self, who, refs):
        self.who, self.r, self.here = who, refs, lax.axis_index(MP)

    def copy(self, kind, slot):
        r = self.r
        device = self.who.across if kind == 1 else self.who.sibling
        return copy_to(r.full.at[slot], r.full.at[slot], r.sent.at[kind], r.came.at[kind], device)

    def begin(self, own):
        self.r.full[self.here] = own.astype(F32).T.astype(BF)
        self.copy(0, self.here).start()
        self.copy(1, self.here).start()

    def hand_on(self):
        self.copy(1, self.who.across[1]).wait_recv()
        self.copy(2, self.who.across[1]).start()

    def finish(self):
        self.copy(0, self.who.sibling[1]).wait_recv()
        self.copy(2, self.who.diagonal[1]).wait_recv()
        for kind, slot in enumerate((self.here, self.here, self.who.across[1])):
            self.copy(kind, slot).wait_send()


def share_scratch():
    return dict(share_sent=pltpu.SemaphoreType.DMA((3,)), share_came=pltpu.SemaphoreType.DMA((3,)))


def key_starts(step, mixed):
    natural = pl.ds(pl.multiple_of(step * BLOCK, BLOCK), 3 * BLOCK)
    if not mixed:
        return natural, natural
    first = (step % 2) * 4 + step // 2
    return natural, pl.ds(pl.multiple_of(first * BLOCK, BLOCK), 3 * BLOCK)


class HeadExchange:
    def __init__(self, who, source, gathered, sent, came):
        self.who, self.source, self.gathered, self.sent, self.came = who, source, gathered, sent, came
        here = lax.axis_index(MP)
        self.here = here
        self.devices = who.sibling, who.across, who.diagonal

    def copy(self, kind, t, slot):
        who = self.who
        rows = who.own(t) if kind == 1 else who.other(t)
        return copy_to(
            self.source.at[rows, :],
            self.gathered.at[slot, who.half(t), :],
            self.sent.at[kind, t],
            self.came.at[kind, t],
            self.devices[kind],
        )

    def give(self, t):
        self.gathered[self.here, self.who.half(t), :] = self.source[self.who.own(t), :]
        for kind in range(3):
            self.copy(kind, t, self.here).start()

    def take(self, t):
        for kind in range(3):
            self.copy(kind, t, self.devices[kind][1]).wait_recv()

    def finish(self, t):
        for kind in range(3):
            self.copy(kind, t, self.here).wait_send()


def attend(query, pair, left, right, seg_query, seg_keys, dilated):
    rows, width = query.shape
    heads = width // DH
    blocks = rows // BLOCK
    keys = 3 * BLOCK
    slots = 2 * blocks
    chunks = rows // WIDE_CHUNK

    def body(r):
        step = pl.program_id(0)
        who = Partners(size=WIDE_CHUNK)
        exchange = HeadExchange(who, r.out, r.landed, r.sent, r.came)

        @pl.when(step == 0)
        def _():
            who.call()
            marked = marked_lanes(r.dilated, heads)
            sort = parity_matrix()
            for which, held in ((0, r.keys), (1, r.values)):
                lanes = slice(which * width, (which + 1) * width)
                padded = jnp.concatenate([r.left[:, lanes], r.pair[:, lanes], r.right[:, lanes]], axis=0)
                natural = jnp.concatenate([padded[BLOCK : (blocks + 3) * BLOCK], padded[: 2 * BLOCK]], axis=0)
                held[...] = jnp.where(marked, split_rows(padded, sort), natural)
            scaled = (r.asked[...].astype(F32) * SCORE_SCALE).astype(BF)
            r.query[...] = jnp.where(marked, arrange_rows(scaled, sort), scaled)

        window = window_mask()
        natural, dilated_near = key_starts(step, True)
        own = pl.ds(pl.multiple_of(step * BLOCK, BLOCK), BLOCK)
        marked = marked_lanes(r.dilated, heads)
        key_block = jnp.where(marked, r.keys[dilated_near, :], r.keys[natural, :])
        value_block = jnp.where(marked, r.values[dilated_near, :], r.values[natural, :])
        query_block = r.query[own, :]
        gathered = jnp.zeros((BLOCK, width), F32)
        flags = head_flags(r.dilated, heads)
        for head, lanes in enumerate(head_lanes(heads)):
            mine = jnp.where(flags[head], r.seg_query[own, 1:2], r.seg_query[own, 0:1])
            theirs = jnp.where(flags[head], r.seg_keys[1:2, dilated_near], r.seg_keys[0:1, natural])
            soft = soft_weights(query_block, key_block, lanes, jnp.logical_and(window, mine == theirs))
            r.soft[head] = soft
            gathered = jnp.where(lanes, dot(soft, value_block), gathered)
        r.arranged[own, :] = gathered.astype(BF)

        for group in range(blocks // 2):

            @pl.when(step == 2 * group + 1)
            def _(group=group):
                part = slice(group * 2 * BLOCK, (group + 1) * 2 * BLOCK)
                arranged = r.arranged[part, :]
                restored = dot_tn(parity_matrix(), arranged).astype(BF)
                r.out[part, :] = jnp.where(marked, restored, arranged)
                if group == 0:
                    who.gather()
                    for t in range(chunks // 2):
                        exchange.give(t)

        @pl.when(step == blocks - 1)
        def _():
            for t in range(chunks // 2):
                exchange.take(t)
                exchange.finish(t)
            r.first[...] = r.landed[...]

    return run_kernel(
        body,
        "attend",
        dict(
            asked=query,
            pair=pair,
            left=left,
            right=right,
            seg_query=seg_query,
            seg_keys=seg_keys,
            dilated=dilated,
        ),
        dict(
            out=((rows, width), BF),
            first=((4, rows // 4, width), BF),
            arranged=((rows, width), BF),
            query=((rows, width), BF),
            keys=((slots * BLOCK, width), BF),
            values=((slots * BLOCK, width), BF),
            soft=((heads, rows, keys), BF),
        ),
        dict(
            landed=pltpu.VMEM((4, rows // 4, width), BF),
            sent=pltpu.SemaphoreType.DMA((3, chunks // 2)),
            came=pltpu.SemaphoreType.DMA((3, chunks // 2)),
        ),
        collective=8,
        flops=4 * rows * keys * 256 * heads,
        grid=(blocks,),
        specs=dict(soft=pl.BlockSpec((heads, BLOCK, keys), lambda i: (0, i, 0))),
        in_smem=("dilated",),
    )


def attend_back(saved, grad_out, dilated, rim, mixed, count, collective):
    rows, width = grad_out.shape
    heads = width // DH
    blocks = rows // BLOCK
    keys = 3 * BLOCK
    slots = 2 * blocks if mixed else blocks + 2

    def body(r):
        step = pl.program_id(0)
        column = Column(count)
        first, last = column.index == 0, column.index == count - 1
        before = (lax.rem(column.index + count - 1, count), column.here)
        after = (lax.rem(column.index + 1, count), column.here)
        copy = copy_to(r.ready_left, r.from_right, r.sent.at[0], r.came.at[0], before)

        @pl.when(step == 0)
        def _():
            barrier = pltpu.get_barrier_semaphore()

            @pl.when(jnp.logical_not(last))
            def _():
                pl.semaphore_signal(barrier, inc=1, device_id=after, device_id_type=MESH)

            grad = r.grad_out[...]
            if mixed:
                grad = jnp.where(marked_lanes(r.dilated, heads), arrange_rows(grad, parity_matrix()), grad)
            r.grad[...] = grad
            r.grad_keys[...] = jnp.zeros_like(r.grad_keys)
            r.grad_values[...] = jnp.zeros_like(r.grad_values)

        natural, dilated_near = key_starts(step, mixed)
        own = pl.ds(pl.multiple_of(step * BLOCK, BLOCK), BLOCK)
        marked = marked_lanes(r.dilated, heads)
        key_block, value_block = r.keys[natural, :], r.values[natural, :]
        if mixed:
            key_block = jnp.where(marked, r.keys[dilated_near, :], key_block)
            value_block = jnp.where(marked, r.values[dilated_near, :], value_block)
        query_block = r.query[own, :]
        grad_block = r.grad[own, :]
        product = grad_block.astype(F32) * r.arranged[own, :].astype(F32)
        grad_query = jnp.zeros((BLOCK, width), F32)
        grad_key = jnp.zeros((keys, width), F32)
        grad_value = jnp.zeros((keys, width), F32)
        for head, lanes in enumerate(head_lanes(heads)):
            soft = r.soft[head]
            grad_head = jnp.where(lanes, grad_block, 0.0).astype(BF)
            row_dot = jnp.sum(jnp.where(lanes, product, 0.0), axis=1, keepdims=True)
            grad_soft = dot_nt(grad_head, value_block)
            grad_scores = (soft.astype(F32) * (grad_soft - row_dot)).astype(BF)
            grad_value += dot_tn(soft, grad_head)
            grad_key += dot_tn(grad_scores, jnp.where(lanes, query_block, 0.0).astype(BF))
            grad_query = jnp.where(lanes, dot(grad_scores, key_block), grad_query)
        r.grad_query[own, :] = (grad_query * SCORE_SCALE).astype(BF)
        if mixed:
            for held, grad in ((r.grad_keys, grad_key), (r.grad_values, grad_value)):
                held[dilated_near, :] += jnp.where(marked, grad, 0.0)
                held[natural, :] += jnp.where(marked, 0.0, grad)
        else:
            r.grad_keys[natural, :] += grad_key
            r.grad_values[natural, :] += grad_value

        def natural_group(g, middle):
            both = []
            for held in (r.grad_keys, r.grad_values):
                plain = middle(held)
                pair = jnp.concatenate(
                    [
                        held[g * BLOCK : (g + 1) * BLOCK, :],
                        held[(blocks + g) * BLOCK : (blocks + g + 1) * BLOCK, :],
                    ],
                    axis=0,
                ).astype(BF)
                both.append(jnp.where(marked, dot_tn(parity_matrix(), pair), plain).astype(BF))
            return jnp.concatenate(both, axis=1)

        edge = jnp.zeros((BLOCK, width), F32)

        @pl.when(step == (1 if mixed else 0))
        def _():
            if mixed:
                r.ready_left[...] = natural_group(0, lambda held: jnp.concatenate([edge, held[:BLOCK, :]], axis=0))
            else:
                r.ready_left[...] = jnp.concatenate(
                    [r.grad_keys[:rim, :], r.grad_values[:rim, :]], axis=1
                ).astype(BF)

            @pl.when(jnp.logical_not(first))
            def _():
                pl.semaphore_wait(pltpu.get_barrier_semaphore(), 1)
                copy.start()

        @pl.when(step == blocks - 1)
        def _():
            if mixed:
                for g in range(blocks // 2):
                    part = slice(g * 2 * BLOCK, (g + 1) * 2 * BLOCK)
                    arranged = r.grad_query[part, :]
                    restored = dot_tn(parity_matrix(), arranged).astype(BF)
                    r.out_query[part, :] = jnp.where(marked, restored, arranged)
                lap = 2 * BLOCK
                r.out_own[:lap, :] = natural_group(1, lambda held: held[BLOCK : 3 * BLOCK, :])
                r.out_own[lap:, :] = natural_group(2, lambda held: held[3 * BLOCK : 5 * BLOCK, :])
                r.out_right[...] = natural_group(
                    3, lambda held: jnp.concatenate([held[5 * BLOCK : 6 * BLOCK, :], edge], axis=0)
                )
            else:
                r.out_query[...] = r.grad_query[...]
                both = jnp.concatenate([r.grad_keys[rim:, :], r.grad_values[rim:, :]], axis=1).astype(BF)
                r.out_own[...] = both[:rows]
                r.out_right[...] = both[rows:]

            @pl.when(jnp.logical_not(last))
            def _():
                copy.wait_recv()
                tail = pl.ds(rows - rim, rim)
                r.out_own[tail, :] = (r.out_own[tail, :].astype(F32) + r.from_right[...].astype(F32)).astype(BF)

            @pl.when(jnp.logical_not(first))
            def _():
                copy.wait_send()

    return run_kernel(
        body,
        "attend_back",
        dict(
            grad_out=grad_out,
            arranged=saved.arranged,
            query=saved.query,
            keys=saved.keys,
            values=saved.values,
            soft=saved.soft,
            dilated=dilated,
        ),
        dict(
            out_query=((rows, width), BF),
            out_own=((rows, 2 * width), BF),
            out_right=((rim, 2 * width), BF),
        ),
        dict(
            grad=pltpu.VMEM((rows, width), BF),
            grad_query=pltpu.VMEM((rows, width), BF),
            grad_keys=pltpu.VMEM((slots * BLOCK, width), F32),
            grad_values=pltpu.VMEM((slots * BLOCK, width), F32),
            ready_left=pltpu.VMEM((rim, 2 * width), BF),
            from_right=pltpu.VMEM((rim, 2 * width), BF),
            sent=pltpu.SemaphoreType.DMA((1,)),
            came=pltpu.SemaphoreType.DMA((1,)),
        ),
        collective=collective,
        flops=8 * rows * keys * 256 * heads,
        grid=(blocks,),
        specs=dict(soft=pl.BlockSpec((heads, BLOCK, keys), lambda i: (0, i, 0))),
        in_smem=("dilated",),
    )


class Partners:
    def __init__(self, count=0, shift=0, size=CHUNK):
        seq = lax.axis_index(SEQ)
        here = lax.axis_index(MP)
        self.core = lax.rem(here, 2)
        self.sibling = (seq, here + 1 - 2 * self.core)
        self.across = (seq, lax.rem(here + 2, 4))
        self.diagonal = (seq, lax.rem(here + 3 - 2 * self.core, 4))
        self.count, self.shift, self.size = count, shift, size

    def others(self, column):
        found = [self.sibling, self.across, self.diagonal]
        if column is not None:
            found += [column.peer(k) for k in range(1, column.count)]
        return found

    def call(self, column=None):
        barrier = pltpu.get_barrier_semaphore()
        for other in self.others(column):
            pl.semaphore_signal(barrier, inc=1, device_id=other, device_id_type=MESH)

    def gather(self, column=None):
        pl.semaphore_wait(pltpu.get_barrier_semaphore(), len(self.others(column)))

    def meet(self, column=None):
        self.call(column)
        self.gather(column)

    def place(self, t):
        return lax.rem(t + self.shift, self.count) if self.shift else t

    def chunk(self, t):
        return pl.ds(pl.multiple_of(self.place(t) * self.size, self.size), self.size)

    def two_chunks(self, t):
        return pl.ds(pl.multiple_of(self.place(t - 1) * self.size, 2 * self.size), 2 * self.size)

    def part(self, t, core):
        half = self.size // 2
        return pl.ds(pl.multiple_of(self.place(t) * self.size + core * half, half), half)

    def own(self, t):
        return self.part(t, self.core)

    def other(self, t):
        return self.part(t, 1 - self.core)

    def half(self, t):
        half = self.size // 2
        return pl.ds(pl.multiple_of(self.place(t) * half, half), half)


def copy_to(source, target, sent, arrived, device):
    return pltpu.make_async_remote_copy(
        src_ref=source, dst_ref=target, send_sem=sent, recv_sem=arrived, device_id=device, device_id_type=MESH
    )


def exchange_scratch(rows):
    count = rows // CHUNK
    return dict(
        part=pltpu.VMEM((rows, D), BF),
        near=pltpu.VMEM((rows // 2, D), BF),
        far=pltpu.VMEM((rows // 2, D), BF),
        core_sent=pltpu.SemaphoreType.DMA((count,)),
        core_came=pltpu.SemaphoreType.DMA((count,)),
        far_sent=pltpu.SemaphoreType.DMA((count,)),
        far_came=pltpu.SemaphoreType.DMA((count,)),
    )


def gather_scratch(rows, width=D, dtype=BF):
    count = rows // CHUNK
    return dict(
        full=pltpu.VMEM((rows, width), dtype),
        sent=pltpu.SemaphoreType.DMA((count,)),
        came=pltpu.SemaphoreType.DMA((count,)),
    )


class Exchange:
    def __init__(self, who, refs):
        self.who, self.r = who, refs

    def core_copy(self, t):
        who, r = self.who, self.r
        return copy_to(
            r.part.at[who.other(t), :], r.near.at[who.half(t), :], r.core_sent.at[t], r.core_came.at[t], who.sibling
        )

    def far_copy(self, t):
        who, r = self.who, self.r
        rows = who.half(t)
        return copy_to(r.near.at[rows, :], r.far.at[rows, :], r.far_sent.at[t], r.far_came.at[t], who.across)

    def give(self, t, part):
        self.r.part[self.who.chunk(t), :] = part.astype(BF)
        self.core_copy(t).start()

    def add(self, t):
        who, r = self.who, self.r
        self.core_copy(t).wait_recv()
        pair = r.part[who.own(t), :].astype(F32) + r.near[who.half(t), :].astype(F32)
        r.near[who.half(t), :] = pair.astype(BF)
        self.far_copy(t).start()

    def take(self, t):
        who, r = self.who, self.r
        self.far_copy(t).wait_recv()
        return r.near[who.half(t), :].astype(F32) + r.far[who.half(t), :].astype(F32)

    def finish(self, t):
        self.core_copy(t).wait_send()
        self.far_copy(t).wait_send()


class Gather:
    def __init__(self, who, refs):
        self.who, self.r = who, refs

    def copy(self, rows, t):
        r = self.r
        return copy_to(r.full.at[rows, :], r.full.at[rows, :], r.sent.at[t], r.came.at[t], self.who.sibling)

    def give(self, t, value):
        rows = self.who.own(t)
        self.r.full[rows, :] = value.astype(self.r.full.dtype)
        self.copy(rows, t).start()

    def take(self, t):
        self.wait(t)
        return self.r.full[self.who.chunk(t), :]

    def wait(self, t):
        self.copy(self.who.other(t), t).wait_recv()

    def finish(self, t):
        self.copy(self.who.own(t), t).wait_send()


class Column:
    def __init__(self, count):
        self.count = count
        self.lines = count // 2
        self.here = lax.axis_index(MP)
        self.index = lax.axis_index(SEQ)
        self.inner = lax.rem(self.index, 2)
        self.outer = lax.div(self.index, 2)

    def peer(self, k):
        return (lax.rem(self.index + k, self.count), self.here)

    def at(self, outer, inner):
        return (2 * outer + inner, self.here)

    def turn(self, k):
        return lax.rem(self.outer + k, self.lines)


def gather_sems(lines):
    return {
        key: pltpu.SemaphoreType.DMA((lines,)) for key in ("pair_sent", "pair_came", "up_sent", "down_sent", "line_came")
    }


class GatherBlocks:
    def __init__(self, column, refs):
        self.c, self.r = column, refs
        self.above = column.outer < column.lines - 1
        self.below = column.outer > 0

    def line_copy(self, source, step):
        c, r = self.c, self.r
        block = 2 * source + c.inner
        sent = r.up_sent if step > 0 else r.down_sent
        return copy_to(
            r.full.at[block], r.full.at[block], sent.at[source], r.line_came.at[source], c.at(c.outer + step, c.inner)
        )

    def pair_copy(self, source, inner):
        c, r = self.c, self.r
        block = 2 * source + inner
        return copy_to(
            r.full.at[block],
            r.full.at[block],
            r.pair_sent.at[source],
            r.pair_came.at[source],
            c.at(c.outer, 1 - c.inner),
        )

    def put(self, value):
        self.r.full[self.c.index] = value

    def start_line(self):
        c = self.c

        @pl.when(self.above)
        def _():
            self.line_copy(c.outer, 1).start()

        @pl.when(self.below)
        def _():
            self.line_copy(c.outer, -1).start()

    def start_pair(self):
        self.pair_copy(self.c.outer, self.c.inner).start()

    def relay(self, k):
        c = self.c

        @pl.when(c.outer >= k)
        def _():
            source = c.outer - k
            self.line_copy(source, 1).wait_recv()

            @pl.when(self.above)
            def _():
                self.line_copy(source, 1).start()

            self.hand_on(source)

        @pl.when(c.outer + k < c.lines)
        def _():
            source = c.outer + k
            self.line_copy(source, -1).wait_recv()

            @pl.when(self.below)
            def _():
                self.line_copy(source, -1).start()

            self.hand_on(source)

    def hand_on(self, source):
        self.pair_copy(source, self.c.inner).start()

    def arrive(self):
        for k in range(self.c.lines):
            self.pair_copy(k, 1 - self.c.inner).wait_recv()

    def finish(self):
        for k in range(self.c.lines):
            self.pair_copy(k, self.c.inner).wait_send()
        self.finish_line()

    def finish_line(self):
        c = self.c
        for k in range(c.lines):

            @pl.when(jnp.logical_and(self.above, c.outer >= k))
            def _(k=k):
                self.line_copy(k, 1).wait_send()

            @pl.when(jnp.logical_and(self.below, c.outer <= k))
            def _(k=k):
                self.line_copy(k, -1).wait_send()


class GatherPairs(GatherBlocks):
    def line_copy(self, source, step):
        c, r = self.c, self.r
        blocks = pl.ds(2 * source, 2)
        sent = r.up_sent if step > 0 else r.down_sent
        return copy_to(
            r.full.at[blocks], r.full.at[blocks], sent.at[source], r.line_came.at[source], c.at(c.outer + step, c.inner)
        )

    def begin(self):
        self.pair_copy(self.c.outer, 1 - self.c.inner).wait_recv()
        self.start_line()

    def hand_on(self, source):
        pass

    def finish(self):
        self.pair_copy(self.c.outer, self.c.inner).wait_send()
        self.finish_line()


def scatter_scratch(lines, block, size, held=True):
    scratch = {
        key: pltpu.SemaphoreType.DMA((lines + 1,))
        for key in ("pair_sent", "pair_came", "line_sent", "line_came", "own_came")
    }
    scratch.update(near=pltpu.VMEM((lines, block, size), BF), far=pltpu.VMEM((lines + 1, block, size), BF))
    if held:
        scratch["own"] = pltpu.VMEM((lines, block, size), BF)
    return scratch


class ScatterBlocks:
    def __init__(self, column, refs, total):
        self.c, self.r, self.total = column, refs, total
        self.above = column.outer < column.lines - 1
        self.below = column.outer > 0
        self.fetched = hasattr(refs, "own")
        order = []
        for k in range(column.lines // 2):
            order += [column.lines - 1 - k, k]
        self.order = order

    def pair_copy(self, outer):
        c, r = self.c, self.r
        return copy_to(
            r.grads.at[2 * outer + 1 - c.inner],
            r.near.at[outer],
            r.pair_sent.at[outer],
            r.pair_came.at[outer],
            c.at(c.outer, 1 - c.inner),
        )

    def own_copy(self, outer):
        c, r = self.c, self.r
        return pltpu.make_async_copy(r.grads.at[2 * outer + c.inner], r.own.at[outer], r.own_came.at[outer])

    def line_copy(self, target, step):
        c, r = self.c, self.r
        slot = target if step > 0 else jnp.where(c.outer - 1 == target, c.lines, target)
        return copy_to(
            r.near.at[target],
            r.far.at[slot],
            r.line_sent.at[target],
            r.line_came.at[slot],
            c.at(c.outer + step, c.inner),
        )

    def landing(self, slot, step):
        c, r = self.c, self.r
        return copy_to(
            r.near.at[c.outer], r.far.at[slot], r.line_sent.at[c.outer], r.line_came.at[slot], c.at(c.outer + step, c.inner)
        )

    def start(self):
        for outer in self.order:
            self.pair_copy(outer).start()
            if self.fetched:
                self.own_copy(outer).start()

    def pair_step(self, k):
        c, r = self.c, self.r
        for outer in self.order[2 * k : 2 * k + 2]:
            self.pair_copy(outer).wait_recv()
            if self.fetched:
                self.own_copy(outer).wait()
                own = r.own[outer]
            else:
                own = r.grads[2 * outer + c.inner]
            r.near[outer] = (own.astype(F32) + r.near[outer].astype(F32)).astype(BF)

    def line_step(self, wave):
        c, r = self.c, self.r
        from_top = c.lines - 1 - c.outer

        def pass_on(target, step, behind):
            @pl.when(behind)
            def _():
                self.landing(target, step).wait_recv()
                r.near[target] = (r.near[target].astype(F32) + r.far[target].astype(F32)).astype(BF)

            self.line_copy(target, step).start()

        @pl.when(c.outer <= wave)
        def _():
            pass_on(from_top + c.outer - wave + c.outer, 1, self.below)

        @pl.when(from_top <= wave)
        def _():
            pass_on(wave - from_top, -1, self.above)

    def close(self):
        c, r = self.c, self.r
        self.total[...] = r.near[c.outer].astype(F32)

        @pl.when(self.below)
        def _():
            self.landing(c.outer, 1).wait_recv()
            self.total[...] += r.far[c.outer].astype(F32)

        @pl.when(self.above)
        def _():
            self.landing(c.lines, -1).wait_recv()
            self.total[...] += r.far[c.lines].astype(F32)

    def finish(self):
        c = self.c
        for outer in self.order:
            self.pair_copy(outer).wait_send()
        for target in range(c.lines):

            @pl.when(c.outer < target)
            def _(target=target):
                self.line_copy(target, 1).wait_send()

            @pl.when(c.outer > target)
            def _(target=target):
                self.line_copy(target, -1).wait_send()

    def ticks(self, times):
        steps = [(times[0], lambda: self.pair_step(0)), (times[0], lambda: self.line_step(0))]
        steps += [(times[1], lambda: self.pair_step(1))]
        steps += [(times[k], lambda k=k: self.line_step(k)) for k in range(1, self.c.lines - 1)]
        steps += [(times[self.c.lines - 1], self.close)]
        return steps


def scatter_pairs_scratch(lines, block, size):
    scratch = {key: pltpu.SemaphoreType.DMA((lines + 1,)) for key in ("pair_sent", "pair_came", "line_sent", "line_came")}
    scratch.update(
        sums=pltpu.VMEM((2 * lines, block, size), BF),
        far=pltpu.VMEM((2 * lines + 2, block, size), BF),
        give=pltpu.VMEM((block, size), BF),
        get=pltpu.VMEM((block, size), BF),
        held=pltpu.SemaphoreType.DMA,
    )
    return scratch


class ScatterPairs:
    def __init__(self, column, refs, total):
        self.c, self.r, self.total = column, refs, total
        self.above = column.outer < column.lines - 1
        self.below = column.outer > 0
        self.fetch = pltpu.make_async_copy(refs.grads, refs.sums, refs.held)

    def line_copy(self, target, step):
        c, r = self.c, self.r
        slot = target if step > 0 else jnp.where(c.outer - 1 == target, c.lines, target)
        return copy_to(
            r.sums.at[pl.ds(2 * target, 2)],
            r.far.at[pl.ds(2 * slot, 2)],
            r.line_sent.at[target],
            r.line_came.at[slot],
            c.at(c.outer + step, c.inner),
        )

    def landing(self, slot, step):
        c, r = self.c, self.r
        return copy_to(
            r.sums.at[pl.ds(2 * c.outer, 2)],
            r.far.at[pl.ds(2 * slot, 2)],
            r.line_sent.at[c.outer],
            r.line_came.at[slot],
            c.at(c.outer + step, c.inner),
        )

    def pair_copy(self):
        c, r = self.c, self.r
        return copy_to(r.give, r.get, r.pair_sent.at[0], r.pair_came.at[0], c.at(c.outer, 1 - c.inner))

    def start(self):
        self.fetch.start()

    def line_step(self, wave):
        c, r = self.c, self.r
        from_top = c.lines - 1 - c.outer
        if wave == 0:
            self.fetch.wait()

        def pass_on(target, step, behind):
            @pl.when(behind)
            def _():
                self.landing(target, step).wait_recv()
                for k in range(2):
                    block = 2 * target + k
                    r.sums[block] = (r.sums[block].astype(F32) + r.far[block].astype(F32)).astype(BF)

            self.line_copy(target, step).start()

        @pl.when(c.outer <= wave)
        def _():
            pass_on(from_top + c.outer - wave + c.outer, 1, self.below)

        @pl.when(from_top <= wave)
        def _():
            pass_on(wave - from_top, -1, self.above)

    def close_line(self):
        c, r = self.c, self.r
        mine, other = 2 * c.outer + c.inner, 2 * c.outer + 1 - c.inner
        self.total[...] = r.sums[mine].astype(F32)

        @pl.when(self.below)
        def _():
            self.landing(c.outer, 1).wait_recv()
            self.total[...] += r.far[mine].astype(F32)
            r.sums[other] = (r.sums[other].astype(F32) + r.far[other].astype(F32)).astype(BF)

        @pl.when(self.above)
        def _():
            self.landing(c.lines, -1).wait_recv()
            self.total[...] += r.far[2 * c.lines + c.inner].astype(F32)
            r.sums[other] = (r.sums[other].astype(F32) + r.far[2 * c.lines + 1 - c.inner].astype(F32)).astype(BF)

        r.give[...] = r.sums[other]
        self.pair_copy().start()

    def close(self):
        self.pair_copy().wait_recv()
        self.total[...] += self.r.get[...].astype(F32)

    def finish(self):
        c = self.c
        self.pair_copy().wait_send()
        for target in range(c.lines):

            @pl.when(c.outer < target)
            def _(target=target):
                self.line_copy(target, 1).wait_send()

            @pl.when(c.outer > target)
            def _(target=target):
                self.line_copy(target, -1).wait_send()

    def ticks(self, times):
        steps = [(times[k], lambda k=k: self.line_step(k)) for k in range(self.c.lines - 1)]
        return steps + [(times[self.c.lines - 1], self.close_line), (times[self.c.lines], self.close)]


class Halo:
    def __init__(self, column, refs, source, rim, size):
        self.c, self.r, self.source, self.rim, self.size = column, refs, source, rim, size
        self.rows = source.shape[0]
        self.before = lax.rem(column.index + column.count - 1, column.count), column.here
        self.after = lax.rem(column.index + 1, column.count), column.here
        self.first, self.last = column.index == 0, column.index == column.count - 1

    def clear(self):
        @pl.when(self.first)
        def _():
            self.r.left[...] = jnp.zeros_like(self.r.left)

        @pl.when(self.last)
        def _():
            self.r.right[...] = jnp.zeros_like(self.r.right)

    def back_copy(self, t):
        rows = pl.ds(pl.multiple_of(t * self.size, self.size), self.size)
        return copy_to(
            self.source.at[rows, :], self.r.right.at[rows, :], self.r.back_sent.at[t], self.r.back_came.at[t], self.before
        )

    def ahead_copy(self, t):
        from_rows = pl.ds(pl.multiple_of(self.rows - self.rim + t * self.size, self.size), self.size)
        rows = pl.ds(pl.multiple_of(t * self.size, self.size), self.size)
        return copy_to(
            self.source.at[from_rows, :],
            self.r.left.at[rows, :],
            self.r.ahead_sent.at[t],
            self.r.ahead_came.at[t],
            self.after,
        )

    def send(self, t):
        count = self.rim // self.size
        offset = (self.rows - self.rim) // self.size

        @pl.when(jnp.logical_and(t < count, jnp.logical_not(self.first)))
        def _():
            self.back_copy(t).start()

        @pl.when(jnp.logical_and(t >= offset, jnp.logical_not(self.last)))
        def _():
            self.ahead_copy(t - offset).start()

    def arrive(self):
        for t in range(self.rim // self.size):

            @pl.when(jnp.logical_not(self.last))
            def _():
                self.back_copy(t).wait_recv()

            @pl.when(jnp.logical_not(self.first))
            def _():
                self.ahead_copy(t).wait_recv()

    def finish(self):
        for t in range(self.rim // self.size):

            @pl.when(jnp.logical_not(self.first))
            def _():
                self.back_copy(t).wait_send()

            @pl.when(jnp.logical_not(self.last))
            def _():
                self.ahead_copy(t).wait_send()


def halo_scratch(count):
    return {
        key: pltpu.SemaphoreType.DMA((count,)) for key in ("back_sent", "back_came", "ahead_sent", "ahead_came")
    }


def pick(r, prefix):
    start = prefix + "_"
    return SimpleNamespace(
        **{key[len(start) :]: value for key, value in vars(r).items() if key.startswith(start)}
    )


def prefixed(prefix, entries):
    return {prefix + "_" + key: value for key, value in entries.items()}


def run_stages(count, stages, ticks=()):
    last = max(delay for delay, _ in stages)

    def step(i, carry):
        for when in sorted({when for when, _ in ticks if when < count + last}):

            @pl.when(i == when)
            def _(when=when):
                for other, tick in ticks:
                    if other == when:
                        tick()

        for delay, stage in stages:

            @pl.when(jnp.logical_and(i >= delay, i < count + delay))
            def _(delay=delay, stage=stage):
                stage(i - delay)

        return carry

    lax.fori_loop(0, count + last, step, 0)
    for when, tick in sorted(ticks, key=lambda entry: entry[0]):
        if when >= count + last:
            tick()


def norm_forward(total, gain, shift):
    center = total - jnp.mean(total, axis=1, keepdims=True)
    spread = jnp.mean(center * center, axis=1, keepdims=True)
    inverse = lax.rsqrt(spread + NORM_EPSILON)
    unit = center * inverse
    return unit, inverse, unit * gain + shift


def norm_back(grad, unit, inverse, gain):
    grad_unit = grad * gain
    first = jnp.mean(grad_unit, axis=1, keepdims=True)
    second = jnp.mean(grad_unit * unit, axis=1, keepdims=True)
    return inverse * (grad_unit - first - unit * second)


def column_sum(value):
    return jnp.sum(value, axis=0, keepdims=True)


def split_two(value):
    high = value.astype(BF)
    return high, (value - high.astype(F32)).astype(BF)


def exact(value, product):
    high, rest = split_two(value)
    low = (value - high.astype(F32) - rest.astype(F32)).astype(BF)
    return product(high) + product(rest) + product(low)


def wide(column):
    return jnp.broadcast_to(column, (column.shape[0], 128))


def forward_refs(rows, width, units):
    return dict(
        unit_one=((rows // 2, D), F32),
        unit_two=((rows // 2, D), F32),
        hidden=((rows, units), BF),
        slope=((rows, units), BF),
    )


def forward_small(rows):
    return dict(inverse_one=((rows // 2, 128), F32), inverse_two=((rows // 2, 128), F32))


def forward_stages(r, who, projected, second, spread):
    def middle(t):
        total = r.residual[who.own(t), :].astype(F32) + projected(t) + r.shared[r.base + 0 : r.base + 1, :]
        unit, inverse, normed = norm_forward(total, r.shared[r.base + 1 : r.base + 2, :], r.shared[r.base + 2 : r.base + 3, :])
        r.unit_one[who.half(t), :] = unit
        r.inverse_one[who.half(t), :] = wide(inverse)
        r.normed[who.half(t), :] = normed
        spread.give(t, normed)

    def feed(t):
        pre = dot(spread.take(t), r.ffn_up[...]) + r.hidden_bias
        chance = 0.5 + 0.5 * lax.erf(pre * (0.5**0.5))
        hidden = (pre * chance).astype(BF)
        r.hidden[who.chunk(t), :] = hidden
        bell = jnp.exp(-0.5 * pre * pre) * 0.3989422804014327
        r.slope[who.chunk(t), :] = (chance + pre * bell).astype(BF)
        second.give(t, dot_nt(hidden, r.ffn_down[...]))

    def final(t):
        total = r.normed[who.half(t), :] + second.take(t) + r.shared[r.base + 3 : r.base + 4, :]
        unit, inverse, result = norm_forward(total, r.shared[r.base + 4 : r.base + 5, :], r.shared[r.base + 5 : r.base + 6, :])
        r.unit_two[who.half(t), :] = unit
        r.inverse_two[who.half(t), :] = wide(inverse)
        return unit, inverse, result

    return middle, feed, final


def backward_stages(r, who, ends, third, mids):
    def enter(t, grad, unit, inverse):
        grad_total = norm_back(grad, unit, inverse, r.shared[r.base + 4 : r.base + 5, :])
        r.vectors[3:4, :] += column_sum(grad_total)
        r.vectors[4:5, :] += column_sum(grad * unit)
        r.vectors[5:6, :] += column_sum(grad)
        r.kept[who.half(t), :] = grad_total
        ends.give(t, grad_total)

    def feed_back(t):
        rows = who.chunk(t)
        grad = ends.take(t)
        grad_pre = (dot(grad, r.ffn_down[...]) * r.slope[rows, :].astype(F32)).astype(BF)
        r.units[0:1, :] += column_sum(grad_pre.astype(F32))
        third.give(t, dot_nt(grad_pre, r.ffn_up[...]))
        r.grad_pre[pl.ds(pl.multiple_of(lax.rem(t, 2) * who.size, who.size), who.size), :] = grad_pre

        @pl.when(lax.rem(t, 2) == 1)
        def _():
            both = who.two_chunks(t)
            r.sum_up[...] += dot_tn(r.spread_full[both, :], r.grad_pre[...])
            r.sum_down[...] += dot_tn(ends.r.full[both, :], r.hidden[both, :])

    def leave(t):
        grad = r.kept[who.half(t), :] + third.take(t)
        unit = r.unit_one[who.half(t), :]
        grad_total = norm_back(grad, unit, r.inverse_one[who.half(t), 0:1], r.shared[r.base + 1 : r.base + 2, :])
        r.vectors[0:1, :] += column_sum(grad_total)
        r.vectors[1:2, :] += column_sum(grad * unit)
        r.vectors[2:3, :] += column_sum(grad)
        if r.grad_one is not None:
            r.grad_one[who.half(t), :] = grad_total
        mids.give(t, grad_total)

    def project_back(t):
        rows = who.chunk(t)
        grad = mids.take(t)
        r.grad_mixed[rows, :] = dot(grad, r.out_proj[...]).astype(BF)

        @pl.when(lax.rem(t, 2) == 1)
        def _():
            both = who.two_chunks(t)
            r.sum_out[...] += dot_tn(mids.r.full[both, :], r.mixed[both, :])

    return enter, feed_back, leave, project_back


def clear(*refs):
    for ref in refs:
        ref[...] = jnp.zeros_like(ref)


def finish_all(count, parts):
    def step(t, carry):
        for part in parts:
            part.finish(t)
        return carry

    lax.fori_loop(0, count, step, 0)


def packed(ref):
    return jnp.concatenate([ref[k].astype(BF) for k in range(ref.shape[0])], axis=1)


def projection_bias(split, width):
    return jnp.concatenate([split[:, :width], jnp.zeros((1, width), F32), split[:, width : 2 * width]], axis=1)


def opening(activations, segments, owners, attn_weights, ffn_weights, split_biases, shared_vectors, count):
    rows = activations.shape[0]
    width, units = attn_weights.shape[3], ffn_weights.shape[3]
    heads = width // DH
    blocks = rows // BLOCK
    lines = count // 2
    block = D // count
    layers = split_biases.shape[0]

    def body(r):
        who = Partners()
        column = Column(count)
        who.meet(column)
        wide_attn = GatherBlocks(column, SimpleNamespace(full=r.full_attn, **vars(pick(r, "ga"))))
        wide_up = GatherBlocks(column, SimpleNamespace(full=r.full_up, **vars(pick(r, "gu"))))
        wide_down = GatherPairs(column, SimpleNamespace(full=r.full_down, **vars(pick(r, "gd"))))
        halo = Halo(column, SimpleNamespace(left=r.left, right=r.right, **vars(pick(r, "halo"))), r.pair, WIN, BLOCK)
        first, last = column.index == 0, column.index == count - 1
        to_before = copy_to(r.ids, r.ids_right, r.ids_sent.at[0], r.ids_came.at[0], halo.before)
        to_after = copy_to(r.ids, r.ids_left, r.ids_sent.at[1], r.ids_came.at[1], halo.after)
        r.late.attn.wait()
        wide_attn.put(packed(r.attn.at[0]))
        wide_attn.start_line()
        wide_attn.start_pair()
        r.ids[...] = r.segments[...].astype(F32)

        @pl.when(first)
        def _():
            r.ids_left[...] = jnp.zeros_like(r.ids_left)

        @pl.when(last)
        def _():
            r.ids_right[...] = jnp.zeros_like(r.ids_right)

        @pl.when(jnp.logical_not(first))
        def _():
            to_before.start()

        @pl.when(jnp.logical_not(last))
        def _():
            to_after.start()

        halo.clear()
        r.late.ffn.wait()
        wide_down.put(r.ffn[0, 1].astype(BF))
        wide_down.start_pair()
        wide_up.put(r.ffn[0, 0].astype(BF))
        for slot in range(count):
            row = lax.broadcasted_iota(jnp.int32, (block, D), 0)
            col = lax.broadcasted_iota(jnp.int32, (block, D), 1)
            target = r.owners[slot] * block + row
            r.turn[slot * block : (slot + 1) * block, :] = jnp.where(col == target, 1.0, 0.0).astype(BF)

        def sort_chunk(t, carry):
            chunk = pl.ds(pl.multiple_of(t * BLOCK, BLOCK), BLOCK)
            r.low[chunk, :] = dot(r.activations[chunk, :], r.turn[...]).astype(BF)
            return carry

        r.flush_whole.turn.start()
        r.late.activations.wait()
        lax.fori_loop(0, blocks, sort_chunk, 0)
        r.flush_whole.low.start()
        wide_attn.relay(1)
        padding = jnp.zeros((16 - 6 * layers, D), F32)
        stacked = [r.shared_vectors[k, layer : layer + 1, :] for layer in range(layers) for k in range(6)]
        stacked = jnp.concatenate(stacked + [padding], axis=0)
        r.shared[...] = exact(stacked, lambda part: dot(part, r.turn[...]))
        wide_attn.relay(2)
        wide_up.start_line()

        @pl.when(jnp.logical_not(last))
        def _():
            to_before.wait_recv()

        @pl.when(jnp.logical_not(first))
        def _():
            to_after.wait_recv()

        def flat(ref):
            return jnp.concatenate([ref[k : k + 1, :] for k in range(ref.shape[0])], axis=1)

        own_ids = flat(r.ids)
        padded = jnp.concatenate([flat(r.ids_left)[:, rows - 2 * WIN :], own_ids, flat(r.ids_right)[:, : 2 * WIN]], axis=1)
        r.id_row[...] = jnp.broadcast_to(padded, r.id_row.shape)
        sort = parity_matrix()
        lap = 2 * BLOCK
        sorted_ids = [
            dot_nt(r.id_row[:, g * lap : (g + 1) * lap].astype(BF), sort) for g in range(2 * blocks // 2)
        ]
        natural = jnp.concatenate([padded[:, WIN : rows + 3 * WIN], padded[:, : 2 * WIN]], axis=1)
        arranged = jnp.concatenate(
            [part[0:1, :BLOCK] for part in sorted_ids] + [part[0:1, BLOCK:] for part in sorted_ids], axis=1
        )
        r.seg_keys[0:1, :] = natural
        r.seg_keys[1:2, :] = arranged
        middle = sorted_ids[1:-1]
        own_arranged = jnp.concatenate([part[0:1, :] for part in middle], axis=1)
        for which, row in ((0, own_ids), (1, own_arranged)):
            for k in range(rows // 128):
                square = jnp.broadcast_to(row[:, k * 128 : (k + 1) * 128], (128, 128))
                r.seg_query[k * 128 : (k + 1) * 128, which : which + 1] = square.T[:, 0:1]

        for k in range(3, lines):
            wide_attn.relay(k)
        wide_up.start_pair()
        wide_up.relay(1)
        wide_attn.arrive()
        r.flush_whole.full_attn.start()
        whole_attn = r.full_attn[...].reshape(D, 4 * width)
        r.proj[...] = whole_attn[:, : 3 * width]
        share = OutShare(who, SimpleNamespace(full=r.full_out, sent=r.share_sent, came=r.share_came))
        share.begin(whole_attn[:, 3 * width :])
        exchange = HeadExchange(who, r.out, r.gathered, r.heads_sent, r.heads_came)
        bias = projection_bias(r.split[0], width)

        def project(t):
            chunk = pl.ds(pl.multiple_of(t * BLOCK, BLOCK), BLOCK)
            value = dot(r.low[chunk, :], r.proj[...]) + bias
            r.query[chunk, :] = (value[:, :width].astype(BF).astype(F32) * SCORE_SCALE).astype(BF)
            pair = value[:, width:].astype(BF)
            r.pair[chunk, :] = pair
            inner = pl.ds(pl.multiple_of((t + 1) * BLOCK, BLOCK), BLOCK)
            r.keys[inner, :] = pair[:, :width]
            r.values[inner, :] = pair[:, width:]

        def outer_project(i, carry):
            t = i * (blocks - 1)
            project(t)
            halo.send(t)
            return carry

        def inner_project(i, carry):
            project(i)
            return carry

        lax.fori_loop(0, 2, outer_project, 0)
        wide_up.relay(2)
        wide_down.begin()
        lax.fori_loop(1, blocks - 1, inner_project, 0)
        for k in range(3, lines):
            wide_up.relay(k)

        def written(step):
            rows_of = pl.ds(pl.multiple_of(step * BLOCK, BLOCK), BLOCK)
            return pltpu.make_async_copy(r.soft.at[:, rows_of, :], r.soft_hbm.at[:, rows_of, :], r.soft_sem.at[step])

        def attend_block(step):
            own = pl.ds(pl.multiple_of(step * BLOCK, BLOCK), BLOCK)
            near = pl.ds(pl.multiple_of(step * BLOCK, BLOCK), 3 * BLOCK)
            key_block, value_block, query_block = r.keys[near, :], r.values[near, :], r.query[own, :]
            mine = r.seg_query[own, 0:1]
            theirs = r.id_row[0:1, pl.ds(pl.multiple_of(step * BLOCK + BLOCK, BLOCK), 3 * BLOCK)]
            allowed = jnp.logical_and(window_mask(), mine == theirs)
            gathered = jnp.zeros((BLOCK, width), F32)
            for head, lanes in enumerate(head_lanes(heads)):
                soft = soft_weights(query_block, key_block, lanes, allowed)
                r.soft[head, own, :] = soft
                gathered = jnp.where(lanes, dot(soft, value_block), gathered)
            r.out[own, :] = gathered.astype(BF)
            written(step).start()
            for k in range(BLOCK // CHUNK):
                exchange.give(BLOCK // CHUNK * step + k)

        def inner_attend(i, carry):
            attend_block(i)
            return carry

        def outer_attend(i, carry):
            attend_block(i * (blocks - 1))
            return carry

        lax.fori_loop(1, blocks - 1, inner_attend, 0)
        wide_down.relay(1)
        share.hand_on()
        halo.arrive()
        for part, start in ((r.left, 0), (r.right, (blocks + 1) * BLOCK)):
            r.keys[pl.ds(start, BLOCK), :] = part[:, :width]
            r.values[pl.ds(start, BLOCK), :] = part[:, width:]
        lax.fori_loop(0, 2, outer_attend, 0)
        for k in range(2, lines):
            wide_down.relay(k)
        wide_up.arrive()

        def exchanged(t, carry):
            exchange.take(t)
            exchange.finish(t)
            return carry

        lax.fori_loop(0, rows // CHUNK, exchanged, 0)
        share.finish()
        for step in range(blocks):
            written(step).wait()
        for copy in vars(r.flush_whole).values():
            copy.wait()
        halo.finish()
        for engine in (wide_attn, wide_up, wide_down):
            engine.finish()

        @pl.when(jnp.logical_not(first))
        def _():
            to_before.wait_send()

        @pl.when(jnp.logical_not(last))
        def _():
            to_after.wait_send()

    scratch = dict(
        proj=pltpu.VMEM((D, 3 * width), BF),
        pair=pltpu.VMEM((rows, 2 * width), BF),
        left=pltpu.VMEM((WIN, 2 * width), BF),
        right=pltpu.VMEM((WIN, 2 * width), BF),
        ids=pltpu.VMEM((rows // 128, 128), F32),
        ids_left=pltpu.VMEM((rows // 128, 128), F32),
        ids_right=pltpu.VMEM((rows // 128, 128), F32),
        ids_sent=pltpu.SemaphoreType.DMA((2,)),
        ids_came=pltpu.SemaphoreType.DMA((2,)),
        id_row=pltpu.VMEM((8, rows + 4 * WIN), F32),
    )
    scratch.update(
        heads_sent=pltpu.SemaphoreType.DMA((3, rows // CHUNK)),
        heads_came=pltpu.SemaphoreType.DMA((3, rows // CHUNK)),
        **share_scratch(),
    )
    scratch.update(prefixed("ga", gather_sems(lines)))
    scratch.update(prefixed("gu", gather_sems(lines)))
    scratch.update(prefixed("gd", gather_sems(lines)))
    scratch.update(prefixed("halo", halo_scratch(1)))
    return run_kernel(
        body,
        "opening",
        dict(
            segments=segments.reshape(rows // 128, 128),
            owners=owners,
            split=split_biases,
            shared_vectors=shared_vectors.transpose(1, 0, 2),
        ),
        dict(
            full_up=((count, block, units), BF),
            full_down=((count, block, units), BF),
            shared=((16, D), F32),
            seg_query=((rows, 2), F32),
            seg_keys=((8, 2 * rows), F32),
            out=((rows, width), BF),
            gathered=((4, rows // 2, width), BF),
            full_out=((4, width, D), BF),
            query=((rows, width), BF),
            keys=((rows + 2 * BLOCK, width), BF),
            values=((rows + 2 * BLOCK, width), BF),
        ),
        scratch,
        collective=5,
        flops=2 * rows * D * (D + 3 * width),
        in_smem=("owners",),
        late=dict(attn=attn_weights, ffn=ffn_weights, activations=activations),
        whole=dict(
            full_attn=((count, block, 4 * width), BF),
            low=((rows, D), BF),
            turn=((D, D), BF),
            soft=((heads, rows, 3 * BLOCK), BF),
        ),
        pieces=blocks,
    )


def middle_forward(gathered, full_out, ffn_up, ffn_down, residual, shared, split_biases, attn_weights, ffn_weights, count):
    rows, width = 2 * gathered.shape[1], gathered.shape[2]
    units = ffn_up.shape[1]
    chunks = rows // CHUNK
    lines = count // 2
    block = D // count

    def body(r):
        who = Partners()
        r.base = 0
        second = Exchange(who, pick(r, "second"))
        spread = Gather(who, SimpleNamespace(full=r.spread_full, sent=r.spread_sent, came=r.spread_came))
        last = Gather(who, SimpleNamespace(full=r.last_full, sent=r.last_sent, came=r.last_came))
        column = Column(count)
        who.meet(column)
        wide_attn = GatherBlocks(column, SimpleNamespace(full=r.full_attn, **vars(pick(r, "ga"))))
        wide_up = GatherBlocks(column, SimpleNamespace(full=r.full_up, **vars(pick(r, "gu"))))
        wide_down = GatherPairs(column, SimpleNamespace(full=r.full_down, **vars(pick(r, "gd"))))
        share = OutShare(who, SimpleNamespace(full=r.next_out, sent=r.share_sent, came=r.share_came))
        halo = Halo(column, SimpleNamespace(left=r.left, right=r.right, **vars(pick(r, "halo"))), r.pair, 2 * WIN, CHUNK)
        r.late.next_attn.wait()
        wide_attn.put(packed(r.next_attn.at[1]))
        wide_attn.start_line()
        wide_attn.start_pair()
        r.late.next_ffn.wait()
        wide_down.put(r.next_ffn[1, 1].astype(BF))
        wide_down.start_pair()
        wide_up.put(r.next_ffn[1, 0].astype(BF))
        halo.clear()
        r.late.full_out.wait()
        r.late.gathered.wait()
        r.hidden_bias = r.split[0][:, 2 * width :]
        next_bias = projection_bias(r.split[1], width)

        def unpack():
            wide_attn.arrive()
            packed_attn = r.full_attn[...].reshape(D, 4 * width)
            r.next_proj[...] = packed_attn[:, : 3 * width]
            share.begin(packed_attn[:, 3 * width :])

        ticks = [(0, r.late.residual.wait), (1, r.late.ffn_up.wait), (1, r.late.ffn_down.wait), (chunks, unpack), (chunks + 6, share.hand_on)]
        ticks += [(when, lambda k=k: wide_attn.relay(k + 1)) for k, when in enumerate(GATHER_TIMES[0])]
        ticks += [(GATHER_TIMES[1][0], wide_up.start_line), (GATHER_TIMES[1][1], wide_up.start_pair)]
        ticks += [(when, lambda k=k: wide_up.relay(k + 1)) for k, when in enumerate(GATHER_TIMES[2])]
        ticks += [(GATHER_TIMES[3][0], wide_down.begin)]
        ticks += [(when, lambda k=k: wide_down.relay(k + 1)) for k, when in enumerate(GATHER_TIMES[3][1:])]

        def projected(t):
            mine = jnp.concatenate([r.gathered[k, who.half(t), :] for k in range(4)], axis=1)
            return dot(mine, r.full_out[...].reshape(D, D))

        middle, feed, final = forward_stages(r, who, projected, second, spread)

        def middle_out(t):
            middle(t)
            r.flush.unit_one.copy(who.half(t), t).start()

        def feed_out(t):
            feed(t)
            for flush in (r.flush.hidden, r.flush.slope, r.flush.spread_full):
                flush.copy(who.chunk(t), t).start()

        def close(t):
            _, _, result = final(t)
            r.flush.unit_two.copy(who.half(t), t).start()
            last.give(t, result)

        def next_project(t):
            value = (dot(last.take(t), r.next_proj[...]) + next_bias).astype(BF)
            r.query[who.chunk(t), :] = value[:, :width]
            r.pair[who.chunk(t), :] = value[:, width:]
            halo.send(t)
            r.flush.last_full.copy(who.chunk(t), t).start()

        run_stages(
            chunks,
            [
                (2, second.add),
                (4, close),
                (0, middle_out),
                (8, next_project),
                (1, feed_out),
            ],
            ticks,
        )
        finish_all(chunks, (second, spread, last))
        halo.arrive()
        share.finish()
        wide_up.arrive()
        halo.finish()
        for engine in (wide_attn, wide_up, wide_down):
            engine.finish()

        def written(t, carry):
            for flush in (r.flush.hidden, r.flush.slope, r.flush.spread_full, r.flush.last_full):
                flush.copy(who.chunk(t), t).wait()
            for flush in (r.flush.unit_one, r.flush.unit_two):
                flush.copy(who.half(t), t).wait()
            return carry

        lax.fori_loop(0, chunks, written, 0)

    outputs = forward_small(rows)
    outputs.update(
        query=((rows, width), BF),
        pair=((rows, 2 * width), BF),
        full_attn=((count, block, 4 * width), BF),
        next_out=((4, width, D), BF),
        full_up=((count, block, units), BF),
        full_down=((count, block, units), BF),
        left=((2 * WIN, 2 * width), BF),
        right=((2 * WIN, 2 * width), BF),
    )
    flushed = forward_refs(rows, width, units)
    flushed.update(spread_full=((rows, D), BF), last_full=((rows, D), BF))
    scratch = dict(
        normed=pltpu.VMEM((rows // 2, D), F32),
        next_proj=pltpu.VMEM((D, 3 * width), BF),
        **share_scratch(),
    )
    scratch.update(prefixed("second", exchange_scratch(rows)))
    for key in ("spread", "last"):
        for part in ("sent", "came"):
            scratch[key + "_" + part] = pltpu.SemaphoreType.DMA((chunks,))
    for key in ("ga", "gu", "gd"):
        scratch.update(prefixed(key, gather_sems(lines)))
    scratch.update(prefixed("halo", halo_scratch(2 * WIN // CHUNK)))
    return run_kernel(
        body,
        "middle_forward",
        dict(shared=shared, split=split_biases),
        outputs,
        scratch,
        collective=1,
        flops=2 * rows * D * (4 * width + 2 * units),
        late=dict(
            next_attn=attn_weights,
            next_ffn=ffn_weights,
            full_out=full_out,
            gathered=gathered,
            residual=residual,
            ffn_up=ffn_up,
            ffn_down=ffn_down,
        ),
        flushed=flushed,
        pieces=chunks,
    )


def turning(mixed, first_mixed, out_proj, attn, ffn_up, ffn_down, residual, shared, split_biases, cotangent, turn):
    rows, width = mixed.shape
    units = ffn_up.shape[1]
    chunks = rows // WIDE_CHUNK

    def body(r):
        who = Partners(size=WIDE_CHUNK)
        r.base, r.grad_one = 6, None
        second, third = Exchange(who, pick(r, "second")), Exchange(who, pick(r, "third"))
        heads = HeadExchange(who, r.mixed, r.gathered, r.heads_sent, r.heads_came)
        spread = Gather(who, pick(r, "spread"))
        ends = Gather(who, pick(r, "ends"))
        mids = Gather(who, SimpleNamespace(full=r.grad_low, sent=r.mids_sent, came=r.mids_came))
        out = Gather(who, SimpleNamespace(full=r.output, sent=r.out_sent, came=r.out_came))
        who.meet()
        r.late.mixed.wait()
        for t in range(chunks // 2, chunks):
            heads.give(t)
        r.late.first_mixed.wait()
        r.gathered[:, : rows // 4, :] = r.first_mixed[...]
        r.late.full_out.wait()
        r.late.attn.wait()
        r.out_proj[...] = r.attn[:, 3 * width :]
        r.hidden_bias = r.split[1][:, 2 * width :]
        clear(r.vectors, r.units, r.sum_up, r.sum_down, r.sum_out)

        def projected(t):
            @pl.when(t >= chunks // 2)
            def _():
                heads.take(t)

            mine = jnp.concatenate([r.gathered[k, who.half(t), :] for k in range(4)], axis=1)
            return dot(mine, r.full_out[...].reshape(D, D))

        middle, feed, final = forward_stages(r, who, projected, second, spread)
        enter, feed_back, leave, project_back = backward_stages(r, who, ends, third, mids)

        ticks = [(0, r.late.residual.wait), (1, r.late.ffn_up.wait), (1, r.late.ffn_down.wait)]
        ticks += [(4, r.late.cotangent.wait), (4, r.late.turn.wait)]

        def close(t):
            unit, inverse, result = final(t)
            grad = dot(r.cotangent[who.own(t), :], r.turn[...])
            enter(t, grad, unit, inverse)
            out.give(t, result)

        run_stages(
            chunks,
            [
                (6, third.add),
                (2, second.add),
                (8, leave),
                (4, close),
                (0, middle),
                (9, project_back),
                (5, feed_back),
                (1, feed),
            ],
            ticks,
        )

        def arrive(t, carry):
            out.wait(t)
            return carry

        lax.fori_loop(0, chunks, arrive, 0)
        finish_all(chunks, (second, third, spread, ends, mids, out))
        for t in range(chunks // 2, chunks):
            heads.finish(t)
        r.up[...] = r.sum_up[...].astype(BF)
        r.down[...] = r.sum_down[...].astype(BF)
        r.proj[...] = r.sum_out[...].astype(BF)

    outputs = dict(
        output=((rows, D), BF),
        up=((D, units), BF),
        down=((D, units), BF),
        proj=((D, width), BF),
        grad_low=((rows, D), BF),
        grad_mixed=((rows, width), BF),
        vectors=((8, D), F32),
        units=((8, units), F32),
    )
    scratch = dict(
        normed=pltpu.VMEM((rows // 2, D), F32),
        kept=pltpu.VMEM((rows // 2, D), F32),
        grad_pre=pltpu.VMEM((2 * WIDE_CHUNK, units), BF),
        out_proj=pltpu.VMEM((D, width), BF),
        gathered=pltpu.VMEM((4, rows // 2, width), BF),
        heads_sent=pltpu.SemaphoreType.DMA((3, chunks)),
        heads_came=pltpu.SemaphoreType.DMA((3, chunks)),
        sum_up=pltpu.VMEM((D, units), F32),
        sum_down=pltpu.VMEM((D, units), F32),
        sum_out=pltpu.VMEM((D, width), F32),
        mids_sent=pltpu.SemaphoreType.DMA((chunks,)),
        mids_came=pltpu.SemaphoreType.DMA((chunks,)),
        out_sent=pltpu.SemaphoreType.DMA((chunks,)),
        out_came=pltpu.SemaphoreType.DMA((chunks,)),
    )
    for key, (shape, dtype) in {**forward_refs(rows, width, units), **forward_small(rows)}.items():
        scratch[key] = pltpu.VMEM(shape, dtype)
    for key in ("second", "third"):
        scratch.update(prefixed(key, exchange_scratch(rows)))
    for key in ("spread", "ends"):
        scratch.update(prefixed(key, gather_scratch(rows)))
    return run_kernel(
        body,
        "turning",
        dict(
            shared=shared,
            split=split_biases,
        ),
        outputs,
        scratch,
        collective=2,
        flops=2 * rows * D * (3 * width + 6 * units),
        late=dict(
            mixed=mixed,
            first_mixed=first_mixed,
            full_out=out_proj,
            attn=attn,
            residual=residual,
            ffn_up=ffn_up,
            ffn_down=ffn_down,
            cotangent=cotangent,
            turn=turn,
        ),
    )


def projection_back_stage(r, who, column, exchange):
    rows, width = r.grad_query.shape
    rim = r.out_right.shape[0]
    first, last = column.index == 0, column.index == column.count - 1
    after = (lax.rem(column.index + 1, column.count), column.here)
    copy = copy_to(r.out_right, r.from_left, r.halo_sent.at[0], r.halo_came.at[0], after)

    def begin():
        r.grad_pair[...] = r.grad_own[...]

        @pl.when(jnp.logical_not(last))
        def _():
            copy.start()

    def absorb():
        @pl.when(jnp.logical_not(first))
        def _():
            copy.wait_recv()
            where = pl.ds(0, rim)
            total = r.grad_pair[where, :].astype(F32) + r.from_left[...].astype(F32)
            r.grad_pair[where, :] = total.astype(BF)

    def end():
        @pl.when(jnp.logical_not(last))
        def _():
            copy.wait_send()

    def stage(k):
        both = who.two_chunks(2 * k + 1)
        parts = jnp.concatenate([r.grad_query[both, :], r.grad_pair[both, :]], axis=1)
        exchange.r.part[both, :] = dot_nt(parts, r.next_attn[:, : 3 * width]).astype(BF)
        for t in (2 * k, 2 * k + 1):
            exchange.core_copy(t).start()
        r.sum_three[...] += dot_tn(r.low[both, :], parts)
        r.biases[0:1, :] += column_sum(parts.astype(F32))

    half = rows // CHUNK // 2
    steps = [(0 if k < half // 2 else half, k) for k in range(half)]
    ticks = [(half, absorb)] + [(first_time + k % (half // 2), lambda k=k: stage(k)) for first_time, k in steps]
    return begin, end, ticks


def projection_back_scratch(rows, rim, width):
    return dict(
        grad_pair=pltpu.VMEM((rows, 2 * width), BF),
        from_left=pltpu.VMEM((rim, 2 * width), BF),
        halo_sent=pltpu.SemaphoreType.DMA((1,)),
        halo_came=pltpu.SemaphoreType.DMA((1,)),
        sum_three=pltpu.VMEM((D, 3 * width), F32),
    )


def scatter_three(column, r, totals):
    return (
        ScatterPairs(column, SimpleNamespace(grads=r.above_up, **vars(pick(r, "ru"))), totals[0]),
        ScatterBlocks(column, SimpleNamespace(grads=r.above_down, **vars(pick(r, "rd"))), totals[1]),
        ScatterBlocks(column, SimpleNamespace(grads=r.packed, **vars(pick(r, "ra"))), totals[2]),
    )


def scatter_three_scratch(count, width, units):
    lines, block = count // 2, D // count
    scratch = dict(packed=pltpu.VMEM((count, block, 4 * width), BF))
    scratch.update(prefixed("ru", scatter_pairs_scratch(lines, block, units)))
    scratch.update(prefixed("rd", scatter_scratch(lines, block, units)))
    scratch.update(prefixed("ra", scatter_scratch(lines, block, 4 * width, held=False)))
    return scratch


def pack_attention(r):
    both = jnp.concatenate([r.sum_three[...].astype(BF), r.above_proj[...]], axis=1)
    r.packed[...] = both.reshape(r.packed.shape)


def middle_backward(back, next_attn, grad_above, low, saved, mixed, attn, ffn_up, ffn_down, shared, above, count):
    rows, width = mixed.shape
    units = ffn_up.shape[1]
    chunks = rows // CHUNK
    block = D // count
    rim = back.out_right.shape[0]

    def body(r):
        who = Partners(chunks, chunks // 2)
        r.base = 0
        zeroth, third = Exchange(who, pick(r, "zeroth")), Exchange(who, pick(r, "third"))
        ends, mids = Gather(who, pick(r, "ends")), Gather(who, pick(r, "mids"))
        column = Column(count)
        who.meet(column)
        up, down, three = scatter_three(column, r, (r.up_total, r.down_total, r.attn_total))
        begin, end, back_ticks = projection_back_stage(r, who, column, zeroth)
        for copy in (r.late.out_right, r.late.grad_own, r.late.grad_query, r.late.next_attn, r.late.low):
            copy.wait()
        begin()
        up.start()
        down.start()

        def start_three():
            pack_attention(r)
            three.start()

        ticks = [tick for engine, times in zip((up, down, three), BACK_TIMES) for tick in engine.ticks(times)]
        ticks += [(chunks // 2 + 2, start_three)]
        ticks += [(3, r.late.unit_two.wait), (3, r.late.grad_above.wait), (4, r.late.ffn_up.wait)]
        ticks += [(4, r.late.ffn_down.wait), (4, r.late.slope.wait), (4, r.late.hidden.wait)]
        ticks += [(4, r.late.spread_full.wait), (7, r.late.unit_one.wait), (8, r.late.mixed.wait)]
        ticks = back_ticks + ticks
        r.late.attn.wait()
        r.out_proj[...] = r.attn[:, 3 * width :]
        clear(r.vectors, r.units, r.biases, r.sum_up, r.sum_down, r.sum_out, r.sum_three)
        enter, feed_back, leave, project_back = backward_stages(r, who, ends, third, mids)

        def start(t):
            half = who.half(t)
            enter(t, r.grad_above[who.own(t), :].astype(F32) + zeroth.take(t), r.unit_two[half, :], r.inverse_two[half, 0:1])

        run_stages(
            chunks,
            [
                (5, third.add),
                (1, zeroth.add),
                (7, leave),
                (3, start),
                (8, project_back),
                (4, feed_back),
            ],
            ticks,
        )
        finish_all(chunks, (zeroth, third, ends, mids))
        end()
        r.up[...] = r.sum_up[...].astype(BF)
        r.down[...] = r.sum_down[...].astype(BF)
        r.proj[...] = r.sum_out[...].astype(BF)
        for engine in (up, down, three):
            engine.finish()

    outputs = dict(
        up=((D, units), BF),
        down=((D, units), BF),
        proj=((D, width), BF),
        grad_one=((rows // 2, D), F32),
        grad_mixed=((rows, width), BF),
        vectors=((8, D), F32),
        units=((8, units), F32),
        biases=((8, 3 * width), F32),
        up_total=((block, units), F32),
        down_total=((block, units), F32),
        attn_total=((block, 4 * width), F32),
    )
    scratch = dict(
        kept=pltpu.VMEM((rows // 2, D), F32),
        grad_pre=pltpu.VMEM((2 * CHUNK, units), BF),
        out_proj=pltpu.VMEM((D, width), BF),
        sum_up=pltpu.VMEM((D, units), F32),
        sum_down=pltpu.VMEM((D, units), F32),
        sum_out=pltpu.VMEM((D, width), F32),
    )
    scratch.update(projection_back_scratch(rows, rim, width))
    scratch.update(scatter_three_scratch(count, width, units))
    for key in ("zeroth", "third"):
        scratch.update(prefixed(key, exchange_scratch(rows)))
    for key in ("ends", "mids"):
        scratch.update(prefixed(key, gather_scratch(rows)))
    return run_kernel(
        body,
        "middle_backward",
        dict(
            inverse_one=saved.inverse_one,
            inverse_two=saved.inverse_two,
            shared=shared,
            above_up=above.up.reshape(count, block, units),
            above_down=above.down.reshape(count, block, units),
            above_proj=above.proj,
        ),
        outputs,
        scratch,
        collective=3,
        flops=2 * rows * D * (8 * width + 4 * units),
        in_hbm=("above_up", "above_down"),
        late=dict(
            out_right=back.out_right,
            grad_own=back.out_own,
            grad_query=back.out_query,
            next_attn=next_attn,
            low=low,
            attn=attn,
            unit_two=saved.unit_two,
            grad_above=grad_above,
            ffn_down=ffn_down,
            slope=saved.slope,
            ffn_up=ffn_up,
            hidden=saved.hidden,
            spread_full=saved.spread_full,
            unit_one=saved.unit_one,
            mixed=mixed,
        ),
    )


class SmallSum:
    def __init__(self, who, column, refs):
        self.who, self.c, self.r = who, column, refs

    def copy(self, slot, source, device):
        r = self.r
        return copy_to(r.kept.at[source], r.came.at[slot], r.sent_sem.at[slot], r.came_sem.at[slot], device)

    def core_copy(self):
        return self.copy(0, 0, self.who.sibling)

    def pair_copy(self):
        return self.copy(1, 1, self.c.at(self.c.outer, 1 - self.c.inner))

    def line_copy(self, target, slot):
        c, r = self.c, self.r
        return copy_to(
            r.kept.at[2], r.came.at[2 + slot], r.sent_sem.at[2 + target], r.came_sem.at[2 + slot], c.at(target, c.inner)
        )

    def second(self, both):
        r = self.r
        self.core_copy().wait_recv()
        row = lax.broadcasted_iota(jnp.int32, r.kept.shape[1:], 0)
        r.kept[1] = r.kept[0] + jnp.where(row < both, r.came[0], 0.0)
        self.pair_copy().start()

    def third(self):
        r, c = self.r, self.c
        self.pair_copy().wait_recv()
        r.kept[2] = r.kept[1] + r.came[1]
        for k in range(1, c.lines):
            self.line_copy(c.turn(k), c.outer).start()
        r.came[2 + c.outer] = r.kept[2]

    def result(self):
        r, c = self.r, self.c
        for k in range(1, c.lines):
            source = c.turn(k)
            self.line_copy(source, source).wait_recv()
        return sum(r.came[2 + k] for k in range(c.lines))

    def finish(self):
        c = self.c
        self.core_copy().wait_send()
        self.pair_copy().wait_send()
        for k in range(1, c.lines):
            self.line_copy(c.turn(k), c.outer).wait_send()


def small_scratch(lines, shape):
    return dict(
        kept=pltpu.VMEM((3,) + shape, F32),
        came=pltpu.VMEM((2 + lines,) + shape, F32),
        sent_sem=pltpu.SemaphoreType.DMA((2 + lines,)),
        came_sem=pltpu.SemaphoreType.DMA((2 + lines,)),
    )


class NormSum:
    def __init__(self, who, column, refs):
        self.who, self.c, self.r = who, column, refs

    def mp_copy(self, device, target, slot):
        r = self.r
        return copy_to(r.mp_came.at[slot], r.mp_came.at[slot], r.mp_sent.at[target], r.mp_sem.at[slot], device)

    def seq_copy(self, device, target, slot):
        r = self.r
        return copy_to(r.seq_came.at[slot], r.seq_came.at[slot], r.seq_sent.at[target], r.seq_sem.at[slot], device)

    def run(self, value):
        who, c, r = self.who, self.c, self.r
        here = c.here
        r.mp_came[here] = jnp.full((8, 128), 1.0, F32) * value
        for k in range(1, 4):
            target = lax.rem(here + k, 4)
            self.mp_copy((c.index, target), target, here).start()
        for k in range(1, 4):
            source = lax.rem(here + k, 4)
            self.mp_copy((c.index, source), source, source).wait_recv()
        r.seq_came[c.index] = sum(r.mp_came[k] for k in range(4))
        for k in range(1, c.count):
            target = lax.rem(c.index + k, c.count)
            self.seq_copy((target, here), target, c.index).start()
        for k in range(1, c.count):
            source = lax.rem(c.index + k, c.count)
            self.seq_copy((source, here), source, source).wait_recv()
        total = sum(r.seq_came[k] for k in range(c.count))
        for k in range(1, 4):
            target = lax.rem(here + k, 4)
            self.mp_copy((c.index, target), target, here).wait_send()
        for k in range(1, c.count):
            target = lax.rem(c.index + k, c.count)
            self.seq_copy((target, here), target, c.index).wait_send()
        return total


def norm_scratch(count):
    return dict(
        mp_came=pltpu.VMEM((4, 8, 128), F32),
        mp_sent=pltpu.SemaphoreType.DMA((4,)),
        mp_sem=pltpu.SemaphoreType.DMA((4,)),
        seq_came=pltpu.VMEM((count, 8, 128), F32),
        seq_sent=pltpu.SemaphoreType.DMA((count,)),
        seq_sem=pltpu.SemaphoreType.DMA((count,)),
    )


def squares(ref):
    value = ref[...]
    return jnp.sum(value * value)


def ending(back, next_attn, grad_above, low, above, top, count):
    rows, width = back.out_query.shape
    chunks = rows // CHUNK
    lines, block = count // 2, D // count
    units = above.units.shape[1]
    rim = back.out_right.shape[0]

    def body(r):
        who = Partners(chunks, chunks // 2)
        zeroth = Exchange(who, pick(r, "zeroth"))
        out = Gather(who, SimpleNamespace(full=r.output, sent=r.out_sent, came=r.out_came))
        column = Column(count)
        who.meet(column)
        up, down, three = scatter_three(column, r, (r.ffn_grads.at[0], r.ffn_grads.at[1], r.attn_grads.at[0]))
        small = SmallSum(who, column, pick(r, "small"))
        begin, end, back_ticks = projection_back_stage(r, who, column, zeroth)
        for copy in (r.late.out_right, r.late.grad_own, r.late.grad_query, r.late.next_attn, r.late.low):
            copy.wait()
        begin()
        up.start()
        down.start()

        def start_three():
            small.second(12)
            pack_attention(r)
            three.start()

        def start_small():
            r.small_kept[0, 0:6, :] = r.vectors_low[0:6, :]
            r.small_kept[0, 6:12, :] = r.vectors_top[0:6, :]
            r.small_kept[0, 12:13, :] = r.units_low[0:1, :]
            r.small_kept[0, 13:14, :] = r.units_top[0:1, :]
            pieces = []
            for ref in (r.biases, r.biases_top):
                pieces += [ref[0:1, :width], ref[0:1, 2 * width :]]
            r.small_kept[0, 14:15, :] = jnp.concatenate(pieces, axis=1)
            r.small_kept[0, 15:16, :] = jnp.zeros((1, D), F32)
            small.core_copy().start()

        ticks = [tick for engine, times in zip((up, down, three), END_TIMES) for tick in engine.ticks(times)]
        ticks += [(3, r.late.grad_above.wait)]
        ticks += [(chunks // 2 + 2, start_small), (SMALL_TIMES[0], start_three), (SMALL_TIMES[1], small.third)]
        ticks = back_ticks + ticks
        clear(r.biases, r.sum_three)

        def close(t):
            out.give(t, r.grad_above[who.half(t), :] + zeroth.take(t))

        run_stages(chunks, [(1, zeroth.add), (3, close)], ticks)
        vectors = small.result()
        r.vectors[...] = vectors
        r.ffn_grads[2] = r.up_top[...]
        r.ffn_grads[3] = r.down_top[...]
        r.attn_grads[1] = r.attn_top[...]
        row = lax.broadcasted_iota(jnp.int32, (16, D), 0)
        squared = vectors * vectors
        split = jnp.sum(jnp.where(row >= 12, squared, 0.0))
        shared = jnp.sum(jnp.where(row < 12, squared, 0.0))
        first_seq = column.index == 0
        first_both = jnp.logical_and(first_seq, column.here == 0)
        value = squares(r.ffn_grads) + squares(r.attn_grads)
        value = value + jnp.where(first_seq, split, 0.0) + jnp.where(first_both, shared, 0.0)
        total = NormSum(who, column, pick(r, "norm")).run(value)
        r.norm[...] = jnp.sqrt(total)

        def arrive(t, carry):
            out.wait(t)
            return carry

        lax.fori_loop(0, chunks, arrive, 0)
        finish_all(chunks, (zeroth, out))
        end()
        for engine in (up, down, three, small):
            engine.finish()

    outputs = dict(
        output=((rows, D), BF),
        ffn_grads=((4, block, units), F32),
        attn_grads=((2, block, 4 * width), F32),
        vectors=((16, D), F32),
        norm=((8, 128), F32),
    )
    scratch = dict(
        biases=pltpu.VMEM((8, 3 * width), F32),
        out_sent=pltpu.SemaphoreType.DMA((chunks,)),
        out_came=pltpu.SemaphoreType.DMA((chunks,)),
    )
    scratch.update(projection_back_scratch(rows, rim, width))
    scratch.update(scatter_three_scratch(count, width, units))
    scratch.update(prefixed("zeroth", exchange_scratch(rows)))
    scratch.update(prefixed("small", small_scratch(lines, (16, D))))
    scratch.update(prefixed("norm", norm_scratch(count)))
    return run_kernel(
        body,
        "ending",
        dict(
            above_up=above.up.reshape(count, block, units),
            above_down=above.down.reshape(count, block, units),
            above_proj=above.proj,
            up_top=above.up_total,
            down_top=above.down_total,
            attn_top=above.attn_total,
            vectors_low=above.vectors,
            vectors_top=top.vectors,
            units_low=above.units,
            units_top=top.units,
            biases_top=above.biases,
        ),
        outputs,
        scratch,
        collective=4,
        flops=2 * rows * D * 6 * width,
        in_hbm=("above_up", "above_down"),
        late=dict(
            out_right=back.out_right,
            grad_own=back.out_own,
            grad_query=back.out_query,
            next_attn=next_attn,
            low=low,
            grad_above=grad_above,
        ),
    )


def moments(grad, first, second):
    first_new = BETA_FIRST * first + (1.0 - BETA_FIRST) * grad
    second_new = BETA_SECOND * second + (1.0 - BETA_SECOND) * grad * grad
    size = jnp.sqrt(second_new / (1.0 - BETA_SECOND**STEP)) + ADAM_EPSILON
    return first_new, second_new, first_new / (1.0 - BETA_FIRST**STEP) / size


def update(result, end, turn, attn, ffn, split, shared):
    block, units = ffn[0].shape[2:]
    width = attn[0].shape[3]
    rates = [0.5 * D ** (-0.5)] * 3 + [0.5 * (WIN / D) ** 0.5]
    names = ("weights", "first", "second", "average", "basis")

    def matrix(grad, weight, first, second, average, basis, rate):
        basis = basis.astype(BF)
        turned = dot(grad.astype(BF), basis)
        first_new, second_new, direction = moments(turned, first, second)
        back = dot_nt(direction.astype(BF), basis)
        weight_new = weight - rate * (back + DECAY_RATE * weight)
        return weight_new, first_new, second_new, AVERAGE_RATE * average + (1.0 - AVERAGE_RATE) * weight_new

    def body(r):
        step = pl.program_id(0)
        factor = CLIP_LEVEL / jnp.maximum(r.norm[0:1, 0:1], CLIP_LEVEL)
        r.result_real[...] = dot_nt(r.result[...], r.turn[...])
        r.grad_real[...] = dot_nt(r.grad[...], r.turn[...])
        rate = jnp.where(step % 2 == 0, 0.5 * D ** (-0.5), 0.5 * FF ** (-0.5))
        results = matrix(
            factor * r.ffn_grads[...],
            r.ffn_weights[...],
            r.ffn_first[...],
            r.ffn_second[...],
            r.ffn_average[...],
            r.ffn_basis[...],
            rate,
        )
        for key, value in zip(names, results):
            getattr(r, "ffn_" + key + "_new")[...] = value

        for k in range(2):
            last = jnp.logical_and(step % 2 == 1, k == 1)
            weight, first, second, average = matrix(
                factor * r.attn_grads[:, k * width : (k + 1) * width],
                r.attn_weights[k],
                r.attn_first[k],
                r.attn_second[k],
                r.attn_average[k],
                r.attn_basis[k],
                jnp.where(last, rates[3], rates[0]),
            )
            r.attn_weights_new[k] = weight
            r.attn_first_new[k] = first
            r.attn_average_new[k] = average

            @pl.when(step % 2 == 0)
            def _(k=k, second=second):
                r.attn_second_new[step // 2, k] = second

            @pl.when(step % 2 == 1)
            def _(k=k, second=second):
                if k == 0:
                    r.attn_second_new[step // 2, 2] = second
                else:
                    r.projection_second[step // 2] = second

        @pl.when(step == 0)
        def _():
            r.norm_out[0, 0] = jnp.max(r.norm[0:1, :])
            real = exact(r.vectors[...], lambda part: dot_nt(part, r.turn[...]))
            for layer in range(2):
                tail = r.vectors[14:15, layer * 2 * width : (layer + 1) * 2 * width]
                split_grad = jnp.concatenate([tail, r.vectors[12 + layer : 13 + layer, :]], axis=1)
                grad = factor * split_grad
                first_new, second_new, direction = moments(grad, r.split_first[layer], r.split_second[layer])
                r.split_old_new[layer] = r.split_old[layer] - VECTOR_RATE * direction
                r.split_first_new[layer] = first_new
                r.split_second_new[layer] = second_new
            for k in range(6):
                grad = factor * jnp.concatenate([real[k : k + 1], real[6 + k : 7 + k]], axis=0)
                first_new, second_new, direction = moments(grad, r.shared_first[k], r.shared_second[k])
                r.shared_old_new[k] = r.shared_old[k] - VECTOR_RATE * direction
                r.shared_first_new[k] = first_new
                r.shared_second_new[k] = second_new

    inputs = dict(
        ffn_grads=end.ffn_grads, attn_grads=end.attn_grads, vectors=end.vectors, norm=end.norm, turn=turn
    )
    rows = result.shape[0]
    inputs.update(result=result, grad=end.output)
    outputs = dict(result_real=((rows, D), F32), grad_real=((rows, D), F32))
    row_spec = pl.BlockSpec((rows // 4, D), lambda i: (i, 0))
    specs = dict(result=row_spec, grad=row_spec, result_real=row_spec, grad_real=row_spec)
    specs["ffn_grads"] = pl.BlockSpec((None, block, units), lambda i: (i, 0, 0))
    matrix_spec = pl.BlockSpec((None, None, block, units), lambda i: (i // 2, i % 2, 0, 0))
    for key, array in zip(names, ffn):
        inputs["ffn_" + key] = array
        specs["ffn_" + key] = matrix_spec
    specs["ffn_basis"] = pl.BlockSpec((None, None, None, None, units, units), lambda i: (i // 2, i % 2, 0, 0, 0, 0))
    pair_spec = pl.BlockSpec((None, 2, block, width), lambda i: (i // 2, i % 2, 0, 0))
    for key, array in zip(names, attn):
        inputs["attn_" + key] = array
        specs["attn_" + key] = pair_spec
    specs["attn_basis"] = pl.BlockSpec((None, 2, None, None, width, width), lambda i: (i // 2, i % 2, 0, 0, 0, 0))
    specs["attn_grads"] = pl.BlockSpec((None, block, 2 * width), lambda i: (i // 2, 0, i % 2))
    for prefix, group in (("split", split), ("shared", shared)):
        for key, array in zip(("old", "first", "second"), group):
            inputs[prefix + "_" + key] = array
    for key in ("weights", "first", "second", "average"):
        outputs["ffn_" + key + "_new"] = (ffn[0].shape, F32)
        specs["ffn_" + key + "_new"] = matrix_spec
        outputs["attn_" + key + "_new"] = (attn[0].shape, F32)
        specs["attn_" + key + "_new"] = pair_spec
    outputs["attn_second_new"] = ((2, 3, block, width), F32)
    del specs["attn_second_new"]
    outputs["projection_second"] = ((2, block, width), F32)
    for prefix, group in (("split", split), ("shared", shared)):
        for key in ("old", "first", "second"):
            outputs[prefix + "_" + key + "_new"] = (group[0].shape, F32)
    outputs["norm_out"] = ((1, 1), F32)
    return run_kernel(
        body,
        "update",
        inputs,
        outputs,
        {},
        flops=4 * block * units * units * 4,
        grid=(4,),
        specs=specs,
        in_smem=("norm_out",),
    )


def direct(
    activations,
    cotangent,
    segments,
    dilated_heads,
    owners,
    attn_weights,
    attn_first,
    attn_second,
    attn_average,
    attn_basis,
    ffn_weights,
    ffn_first,
    ffn_second,
    ffn_average,
    ffn_basis,
    split_biases,
    split_first,
    split_second,
    shared_vectors,
    shared_first,
    shared_second,
):
    count = lax.axis_size(SEQ)
    near = opening(
        activations, segments, owners, attn_weights, ffn_weights, split_biases, shared_vectors, count
    )
    near.arranged = near.out
    attn_zero, up_zero, down_zero = (
        full.reshape(D, -1) for full in (near.full_attn, near.full_up, near.full_down)
    )
    mid = middle_forward(
        near.gathered,
        near.full_out,
        up_zero,
        down_zero,
        near.low,
        near.shared,
        split_biases,
        attn_weights,
        ffn_weights,
        count,
    )
    far = attend(
        mid.query,
        mid.pair,
        mid.left,
        mid.right,
        near.seg_query,
        near.seg_keys,
        dilated_heads,
    )
    attn_one, up_one, down_one = (full.reshape(D, -1) for full in (mid.full_attn, mid.full_up, mid.full_down))
    top = turning(
        far.out, far.first, mid.next_out, attn_one, up_one, down_one, mid.last_full, near.shared, split_biases, cotangent, near.turn
    )
    far_back = attend_back(far, top.grad_mixed, dilated_heads, 2 * WIN, True, count, 6)
    low = middle_backward(
        far_back,
        attn_one,
        top.grad_low,
        mid.last_full,
        mid,
        near.out,
        attn_zero,
        up_zero,
        down_zero,
        near.shared,
        top,
        count,
    )
    near_back = attend_back(near, low.grad_mixed, dilated_heads, WIN, False, count, 7)
    end = ending(near_back, attn_zero, low.grad_one, near.low, low, top, count)
    new = update(
        top.output,
        end,
        near.turn,
        (attn_weights, attn_first, attn_second, attn_average, attn_basis),
        (ffn_weights, ffn_first, ffn_second, ffn_average, ffn_basis),
        (split_biases, split_first, split_second),
        tuple(array.transpose(1, 0, 2) for array in (shared_vectors, shared_first, shared_second)),
    )
    return (
        new.result_real,
        new.grad_real,
        new.attn_weights_new,
        new.attn_first_new,
        new.attn_second_new,
        new.projection_second,
        new.attn_average_new,
        new.ffn_weights_new,
        new.ffn_first_new,
        new.ffn_second_new,
        new.ffn_average_new,
        new.split_old_new,
        new.split_first_new,
        new.split_second_new,
        new.shared_old_new.transpose(1, 0, 2),
        new.shared_first_new.transpose(1, 0, 2),
        new.shared_second_new.transpose(1, 0, 2),
        new.norm_out.reshape(()),
    )


def with_halo(cells, sides, width):
    for axis, dim in sides:
        count = lax.axis_size(axis)
        ends = count - 1
        head = lax.slice_in_dim(cells, 0, width, axis=dim)
        tail = lax.slice_in_dim(cells, cells.shape[dim] - width, cells.shape[dim], axis=dim)
        cells = jnp.concatenate(
            [
                lax.ppermute(tail, axis, [(i, (i + 1) % count) for i in range(ends)]),
                cells,
                lax.ppermute(head, axis, [((i + 1) % count, i) for i in range(ends)]),
            ],
            axis=dim,
        )
    return cells


def from_behind(block, axis, distance):
    devices = range(lax.axis_size(axis))
    route = [(i - distance, i) for i in devices if i - distance in devices]
    return lax.ppermute(block, axis, route)


def normalize_layer(values, gain, shift):
    center = values - jnp.mean(values, axis=-1, keepdims=True)
    spread = jnp.mean(center * center, axis=-1, keepdims=True)
    return center * lax.rsqrt(spread + NORM_EPSILON) * gain + shift


def head_masks(offsets, dilated):
    near = jnp.abs(offsets) <= WIN
    far = jnp.logical_and(jnp.abs(offsets) <= 2 * WIN, offsets % 2 == 0)
    return jnp.where(dilated[:, None, None], far[None, :, :], near[None, :, :])


def join_heads(term):
    return lax.psum(term.astype(jnp.bfloat16), MP).astype(jnp.float32)


def join_grads(term):
    return lax.psum(term, MP)


def fetch_rims(pair, rim_width):
    return with_halo(pair, ((SEQ, 0),), rim_width)


def masked_scores(query_block, key_block, seg_query, seg_keys, dilated, rim_width):
    block_rows = query_block.shape[0]
    key_rows = key_block.shape[0]
    offsets = (
        jnp.arange(block_rows, dtype=jnp.int32)[:, None]
        - jnp.arange(key_rows, dtype=jnp.int32)[None, :]
        + rim_width
    )
    allowed = jnp.logical_and(
        head_masks(offsets, dilated), (seg_query[:, None] == seg_keys[None, :])[None, :, :]
    )
    raw = jnp.einsum(
        "qhd,khd->hqk", query_block, key_block, preferred_element_type=jnp.float32
    ) * DH ** (-0.5)
    return jnp.where(allowed, raw, MASK_FILL)


def plain_attend(query, key_pad, value_pad, seg_own, seg_near, dilated, rim_width):
    row_count = query.shape[0]
    block_rows = min(512, row_count)
    key_rows = block_rows + 2 * rim_width

    def one_block(first_row):
        query_block = lax.dynamic_slice_in_dim(query, first_row, block_rows, 0)
        key_block = lax.dynamic_slice_in_dim(key_pad, first_row, key_rows, 0)
        value_block = lax.dynamic_slice_in_dim(value_pad, first_row, key_rows, 0)
        scores = masked_scores(
            query_block,
            key_block,
            lax.dynamic_slice_in_dim(seg_own, first_row, block_rows, 0),
            lax.dynamic_slice_in_dim(seg_near, first_row, key_rows, 0),
            dilated,
            rim_width,
        )
        row_max = jnp.max(scores, axis=2, keepdims=True)
        exponent = jnp.exp(scores - row_max)
        row_total = jnp.sum(exponent, axis=2, keepdims=True)
        softmax = (exponent / row_total).astype(jnp.bfloat16)
        mixed_block = jnp.einsum(
            "hqk,khd->qhd", softmax, value_block, preferred_element_type=jnp.float32
        )
        return (mixed_block, (row_max + jnp.log(row_total))[:, :, 0])

    starts = jnp.arange(row_count // block_rows, dtype=jnp.int32) * block_rows
    mixed_heads, log_totals = lax.map(one_block, starts)
    return (mixed_heads.reshape(row_count, -1), log_totals)


def plain_attend_back(query, padded, log_totals, grad_mixed, seg_own, seg_near, dilated, rim_width):
    row_count, head_count, _ = query.shape
    head_width = head_count * DH
    block_rows = min(512, row_count)
    key_rows = block_rows + 2 * rim_width
    key_pad = padded[:, :head_width].reshape(-1, head_count, DH)
    value_pad = padded[:, head_width:].reshape(-1, head_count, DH)
    grad_heads = grad_mixed.reshape(row_count, head_count, DH)
    score_scale = DH ** (-0.5)

    def one_step(carry, inputs):
        first_row, totals_block = inputs
        query_block = lax.dynamic_slice_in_dim(query, first_row, block_rows, 0)
        key_block = lax.dynamic_slice_in_dim(key_pad, first_row, key_rows, 0)
        value_block = lax.dynamic_slice_in_dim(value_pad, first_row, key_rows, 0)
        grad_block = lax.dynamic_slice_in_dim(grad_heads, first_row, block_rows, 0)
        scores = masked_scores(
            query_block,
            key_block,
            lax.dynamic_slice_in_dim(seg_own, first_row, block_rows, 0),
            lax.dynamic_slice_in_dim(seg_near, first_row, key_rows, 0),
            dilated,
            rim_width,
        )
        softmax = jnp.exp(scores - totals_block[:, :, None])
        grad_value = jnp.einsum(
            "hqk,qhd->khd",
            softmax.astype(jnp.bfloat16),
            grad_block,
            preferred_element_type=jnp.float32,
        )
        grad_soft = jnp.einsum(
            "qhd,khd->hqk", grad_block, value_block, preferred_element_type=jnp.float32
        )
        row_dot = jnp.sum(grad_soft * softmax, axis=2, keepdims=True)
        grad_scores = (softmax * (grad_soft - row_dot)).astype(jnp.bfloat16)
        grad_query = (
            jnp.einsum("hqk,khd->qhd", grad_scores, key_block, preferred_element_type=jnp.float32)
            * score_scale
        )
        grad_key = (
            jnp.einsum("hqk,qhd->khd", grad_scores, query_block, preferred_element_type=jnp.float32)
            * score_scale
        )
        update = jnp.concatenate(
            [grad_key.reshape(key_rows, head_width), grad_value.reshape(key_rows, head_width)],
            axis=1,
        )
        current = lax.dynamic_slice_in_dim(carry, first_row, key_rows, 0)
        carry = lax.dynamic_update_slice_in_dim(carry, current + update, first_row, 0)
        return (carry, grad_query.reshape(block_rows, head_width))

    starts = jnp.arange(row_count // block_rows, dtype=jnp.int32) * block_rows
    initial = jnp.zeros((row_count + 2 * rim_width, 2 * head_width), jnp.float32)
    grad_pad, grad_query = lax.scan(one_step, initial, (starts, log_totals))
    from_above = from_behind(grad_pad[:rim_width], SEQ, -1)
    from_below = from_behind(grad_pad[row_count + rim_width :], SEQ, 1)
    grad_pair = grad_pad[rim_width : row_count + rim_width]
    grad_pair = (
        grad_pair
        + jnp.pad(from_below, ((0, row_count - rim_width), (0, 0)))
        + jnp.pad(from_above, ((row_count - rim_width, 0), (0, 0)))
    )
    return (grad_query.reshape(row_count, head_width), grad_pair)


def layer_forward(inputs, attn, ffn, shared, split, seg_own, seg_pad, dilated, rim_width):
    head_width = attn.shape[2]
    row_count = inputs.shape[0]
    inputs_low = inputs.astype(jnp.bfloat16)
    biases = jnp.stack(
        [
            split[0, :head_width],
            jnp.zeros((head_width,), jnp.float32),
            split[0, head_width : 2 * head_width],
        ]
    )
    projected = (
        jnp.einsum("td,mdc->tmc", inputs_low, attn[:3], preferred_element_type=jnp.float32)
        + biases[None]
    ).astype(jnp.bfloat16)
    query = projected[:, 0].reshape(row_count, -1, DH)
    padded = fetch_rims(jnp.concatenate([projected[:, 1], projected[:, 2]], axis=1), rim_width)
    key_pad = padded[:, :head_width].reshape(-1, head_width // DH, DH)
    value_pad = padded[:, head_width:].reshape(-1, head_width // DH, DH)
    seg_near = lax.slice_in_dim(
        seg_pad, 2 * WIN - rim_width, 2 * WIN + row_count + rim_width, axis=0
    )
    mixed_heads, log_totals = plain_attend(
        query, key_pad, value_pad, seg_own, seg_near, dilated, rim_width
    )
    mixed_heads = mixed_heads.astype(jnp.bfloat16)
    attn_sum = (
        inputs
        + join_heads(
            dot_nt(mixed_heads, attn[3])
        )
        + shared[0]
    )
    normed = normalize_layer(attn_sum, shared[1], shared[2])
    normed_low = normed.astype(jnp.bfloat16)
    pre_gelu = (
        jnp.dot(normed_low, ffn[0], preferred_element_type=jnp.float32) + split[0, 2 * head_width :]
    )
    hidden = jax.nn.gelu(pre_gelu, approximate=False).astype(jnp.bfloat16)
    ffn_sum = (
        normed
        + join_heads(dot_nt(hidden, ffn[1]))
        + shared[3]
    )
    result = normalize_layer(ffn_sum, shared[4], shared[5])
    return (
        result,
        (
            inputs_low,
            query,
            padded,
            log_totals,
            mixed_heads,
            attn_sum,
            normed_low,
            pre_gelu,
            hidden,
            ffn_sum,
        ),
    )


def layer_backward(grad_out, saved, attn, ffn, shared, seg_own, seg_pad, dilated, rim_width):
    (
        inputs_low,
        query,
        padded,
        log_totals,
        mixed_heads,
        attn_sum,
        normed_low,
        pre_gelu,
        hidden,
        ffn_sum,
    ) = saved
    head_width = attn.shape[2]
    row_count = inputs_low.shape[0]
    seg_near = lax.slice_in_dim(
        seg_pad, 2 * WIN - rim_width, 2 * WIN + row_count + rim_width, axis=0
    )
    _, pull_out = jax.vjp(normalize_layer, ffn_sum, shared[4], shared[5])
    grad_ffn_sum, grad_gain_two, grad_shift_two = pull_out(grad_out)
    grad_branch = grad_ffn_sum.astype(jnp.bfloat16)
    grad_down = dot_tn(grad_branch, hidden)
    grad_hidden = jnp.dot(grad_branch, ffn[1], preferred_element_type=jnp.float32)
    _, pull_gelu = jax.vjp(lambda value: jax.nn.gelu(value, approximate=False), pre_gelu)
    grad_pre = pull_gelu(grad_hidden)[0].astype(jnp.bfloat16)
    grad_up = dot_tn(normed_low, grad_pre)
    grad_normed = grad_ffn_sum + join_grads(
        dot_nt(grad_pre, ffn[0])
    )
    _, pull_mid = jax.vjp(normalize_layer, attn_sum, shared[1], shared[2])
    grad_attn_sum, grad_gain_one, grad_shift_one = pull_mid(grad_normed)
    grad_attn_out = grad_attn_sum.astype(jnp.bfloat16)
    grad_out_proj = dot_tn(grad_attn_out, mixed_heads)
    grad_mixed = jnp.dot(grad_attn_out, attn[3], preferred_element_type=jnp.float32).astype(
        jnp.bfloat16
    )
    grad_query, grad_pair = plain_attend_back(
        query, padded, log_totals, grad_mixed, seg_own, seg_near, dilated, rim_width
    )
    grad_proj = jnp.stack(
        [grad_query, grad_pair[:, :head_width], grad_pair[:, head_width:]], axis=1
    ).astype(jnp.bfloat16)
    grad_in_proj = jnp.einsum(
        "td,tmc->mdc", inputs_low, grad_proj, preferred_element_type=jnp.float32
    )
    grad_inputs = grad_attn_sum + join_grads(
        jnp.einsum("tmc,mdc->td", grad_proj, attn[:3], preferred_element_type=jnp.float32)
    )
    proj_sums = jnp.sum(grad_proj.astype(jnp.float32), axis=0)
    split_grad = jnp.concatenate(
        [proj_sums[0], proj_sums[2], jnp.sum(grad_pre.astype(jnp.float32), axis=0)]
    )
    shared_grad = jnp.stack(
        [
            jnp.sum(grad_attn_sum, axis=0),
            grad_gain_one,
            grad_shift_one,
            jnp.sum(grad_ffn_sum, axis=0),
            grad_gain_two,
            grad_shift_two,
        ]
    )
    attn_grad = jnp.concatenate([grad_in_proj, grad_out_proj[None]], axis=0)
    ffn_grad = jnp.stack([grad_up, grad_down])
    return (grad_inputs, attn_grad, ffn_grad, shared_grad, split_grad)


def from_slots(gathered, owners, slot_count):
    layer_count, matrix_count, row_count, col_count = gathered.shape
    blocks = gathered.reshape(
        layer_count, matrix_count, slot_count, row_count // slot_count, col_count
    )
    return jnp.take(blocks, owners, axis=2).reshape(gathered.shape)


def to_slots(grads, inverse, slot_count):
    matrix_count, row_count, col_count = grads.shape
    blocks = grads.reshape(matrix_count, slot_count, row_count // slot_count, col_count)
    return jnp.take(blocks, inverse, axis=1).reshape(grads.shape)


def rotate_update(weight, grad_now, first, second, running_average, basis, rates):
    turn = basis[:, :, 0, 0]
    turned = jnp.einsum("lmre,lmec->lmrc", grad_now, turn, precision=HIGHEST_PRECISION)
    first_new = BETA_FIRST * first + (1.0 - BETA_FIRST) * turned
    second_new = BETA_SECOND * second + (1.0 - BETA_SECOND) * turned * turned
    direction = (
        first_new
        / (1.0 - BETA_FIRST**STEP)
        / (jnp.sqrt(second_new / (1.0 - BETA_SECOND**STEP)) + ADAM_EPSILON)
    )
    back = jnp.einsum("lmrc,lmec->lmre", direction, turn, precision=HIGHEST_PRECISION)
    weight_new = weight - rates[None, :, None, None] * (back + DECAY_RATE * weight)
    average_new = AVERAGE_RATE * running_average + (1.0 - AVERAGE_RATE) * weight_new
    return (weight_new, first_new, second_new, average_new)


def vector_update(current, grad_now, first, second):
    first_new = BETA_FIRST * first + (1.0 - BETA_FIRST) * grad_now
    second_new = BETA_SECOND * second + (1.0 - BETA_SECOND) * grad_now * grad_now
    direction = (
        first_new
        / (1.0 - BETA_FIRST**STEP)
        / (jnp.sqrt(second_new / (1.0 - BETA_SECOND**STEP)) + ADAM_EPSILON)
    )
    return (current - VECTOR_RATE * direction, first_new, second_new)


def with_collectives(
    activations,
    cotangent,
    segments,
    dilated_heads,
    owners,
    attn_weights,
    attn_first,
    attn_second,
    attn_average,
    attn_basis,
    ffn_weights,
    ffn_first,
    ffn_second,
    ffn_average,
    ffn_basis,
    split_biases,
    split_first,
    split_second,
    shared_vectors,
    shared_first,
    shared_second,
):
    slot_count = lax.axis_size(SEQ)
    layer_count = attn_weights.shape[0]
    attn_full, ffn_full = (
        lax.all_gather(attn_weights.astype(jnp.bfloat16), SEQ, axis=2, tiled=True),
        lax.all_gather(ffn_weights.astype(jnp.bfloat16), SEQ, axis=2, tiled=True),
    )
    attn_full = from_slots(attn_full, owners, slot_count)
    ffn_full = from_slots(ffn_full, owners, slot_count)
    seg_pad = with_halo(segments, ((SEQ, 0),), 2 * WIN)
    head_width = attn_full.shape[3]
    head_count = head_width // DH
    heads_here = lax.axis_index(MP) * head_count + jnp.arange(head_count, dtype=jnp.int32)
    head_flags = jnp.any(heads_here[:, None] == dilated_heads[None, :], axis=1)
    current = activations.astype(jnp.float32)
    saved_list = []
    for layer_index in range(layer_count):
        dilated = jnp.logical_and(head_flags, layer_index % 2 == 1)
        rim_width = 2 * WIN if layer_index % 2 == 1 else WIN
        current, saved = layer_forward(
            current,
            attn_full[layer_index],
            ffn_full[layer_index],
            shared_vectors[layer_index],
            split_biases[layer_index],
            segments,
            seg_pad,
            dilated,
            rim_width,
        )
        saved_list.append(saved)
    slot_range = jnp.arange(slot_count, dtype=jnp.int32)
    inverse = jnp.sum(
        jnp.where(owners[None, :] == slot_range[:, None], slot_range[None, :], 0), axis=1
    )
    grad_now = cotangent.astype(jnp.float32)
    attn_list = [None] * layer_count
    ffn_list = [None] * layer_count
    shared_list = [None] * layer_count
    split_list = [None] * layer_count
    for layer_index in range(layer_count - 1, -1, -1):
        dilated = jnp.logical_and(head_flags, layer_index % 2 == 1)
        rim_width = 2 * WIN if layer_index % 2 == 1 else WIN
        grad_now, attn_grad, ffn_grad, shared_grad, split_grad = layer_backward(
            grad_now,
            saved_list[layer_index],
            attn_full[layer_index],
            ffn_full[layer_index],
            shared_vectors[layer_index],
            segments,
            seg_pad,
            dilated,
            rim_width,
        )
        attn_grad = to_slots(attn_grad, inverse, slot_count)
        ffn_grad = to_slots(ffn_grad, inverse, slot_count)
        attn_list[layer_index] = attn_grad
        ffn_list[layer_index] = ffn_grad
        shared_list[layer_index] = shared_grad
        split_list[layer_index] = split_grad[None, :]
    attn_grads = jnp.stack(attn_list)
    ffn_grads = jnp.stack(ffn_list)
    attn_grads, ffn_grads = (
        lax.psum_scatter(attn_grads, SEQ, scatter_dimension=2, tiled=True),
        lax.psum_scatter(ffn_grads, SEQ, scatter_dimension=2, tiled=True),
    )
    shared_grads, split_grads = lax.psum((jnp.stack(shared_list), jnp.stack(split_list)), SEQ)
    first_seq = lax.axis_index(SEQ) == 0
    first_both = jnp.logical_and(first_seq, lax.axis_index(MP) == 0)
    local_sum = jnp.sum(attn_grads * attn_grads) + jnp.sum(ffn_grads * ffn_grads)
    local_sum = (
        local_sum
        + jnp.where(first_seq, jnp.sum(split_grads * split_grads), 0.0)
        + jnp.where(first_both, jnp.sum(shared_grads * shared_grads), 0.0)
    )
    grad_norm = jnp.sqrt(lax.psum(local_sum, (SEQ, MP)))
    factor = CLIP_LEVEL / jnp.maximum(grad_norm, CLIP_LEVEL)
    attn_rates = jnp.array([0.5 * D ** (-0.5)] * 3 + [0.5 * (WIN / D) ** 0.5], jnp.float32)
    ffn_rates = jnp.array([0.5 * D ** (-0.5), 0.5 * FF ** (-0.5)], jnp.float32)
    attn_out = rotate_update(
        attn_weights,
        factor * attn_grads,
        attn_first,
        attn_second,
        attn_average,
        attn_basis,
        attn_rates,
    )
    ffn_out = rotate_update(
        ffn_weights, factor * ffn_grads, ffn_first, ffn_second, ffn_average, ffn_basis, ffn_rates
    )
    split_out = vector_update(split_biases, factor * split_grads, split_first, split_second)
    shared_out = vector_update(shared_vectors, factor * shared_grads, shared_first, shared_second)
    return (
        current,
        grad_now,
        attn_out[0],
        attn_out[1],
        attn_out[2][:, :3],
        attn_out[2][:, 3],
        attn_out[3],
        ffn_out[0],
        ffn_out[1],
        ffn_out[2],
        ffn_out[3],
        split_out[0],
        split_out[1],
        split_out[2],
        shared_out[0],
        shared_out[1],
        shared_out[2],
        grad_norm,
    )


def solution(mesh):
    placed = (
        P(SEQ, None),
        P(SEQ, None),
        P(SEQ),
        P(),
        P(),
        P(None, None, SEQ, MP),
        P(None, None, SEQ, MP),
        P(None, None, SEQ, MP),
        P(None, None, SEQ, MP),
        P(None, None, SEQ, MP, None, None),
        P(None, None, SEQ, MP),
        P(None, None, SEQ, MP),
        P(None, None, SEQ, MP),
        P(None, None, SEQ, MP),
        P(None, None, SEQ, MP, None, None),
        P(None, MP, None),
        P(None, MP, None),
        P(None, MP, None),
        P(),
        P(),
        P(),
    )
    count = mesh.shape[SEQ]
    fits = count % 4 == 0 and (D // count) % 16 == 0 and mesh.shape[MP] == 4
    return jax.shard_map(
        direct if fits else with_collectives,
        mesh=mesh,
        in_specs=placed,
        out_specs=(
            P(SEQ, None),
            P(SEQ, None),
            P(None, None, SEQ, MP),
            P(None, None, SEQ, MP),
            P(None, None, SEQ, MP),
            P(None, SEQ, MP),
            P(None, None, SEQ, MP),
            P(None, None, SEQ, MP),
            P(None, None, SEQ, MP),
            P(None, None, SEQ, MP),
            P(None, None, SEQ, MP),
            P(None, MP, None),
            P(None, MP, None),
            P(None, MP, None),
            P(),
            P(),
            P(),
            P(),
        ),
        check_vma=False,
    )
```

```python
from types import SimpleNamespace

import jax
import jax.numpy as jnp
from jax import lax
from jax.experimental import pallas as pl
from jax.experimental.pallas import tpu as pltpu
from jax.sharding import PartitionSpec as P

D = 768
DH = 64
FF = 3072
WIN = 256
STEP = 10

HIGHEST_PRECISION = lax.Precision.HIGHEST
NORM_EPSILON = 1e-05
MASK_FILL = -1e30
CLIP_LEVEL = 1.0
BETA_FIRST = 0.5
BETA_SECOND = 0.5
ADAM_EPSILON = 1e-08
DECAY_RATE = 0.01
AVERAGE_RATE = 0.7
VECTOR_RATE = 0.3

BF = jnp.bfloat16
SEQ, MP = "seq", "mp"
F32 = jnp.float32
MESH = pl.DeviceIdType.MESH
BLOCK = 256
CHUNK = 128
WIDE_CHUNK = 256
VMEM_LIMIT = 56 * 1024 * 1024
SCORE_SCALE = DH ** (-0.5)

GATHER_TIMES = ((2, 3, 5), (3, 5), (6, 7, 9), (7, 10, 13, 16))
PROJECT_TIMES = (8, 9, 10, 12)
BACK_TIMES = ((1, 4, 7, 10, 12), (6, 8, 10, 12), (9, 12, 14, 16))
END_TIMES = ((1, 4, 7, 10, 13), (5, 8, 10, 12), (11, 14, 15, 16))
SMALL_TIMES = (7, 12)


def dot(left, right):
    return jnp.dot(left, right, preferred_element_type=F32)


def dot_nt(left, right):
    return lax.dot_general(left, right, (((1,), (1,)), ((), ())), preferred_element_type=F32)


def dot_tn(left, right):
    return lax.dot_general(left, right, (((0,), (0,)), ((), ())), preferred_element_type=F32)


class Flush:
    def __init__(self, held, out, sems):
        self.held, self.out, self.sems = held, out, sems

    def copy(self, rows, t):
        return pltpu.make_async_copy(self.held.at[rows, :], self.out.at[rows, :], self.sems.at[t])


def run_kernel(
    body,
    name,
    inputs,
    outputs,
    scratch,
    collective=None,
    flops=0,
    grid=None,
    specs=None,
    in_smem=(),
    in_hbm=(),
    late=None,
    flushed=None,
    whole=None,
    pieces=0,
):
    specs, late, flushed, whole = specs or {}, late or {}, flushed or {}, whole or {}

    def kernel(*refs):
        refs = list(refs)

        def take(keys):
            got = refs[: len(keys)]
            del refs[: len(keys)]
            return dict(zip(keys, got))

        given, distant, made, written, far, held = (
            take(keys) for keys in (inputs, late, outputs, flushed, whole, scratch)
        )
        fetched, fetched_sems, filled, filled_sems = (take(keys) for keys in (late, late, flushed, flushed))
        kept, kept_sems = take(whole), take(whole)
        r = SimpleNamespace(**given, **made, **held, **fetched, **filled, **kept)
        if whole:
            *first, last = whole
            r.flush_whole = SimpleNamespace(
                **{key: pltpu.make_async_copy(kept[key], far[key], kept_sems[key].at[0]) for key in first}
            )
            r.soft_hbm, r.soft_sem = far[last], kept_sems[last]
        r.late = SimpleNamespace(
            **{key: pltpu.make_async_copy(distant[key], fetched[key], fetched_sems[key]) for key in late}
        )
        r.flush = SimpleNamespace(**{key: Flush(filled[key], written[key], filled_sems[key]) for key in flushed})
        for copy in vars(r.late).values():
            copy.start()
        body(r)

    def spec_of(key):
        if key in specs:
            return specs[key]
        if key in in_hbm or key in late or key in flushed or key in whole:
            return pl.BlockSpec(memory_space=pl.ANY)
        return pl.BlockSpec(memory_space=pltpu.SMEM if key in in_smem else pltpu.VMEM)

    arguments = {**inputs, **late}
    gives = {**outputs, **flushed, **whole}
    shapes = [jax.ShapeDtypeStruct(shape, dtype) for shape, dtype in gives.values()]
    moved = sum(v.size * v.dtype.itemsize for v in arguments.values())
    moved += sum(v.size * v.dtype.itemsize for v in shapes)
    extra = {} if grid is None else dict(grid=grid)
    params = dict(vmem_limit_bytes=VMEM_LIMIT)
    if collective is not None:
        params.update(collective_id=collective, has_side_effects=True)
    results = pl.pallas_call(
        kernel,
        out_shape=shapes,
        in_specs=[spec_of(key) for key in arguments],
        out_specs=[spec_of(key) for key in gives],
        scratch_shapes=list(scratch.values())
        + [pltpu.VMEM(v.shape, v.dtype) for v in late.values()]
        + [pltpu.SemaphoreType.DMA for _ in late]
        + [pltpu.VMEM(shape, dtype) for shape, dtype in flushed.values()]
        + [pltpu.SemaphoreType.DMA((pieces,)) for _ in flushed]
        + [pltpu.VMEM(shape, dtype) for shape, dtype in whole.values()]
        + [pltpu.SemaphoreType.DMA((pieces,)) for _ in whole],
        compiler_params=pltpu.CompilerParams(**params),
        cost_estimate=pl.CostEstimate(flops=int(flops), bytes_accessed=int(moved), transcendentals=0),
        name=name,
        **extra,
    )(*arguments.values())
    return SimpleNamespace(**dict(zip(gives, results)))


def parity_matrix():
    row = lax.broadcasted_iota(jnp.int32, (2 * BLOCK, 2 * BLOCK), 0)
    col = lax.broadcasted_iota(jnp.int32, (2 * BLOCK, 2 * BLOCK), 1)
    source = 2 * (row % BLOCK) + row // BLOCK
    return jnp.where(col == source, 1.0, 0.0).astype(BF)


def head_lanes(count):
    lane = lax.broadcasted_iota(jnp.int32, (1, count * DH), 1)
    return [lane // DH == head for head in range(count)]


def head_flags(dilated, count):
    first = lax.axis_index(MP) * count
    return [jnp.logical_or(dilated[0] == first + head, dilated[1] == first + head) for head in range(count)]


def marked_lanes(dilated, count):
    marked = jnp.zeros((1, count * DH), jnp.int32)
    for flag, lanes in zip(head_flags(dilated, count), head_lanes(count)):
        marked = jnp.where(lanes, flag.astype(jnp.int32), marked)
    return marked > 0


def sorted_groups(natural, sort):
    groups = natural.shape[0] // (2 * BLOCK)
    return [dot(sort, natural[g * 2 * BLOCK : (g + 1) * 2 * BLOCK]).astype(BF) for g in range(groups)]


def arrange_rows(natural, sort):
    return jnp.concatenate(sorted_groups(natural, sort), axis=0)


def split_rows(natural, sort):
    parts = sorted_groups(natural, sort)
    return jnp.concatenate([p[:BLOCK] for p in parts] + [p[BLOCK:] for p in parts], axis=0)


def soft_weights(query_block, key_block, lanes, allowed):
    raw = dot_nt(jnp.where(lanes, query_block, 0.0).astype(BF), key_block)
    scores = jnp.where(allowed, raw, MASK_FILL)
    top = jnp.max(scores, axis=1, keepdims=True)
    exponent = jnp.exp(scores - top)
    total = jnp.sum(exponent, axis=1, keepdims=True)
    return (exponent * (1.0 / total)).astype(BF)


def window_mask():
    row = lax.broadcasted_iota(jnp.int32, (BLOCK, 3 * BLOCK), 0)
    col = lax.broadcasted_iota(jnp.int32, (BLOCK, 3 * BLOCK), 1)
    return jnp.abs(row - col + BLOCK) <= WIN


class OutShare:
    def __init__(self, who, refs):
        self.who, self.r, self.here = who, refs, lax.axis_index(MP)

    def copy(self, kind, slot):
        r = self.r
        device = self.who.across if kind == 1 else self.who.sibling
        return copy_to(r.full.at[slot], r.full.at[slot], r.sent.at[kind], r.came.at[kind], device)

    def begin(self, own):
        self.r.full[self.here] = own.astype(F32).T.astype(BF)
        self.copy(0, self.here).start()
        self.copy(1, self.here).start()

    def hand_on(self):
        self.copy(1, self.who.across[1]).wait_recv()
        self.copy(2, self.who.across[1]).start()

    def finish(self):
        self.copy(0, self.who.sibling[1]).wait_recv()
        self.copy(2, self.who.diagonal[1]).wait_recv()
        for kind, slot in enumerate((self.here, self.here, self.who.across[1])):
            self.copy(kind, slot).wait_send()


def share_scratch():
    return dict(share_sent=pltpu.SemaphoreType.DMA((3,)), share_came=pltpu.SemaphoreType.DMA((3,)))


def key_starts(step, mixed):
    natural = pl.ds(pl.multiple_of(step * BLOCK, BLOCK), 3 * BLOCK)
    if not mixed:
        return natural, natural
    first = (step % 2) * 4 + step // 2
    return natural, pl.ds(pl.multiple_of(first * BLOCK, BLOCK), 3 * BLOCK)


class HeadExchange:
    def __init__(self, who, source, gathered, sent, came):
        self.who, self.source, self.gathered, self.sent, self.came = who, source, gathered, sent, came
        here = lax.axis_index(MP)
        self.here = here
        self.devices = who.sibling, who.across, who.diagonal

    def copy(self, kind, t, slot):
        who = self.who
        rows = who.own(t) if kind == 1 else who.other(t)
        return copy_to(
            self.source.at[rows, :],
            self.gathered.at[slot, who.half(t), :],
            self.sent.at[kind, t],
            self.came.at[kind, t],
            self.devices[kind],
        )

    def give(self, t):
        self.gathered[self.here, self.who.half(t), :] = self.source[self.who.own(t), :]
        for kind in range(3):
            self.copy(kind, t, self.here).start()

    def take(self, t):
        for kind in range(3):
            self.copy(kind, t, self.devices[kind][1]).wait_recv()

    def finish(self, t):
        for kind in range(3):
            self.copy(kind, t, self.here).wait_send()


def attend(query, pair, left, right, seg_query, seg_keys, dilated):
    rows, width = query.shape
    heads = width // DH
    blocks = rows // BLOCK
    keys = 3 * BLOCK
    slots = 2 * blocks
    chunks = rows // WIDE_CHUNK

    def body(r):
        step = pl.program_id(0)
        who = Partners(size=WIDE_CHUNK)
        exchange = HeadExchange(who, r.out, r.landed, r.sent, r.came)

        @pl.when(step == 0)
        def _():
            who.call()
            marked = marked_lanes(r.dilated, heads)
            sort = parity_matrix()
            for which, held in ((0, r.keys), (1, r.values)):
                lanes = slice(which * width, (which + 1) * width)
                padded = jnp.concatenate([r.left[:, lanes], r.pair[:, lanes], r.right[:, lanes]], axis=0)
                natural = jnp.concatenate([padded[BLOCK : (blocks + 3) * BLOCK], padded[: 2 * BLOCK]], axis=0)
                held[...] = jnp.where(marked, split_rows(padded, sort), natural)
            scaled = (r.asked[...].astype(F32) * SCORE_SCALE).astype(BF)
            r.query[...] = jnp.where(marked, arrange_rows(scaled, sort), scaled)

        window = window_mask()
        natural, dilated_near = key_starts(step, True)
        own = pl.ds(pl.multiple_of(step * BLOCK, BLOCK), BLOCK)
        marked = marked_lanes(r.dilated, heads)
        key_block = jnp.where(marked, r.keys[dilated_near, :], r.keys[natural, :])
        value_block = jnp.where(marked, r.values[dilated_near, :], r.values[natural, :])
        query_block = r.query[own, :]
        gathered = jnp.zeros((BLOCK, width), F32)
        flags = head_flags(r.dilated, heads)
        for head, lanes in enumerate(head_lanes(heads)):
            mine = jnp.where(flags[head], r.seg_query[own, 1:2], r.seg_query[own, 0:1])
            theirs = jnp.where(flags[head], r.seg_keys[1:2, dilated_near], r.seg_keys[0:1, natural])
            soft = soft_weights(query_block, key_block, lanes, jnp.logical_and(window, mine == theirs))
            r.soft[head] = soft
            gathered = jnp.where(lanes, dot(soft, value_block), gathered)
        r.arranged[own, :] = gathered.astype(BF)

        for group in range(blocks // 2):

            @pl.when(step == 2 * group + 1)
            def _(group=group):
                part = slice(group * 2 * BLOCK, (group + 1) * 2 * BLOCK)
                arranged = r.arranged[part, :]
                restored = dot_tn(parity_matrix(), arranged).astype(BF)
                r.out[part, :] = jnp.where(marked, restored, arranged)
                if group == 0:
                    who.gather()
                    for t in range(chunks // 2):
                        exchange.give(t)

        @pl.when(step == blocks - 1)
        def _():
            for t in range(chunks // 2):
                exchange.take(t)
                exchange.finish(t)
            r.first[...] = r.landed[...]

    return run_kernel(
        body,
        "attend",
        dict(
            asked=query,
            pair=pair,
            left=left,
            right=right,
            seg_query=seg_query,
            seg_keys=seg_keys,
            dilated=dilated,
        ),
        dict(
            out=((rows, width), BF),
            first=((4, rows // 4, width), BF),
            arranged=((rows, width), BF),
            query=((rows, width), BF),
            keys=((slots * BLOCK, width), BF),
            values=((slots * BLOCK, width), BF),
            soft=((heads, rows, keys), BF),
        ),
        dict(
            landed=pltpu.VMEM((4, rows // 4, width), BF),
            sent=pltpu.SemaphoreType.DMA((3, chunks // 2)),
            came=pltpu.SemaphoreType.DMA((3, chunks // 2)),
        ),
        collective=8,
        flops=4 * rows * keys * 256 * heads,
        grid=(blocks,),
        specs=dict(soft=pl.BlockSpec((heads, BLOCK, keys), lambda i: (0, i, 0))),
        in_smem=("dilated",),
    )


def attend_back(saved, grad_out, dilated, rim, mixed, count, collective):
    rows, width = grad_out.shape
    heads = width // DH
    blocks = rows // BLOCK
    keys = 3 * BLOCK
    slots = 2 * blocks if mixed else blocks + 2

    def body(r):
        step = pl.program_id(0)
        column = Column(count)
        first, last = column.index == 0, column.index == count - 1
        before = (lax.rem(column.index + count - 1, count), column.here)
        after = (lax.rem(column.index + 1, count), column.here)
        copy = copy_to(r.ready_left, r.from_right, r.sent.at[0], r.came.at[0], before)

        @pl.when(step == 0)
        def _():
            barrier = pltpu.get_barrier_semaphore()

            @pl.when(jnp.logical_not(last))
            def _():
                pl.semaphore_signal(barrier, inc=1, device_id=after, device_id_type=MESH)

            grad = r.grad_out[...]
            if mixed:
                grad = jnp.where(marked_lanes(r.dilated, heads), arrange_rows(grad, parity_matrix()), grad)
            r.grad[...] = grad
            r.grad_keys[...] = jnp.zeros_like(r.grad_keys)
            r.grad_values[...] = jnp.zeros_like(r.grad_values)

        natural, dilated_near = key_starts(step, mixed)
        own = pl.ds(pl.multiple_of(step * BLOCK, BLOCK), BLOCK)
        marked = marked_lanes(r.dilated, heads)
        key_block, value_block = r.keys[natural, :], r.values[natural, :]
        if mixed:
            key_block = jnp.where(marked, r.keys[dilated_near, :], key_block)
            value_block = jnp.where(marked, r.values[dilated_near, :], value_block)
        query_block = r.query[own, :]
        grad_block = r.grad[own, :]
        product = grad_block.astype(F32) * r.arranged[own, :].astype(F32)
        grad_query = jnp.zeros((BLOCK, width), F32)
        grad_key = jnp.zeros((keys, width), F32)
        grad_value = jnp.zeros((keys, width), F32)
        for head, lanes in enumerate(head_lanes(heads)):
            soft = r.soft[head]
            grad_head = jnp.where(lanes, grad_block, 0.0).astype(BF)
            row_dot = jnp.sum(jnp.where(lanes, product, 0.0), axis=1, keepdims=True)
            grad_soft = dot_nt(grad_head, value_block)
            grad_scores = (soft.astype(F32) * (grad_soft - row_dot)).astype(BF)
            grad_value += dot_tn(soft, grad_head)
            grad_key += dot_tn(grad_scores, jnp.where(lanes, query_block, 0.0).astype(BF))
            grad_query = jnp.where(lanes, dot(grad_scores, key_block), grad_query)
        r.grad_query[own, :] = (grad_query * SCORE_SCALE).astype(BF)
        if mixed:
            for held, grad in ((r.grad_keys, grad_key), (r.grad_values, grad_value)):
                held[dilated_near, :] += jnp.where(marked, grad, 0.0)
                held[natural, :] += jnp.where(marked, 0.0, grad)
        else:
            r.grad_keys[natural, :] += grad_key
            r.grad_values[natural, :] += grad_value

        def natural_group(g, middle):
            both = []
            for held in (r.grad_keys, r.grad_values):
                plain = middle(held)
                pair = jnp.concatenate(
                    [
                        held[g * BLOCK : (g + 1) * BLOCK, :],
                        held[(blocks + g) * BLOCK : (blocks + g + 1) * BLOCK, :],
                    ],
                    axis=0,
                ).astype(BF)
                both.append(jnp.where(marked, dot_tn(parity_matrix(), pair), plain).astype(BF))
            return jnp.concatenate(both, axis=1)

        edge = jnp.zeros((BLOCK, width), F32)

        @pl.when(step == (1 if mixed else 0))
        def _():
            if mixed:
                r.ready_left[...] = natural_group(0, lambda held: jnp.concatenate([edge, held[:BLOCK, :]], axis=0))
            else:
                r.ready_left[...] = jnp.concatenate(
                    [r.grad_keys[:rim, :], r.grad_values[:rim, :]], axis=1
                ).astype(BF)

            @pl.when(jnp.logical_not(first))
            def _():
                pl.semaphore_wait(pltpu.get_barrier_semaphore(), 1)
                copy.start()

        @pl.when(step == blocks - 1)
        def _():
            if mixed:
                for g in range(blocks // 2):
                    part = slice(g * 2 * BLOCK, (g + 1) * 2 * BLOCK)
                    arranged = r.grad_query[part, :]
                    restored = dot_tn(parity_matrix(), arranged).astype(BF)
                    r.out_query[part, :] = jnp.where(marked, restored, arranged)
                lap = 2 * BLOCK
                r.out_own[:lap, :] = natural_group(1, lambda held: held[BLOCK : 3 * BLOCK, :])
                r.out_own[lap:, :] = natural_group(2, lambda held: held[3 * BLOCK : 5 * BLOCK, :])
                r.out_right[...] = natural_group(
                    3, lambda held: jnp.concatenate([held[5 * BLOCK : 6 * BLOCK, :], edge], axis=0)
                )
            else:
                r.out_query[...] = r.grad_query[...]
                both = jnp.concatenate([r.grad_keys[rim:, :], r.grad_values[rim:, :]], axis=1).astype(BF)
                r.out_own[...] = both[:rows]
                r.out_right[...] = both[rows:]

            @pl.when(jnp.logical_not(last))
            def _():
                copy.wait_recv()
                tail = pl.ds(rows - rim, rim)
                r.out_own[tail, :] = (r.out_own[tail, :].astype(F32) + r.from_right[...].astype(F32)).astype(BF)

            @pl.when(jnp.logical_not(first))
            def _():
                copy.wait_send()

    return run_kernel(
        body,
        "attend_back",
        dict(
            grad_out=grad_out,
            arranged=saved.arranged,
            query=saved.query,
            keys=saved.keys,
            values=saved.values,
            soft=saved.soft,
            dilated=dilated,
        ),
        dict(
            out_query=((rows, width), BF),
            out_own=((rows, 2 * width), BF),
            out_right=((rim, 2 * width), BF),
        ),
        dict(
            grad=pltpu.VMEM((rows, width), BF),
            grad_query=pltpu.VMEM((rows, width), BF),
            grad_keys=pltpu.VMEM((slots * BLOCK, width), F32),
            grad_values=pltpu.VMEM((slots * BLOCK, width), F32),
            ready_left=pltpu.VMEM((rim, 2 * width), BF),
            from_right=pltpu.VMEM((rim, 2 * width), BF),
            sent=pltpu.SemaphoreType.DMA((1,)),
            came=pltpu.SemaphoreType.DMA((1,)),
        ),
        collective=collective,
        flops=8 * rows * keys * 256 * heads,
        grid=(blocks,),
        specs=dict(soft=pl.BlockSpec((heads, BLOCK, keys), lambda i: (0, i, 0))),
        in_smem=("dilated",),
    )


class Partners:
    def __init__(self, count=0, shift=0, size=CHUNK):
        seq = lax.axis_index(SEQ)
        here = lax.axis_index(MP)
        self.core = lax.rem(here, 2)
        self.sibling = (seq, here + 1 - 2 * self.core)
        self.across = (seq, lax.rem(here + 2, 4))
        self.diagonal = (seq, lax.rem(here + 3 - 2 * self.core, 4))
        self.count, self.shift, self.size = count, shift, size

    def others(self, column):
        found = [self.sibling, self.across, self.diagonal]
        if column is not None:
            found += [column.peer(k) for k in range(1, column.count)]
        return found

    def call(self, column=None):
        barrier = pltpu.get_barrier_semaphore()
        for other in self.others(column):
            pl.semaphore_signal(barrier, inc=1, device_id=other, device_id_type=MESH)

    def gather(self, column=None):
        pl.semaphore_wait(pltpu.get_barrier_semaphore(), len(self.others(column)))

    def meet(self, column=None):
        self.call(column)
        self.gather(column)

    def place(self, t):
        return lax.rem(t + self.shift, self.count) if self.shift else t

    def chunk(self, t):
        return pl.ds(pl.multiple_of(self.place(t) * self.size, self.size), self.size)

    def two_chunks(self, t):
        return pl.ds(pl.multiple_of(self.place(t - 1) * self.size, 2 * self.size), 2 * self.size)

    def part(self, t, core):
        half = self.size // 2
        return pl.ds(pl.multiple_of(self.place(t) * self.size + core * half, half), half)

    def own(self, t):
        return self.part(t, self.core)

    def other(self, t):
        return self.part(t, 1 - self.core)

    def half(self, t):
        half = self.size // 2
        return pl.ds(pl.multiple_of(self.place(t) * half, half), half)


def copy_to(source, target, sent, arrived, device):
    return pltpu.make_async_remote_copy(
        src_ref=source, dst_ref=target, send_sem=sent, recv_sem=arrived, device_id=device, device_id_type=MESH
    )


def exchange_scratch(rows):
    count = rows // CHUNK
    return dict(
        part=pltpu.VMEM((rows, D), BF),
        near=pltpu.VMEM((rows // 2, D), BF),
        far=pltpu.VMEM((rows // 2, D), BF),
        core_sent=pltpu.SemaphoreType.DMA((count,)),
        core_came=pltpu.SemaphoreType.DMA((count,)),
        far_sent=pltpu.SemaphoreType.DMA((count,)),
        far_came=pltpu.SemaphoreType.DMA((count,)),
    )


def gather_scratch(rows, width=D, dtype=BF):
    count = rows // CHUNK
    return dict(
        full=pltpu.VMEM((rows, width), dtype),
        sent=pltpu.SemaphoreType.DMA((count,)),
        came=pltpu.SemaphoreType.DMA((count,)),
    )


class Exchange:
    def __init__(self, who, refs):
        self.who, self.r = who, refs

    def core_copy(self, t):
        who, r = self.who, self.r
        return copy_to(
            r.part.at[who.other(t), :], r.near.at[who.half(t), :], r.core_sent.at[t], r.core_came.at[t], who.sibling
        )

    def far_copy(self, t):
        who, r = self.who, self.r
        rows = who.half(t)
        return copy_to(r.near.at[rows, :], r.far.at[rows, :], r.far_sent.at[t], r.far_came.at[t], who.across)

    def give(self, t, part):
        self.r.part[self.who.chunk(t), :] = part.astype(BF)
        self.core_copy(t).start()

    def add(self, t):
        who, r = self.who, self.r
        self.core_copy(t).wait_recv()
        pair = r.part[who.own(t), :].astype(F32) + r.near[who.half(t), :].astype(F32)
        r.near[who.half(t), :] = pair.astype(BF)
        self.far_copy(t).start()

    def take(self, t):
        who, r = self.who, self.r
        self.far_copy(t).wait_recv()
        return r.near[who.half(t), :].astype(F32) + r.far[who.half(t), :].astype(F32)

    def finish(self, t):
        self.core_copy(t).wait_send()
        self.far_copy(t).wait_send()


class Gather:
    def __init__(self, who, refs):
        self.who, self.r = who, refs

    def copy(self, rows, t):
        r = self.r
        return copy_to(r.full.at[rows, :], r.full.at[rows, :], r.sent.at[t], r.came.at[t], self.who.sibling)

    def give(self, t, value):
        rows = self.who.own(t)
        self.r.full[rows, :] = value.astype(self.r.full.dtype)
        self.copy(rows, t).start()

    def take(self, t):
        self.wait(t)
        return self.r.full[self.who.chunk(t), :]

    def wait(self, t):
        self.copy(self.who.other(t), t).wait_recv()

    def finish(self, t):
        self.copy(self.who.own(t), t).wait_send()


class Column:
    def __init__(self, count):
        self.count = count
        self.lines = count // 2
        self.here = lax.axis_index(MP)
        self.index = lax.axis_index(SEQ)
        self.inner = lax.rem(self.index, 2)
        self.outer = lax.div(self.index, 2)

    def peer(self, k):
        return (lax.rem(self.index + k, self.count), self.here)

    def at(self, outer, inner):
        return (2 * outer + inner, self.here)

    def turn(self, k):
        return lax.rem(self.outer + k, self.lines)


def gather_sems(lines):
    return {
        key: pltpu.SemaphoreType.DMA((lines,)) for key in ("pair_sent", "pair_came", "up_sent", "down_sent", "line_came")
    }


class GatherBlocks:
    def __init__(self, column, refs):
        self.c, self.r = column, refs
        self.above = column.outer < column.lines - 1
        self.below = column.outer > 0

    def line_copy(self, source, step):
        c, r = self.c, self.r
        block = 2 * source + c.inner
        sent = r.up_sent if step > 0 else r.down_sent
        return copy_to(
            r.full.at[block], r.full.at[block], sent.at[source], r.line_came.at[source], c.at(c.outer + step, c.inner)
        )

    def pair_copy(self, source, inner):
        c, r = self.c, self.r
        block = 2 * source + inner
        return copy_to(
            r.full.at[block],
            r.full.at[block],
            r.pair_sent.at[source],
            r.pair_came.at[source],
            c.at(c.outer, 1 - c.inner),
        )

    def put(self, value):
        self.r.full[self.c.index] = value

    def start_line(self):
        c = self.c

        @pl.when(self.above)
        def _():
            self.line_copy(c.outer, 1).start()

        @pl.when(self.below)
        def _():
            self.line_copy(c.outer, -1).start()

    def start_pair(self):
        self.pair_copy(self.c.outer, self.c.inner).start()

    def relay(self, k):
        c = self.c

        @pl.when(c.outer >= k)
        def _():
            source = c.outer - k
            self.line_copy(source, 1).wait_recv()

            @pl.when(self.above)
            def _():
                self.line_copy(source, 1).start()

            self.hand_on(source)

        @pl.when(c.outer + k < c.lines)
        def _():
            source = c.outer + k
            self.line_copy(source, -1).wait_recv()

            @pl.when(self.below)
            def _():
                self.line_copy(source, -1).start()

            self.hand_on(source)

    def hand_on(self, source):
        self.pair_copy(source, self.c.inner).start()

    def arrive(self):
        for k in range(self.c.lines):
            self.pair_copy(k, 1 - self.c.inner).wait_recv()

    def finish(self):
        for k in range(self.c.lines):
            self.pair_copy(k, self.c.inner).wait_send()
        self.finish_line()

    def finish_line(self):
        c = self.c
        for k in range(c.lines):

            @pl.when(jnp.logical_and(self.above, c.outer >= k))
            def _(k=k):
                self.line_copy(k, 1).wait_send()

            @pl.when(jnp.logical_and(self.below, c.outer <= k))
            def _(k=k):
                self.line_copy(k, -1).wait_send()


class GatherPairs(GatherBlocks):
    def line_copy(self, source, step):
        c, r = self.c, self.r
        blocks = pl.ds(2 * source, 2)
        sent = r.up_sent if step > 0 else r.down_sent
        return copy_to(
            r.full.at[blocks], r.full.at[blocks], sent.at[source], r.line_came.at[source], c.at(c.outer + step, c.inner)
        )

    def begin(self):
        self.pair_copy(self.c.outer, 1 - self.c.inner).wait_recv()
        self.start_line()

    def hand_on(self, source):
        pass

    def finish(self):
        self.pair_copy(self.c.outer, self.c.inner).wait_send()
        self.finish_line()


def scatter_scratch(lines, block, size, held=True):
    scratch = {
        key: pltpu.SemaphoreType.DMA((lines + 1,))
        for key in ("pair_sent", "pair_came", "line_sent", "line_came", "own_came")
    }
    scratch.update(near=pltpu.VMEM((lines, block, size), BF), far=pltpu.VMEM((lines + 1, block, size), BF))
    if held:
        scratch["own"] = pltpu.VMEM((lines, block, size), BF)
    return scratch


class ScatterBlocks:
    def __init__(self, column, refs, total):
        self.c, self.r, self.total = column, refs, total
        self.above = column.outer < column.lines - 1
        self.below = column.outer > 0
        self.fetched = hasattr(refs, "own")
        order = []
        for k in range(column.lines // 2):
            order += [column.lines - 1 - k, k]
        self.order = order

    def pair_copy(self, outer):
        c, r = self.c, self.r
        return copy_to(
            r.grads.at[2 * outer + 1 - c.inner],
            r.near.at[outer],
            r.pair_sent.at[outer],
            r.pair_came.at[outer],
            c.at(c.outer, 1 - c.inner),
        )

    def own_copy(self, outer):
        c, r = self.c, self.r
        return pltpu.make_async_copy(r.grads.at[2 * outer + c.inner], r.own.at[outer], r.own_came.at[outer])

    def line_copy(self, target, step):
        c, r = self.c, self.r
        slot = target if step > 0 else jnp.where(c.outer - 1 == target, c.lines, target)
        return copy_to(
            r.near.at[target],
            r.far.at[slot],
            r.line_sent.at[target],
            r.line_came.at[slot],
            c.at(c.outer + step, c.inner),
        )

    def landing(self, slot, step):
        c, r = self.c, self.r
        return copy_to(
            r.near.at[c.outer], r.far.at[slot], r.line_sent.at[c.outer], r.line_came.at[slot], c.at(c.outer + step, c.inner)
        )

    def start(self):
        for outer in self.order:
            self.pair_copy(outer).start()
            if self.fetched:
                self.own_copy(outer).start()

    def pair_step(self, k):
        c, r = self.c, self.r
        for outer in self.order[2 * k : 2 * k + 2]:
            self.pair_copy(outer).wait_recv()
            if self.fetched:
                self.own_copy(outer).wait()
                own = r.own[outer]
            else:
                own = r.grads[2 * outer + c.inner]
            r.near[outer] = (own.astype(F32) + r.near[outer].astype(F32)).astype(BF)

    def line_step(self, wave):
        c, r = self.c, self.r
        from_top = c.lines - 1 - c.outer

        def pass_on(target, step, behind):
            @pl.when(behind)
            def _():
                self.landing(target, step).wait_recv()
                r.near[target] = (r.near[target].astype(F32) + r.far[target].astype(F32)).astype(BF)

            self.line_copy(target, step).start()

        @pl.when(c.outer <= wave)
        def _():
            pass_on(from_top + c.outer - wave + c.outer, 1, self.below)

        @pl.when(from_top <= wave)
        def _():
            pass_on(wave - from_top, -1, self.above)

    def close(self):
        c, r = self.c, self.r
        self.total[...] = r.near[c.outer].astype(F32)

        @pl.when(self.below)
        def _():
            self.landing(c.outer, 1).wait_recv()
            self.total[...] += r.far[c.outer].astype(F32)

        @pl.when(self.above)
        def _():
            self.landing(c.lines, -1).wait_recv()
            self.total[...] += r.far[c.lines].astype(F32)

    def finish(self):
        c = self.c
        for outer in self.order:
            self.pair_copy(outer).wait_send()
        for target in range(c.lines):

            @pl.when(c.outer < target)
            def _(target=target):
                self.line_copy(target, 1).wait_send()

            @pl.when(c.outer > target)
            def _(target=target):
                self.line_copy(target, -1).wait_send()

    def ticks(self, times):
        steps = [(times[0], lambda: self.pair_step(0)), (times[0], lambda: self.line_step(0))]
        steps += [(times[1], lambda: self.pair_step(1))]
        steps += [(times[k], lambda k=k: self.line_step(k)) for k in range(1, self.c.lines - 1)]
        steps += [(times[self.c.lines - 1], self.close)]
        return steps


def scatter_pairs_scratch(lines, block, size):
    scratch = {key: pltpu.SemaphoreType.DMA((lines + 1,)) for key in ("pair_sent", "pair_came", "line_sent", "line_came")}
    scratch.update(
        sums=pltpu.VMEM((2 * lines, block, size), BF),
        far=pltpu.VMEM((2 * lines + 2, block, size), BF),
        give=pltpu.VMEM((block, size), BF),
        get=pltpu.VMEM((block, size), BF),
        held=pltpu.SemaphoreType.DMA,
    )
    return scratch


class ScatterPairs:
    def __init__(self, column, refs, total):
        self.c, self.r, self.total = column, refs, total
        self.above = column.outer < column.lines - 1
        self.below = column.outer > 0
        self.fetch = pltpu.make_async_copy(refs.grads, refs.sums, refs.held)

    def line_copy(self, target, step):
        c, r = self.c, self.r
        slot = target if step > 0 else jnp.where(c.outer - 1 == target, c.lines, target)
        return copy_to(
            r.sums.at[pl.ds(2 * target, 2)],
            r.far.at[pl.ds(2 * slot, 2)],
            r.line_sent.at[target],
            r.line_came.at[slot],
            c.at(c.outer + step, c.inner),
        )

    def landing(self, slot, step):
        c, r = self.c, self.r
        return copy_to(
            r.sums.at[pl.ds(2 * c.outer, 2)],
            r.far.at[pl.ds(2 * slot, 2)],
            r.line_sent.at[c.outer],
            r.line_came.at[slot],
            c.at(c.outer + step, c.inner),
        )

    def pair_copy(self):
        c, r = self.c, self.r
        return copy_to(r.give, r.get, r.pair_sent.at[0], r.pair_came.at[0], c.at(c.outer, 1 - c.inner))

    def start(self):
        self.fetch.start()

    def line_step(self, wave):
        c, r = self.c, self.r
        from_top = c.lines - 1 - c.outer
        if wave == 0:
            self.fetch.wait()

        def pass_on(target, step, behind):
            @pl.when(behind)
            def _():
                self.landing(target, step).wait_recv()
                for k in range(2):
                    block = 2 * target + k
                    r.sums[block] = (r.sums[block].astype(F32) + r.far[block].astype(F32)).astype(BF)

            self.line_copy(target, step).start()

        @pl.when(c.outer <= wave)
        def _():
            pass_on(from_top + c.outer - wave + c.outer, 1, self.below)

        @pl.when(from_top <= wave)
        def _():
            pass_on(wave - from_top, -1, self.above)

    def close_line(self):
        c, r = self.c, self.r
        mine, other = 2 * c.outer + c.inner, 2 * c.outer + 1 - c.inner
        self.total[...] = r.sums[mine].astype(F32)

        @pl.when(self.below)
        def _():
            self.landing(c.outer, 1).wait_recv()
            self.total[...] += r.far[mine].astype(F32)
            r.sums[other] = (r.sums[other].astype(F32) + r.far[other].astype(F32)).astype(BF)

        @pl.when(self.above)
        def _():
            self.landing(c.lines, -1).wait_recv()
            self.total[...] += r.far[2 * c.lines + c.inner].astype(F32)
            r.sums[other] = (r.sums[other].astype(F32) + r.far[2 * c.lines + 1 - c.inner].astype(F32)).astype(BF)

        r.give[...] = r.sums[other]
        self.pair_copy().start()

    def close(self):
        self.pair_copy().wait_recv()
        self.total[...] += self.r.get[...].astype(F32)

    def finish(self):
        c = self.c
        self.pair_copy().wait_send()
        for target in range(c.lines):

            @pl.when(c.outer < target)
            def _(target=target):
                self.line_copy(target, 1).wait_send()

            @pl.when(c.outer > target)
            def _(target=target):
                self.line_copy(target, -1).wait_send()

    def ticks(self, times):
        steps = [(times[k], lambda k=k: self.line_step(k)) for k in range(self.c.lines - 1)]
        return steps + [(times[self.c.lines - 1], self.close_line), (times[self.c.lines], self.close)]


class Halo:
    def __init__(self, column, refs, source, rim, size):
        self.c, self.r, self.source, self.rim, self.size = column, refs, source, rim, size
        self.rows = source.shape[0]
        self.before = lax.rem(column.index + column.count - 1, column.count), column.here
        self.after = lax.rem(column.index + 1, column.count), column.here
        self.first, self.last = column.index == 0, column.index == column.count - 1

    def clear(self):
        @pl.when(self.first)
        def _():
            self.r.left[...] = jnp.zeros_like(self.r.left)

        @pl.when(self.last)
        def _():
            self.r.right[...] = jnp.zeros_like(self.r.right)

    def back_copy(self, t):
        rows = pl.ds(pl.multiple_of(t * self.size, self.size), self.size)
        return copy_to(
            self.source.at[rows, :], self.r.right.at[rows, :], self.r.back_sent.at[t], self.r.back_came.at[t], self.before
        )

    def ahead_copy(self, t):
        from_rows = pl.ds(pl.multiple_of(self.rows - self.rim + t * self.size, self.size), self.size)
        rows = pl.ds(pl.multiple_of(t * self.size, self.size), self.size)
        return copy_to(
            self.source.at[from_rows, :],
            self.r.left.at[rows, :],
            self.r.ahead_sent.at[t],
            self.r.ahead_came.at[t],
            self.after,
        )

    def send(self, t):
        count = self.rim // self.size
        offset = (self.rows - self.rim) // self.size

        @pl.when(jnp.logical_and(t < count, jnp.logical_not(self.first)))
        def _():
            self.back_copy(t).start()

        @pl.when(jnp.logical_and(t >= offset, jnp.logical_not(self.last)))
        def _():
            self.ahead_copy(t - offset).start()

    def arrive(self):
        for t in range(self.rim // self.size):

            @pl.when(jnp.logical_not(self.last))
            def _():
                self.back_copy(t).wait_recv()

            @pl.when(jnp.logical_not(self.first))
            def _():
                self.ahead_copy(t).wait_recv()

    def finish(self):
        for t in range(self.rim // self.size):

            @pl.when(jnp.logical_not(self.first))
            def _():
                self.back_copy(t).wait_send()

            @pl.when(jnp.logical_not(self.last))
            def _():
                self.ahead_copy(t).wait_send()


def halo_scratch(count):
    return {
        key: pltpu.SemaphoreType.DMA((count,)) for key in ("back_sent", "back_came", "ahead_sent", "ahead_came")
    }


def pick(r, prefix):
    start = prefix + "_"
    return SimpleNamespace(
        **{key[len(start) :]: value for key, value in vars(r).items() if key.startswith(start)}
    )


def prefixed(prefix, entries):
    return {prefix + "_" + key: value for key, value in entries.items()}


def run_stages(count, stages, ticks=()):
    last = max(delay for delay, _ in stages)

    def step(i, carry):
        for when in sorted({when for when, _ in ticks if when < count + last}):

            @pl.when(i == when)
            def _(when=when):
                for other, tick in ticks:
                    if other == when:
                        tick()

        for delay, stage in stages:

            @pl.when(jnp.logical_and(i >= delay, i < count + delay))
            def _(delay=delay, stage=stage):
                stage(i - delay)

        return carry

    lax.fori_loop(0, count + last, step, 0)
    for when, tick in sorted(ticks, key=lambda entry: entry[0]):
        if when >= count + last:
            tick()


def norm_forward(total, gain, shift):
    center = total - jnp.mean(total, axis=1, keepdims=True)
    spread = jnp.mean(center * center, axis=1, keepdims=True)
    inverse = lax.rsqrt(spread + NORM_EPSILON)
    unit = center * inverse
    return unit, inverse, unit * gain + shift


def norm_back(grad, unit, inverse, gain):
    grad_unit = grad * gain
    first = jnp.mean(grad_unit, axis=1, keepdims=True)
    second = jnp.mean(grad_unit * unit, axis=1, keepdims=True)
    return inverse * (grad_unit - first - unit * second)


def column_sum(value):
    return jnp.sum(value, axis=0, keepdims=True)


def split_two(value):
    high = value.astype(BF)
    return high, (value - high.astype(F32)).astype(BF)


def exact(value, product):
    high, rest = split_two(value)
    low = (value - high.astype(F32) - rest.astype(F32)).astype(BF)
    return product(high) + product(rest) + product(low)


def wide(column):
    return jnp.broadcast_to(column, (column.shape[0], 128))


def forward_refs(rows, width, units):
    return dict(
        unit_one=((rows // 2, D), F32),
        unit_two=((rows // 2, D), F32),
        hidden=((rows, units), BF),
        slope=((rows, units), BF),
    )


def forward_small(rows):
    return dict(inverse_one=((rows // 2, 128), F32), inverse_two=((rows // 2, 128), F32))


def forward_stages(r, who, projected, second, spread):
    def middle(t):
        total = r.residual[who.own(t), :].astype(F32) + projected(t) + r.shared[r.base + 0 : r.base + 1, :]
        unit, inverse, normed = norm_forward(total, r.shared[r.base + 1 : r.base + 2, :], r.shared[r.base + 2 : r.base + 3, :])
        r.unit_one[who.half(t), :] = unit
        r.inverse_one[who.half(t), :] = wide(inverse)
        r.normed[who.half(t), :] = normed
        spread.give(t, normed)

    def feed(t):
        pre = dot(spread.take(t), r.ffn_up[...]) + r.hidden_bias
        chance = 0.5 + 0.5 * lax.erf(pre * (0.5**0.5))
        hidden = (pre * chance).astype(BF)
        r.hidden[who.chunk(t), :] = hidden
        bell = jnp.exp(-0.5 * pre * pre) * 0.3989422804014327
        r.slope[who.chunk(t), :] = (chance + pre * bell).astype(BF)
        second.give(t, dot_nt(hidden, r.ffn_down[...]))

    def final(t):
        total = r.normed[who.half(t), :] + second.take(t) + r.shared[r.base + 3 : r.base + 4, :]
        unit, inverse, result = norm_forward(total, r.shared[r.base + 4 : r.base + 5, :], r.shared[r.base + 5 : r.base + 6, :])
        r.unit_two[who.half(t), :] = unit
        r.inverse_two[who.half(t), :] = wide(inverse)
        return unit, inverse, result

    return middle, feed, final


def backward_stages(r, who, ends, third, mids):
    def enter(t, grad, unit, inverse):
        grad_total = norm_back(grad, unit, inverse, r.shared[r.base + 4 : r.base + 5, :])
        r.vectors[3:4, :] += column_sum(grad_total)
        r.vectors[4:5, :] += column_sum(grad * unit)
        r.vectors[5:6, :] += column_sum(grad)
        r.kept[who.half(t), :] = grad_total
        ends.give(t, grad_total)

    def feed_back(t):
        rows = who.chunk(t)
        grad = ends.take(t)
        grad_pre = (dot(grad, r.ffn_down[...]) * r.slope[rows, :].astype(F32)).astype(BF)
        r.units[0:1, :] += column_sum(grad_pre.astype(F32))
        third.give(t, dot_nt(grad_pre, r.ffn_up[...]))
        r.grad_pre[pl.ds(pl.multiple_of(lax.rem(t, 2) * who.size, who.size), who.size), :] = grad_pre

        @pl.when(lax.rem(t, 2) == 1)
        def _():
            both = who.two_chunks(t)
            r.sum_up[...] += dot_tn(r.spread_full[both, :], r.grad_pre[...])
            r.sum_down[...] += dot_tn(ends.r.full[both, :], r.hidden[both, :])

    def leave(t):
        grad = r.kept[who.half(t), :] + third.take(t)
        unit = r.unit_one[who.half(t), :]
        grad_total = norm_back(grad, unit, r.inverse_one[who.half(t), 0:1], r.shared[r.base + 1 : r.base + 2, :])
        r.vectors[0:1, :] += column_sum(grad_total)
        r.vectors[1:2, :] += column_sum(grad * unit)
        r.vectors[2:3, :] += column_sum(grad)
        if r.grad_one is not None:
            r.grad_one[who.half(t), :] = grad_total
        mids.give(t, grad_total)

    def project_back(t):
        rows = who.chunk(t)
        grad = mids.take(t)
        r.grad_mixed[rows, :] = dot(grad, r.out_proj[...]).astype(BF)

        @pl.when(lax.rem(t, 2) == 1)
        def _():
            both = who.two_chunks(t)
            r.sum_out[...] += dot_tn(mids.r.full[both, :], r.mixed[both, :])

    return enter, feed_back, leave, project_back


def clear(*refs):
    for ref in refs:
        ref[...] = jnp.zeros_like(ref)


def finish_all(count, parts):
    def step(t, carry):
        for part in parts:
            part.finish(t)
        return carry

    lax.fori_loop(0, count, step, 0)


def packed(ref):
    return jnp.concatenate([ref[k].astype(BF) for k in range(ref.shape[0])], axis=1)


def projection_bias(split, width):
    return jnp.concatenate([split[:, :width], jnp.zeros((1, width), F32), split[:, width : 2 * width]], axis=1)


def opening(activations, segments, owners, attn_weights, ffn_weights, split_biases, shared_vectors, count):
    rows = activations.shape[0]
    width, units = attn_weights.shape[3], ffn_weights.shape[3]
    heads = width // DH
    blocks = rows // BLOCK
    lines = count // 2
    block = D // count
    layers = split_biases.shape[0]

    def body(r):
        who = Partners()
        column = Column(count)
        who.meet(column)
        wide_attn = GatherBlocks(column, SimpleNamespace(full=r.full_attn, **vars(pick(r, "ga"))))
        wide_up = GatherBlocks(column, SimpleNamespace(full=r.full_up, **vars(pick(r, "gu"))))
        wide_down = GatherPairs(column, SimpleNamespace(full=r.full_down, **vars(pick(r, "gd"))))
        halo = Halo(column, SimpleNamespace(left=r.left, right=r.right, **vars(pick(r, "halo"))), r.pair, WIN, BLOCK)
        first, last = column.index == 0, column.index == count - 1
        to_before = copy_to(r.ids, r.ids_right, r.ids_sent.at[0], r.ids_came.at[0], halo.before)
        to_after = copy_to(r.ids, r.ids_left, r.ids_sent.at[1], r.ids_came.at[1], halo.after)
        r.late.attn.wait()
        wide_attn.put(packed(r.attn.at[0]))
        wide_attn.start_line()
        wide_attn.start_pair()
        r.ids[...] = r.segments[...].astype(F32)

        @pl.when(first)
        def _():
            r.ids_left[...] = jnp.zeros_like(r.ids_left)

        @pl.when(last)
        def _():
            r.ids_right[...] = jnp.zeros_like(r.ids_right)

        @pl.when(jnp.logical_not(first))
        def _():
            to_before.start()

        @pl.when(jnp.logical_not(last))
        def _():
            to_after.start()

        halo.clear()
        r.late.ffn.wait()
        wide_down.put(r.ffn[0, 1].astype(BF))
        wide_down.start_pair()
        wide_up.put(r.ffn[0, 0].astype(BF))
        for slot in range(count):
            row = lax.broadcasted_iota(jnp.int32, (block, D), 0)
            col = lax.broadcasted_iota(jnp.int32, (block, D), 1)
            target = r.owners[slot] * block + row
            r.turn[slot * block : (slot + 1) * block, :] = jnp.where(col == target, 1.0, 0.0).astype(BF)

        def sort_chunk(t, carry):
            chunk = pl.ds(pl.multiple_of(t * BLOCK, BLOCK), BLOCK)
            r.low[chunk, :] = dot(r.activations[chunk, :], r.turn[...]).astype(BF)
            return carry

        r.flush_whole.turn.start()
        r.late.activations.wait()
        lax.fori_loop(0, blocks, sort_chunk, 0)
        r.flush_whole.low.start()
        wide_attn.relay(1)
        padding = jnp.zeros((16 - 6 * layers, D), F32)
        stacked = [r.shared_vectors[k, layer : layer + 1, :] for layer in range(layers) for k in range(6)]
        stacked = jnp.concatenate(stacked + [padding], axis=0)
        r.shared[...] = exact(stacked, lambda part: dot(part, r.turn[...]))
        wide_attn.relay(2)
        wide_up.start_line()

        @pl.when(jnp.logical_not(last))
        def _():
            to_before.wait_recv()

        @pl.when(jnp.logical_not(first))
        def _():
            to_after.wait_recv()

        def flat(ref):
            return jnp.concatenate([ref[k : k + 1, :] for k in range(ref.shape[0])], axis=1)

        own_ids = flat(r.ids)
        padded = jnp.concatenate([flat(r.ids_left)[:, rows - 2 * WIN :], own_ids, flat(r.ids_right)[:, : 2 * WIN]], axis=1)
        r.id_row[...] = jnp.broadcast_to(padded, r.id_row.shape)
        sort = parity_matrix()
        lap = 2 * BLOCK
        sorted_ids = [
            dot_nt(r.id_row[:, g * lap : (g + 1) * lap].astype(BF), sort) for g in range(2 * blocks // 2)
        ]
        natural = jnp.concatenate([padded[:, WIN : rows + 3 * WIN], padded[:, : 2 * WIN]], axis=1)
        arranged = jnp.concatenate(
            [part[0:1, :BLOCK] for part in sorted_ids] + [part[0:1, BLOCK:] for part in sorted_ids], axis=1
        )
        r.seg_keys[0:1, :] = natural
        r.seg_keys[1:2, :] = arranged
        middle = sorted_ids[1:-1]
        own_arranged = jnp.concatenate([part[0:1, :] for part in middle], axis=1)
        for which, row in ((0, own_ids), (1, own_arranged)):
            for k in range(rows // 128):
                square = jnp.broadcast_to(row[:, k * 128 : (k + 1) * 128], (128, 128))
                r.seg_query[k * 128 : (k + 1) * 128, which : which + 1] = square.T[:, 0:1]

        for k in range(3, lines):
            wide_attn.relay(k)
        wide_up.start_pair()
        wide_up.relay(1)
        wide_attn.arrive()
        r.flush_whole.full_attn.start()
        whole_attn = r.full_attn[...].reshape(D, 4 * width)
        r.proj[...] = whole_attn[:, : 3 * width]
        share = OutShare(who, SimpleNamespace(full=r.full_out, sent=r.share_sent, came=r.share_came))
        share.begin(whole_attn[:, 3 * width :])
        exchange = HeadExchange(who, r.out, r.gathered, r.heads_sent, r.heads_came)
        bias = projection_bias(r.split[0], width)

        def project(t):
            chunk = pl.ds(pl.multiple_of(t * BLOCK, BLOCK), BLOCK)
            value = dot(r.low[chunk, :], r.proj[...]) + bias
            r.query[chunk, :] = (value[:, :width].astype(BF).astype(F32) * SCORE_SCALE).astype(BF)
            pair = value[:, width:].astype(BF)
            r.pair[chunk, :] = pair
            inner = pl.ds(pl.multiple_of((t + 1) * BLOCK, BLOCK), BLOCK)
            r.keys[inner, :] = pair[:, :width]
            r.values[inner, :] = pair[:, width:]

        def outer_project(i, carry):
            t = i * (blocks - 1)
            project(t)
            halo.send(t)
            return carry

        def inner_project(i, carry):
            project(i)
            return carry

        lax.fori_loop(0, 2, outer_project, 0)
        wide_up.relay(2)
        wide_down.begin()
        lax.fori_loop(1, blocks - 1, inner_project, 0)
        for k in range(3, lines):
            wide_up.relay(k)

        def written(step):
            rows_of = pl.ds(pl.multiple_of(step * BLOCK, BLOCK), BLOCK)
            return pltpu.make_async_copy(r.soft.at[:, rows_of, :], r.soft_hbm.at[:, rows_of, :], r.soft_sem.at[step])

        def attend_block(step):
            own = pl.ds(pl.multiple_of(step * BLOCK, BLOCK), BLOCK)
            near = pl.ds(pl.multiple_of(step * BLOCK, BLOCK), 3 * BLOCK)
            key_block, value_block, query_block = r.keys[near, :], r.values[near, :], r.query[own, :]
            mine = r.seg_query[own, 0:1]
            theirs = r.id_row[0:1, pl.ds(pl.multiple_of(step * BLOCK + BLOCK, BLOCK), 3 * BLOCK)]
            allowed = jnp.logical_and(window_mask(), mine == theirs)
            gathered = jnp.zeros((BLOCK, width), F32)
            for head, lanes in enumerate(head_lanes(heads)):
                soft = soft_weights(query_block, key_block, lanes, allowed)
                r.soft[head, own, :] = soft
                gathered = jnp.where(lanes, dot(soft, value_block), gathered)
            r.out[own, :] = gathered.astype(BF)
            written(step).start()
            for k in range(BLOCK // CHUNK):
                exchange.give(BLOCK // CHUNK * step + k)

        def inner_attend(i, carry):
            attend_block(i)
            return carry

        def outer_attend(i, carry):
            attend_block(i * (blocks - 1))
            return carry

        lax.fori_loop(1, blocks - 1, inner_attend, 0)
        wide_down.relay(1)
        share.hand_on()
        halo.arrive()
        for part, start in ((r.left, 0), (r.right, (blocks + 1) * BLOCK)):
            r.keys[pl.ds(start, BLOCK), :] = part[:, :width]
            r.values[pl.ds(start, BLOCK), :] = part[:, width:]
        lax.fori_loop(0, 2, outer_attend, 0)
        for k in range(2, lines):
            wide_down.relay(k)
        wide_up.arrive()

        def exchanged(t, carry):
            exchange.take(t)
            exchange.finish(t)
            return carry

        lax.fori_loop(0, rows // CHUNK, exchanged, 0)
        share.finish()
        for step in range(blocks):
            written(step).wait()
        for copy in vars(r.flush_whole).values():
            copy.wait()
        halo.finish()
        for engine in (wide_attn, wide_up, wide_down):
            engine.finish()

        @pl.when(jnp.logical_not(first))
        def _():
            to_before.wait_send()

        @pl.when(jnp.logical_not(last))
        def _():
            to_after.wait_send()

    scratch = dict(
        proj=pltpu.VMEM((D, 3 * width), BF),
        pair=pltpu.VMEM((rows, 2 * width), BF),
        left=pltpu.VMEM((WIN, 2 * width), BF),
        right=pltpu.VMEM((WIN, 2 * width), BF),
        ids=pltpu.VMEM((rows // 128, 128), F32),
        ids_left=pltpu.VMEM((rows // 128, 128), F32),
        ids_right=pltpu.VMEM((rows // 128, 128), F32),
        ids_sent=pltpu.SemaphoreType.DMA((2,)),
        ids_came=pltpu.SemaphoreType.DMA((2,)),
        id_row=pltpu.VMEM((8, rows + 4 * WIN), F32),
    )
    scratch.update(
        heads_sent=pltpu.SemaphoreType.DMA((3, rows // CHUNK)),
        heads_came=pltpu.SemaphoreType.DMA((3, rows // CHUNK)),
        **share_scratch(),
    )
    scratch.update(prefixed("ga", gather_sems(lines)))
    scratch.update(prefixed("gu", gather_sems(lines)))
    scratch.update(prefixed("gd", gather_sems(lines)))
    scratch.update(prefixed("halo", halo_scratch(1)))
    return run_kernel(
        body,
        "opening",
        dict(
            segments=segments.reshape(rows // 128, 128),
            owners=owners,
            split=split_biases,
            shared_vectors=shared_vectors.transpose(1, 0, 2),
        ),
        dict(
            full_up=((count, block, units), BF),
            full_down=((count, block, units), BF),
            shared=((16, D), F32),
            seg_query=((rows, 2), F32),
            seg_keys=((8, 2 * rows), F32),
            out=((rows, width), BF),
            gathered=((4, rows // 2, width), BF),
            full_out=((4, width, D), BF),
            query=((rows, width), BF),
            keys=((rows + 2 * BLOCK, width), BF),
            values=((rows + 2 * BLOCK, width), BF),
        ),
        scratch,
        collective=5,
        flops=2 * rows * D * (D + 3 * width),
        in_smem=("owners",),
        late=dict(attn=attn_weights, ffn=ffn_weights, activations=activations),
        whole=dict(
            full_attn=((count, block, 4 * width), BF),
            low=((rows, D), BF),
            turn=((D, D), BF),
            soft=((heads, rows, 3 * BLOCK), BF),
        ),
        pieces=blocks,
    )


def middle_forward(gathered, full_out, ffn_up, ffn_down, residual, shared, split_biases, attn_weights, ffn_weights, count):
    rows, width = 2 * gathered.shape[1], gathered.shape[2]
    units = ffn_up.shape[1]
    chunks = rows // CHUNK
    lines = count // 2
    block = D // count

    def body(r):
        who = Partners()
        r.base = 0
        second = Exchange(who, pick(r, "second"))
        spread = Gather(who, SimpleNamespace(full=r.spread_full, sent=r.spread_sent, came=r.spread_came))
        last = Gather(who, SimpleNamespace(full=r.last_full, sent=r.last_sent, came=r.last_came))
        column = Column(count)
        who.meet(column)
        wide_attn = GatherBlocks(column, SimpleNamespace(full=r.full_attn, **vars(pick(r, "ga"))))
        wide_up = GatherBlocks(column, SimpleNamespace(full=r.full_up, **vars(pick(r, "gu"))))
        wide_down = GatherPairs(column, SimpleNamespace(full=r.full_down, **vars(pick(r, "gd"))))
        share = OutShare(who, SimpleNamespace(full=r.next_out, sent=r.share_sent, came=r.share_came))
        halo = Halo(column, SimpleNamespace(left=r.left, right=r.right, **vars(pick(r, "halo"))), r.pair, 2 * WIN, CHUNK)
        r.late.next_attn.wait()
        wide_attn.put(packed(r.next_attn.at[1]))
        wide_attn.start_line()
        wide_attn.start_pair()
        r.late.next_ffn.wait()
        wide_down.put(r.next_ffn[1, 1].astype(BF))
        wide_down.start_pair()
        wide_up.put(r.next_ffn[1, 0].astype(BF))
        halo.clear()
        r.late.full_out.wait()
        r.late.gathered.wait()
        r.hidden_bias = r.split[0][:, 2 * width :]
        next_bias = projection_bias(r.split[1], width)

        def unpack():
            wide_attn.arrive()
            packed_attn = r.full_attn[...].reshape(D, 4 * width)
            r.next_proj[...] = packed_attn[:, : 3 * width]
            share.begin(packed_attn[:, 3 * width :])

        ticks = [(0, r.late.residual.wait), (1, r.late.ffn_up.wait), (1, r.late.ffn_down.wait), (chunks, unpack), (chunks + 6, share.hand_on)]
        ticks += [(when, lambda k=k: wide_attn.relay(k + 1)) for k, when in enumerate(GATHER_TIMES[0])]
        ticks += [(GATHER_TIMES[1][0], wide_up.start_line), (GATHER_TIMES[1][1], wide_up.start_pair)]
        ticks += [(when, lambda k=k: wide_up.relay(k + 1)) for k, when in enumerate(GATHER_TIMES[2])]
        ticks += [(GATHER_TIMES[3][0], wide_down.begin)]
        ticks += [(when, lambda k=k: wide_down.relay(k + 1)) for k, when in enumerate(GATHER_TIMES[3][1:])]

        def projected(t):
            mine = jnp.concatenate([r.gathered[k, who.half(t), :] for k in range(4)], axis=1)
            return dot(mine, r.full_out[...].reshape(D, D))

        middle, feed, final = forward_stages(r, who, projected, second, spread)

        def middle_out(t):
            middle(t)
            r.flush.unit_one.copy(who.half(t), t).start()

        def feed_out(t):
            feed(t)
            for flush in (r.flush.hidden, r.flush.slope, r.flush.spread_full):
                flush.copy(who.chunk(t), t).start()

        def close(t):
            _, _, result = final(t)
            r.flush.unit_two.copy(who.half(t), t).start()
            last.give(t, result)

        def next_project(k):
            chunk_pair = (2 * k, 2 * k + 1)
            for t in chunk_pair:
                last.wait(t)
            both = who.two_chunks(2 * k + 1)
            value = (dot(r.last_full[both, :], r.next_proj[...]) + next_bias).astype(BF)
            r.query[both, :] = value[:, :width]
            r.pair[both, :] = value[:, width:]
            for t in chunk_pair:
                halo.send(t)
                r.flush.last_full.copy(who.chunk(t), t).start()

        ticks += [(when, lambda k=k: next_project(k)) for k, when in enumerate(PROJECT_TIMES)]

        run_stages(
            chunks,
            [
                (2, second.add),
                (4, close),
                (0, middle_out),
                (1, feed_out),
            ],
            ticks,
        )
        finish_all(chunks, (second, spread, last))
        halo.arrive()
        share.finish()
        wide_up.arrive()
        halo.finish()
        for engine in (wide_attn, wide_up, wide_down):
            engine.finish()

        def written(t, carry):
            for flush in (r.flush.hidden, r.flush.slope, r.flush.spread_full, r.flush.last_full):
                flush.copy(who.chunk(t), t).wait()
            for flush in (r.flush.unit_one, r.flush.unit_two):
                flush.copy(who.half(t), t).wait()
            return carry

        lax.fori_loop(0, chunks, written, 0)

    outputs = forward_small(rows)
    outputs.update(
        query=((rows, width), BF),
        pair=((rows, 2 * width), BF),
        full_attn=((count, block, 4 * width), BF),
        next_out=((4, width, D), BF),
        full_up=((count, block, units), BF),
        full_down=((count, block, units), BF),
        left=((2 * WIN, 2 * width), BF),
        right=((2 * WIN, 2 * width), BF),
    )
    flushed = forward_refs(rows, width, units)
    flushed.update(spread_full=((rows, D), BF), last_full=((rows, D), BF))
    scratch = dict(
        normed=pltpu.VMEM((rows // 2, D), F32),
        next_proj=pltpu.VMEM((D, 3 * width), BF),
        **share_scratch(),
    )
    scratch.update(prefixed("second", exchange_scratch(rows)))
    for key in ("spread", "last"):
        for part in ("sent", "came"):
            scratch[key + "_" + part] = pltpu.SemaphoreType.DMA((chunks,))
    for key in ("ga", "gu", "gd"):
        scratch.update(prefixed(key, gather_sems(lines)))
    scratch.update(prefixed("halo", halo_scratch(2 * WIN // CHUNK)))
    return run_kernel(
        body,
        "middle_forward",
        dict(shared=shared, split=split_biases),
        outputs,
        scratch,
        collective=1,
        flops=2 * rows * D * (4 * width + 2 * units),
        late=dict(
            next_attn=attn_weights,
            next_ffn=ffn_weights,
            full_out=full_out,
            gathered=gathered,
            residual=residual,
            ffn_up=ffn_up,
            ffn_down=ffn_down,
        ),
        flushed=flushed,
        pieces=chunks,
    )


def turning(mixed, first_mixed, out_proj, attn, ffn_up, ffn_down, residual, shared, split_biases, cotangent, turn):
    rows, width = mixed.shape
    units = ffn_up.shape[1]
    chunks = rows // WIDE_CHUNK

    def body(r):
        who = Partners(size=WIDE_CHUNK)
        r.base, r.grad_one = 6, None
        second, third = Exchange(who, pick(r, "second")), Exchange(who, pick(r, "third"))
        heads = HeadExchange(who, r.mixed, r.gathered, r.heads_sent, r.heads_came)
        spread = Gather(who, pick(r, "spread"))
        ends = Gather(who, pick(r, "ends"))
        mids = Gather(who, SimpleNamespace(full=r.grad_low, sent=r.mids_sent, came=r.mids_came))
        out = Gather(who, SimpleNamespace(full=r.output, sent=r.out_sent, came=r.out_came))
        who.meet()
        r.late.mixed.wait()
        for t in range(chunks // 2, chunks):
            heads.give(t)
        r.late.first_mixed.wait()
        r.gathered[:, : rows // 4, :] = r.first_mixed[...]
        r.late.full_out.wait()
        r.late.attn.wait()
        r.out_proj[...] = r.attn[:, 3 * width :]
        r.hidden_bias = r.split[1][:, 2 * width :]
        clear(r.vectors, r.units, r.sum_up, r.sum_down, r.sum_out)

        def projected(t):
            @pl.when(t >= chunks // 2)
            def _():
                heads.take(t)

            mine = jnp.concatenate([r.gathered[k, who.half(t), :] for k in range(4)], axis=1)
            return dot(mine, r.full_out[...].reshape(D, D))

        middle, feed, final = forward_stages(r, who, projected, second, spread)
        enter, feed_back, leave, project_back = backward_stages(r, who, ends, third, mids)

        ticks = [(0, r.late.residual.wait), (1, r.late.ffn_up.wait), (1, r.late.ffn_down.wait)]
        ticks += [(4, r.late.cotangent.wait), (4, r.late.turn.wait)]

        def close(t):
            unit, inverse, result = final(t)
            grad = dot(r.cotangent[who.own(t), :], r.turn[...])
            enter(t, grad, unit, inverse)
            out.give(t, result)

        run_stages(
            chunks,
            [
                (6, third.add),
                (2, second.add),
                (8, leave),
                (4, close),
                (0, middle),
                (9, project_back),
                (5, feed_back),
                (1, feed),
            ],
            ticks,
        )

        def arrive(t, carry):
            out.wait(t)
            return carry

        lax.fori_loop(0, chunks, arrive, 0)
        finish_all(chunks, (second, third, spread, ends, mids, out))
        for t in range(chunks // 2, chunks):
            heads.finish(t)
        r.up[...] = r.sum_up[...].astype(BF)
        r.down[...] = r.sum_down[...].astype(BF)
        r.proj[...] = r.sum_out[...].astype(BF)

    outputs = dict(
        output=((rows, D), BF),
        up=((D, units), BF),
        down=((D, units), BF),
        proj=((D, width), BF),
        grad_low=((rows, D), BF),
        grad_mixed=((rows, width), BF),
        vectors=((8, D), F32),
        units=((8, units), F32),
    )
    scratch = dict(
        normed=pltpu.VMEM((rows // 2, D), F32),
        kept=pltpu.VMEM((rows // 2, D), F32),
        grad_pre=pltpu.VMEM((2 * WIDE_CHUNK, units), BF),
        out_proj=pltpu.VMEM((D, width), BF),
        gathered=pltpu.VMEM((4, rows // 2, width), BF),
        heads_sent=pltpu.SemaphoreType.DMA((3, chunks)),
        heads_came=pltpu.SemaphoreType.DMA((3, chunks)),
        sum_up=pltpu.VMEM((D, units), F32),
        sum_down=pltpu.VMEM((D, units), F32),
        sum_out=pltpu.VMEM((D, width), F32),
        mids_sent=pltpu.SemaphoreType.DMA((chunks,)),
        mids_came=pltpu.SemaphoreType.DMA((chunks,)),
        out_sent=pltpu.SemaphoreType.DMA((chunks,)),
        out_came=pltpu.SemaphoreType.DMA((chunks,)),
    )
    for key, (shape, dtype) in {**forward_refs(rows, width, units), **forward_small(rows)}.items():
        scratch[key] = pltpu.VMEM(shape, dtype)
    for key in ("second", "third"):
        scratch.update(prefixed(key, exchange_scratch(rows)))
    for key in ("spread", "ends"):
        scratch.update(prefixed(key, gather_scratch(rows)))
    return run_kernel(
        body,
        "turning",
        dict(
            shared=shared,
            split=split_biases,
        ),
        outputs,
        scratch,
        collective=2,
        flops=2 * rows * D * (3 * width + 6 * units),
        late=dict(
            mixed=mixed,
            first_mixed=first_mixed,
            full_out=out_proj,
            attn=attn,
            residual=residual,
            ffn_up=ffn_up,
            ffn_down=ffn_down,
            cotangent=cotangent,
            turn=turn,
        ),
    )


def projection_back_stage(r, who, column, exchange):
    rows, width = r.grad_query.shape
    rim = r.out_right.shape[0]
    first, last = column.index == 0, column.index == column.count - 1
    after = (lax.rem(column.index + 1, column.count), column.here)
    copy = copy_to(r.out_right, r.from_left, r.halo_sent.at[0], r.halo_came.at[0], after)

    def begin():
        r.grad_pair[...] = r.grad_own[...]

        @pl.when(jnp.logical_not(last))
        def _():
            copy.start()

    def absorb():
        @pl.when(jnp.logical_not(first))
        def _():
            copy.wait_recv()
            where = pl.ds(0, rim)
            total = r.grad_pair[where, :].astype(F32) + r.from_left[...].astype(F32)
            r.grad_pair[where, :] = total.astype(BF)

    def end():
        @pl.when(jnp.logical_not(last))
        def _():
            copy.wait_send()

    def stage(k):
        both = who.two_chunks(2 * k + 1)
        parts = jnp.concatenate([r.grad_query[both, :], r.grad_pair[both, :]], axis=1)
        exchange.r.part[both, :] = dot_nt(parts, r.next_attn[:, : 3 * width]).astype(BF)
        for t in (2 * k, 2 * k + 1):
            exchange.core_copy(t).start()
        r.sum_three[...] += dot_tn(r.low[both, :], parts)
        r.biases[0:1, :] += column_sum(parts.astype(F32))

    half = rows // CHUNK // 2
    steps = [(0 if k < half // 2 else half, k) for k in range(half)]
    ticks = [(half, absorb)] + [(first_time + k % (half // 2), lambda k=k: stage(k)) for first_time, k in steps]
    return begin, end, ticks


def projection_back_scratch(rows, rim, width):
    return dict(
        grad_pair=pltpu.VMEM((rows, 2 * width), BF),
        from_left=pltpu.VMEM((rim, 2 * width), BF),
        halo_sent=pltpu.SemaphoreType.DMA((1,)),
        halo_came=pltpu.SemaphoreType.DMA((1,)),
        sum_three=pltpu.VMEM((D, 3 * width), F32),
    )


def scatter_three(column, r, totals):
    return (
        ScatterPairs(column, SimpleNamespace(grads=r.above_up, **vars(pick(r, "ru"))), totals[0]),
        ScatterBlocks(column, SimpleNamespace(grads=r.above_down, **vars(pick(r, "rd"))), totals[1]),
        ScatterBlocks(column, SimpleNamespace(grads=r.packed, **vars(pick(r, "ra"))), totals[2]),
    )


def scatter_three_scratch(count, width, units):
    lines, block = count // 2, D // count
    scratch = dict(packed=pltpu.VMEM((count, block, 4 * width), BF))
    scratch.update(prefixed("ru", scatter_pairs_scratch(lines, block, units)))
    scratch.update(prefixed("rd", scatter_scratch(lines, block, units)))
    scratch.update(prefixed("ra", scatter_scratch(lines, block, 4 * width, held=False)))
    return scratch


def pack_attention(r):
    both = jnp.concatenate([r.sum_three[...].astype(BF), r.above_proj[...]], axis=1)
    r.packed[...] = both.reshape(r.packed.shape)


def middle_backward(back, next_attn, grad_above, low, saved, mixed, attn, ffn_up, ffn_down, shared, above, count):
    rows, width = mixed.shape
    units = ffn_up.shape[1]
    chunks = rows // CHUNK
    block = D // count
    rim = back.out_right.shape[0]

    def body(r):
        who = Partners(chunks, chunks // 2)
        r.base = 0
        zeroth, third = Exchange(who, pick(r, "zeroth")), Exchange(who, pick(r, "third"))
        ends, mids = Gather(who, pick(r, "ends")), Gather(who, pick(r, "mids"))
        column = Column(count)
        who.meet(column)
        up, down, three = scatter_three(column, r, (r.up_total, r.down_total, r.attn_total))
        begin, end, back_ticks = projection_back_stage(r, who, column, zeroth)
        for copy in (r.late.out_right, r.late.grad_own, r.late.grad_query, r.late.next_attn, r.late.low):
            copy.wait()
        begin()
        up.start()
        down.start()

        def start_three():
            pack_attention(r)
            three.start()

        ticks = [tick for engine, times in zip((up, down, three), BACK_TIMES) for tick in engine.ticks(times)]
        ticks += [(chunks // 2 + 2, start_three)]
        ticks += [(3, r.late.unit_two.wait), (3, r.late.grad_above.wait), (4, r.late.ffn_up.wait)]
        ticks += [(4, r.late.ffn_down.wait), (4, r.late.slope.wait), (4, r.late.hidden.wait)]
        ticks += [(4, r.late.spread_full.wait), (7, r.late.unit_one.wait), (8, r.late.mixed.wait)]
        ticks = back_ticks + ticks
        r.late.attn.wait()
        r.out_proj[...] = r.attn[:, 3 * width :]
        clear(r.vectors, r.units, r.biases, r.sum_up, r.sum_down, r.sum_out, r.sum_three)
        enter, feed_back, leave, project_back = backward_stages(r, who, ends, third, mids)

        def start(t):
            half = who.half(t)
            enter(t, r.grad_above[who.own(t), :].astype(F32) + zeroth.take(t), r.unit_two[half, :], r.inverse_two[half, 0:1])

        run_stages(
            chunks,
            [
                (5, third.add),
                (1, zeroth.add),
                (7, leave),
                (3, start),
                (8, project_back),
                (4, feed_back),
            ],
            ticks,
        )
        finish_all(chunks, (zeroth, third, ends, mids))
        end()
        r.up[...] = r.sum_up[...].astype(BF)
        r.down[...] = r.sum_down[...].astype(BF)
        r.proj[...] = r.sum_out[...].astype(BF)
        for engine in (up, down, three):
            engine.finish()

    outputs = dict(
        up=((D, units), BF),
        down=((D, units), BF),
        proj=((D, width), BF),
        grad_one=((rows // 2, D), F32),
        grad_mixed=((rows, width), BF),
        vectors=((8, D), F32),
        units=((8, units), F32),
        biases=((8, 3 * width), F32),
        up_total=((block, units), F32),
        down_total=((block, units), F32),
        attn_total=((block, 4 * width), F32),
    )
    scratch = dict(
        kept=pltpu.VMEM((rows // 2, D), F32),
        grad_pre=pltpu.VMEM((2 * CHUNK, units), BF),
        out_proj=pltpu.VMEM((D, width), BF),
        sum_up=pltpu.VMEM((D, units), F32),
        sum_down=pltpu.VMEM((D, units), F32),
        sum_out=pltpu.VMEM((D, width), F32),
    )
    scratch.update(projection_back_scratch(rows, rim, width))
    scratch.update(scatter_three_scratch(count, width, units))
    for key in ("zeroth", "third"):
        scratch.update(prefixed(key, exchange_scratch(rows)))
    for key in ("ends", "mids"):
        scratch.update(prefixed(key, gather_scratch(rows)))
    return run_kernel(
        body,
        "middle_backward",
        dict(
            inverse_one=saved.inverse_one,
            inverse_two=saved.inverse_two,
            shared=shared,
            above_up=above.up.reshape(count, block, units),
            above_down=above.down.reshape(count, block, units),
            above_proj=above.proj,
        ),
        outputs,
        scratch,
        collective=3,
        flops=2 * rows * D * (8 * width + 4 * units),
        in_hbm=("above_up", "above_down"),
        late=dict(
            out_right=back.out_right,
            grad_own=back.out_own,
            grad_query=back.out_query,
            next_attn=next_attn,
            low=low,
            attn=attn,
            unit_two=saved.unit_two,
            grad_above=grad_above,
            ffn_down=ffn_down,
            slope=saved.slope,
            ffn_up=ffn_up,
            hidden=saved.hidden,
            spread_full=saved.spread_full,
            unit_one=saved.unit_one,
            mixed=mixed,
        ),
    )


class SmallSum:
    def __init__(self, who, column, refs):
        self.who, self.c, self.r = who, column, refs

    def copy(self, slot, source, device):
        r = self.r
        return copy_to(r.kept.at[source], r.came.at[slot], r.sent_sem.at[slot], r.came_sem.at[slot], device)

    def core_copy(self):
        return self.copy(0, 0, self.who.sibling)

    def pair_copy(self):
        return self.copy(1, 1, self.c.at(self.c.outer, 1 - self.c.inner))

    def line_copy(self, target, slot):
        c, r = self.c, self.r
        return copy_to(
            r.kept.at[2], r.came.at[2 + slot], r.sent_sem.at[2 + target], r.came_sem.at[2 + slot], c.at(target, c.inner)
        )

    def second(self, both):
        r = self.r
        self.core_copy().wait_recv()
        row = lax.broadcasted_iota(jnp.int32, r.kept.shape[1:], 0)
        r.kept[1] = r.kept[0] + jnp.where(row < both, r.came[0], 0.0)
        self.pair_copy().start()

    def third(self):
        r, c = self.r, self.c
        self.pair_copy().wait_recv()
        r.kept[2] = r.kept[1] + r.came[1]
        for k in range(1, c.lines):
            self.line_copy(c.turn(k), c.outer).start()
        r.came[2 + c.outer] = r.kept[2]

    def result(self):
        r, c = self.r, self.c
        for k in range(1, c.lines):
            source = c.turn(k)
            self.line_copy(source, source).wait_recv()
        return sum(r.came[2 + k] for k in range(c.lines))

    def finish(self):
        c = self.c
        self.core_copy().wait_send()
        self.pair_copy().wait_send()
        for k in range(1, c.lines):
            self.line_copy(c.turn(k), c.outer).wait_send()


def small_scratch(lines, shape):
    return dict(
        kept=pltpu.VMEM((3,) + shape, F32),
        came=pltpu.VMEM((2 + lines,) + shape, F32),
        sent_sem=pltpu.SemaphoreType.DMA((2 + lines,)),
        came_sem=pltpu.SemaphoreType.DMA((2 + lines,)),
    )


class NormSum:
    def __init__(self, who, column, refs):
        self.who, self.c, self.r = who, column, refs

    def mp_copy(self, device, target, slot):
        r = self.r
        return copy_to(r.mp_came.at[slot], r.mp_came.at[slot], r.mp_sent.at[target], r.mp_sem.at[slot], device)

    def seq_copy(self, device, target, slot):
        r = self.r
        return copy_to(r.seq_came.at[slot], r.seq_came.at[slot], r.seq_sent.at[target], r.seq_sem.at[slot], device)

    def run(self, value):
        who, c, r = self.who, self.c, self.r
        here = c.here
        r.mp_came[here] = jnp.full((8, 128), 1.0, F32) * value
        for k in range(1, 4):
            target = lax.rem(here + k, 4)
            self.mp_copy((c.index, target), target, here).start()
        for k in range(1, 4):
            source = lax.rem(here + k, 4)
            self.mp_copy((c.index, source), source, source).wait_recv()
        r.seq_came[c.index] = sum(r.mp_came[k] for k in range(4))
        for k in range(1, c.count):
            target = lax.rem(c.index + k, c.count)
            self.seq_copy((target, here), target, c.index).start()
        for k in range(1, c.count):
            source = lax.rem(c.index + k, c.count)
            self.seq_copy((source, here), source, source).wait_recv()
        total = sum(r.seq_came[k] for k in range(c.count))
        for k in range(1, 4):
            target = lax.rem(here + k, 4)
            self.mp_copy((c.index, target), target, here).wait_send()
        for k in range(1, c.count):
            target = lax.rem(c.index + k, c.count)
            self.seq_copy((target, here), target, c.index).wait_send()
        return total


def norm_scratch(count):
    return dict(
        mp_came=pltpu.VMEM((4, 8, 128), F32),
        mp_sent=pltpu.SemaphoreType.DMA((4,)),
        mp_sem=pltpu.SemaphoreType.DMA((4,)),
        seq_came=pltpu.VMEM((count, 8, 128), F32),
        seq_sent=pltpu.SemaphoreType.DMA((count,)),
        seq_sem=pltpu.SemaphoreType.DMA((count,)),
    )


def squares(ref):
    value = ref[...]
    return jnp.sum(value * value)


def ending(back, next_attn, grad_above, low, above, top, count):
    rows, width = back.out_query.shape
    chunks = rows // CHUNK
    lines, block = count // 2, D // count
    units = above.units.shape[1]
    rim = back.out_right.shape[0]

    def body(r):
        who = Partners(chunks, chunks // 2)
        zeroth = Exchange(who, pick(r, "zeroth"))
        out = Gather(who, SimpleNamespace(full=r.output, sent=r.out_sent, came=r.out_came))
        column = Column(count)
        who.meet(column)
        up, down, three = scatter_three(column, r, (r.ffn_grads.at[0], r.ffn_grads.at[1], r.attn_grads.at[0]))
        small = SmallSum(who, column, pick(r, "small"))
        begin, end, back_ticks = projection_back_stage(r, who, column, zeroth)
        for copy in (r.late.out_right, r.late.grad_own, r.late.grad_query, r.late.next_attn, r.late.low):
            copy.wait()
        begin()
        up.start()
        down.start()

        def start_three():
            small.second(12)
            pack_attention(r)
            three.start()

        def start_small():
            r.small_kept[0, 0:6, :] = r.vectors_low[0:6, :]
            r.small_kept[0, 6:12, :] = r.vectors_top[0:6, :]
            r.small_kept[0, 12:13, :] = r.units_low[0:1, :]
            r.small_kept[0, 13:14, :] = r.units_top[0:1, :]
            pieces = []
            for ref in (r.biases, r.biases_top):
                pieces += [ref[0:1, :width], ref[0:1, 2 * width :]]
            r.small_kept[0, 14:15, :] = jnp.concatenate(pieces, axis=1)
            r.small_kept[0, 15:16, :] = jnp.zeros((1, D), F32)
            small.core_copy().start()

        ticks = [tick for engine, times in zip((up, down, three), END_TIMES) for tick in engine.ticks(times)]
        ticks += [(3, r.late.grad_above.wait)]
        ticks += [(chunks // 2 + 2, start_small), (SMALL_TIMES[0], start_three), (SMALL_TIMES[1], small.third)]
        ticks = back_ticks + ticks
        clear(r.biases, r.sum_three)

        def close(t):
            out.give(t, r.grad_above[who.half(t), :] + zeroth.take(t))

        run_stages(chunks, [(1, zeroth.add), (3, close)], ticks)
        vectors = small.result()
        r.vectors[...] = vectors
        r.ffn_grads[2] = r.up_top[...]
        r.ffn_grads[3] = r.down_top[...]
        r.attn_grads[1] = r.attn_top[...]
        row = lax.broadcasted_iota(jnp.int32, (16, D), 0)
        squared = vectors * vectors
        split = jnp.sum(jnp.where(row >= 12, squared, 0.0))
        shared = jnp.sum(jnp.where(row < 12, squared, 0.0))
        first_seq = column.index == 0
        first_both = jnp.logical_and(first_seq, column.here == 0)
        value = squares(r.ffn_grads) + squares(r.attn_grads)
        value = value + jnp.where(first_seq, split, 0.0) + jnp.where(first_both, shared, 0.0)
        total = NormSum(who, column, pick(r, "norm")).run(value)
        r.norm[...] = jnp.sqrt(total)

        def arrive(t, carry):
            out.wait(t)
            return carry

        lax.fori_loop(0, chunks, arrive, 0)
        finish_all(chunks, (zeroth, out))
        end()
        for engine in (up, down, three, small):
            engine.finish()

    outputs = dict(
        output=((rows, D), BF),
        ffn_grads=((4, block, units), F32),
        attn_grads=((2, block, 4 * width), F32),
        vectors=((16, D), F32),
        norm=((8, 128), F32),
    )
    scratch = dict(
        biases=pltpu.VMEM((8, 3 * width), F32),
        out_sent=pltpu.SemaphoreType.DMA((chunks,)),
        out_came=pltpu.SemaphoreType.DMA((chunks,)),
    )
    scratch.update(projection_back_scratch(rows, rim, width))
    scratch.update(scatter_three_scratch(count, width, units))
    scratch.update(prefixed("zeroth", exchange_scratch(rows)))
    scratch.update(prefixed("small", small_scratch(lines, (16, D))))
    scratch.update(prefixed("norm", norm_scratch(count)))
    return run_kernel(
        body,
        "ending",
        dict(
            above_up=above.up.reshape(count, block, units),
            above_down=above.down.reshape(count, block, units),
            above_proj=above.proj,
            up_top=above.up_total,
            down_top=above.down_total,
            attn_top=above.attn_total,
            vectors_low=above.vectors,
            vectors_top=top.vectors,
            units_low=above.units,
            units_top=top.units,
            biases_top=above.biases,
        ),
        outputs,
        scratch,
        collective=4,
        flops=2 * rows * D * 6 * width,
        in_hbm=("above_up", "above_down"),
        late=dict(
            out_right=back.out_right,
            grad_own=back.out_own,
            grad_query=back.out_query,
            next_attn=next_attn,
            low=low,
            grad_above=grad_above,
        ),
    )


def moments(grad, first, second):
    first_new = BETA_FIRST * first + (1.0 - BETA_FIRST) * grad
    second_new = BETA_SECOND * second + (1.0 - BETA_SECOND) * grad * grad
    size = jnp.sqrt(second_new / (1.0 - BETA_SECOND**STEP)) + ADAM_EPSILON
    return first_new, second_new, first_new / (1.0 - BETA_FIRST**STEP) / size


def update(result, end, turn, attn, ffn, split, shared):
    block, units = ffn[0].shape[2:]
    width = attn[0].shape[3]
    rates = [0.5 * D ** (-0.5)] * 3 + [0.5 * (WIN / D) ** 0.5]
    names = ("weights", "first", "second", "average", "basis")

    def matrix(grad, weight, first, second, average, basis, rate):
        basis = basis.astype(BF)
        turned = dot(grad.astype(BF), basis)
        first_new, second_new, direction = moments(turned, first, second)
        back = dot_nt(direction.astype(BF), basis)
        weight_new = weight - rate * (back + DECAY_RATE * weight)
        return weight_new, first_new, second_new, AVERAGE_RATE * average + (1.0 - AVERAGE_RATE) * weight_new

    def body(r):
        step = pl.program_id(0)
        factor = CLIP_LEVEL / jnp.maximum(r.norm[0:1, 0:1], CLIP_LEVEL)
        r.result_real[...] = dot_nt(r.result[...], r.turn[...])
        r.grad_real[...] = dot_nt(r.grad[...], r.turn[...])
        rate = jnp.where(step % 2 == 0, 0.5 * D ** (-0.5), 0.5 * FF ** (-0.5))
        results = matrix(
            factor * r.ffn_grads[...],
            r.ffn_weights[...],
            r.ffn_first[...],
            r.ffn_second[...],
            r.ffn_average[...],
            r.ffn_basis[...],
            rate,
        )
        for key, value in zip(names, results):
            getattr(r, "ffn_" + key + "_new")[...] = value

        for k in range(2):
            last = jnp.logical_and(step % 2 == 1, k == 1)
            weight, first, second, average = matrix(
                factor * r.attn_grads[:, k * width : (k + 1) * width],
                r.attn_weights[k],
                r.attn_first[k],
                r.attn_second[k],
                r.attn_average[k],
                r.attn_basis[k],
                jnp.where(last, rates[3], rates[0]),
            )
            r.attn_weights_new[k] = weight
            r.attn_first_new[k] = first
            r.attn_average_new[k] = average

            @pl.when(step % 2 == 0)
            def _(k=k, second=second):
                r.attn_second_new[step // 2, k] = second

            @pl.when(step % 2 == 1)
            def _(k=k, second=second):
                if k == 0:
                    r.attn_second_new[step // 2, 2] = second
                else:
                    r.projection_second[step // 2] = second

        @pl.when(step == 0)
        def _():
            r.norm_out[0, 0] = jnp.max(r.norm[0:1, :])
            real = exact(r.vectors[...], lambda part: dot_nt(part, r.turn[...]))
            for layer in range(2):
                tail = r.vectors[14:15, layer * 2 * width : (layer + 1) * 2 * width]
                split_grad = jnp.concatenate([tail, r.vectors[12 + layer : 13 + layer, :]], axis=1)
                grad = factor * split_grad
                first_new, second_new, direction = moments(grad, r.split_first[layer], r.split_second[layer])
                r.split_old_new[layer] = r.split_old[layer] - VECTOR_RATE * direction
                r.split_first_new[layer] = first_new
                r.split_second_new[layer] = second_new
            for k in range(6):
                grad = factor * jnp.concatenate([real[k : k + 1], real[6 + k : 7 + k]], axis=0)
                first_new, second_new, direction = moments(grad, r.shared_first[k], r.shared_second[k])
                r.shared_old_new[k] = r.shared_old[k] - VECTOR_RATE * direction
                r.shared_first_new[k] = first_new
                r.shared_second_new[k] = second_new

    inputs = dict(
        ffn_grads=end.ffn_grads, attn_grads=end.attn_grads, vectors=end.vectors, norm=end.norm, turn=turn
    )
    rows = result.shape[0]
    inputs.update(result=result, grad=end.output)
    outputs = dict(result_real=((rows, D), F32), grad_real=((rows, D), F32))
    row_spec = pl.BlockSpec((rows // 4, D), lambda i: (i, 0))
    specs = dict(result=row_spec, grad=row_spec, result_real=row_spec, grad_real=row_spec)
    specs["ffn_grads"] = pl.BlockSpec((None, block, units), lambda i: (i, 0, 0))
    matrix_spec = pl.BlockSpec((None, None, block, units), lambda i: (i // 2, i % 2, 0, 0))
    for key, array in zip(names, ffn):
        inputs["ffn_" + key] = array
        specs["ffn_" + key] = matrix_spec
    specs["ffn_basis"] = pl.BlockSpec((None, None, None, None, units, units), lambda i: (i // 2, i % 2, 0, 0, 0, 0))
    pair_spec = pl.BlockSpec((None, 2, block, width), lambda i: (i // 2, i % 2, 0, 0))
    for key, array in zip(names, attn):
        inputs["attn_" + key] = array
        specs["attn_" + key] = pair_spec
    specs["attn_basis"] = pl.BlockSpec((None, 2, None, None, width, width), lambda i: (i // 2, i % 2, 0, 0, 0, 0))
    specs["attn_grads"] = pl.BlockSpec((None, block, 2 * width), lambda i: (i // 2, 0, i % 2))
    for prefix, group in (("split", split), ("shared", shared)):
        for key, array in zip(("old", "first", "second"), group):
            inputs[prefix + "_" + key] = array
    for key in ("weights", "first", "second", "average"):
        outputs["ffn_" + key + "_new"] = (ffn[0].shape, F32)
        specs["ffn_" + key + "_new"] = matrix_spec
        outputs["attn_" + key + "_new"] = (attn[0].shape, F32)
        specs["attn_" + key + "_new"] = pair_spec
    outputs["attn_second_new"] = ((2, 3, block, width), F32)
    del specs["attn_second_new"]
    outputs["projection_second"] = ((2, block, width), F32)
    for prefix, group in (("split", split), ("shared", shared)):
        for key in ("old", "first", "second"):
            outputs[prefix + "_" + key + "_new"] = (group[0].shape, F32)
    outputs["norm_out"] = ((1, 1), F32)
    return run_kernel(
        body,
        "update",
        inputs,
        outputs,
        {},
        flops=4 * block * units * units * 4,
        grid=(4,),
        specs=specs,
        in_smem=("norm_out",),
    )


def direct(
    activations,
    cotangent,
    segments,
    dilated_heads,
    owners,
    attn_weights,
    attn_first,
    attn_second,
    attn_average,
    attn_basis,
    ffn_weights,
    ffn_first,
    ffn_second,
    ffn_average,
    ffn_basis,
    split_biases,
    split_first,
    split_second,
    shared_vectors,
    shared_first,
    shared_second,
):
    count = lax.axis_size(SEQ)
    near = opening(
        activations, segments, owners, attn_weights, ffn_weights, split_biases, shared_vectors, count
    )
    near.arranged = near.out
    attn_zero, up_zero, down_zero = (
        full.reshape(D, -1) for full in (near.full_attn, near.full_up, near.full_down)
    )
    mid = middle_forward(
        near.gathered,
        near.full_out,
        up_zero,
        down_zero,
        near.low,
        near.shared,
        split_biases,
        attn_weights,
        ffn_weights,
        count,
    )
    far = attend(
        mid.query,
        mid.pair,
        mid.left,
        mid.right,
        near.seg_query,
        near.seg_keys,
        dilated_heads,
    )
    attn_one, up_one, down_one = (full.reshape(D, -1) for full in (mid.full_attn, mid.full_up, mid.full_down))
    top = turning(
        far.out, far.first, mid.next_out, attn_one, up_one, down_one, mid.last_full, near.shared, split_biases, cotangent, near.turn
    )
    far_back = attend_back(far, top.grad_mixed, dilated_heads, 2 * WIN, True, count, 6)
    low = middle_backward(
        far_back,
        attn_one,
        top.grad_low,
        mid.last_full,
        mid,
        near.out,
        attn_zero,
        up_zero,
        down_zero,
        near.shared,
        top,
        count,
    )
    near_back = attend_back(near, low.grad_mixed, dilated_heads, WIN, False, count, 7)
    end = ending(near_back, attn_zero, low.grad_one, near.low, low, top, count)
    new = update(
        top.output,
        end,
        near.turn,
        (attn_weights, attn_first, attn_second, attn_average, attn_basis),
        (ffn_weights, ffn_first, ffn_second, ffn_average, ffn_basis),
        (split_biases, split_first, split_second),
        tuple(array.transpose(1, 0, 2) for array in (shared_vectors, shared_first, shared_second)),
    )
    return (
        new.result_real,
        new.grad_real,
        new.attn_weights_new,
        new.attn_first_new,
        new.attn_second_new,
        new.projection_second,
        new.attn_average_new,
        new.ffn_weights_new,
        new.ffn_first_new,
        new.ffn_second_new,
        new.ffn_average_new,
        new.split_old_new,
        new.split_first_new,
        new.split_second_new,
        new.shared_old_new.transpose(1, 0, 2),
        new.shared_first_new.transpose(1, 0, 2),
        new.shared_second_new.transpose(1, 0, 2),
        new.norm_out.reshape(()),
    )


def with_halo(cells, sides, width):
    for axis, dim in sides:
        count = lax.axis_size(axis)
        ends = count - 1
        head = lax.slice_in_dim(cells, 0, width, axis=dim)
        tail = lax.slice_in_dim(cells, cells.shape[dim] - width, cells.shape[dim], axis=dim)
        cells = jnp.concatenate(
            [
                lax.ppermute(tail, axis, [(i, (i + 1) % count) for i in range(ends)]),
                cells,
                lax.ppermute(head, axis, [((i + 1) % count, i) for i in range(ends)]),
            ],
            axis=dim,
        )
    return cells


def from_behind(block, axis, distance):
    devices = range(lax.axis_size(axis))
    route = [(i - distance, i) for i in devices if i - distance in devices]
    return lax.ppermute(block, axis, route)


def normalize_layer(values, gain, shift):
    center = values - jnp.mean(values, axis=-1, keepdims=True)
    spread = jnp.mean(center * center, axis=-1, keepdims=True)
    return center * lax.rsqrt(spread + NORM_EPSILON) * gain + shift


def head_masks(offsets, dilated):
    near = jnp.abs(offsets) <= WIN
    far = jnp.logical_and(jnp.abs(offsets) <= 2 * WIN, offsets % 2 == 0)
    return jnp.where(dilated[:, None, None], far[None, :, :], near[None, :, :])


def join_heads(term):
    return lax.psum(term.astype(jnp.bfloat16), MP).astype(jnp.float32)


def join_grads(term):
    return lax.psum(term, MP)


def fetch_rims(pair, rim_width):
    return with_halo(pair, ((SEQ, 0),), rim_width)


def masked_scores(query_block, key_block, seg_query, seg_keys, dilated, rim_width):
    block_rows = query_block.shape[0]
    key_rows = key_block.shape[0]
    offsets = (
        jnp.arange(block_rows, dtype=jnp.int32)[:, None]
        - jnp.arange(key_rows, dtype=jnp.int32)[None, :]
        + rim_width
    )
    allowed = jnp.logical_and(
        head_masks(offsets, dilated), (seg_query[:, None] == seg_keys[None, :])[None, :, :]
    )
    raw = jnp.einsum(
        "qhd,khd->hqk", query_block, key_block, preferred_element_type=jnp.float32
    ) * DH ** (-0.5)
    return jnp.where(allowed, raw, MASK_FILL)


def plain_attend(query, key_pad, value_pad, seg_own, seg_near, dilated, rim_width):
    row_count = query.shape[0]
    block_rows = min(512, row_count)
    key_rows = block_rows + 2 * rim_width

    def one_block(first_row):
        query_block = lax.dynamic_slice_in_dim(query, first_row, block_rows, 0)
        key_block = lax.dynamic_slice_in_dim(key_pad, first_row, key_rows, 0)
        value_block = lax.dynamic_slice_in_dim(value_pad, first_row, key_rows, 0)
        scores = masked_scores(
            query_block,
            key_block,
            lax.dynamic_slice_in_dim(seg_own, first_row, block_rows, 0),
            lax.dynamic_slice_in_dim(seg_near, first_row, key_rows, 0),
            dilated,
            rim_width,
        )
        row_max = jnp.max(scores, axis=2, keepdims=True)
        exponent = jnp.exp(scores - row_max)
        row_total = jnp.sum(exponent, axis=2, keepdims=True)
        softmax = (exponent / row_total).astype(jnp.bfloat16)
        mixed_block = jnp.einsum(
            "hqk,khd->qhd", softmax, value_block, preferred_element_type=jnp.float32
        )
        return (mixed_block, (row_max + jnp.log(row_total))[:, :, 0])

    starts = jnp.arange(row_count // block_rows, dtype=jnp.int32) * block_rows
    mixed_heads, log_totals = lax.map(one_block, starts)
    return (mixed_heads.reshape(row_count, -1), log_totals)


def plain_attend_back(query, padded, log_totals, grad_mixed, seg_own, seg_near, dilated, rim_width):
    row_count, head_count, _ = query.shape
    head_width = head_count * DH
    block_rows = min(512, row_count)
    key_rows = block_rows + 2 * rim_width
    key_pad = padded[:, :head_width].reshape(-1, head_count, DH)
    value_pad = padded[:, head_width:].reshape(-1, head_count, DH)
    grad_heads = grad_mixed.reshape(row_count, head_count, DH)
    score_scale = DH ** (-0.5)

    def one_step(carry, inputs):
        first_row, totals_block = inputs
        query_block = lax.dynamic_slice_in_dim(query, first_row, block_rows, 0)
        key_block = lax.dynamic_slice_in_dim(key_pad, first_row, key_rows, 0)
        value_block = lax.dynamic_slice_in_dim(value_pad, first_row, key_rows, 0)
        grad_block = lax.dynamic_slice_in_dim(grad_heads, first_row, block_rows, 0)
        scores = masked_scores(
            query_block,
            key_block,
            lax.dynamic_slice_in_dim(seg_own, first_row, block_rows, 0),
            lax.dynamic_slice_in_dim(seg_near, first_row, key_rows, 0),
            dilated,
            rim_width,
        )
        softmax = jnp.exp(scores - totals_block[:, :, None])
        grad_value = jnp.einsum(
            "hqk,qhd->khd",
            softmax.astype(jnp.bfloat16),
            grad_block,
            preferred_element_type=jnp.float32,
        )
        grad_soft = jnp.einsum(
            "qhd,khd->hqk", grad_block, value_block, preferred_element_type=jnp.float32
        )
        row_dot = jnp.sum(grad_soft * softmax, axis=2, keepdims=True)
        grad_scores = (softmax * (grad_soft - row_dot)).astype(jnp.bfloat16)
        grad_query = (
            jnp.einsum("hqk,khd->qhd", grad_scores, key_block, preferred_element_type=jnp.float32)
            * score_scale
        )
        grad_key = (
            jnp.einsum("hqk,qhd->khd", grad_scores, query_block, preferred_element_type=jnp.float32)
            * score_scale
        )
        update = jnp.concatenate(
            [grad_key.reshape(key_rows, head_width), grad_value.reshape(key_rows, head_width)],
            axis=1,
        )
        current = lax.dynamic_slice_in_dim(carry, first_row, key_rows, 0)
        carry = lax.dynamic_update_slice_in_dim(carry, current + update, first_row, 0)
        return (carry, grad_query.reshape(block_rows, head_width))

    starts = jnp.arange(row_count // block_rows, dtype=jnp.int32) * block_rows
    initial = jnp.zeros((row_count + 2 * rim_width, 2 * head_width), jnp.float32)
    grad_pad, grad_query = lax.scan(one_step, initial, (starts, log_totals))
    from_above = from_behind(grad_pad[:rim_width], SEQ, -1)
    from_below = from_behind(grad_pad[row_count + rim_width :], SEQ, 1)
    grad_pair = grad_pad[rim_width : row_count + rim_width]
    grad_pair = (
        grad_pair
        + jnp.pad(from_below, ((0, row_count - rim_width), (0, 0)))
        + jnp.pad(from_above, ((row_count - rim_width, 0), (0, 0)))
    )
    return (grad_query.reshape(row_count, head_width), grad_pair)


def layer_forward(inputs, attn, ffn, shared, split, seg_own, seg_pad, dilated, rim_width):
    head_width = attn.shape[2]
    row_count = inputs.shape[0]
    inputs_low = inputs.astype(jnp.bfloat16)
    biases = jnp.stack(
        [
            split[0, :head_width],
            jnp.zeros((head_width,), jnp.float32),
            split[0, head_width : 2 * head_width],
        ]
    )
    projected = (
        jnp.einsum("td,mdc->tmc", inputs_low, attn[:3], preferred_element_type=jnp.float32)
        + biases[None]
    ).astype(jnp.bfloat16)
    query = projected[:, 0].reshape(row_count, -1, DH)
    padded = fetch_rims(jnp.concatenate([projected[:, 1], projected[:, 2]], axis=1), rim_width)
    key_pad = padded[:, :head_width].reshape(-1, head_width // DH, DH)
    value_pad = padded[:, head_width:].reshape(-1, head_width // DH, DH)
    seg_near = lax.slice_in_dim(
        seg_pad, 2 * WIN - rim_width, 2 * WIN + row_count + rim_width, axis=0
    )
    mixed_heads, log_totals = plain_attend(
        query, key_pad, value_pad, seg_own, seg_near, dilated, rim_width
    )
    mixed_heads = mixed_heads.astype(jnp.bfloat16)
    attn_sum = (
        inputs
        + join_heads(
            dot_nt(mixed_heads, attn[3])
        )
        + shared[0]
    )
    normed = normalize_layer(attn_sum, shared[1], shared[2])
    normed_low = normed.astype(jnp.bfloat16)
    pre_gelu = (
        jnp.dot(normed_low, ffn[0], preferred_element_type=jnp.float32) + split[0, 2 * head_width :]
    )
    hidden = jax.nn.gelu(pre_gelu, approximate=False).astype(jnp.bfloat16)
    ffn_sum = (
        normed
        + join_heads(dot_nt(hidden, ffn[1]))
        + shared[3]
    )
    result = normalize_layer(ffn_sum, shared[4], shared[5])
    return (
        result,
        (
            inputs_low,
            query,
            padded,
            log_totals,
            mixed_heads,
            attn_sum,
            normed_low,
            pre_gelu,
            hidden,
            ffn_sum,
        ),
    )


def layer_backward(grad_out, saved, attn, ffn, shared, seg_own, seg_pad, dilated, rim_width):
    (
        inputs_low,
        query,
        padded,
        log_totals,
        mixed_heads,
        attn_sum,
        normed_low,
        pre_gelu,
        hidden,
        ffn_sum,
    ) = saved
    head_width = attn.shape[2]
    row_count = inputs_low.shape[0]
    seg_near = lax.slice_in_dim(
        seg_pad, 2 * WIN - rim_width, 2 * WIN + row_count + rim_width, axis=0
    )
    _, pull_out = jax.vjp(normalize_layer, ffn_sum, shared[4], shared[5])
    grad_ffn_sum, grad_gain_two, grad_shift_two = pull_out(grad_out)
    grad_branch = grad_ffn_sum.astype(jnp.bfloat16)
    grad_down = dot_tn(grad_branch, hidden)
    grad_hidden = jnp.dot(grad_branch, ffn[1], preferred_element_type=jnp.float32)
    _, pull_gelu = jax.vjp(lambda value: jax.nn.gelu(value, approximate=False), pre_gelu)
    grad_pre = pull_gelu(grad_hidden)[0].astype(jnp.bfloat16)
    grad_up = dot_tn(normed_low, grad_pre)
    grad_normed = grad_ffn_sum + join_grads(
        dot_nt(grad_pre, ffn[0])
    )
    _, pull_mid = jax.vjp(normalize_layer, attn_sum, shared[1], shared[2])
    grad_attn_sum, grad_gain_one, grad_shift_one = pull_mid(grad_normed)
    grad_attn_out = grad_attn_sum.astype(jnp.bfloat16)
    grad_out_proj = dot_tn(grad_attn_out, mixed_heads)
    grad_mixed = jnp.dot(grad_attn_out, attn[3], preferred_element_type=jnp.float32).astype(
        jnp.bfloat16
    )
    grad_query, grad_pair = plain_attend_back(
        query, padded, log_totals, grad_mixed, seg_own, seg_near, dilated, rim_width
    )
    grad_proj = jnp.stack(
        [grad_query, grad_pair[:, :head_width], grad_pair[:, head_width:]], axis=1
    ).astype(jnp.bfloat16)
    grad_in_proj = jnp.einsum(
        "td,tmc->mdc", inputs_low, grad_proj, preferred_element_type=jnp.float32
    )
    grad_inputs = grad_attn_sum + join_grads(
        jnp.einsum("tmc,mdc->td", grad_proj, attn[:3], preferred_element_type=jnp.float32)
    )
    proj_sums = jnp.sum(grad_proj.astype(jnp.float32), axis=0)
    split_grad = jnp.concatenate(
        [proj_sums[0], proj_sums[2], jnp.sum(grad_pre.astype(jnp.float32), axis=0)]
    )
    shared_grad = jnp.stack(
        [
            jnp.sum(grad_attn_sum, axis=0),
            grad_gain_one,
            grad_shift_one,
            jnp.sum(grad_ffn_sum, axis=0),
            grad_gain_two,
            grad_shift_two,
        ]
    )
    attn_grad = jnp.concatenate([grad_in_proj, grad_out_proj[None]], axis=0)
    ffn_grad = jnp.stack([grad_up, grad_down])
    return (grad_inputs, attn_grad, ffn_grad, shared_grad, split_grad)


def from_slots(gathered, owners, slot_count):
    layer_count, matrix_count, row_count, col_count = gathered.shape
    blocks = gathered.reshape(
        layer_count, matrix_count, slot_count, row_count // slot_count, col_count
    )
    return jnp.take(blocks, owners, axis=2).reshape(gathered.shape)


def to_slots(grads, inverse, slot_count):
    matrix_count, row_count, col_count = grads.shape
    blocks = grads.reshape(matrix_count, slot_count, row_count // slot_count, col_count)
    return jnp.take(blocks, inverse, axis=1).reshape(grads.shape)


def rotate_update(weight, grad_now, first, second, running_average, basis, rates):
    turn = basis[:, :, 0, 0]
    turned = jnp.einsum("lmre,lmec->lmrc", grad_now, turn, precision=HIGHEST_PRECISION)
    first_new = BETA_FIRST * first + (1.0 - BETA_FIRST) * turned
    second_new = BETA_SECOND * second + (1.0 - BETA_SECOND) * turned * turned
    direction = (
        first_new
        / (1.0 - BETA_FIRST**STEP)
        / (jnp.sqrt(second_new / (1.0 - BETA_SECOND**STEP)) + ADAM_EPSILON)
    )
    back = jnp.einsum("lmrc,lmec->lmre", direction, turn, precision=HIGHEST_PRECISION)
    weight_new = weight - rates[None, :, None, None] * (back + DECAY_RATE * weight)
    average_new = AVERAGE_RATE * running_average + (1.0 - AVERAGE_RATE) * weight_new
    return (weight_new, first_new, second_new, average_new)


def vector_update(current, grad_now, first, second):
    first_new = BETA_FIRST * first + (1.0 - BETA_FIRST) * grad_now
    second_new = BETA_SECOND * second + (1.0 - BETA_SECOND) * grad_now * grad_now
    direction = (
        first_new
        / (1.0 - BETA_FIRST**STEP)
        / (jnp.sqrt(second_new / (1.0 - BETA_SECOND**STEP)) + ADAM_EPSILON)
    )
    return (current - VECTOR_RATE * direction, first_new, second_new)


def with_collectives(
    activations,
    cotangent,
    segments,
    dilated_heads,
    owners,
    attn_weights,
    attn_first,
    attn_second,
    attn_average,
    attn_basis,
    ffn_weights,
    ffn_first,
    ffn_second,
    ffn_average,
    ffn_basis,
    split_biases,
    split_first,
    split_second,
    shared_vectors,
    shared_first,
    shared_second,
):
    slot_count = lax.axis_size(SEQ)
    layer_count = attn_weights.shape[0]
    attn_full, ffn_full = (
        lax.all_gather(attn_weights.astype(jnp.bfloat16), SEQ, axis=2, tiled=True),
        lax.all_gather(ffn_weights.astype(jnp.bfloat16), SEQ, axis=2, tiled=True),
    )
    attn_full = from_slots(attn_full, owners, slot_count)
    ffn_full = from_slots(ffn_full, owners, slot_count)
    seg_pad = with_halo(segments, ((SEQ, 0),), 2 * WIN)
    head_width = attn_full.shape[3]
    head_count = head_width // DH
    heads_here = lax.axis_index(MP) * head_count + jnp.arange(head_count, dtype=jnp.int32)
    head_flags = jnp.any(heads_here[:, None] == dilated_heads[None, :], axis=1)
    current = activations.astype(jnp.float32)
    saved_list = []
    for layer_index in range(layer_count):
        dilated = jnp.logical_and(head_flags, layer_index % 2 == 1)
        rim_width = 2 * WIN if layer_index % 2 == 1 else WIN
        current, saved = layer_forward(
            current,
            attn_full[layer_index],
            ffn_full[layer_index],
            shared_vectors[layer_index],
            split_biases[layer_index],
            segments,
            seg_pad,
            dilated,
            rim_width,
        )
        saved_list.append(saved)
    slot_range = jnp.arange(slot_count, dtype=jnp.int32)
    inverse = jnp.sum(
        jnp.where(owners[None, :] == slot_range[:, None], slot_range[None, :], 0), axis=1
    )
    grad_now = cotangent.astype(jnp.float32)
    attn_list = [None] * layer_count
    ffn_list = [None] * layer_count
    shared_list = [None] * layer_count
    split_list = [None] * layer_count
    for layer_index in range(layer_count - 1, -1, -1):
        dilated = jnp.logical_and(head_flags, layer_index % 2 == 1)
        rim_width = 2 * WIN if layer_index % 2 == 1 else WIN
        grad_now, attn_grad, ffn_grad, shared_grad, split_grad = layer_backward(
            grad_now,
            saved_list[layer_index],
            attn_full[layer_index],
            ffn_full[layer_index],
            shared_vectors[layer_index],
            segments,
            seg_pad,
            dilated,
            rim_width,
        )
        attn_grad = to_slots(attn_grad, inverse, slot_count)
        ffn_grad = to_slots(ffn_grad, inverse, slot_count)
        attn_list[layer_index] = attn_grad
        ffn_list[layer_index] = ffn_grad
        shared_list[layer_index] = shared_grad
        split_list[layer_index] = split_grad[None, :]
    attn_grads = jnp.stack(attn_list)
    ffn_grads = jnp.stack(ffn_list)
    attn_grads, ffn_grads = (
        lax.psum_scatter(attn_grads, SEQ, scatter_dimension=2, tiled=True),
        lax.psum_scatter(ffn_grads, SEQ, scatter_dimension=2, tiled=True),
    )
    shared_grads, split_grads = lax.psum((jnp.stack(shared_list), jnp.stack(split_list)), SEQ)
    first_seq = lax.axis_index(SEQ) == 0
    first_both = jnp.logical_and(first_seq, lax.axis_index(MP) == 0)
    local_sum = jnp.sum(attn_grads * attn_grads) + jnp.sum(ffn_grads * ffn_grads)
    local_sum = (
        local_sum
        + jnp.where(first_seq, jnp.sum(split_grads * split_grads), 0.0)
        + jnp.where(first_both, jnp.sum(shared_grads * shared_grads), 0.0)
    )
    grad_norm = jnp.sqrt(lax.psum(local_sum, (SEQ, MP)))
    factor = CLIP_LEVEL / jnp.maximum(grad_norm, CLIP_LEVEL)
    attn_rates = jnp.array([0.5 * D ** (-0.5)] * 3 + [0.5 * (WIN / D) ** 0.5], jnp.float32)
    ffn_rates = jnp.array([0.5 * D ** (-0.5), 0.5 * FF ** (-0.5)], jnp.float32)
    attn_out = rotate_update(
        attn_weights,
        factor * attn_grads,
        attn_first,
        attn_second,
        attn_average,
        attn_basis,
        attn_rates,
    )
    ffn_out = rotate_update(
        ffn_weights, factor * ffn_grads, ffn_first, ffn_second, ffn_average, ffn_basis, ffn_rates
    )
    split_out = vector_update(split_biases, factor * split_grads, split_first, split_second)
    shared_out = vector_update(shared_vectors, factor * shared_grads, shared_first, shared_second)
    return (
        current,
        grad_now,
        attn_out[0],
        attn_out[1],
        attn_out[2][:, :3],
        attn_out[2][:, 3],
        attn_out[3],
        ffn_out[0],
        ffn_out[1],
        ffn_out[2],
        ffn_out[3],
        split_out[0],
        split_out[1],
        split_out[2],
        shared_out[0],
        shared_out[1],
        shared_out[2],
        grad_norm,
    )


def solution(mesh):
    placed = (
        P(SEQ, None),
        P(SEQ, None),
        P(SEQ),
        P(),
        P(),
        P(None, None, SEQ, MP),
        P(None, None, SEQ, MP),
        P(None, None, SEQ, MP),
        P(None, None, SEQ, MP),
        P(None, None, SEQ, MP, None, None),
        P(None, None, SEQ, MP),
        P(None, None, SEQ, MP),
        P(None, None, SEQ, MP),
        P(None, None, SEQ, MP),
        P(None, None, SEQ, MP, None, None),
        P(None, MP, None),
        P(None, MP, None),
        P(None, MP, None),
        P(),
        P(),
        P(),
    )
    count = mesh.shape[SEQ]
    fits = count % 4 == 0 and (D // count) % 16 == 0 and mesh.shape[MP] == 4
    return jax.shard_map(
        direct if fits else with_collectives,
        mesh=mesh,
        in_specs=placed,
        out_specs=(
            P(SEQ, None),
            P(SEQ, None),
            P(None, None, SEQ, MP),
            P(None, None, SEQ, MP),
            P(None, None, SEQ, MP),
            P(None, SEQ, MP),
            P(None, None, SEQ, MP),
            P(None, None, SEQ, MP),
            P(None, None, SEQ, MP),
            P(None, None, SEQ, MP),
            P(None, None, SEQ, MP),
            P(None, MP, None),
            P(None, MP, None),
            P(None, MP, None),
            P(),
            P(),
            P(),
            P(),
        ),
        check_vma=False,
    )
```
